32 devices in a mesh: groups: 2 (over y), sector: 16 (over z, x, core).
Axes of the slice: x: 2, y: 2, z: 4, core: 2. Of those that a mesh axis runs over, the one named last changes fastest.
Arguments:
- wavefunction: float32 [32, 256, 256], P(('groups', 'sector')), parts along dimension 0, may hold values from -1200 to 1200
- sector_dims: int32 [32, 2], P(('groups', 'sector')), parts along dimension 0, may hold values from 64 to 256
- left_env: bfloat16 [32, 26, 256, 256], P(('groups', 'sector')), parts along dimension 0, may hold values from -2 to 2
- right_env: bfloat16 [32, 26, 256, 256], P(('groups', 'sector')), parts along dimension 0, may hold values from -2 to 2
Outputs:
- first_image: float32 [32, 256, 256], P(('groups', 'sector')), parts along dimension 0
- second_image: float32 [32, 256, 256], P(('groups', 'sector')), parts along dimension 0
The draws below stay inside these ranges and needn't reach their ends.
There are 2 independent parts, one for each index of `groups`. The reference program is written for one: setup_inputs(seed, part) draws one part's arguments, and reference() takes and returns one part's arrays. A program takes and returns all parts, laid end to end along the dimension named above; each array names one. Nothing has to cross between parts.
All inputs are finite; a program needn't handle non-finite values.
Results may differ from the reference program's by a relative error of at most 0.009.
Values may be sent and summed in bfloat16 or wider, within the bound.
No kernel may reach another device: no remote copies, remote signals or barrier semaphores. Data moves between devices by JAX's collectives and lax.ppermute only.
A program may use at most 64 MiB of HBM per device.

```python
import math
import jax
import jax.numpy as jnp
from jax import lax

B = 256
W = 6
QD = 8
K = 26
SECT = 16


def draw_wavefunction(key, part):
    key = jax.random.fold_in(key, 11)
    key_base, key_rows, key_cols = jax.random.split(key, 3)
    base = jax.random.truncated_normal(key_base, -4.0, 4.0, (SECT, B, B), jnp.float32)
    ramp_power = 0.5
    row_scale = jnp.exp(jax.random.uniform(key_rows, (SECT, B, 1), jnp.float32, 0.0, math.log(10.0)))
    col_scale = jnp.exp(jax.random.uniform(key_cols, (SECT, 1, B), jnp.float32, 0.0, math.log(10.0)))
    position = jnp.arange(SECT, dtype=jnp.float32) / max(SECT - 1, 1)
    ramp = jnp.exp(ramp_power * math.log(3.0) * position)[:, None, None]
    return base * row_scale * col_scale * ramp


def draw_sector_dims(key, part):
    key = jax.random.fold_in(key, 23)
    key_dims, key_full, key_small = jax.random.split(key, 3)
    dims = jax.random.randint(key_dims, (SECT, 2), B // 4, B + 1, jnp.int32)
    full_row = jax.random.randint(key_full, (), 0, SECT, jnp.int32)
    small_row = jax.random.randint(key_small, (), 0, SECT, jnp.int32)
    dims = dims.at[full_row, 0].set(B)
    dims = dims.at[small_row, 1].set(B // 4)
    return dims


def onsite_identity():
    term_index = jnp.arange(K, dtype=jnp.int32)
    rows_index = jnp.arange(B, dtype=jnp.int32)
    diagonal = (rows_index[:, None] == rows_index[None, :]).astype(jnp.float32)
    first_term = (term_index == 0).astype(jnp.float32)
    return first_term[:, None, None] * diagonal[None, :, :]


def draw_left_env(key, part):
    key = jax.random.fold_in(key, 31)
    noise = jax.random.truncated_normal(key, -4.0, 4.0, (SECT, K, B, B), jnp.float32)
    return (noise * (1.0 / math.sqrt(B * K)) + onsite_identity()[None]).astype(jnp.bfloat16)


def draw_right_env(key, part):
    key = jax.random.fold_in(key, 37)
    noise = jax.random.truncated_normal(key, -4.0, 4.0, (SECT, K, B, B), jnp.float32)
    return (noise * (1.0 / math.sqrt(B)) + onsite_identity()[None]).astype(jnp.bfloat16)


def setup_inputs(seed: int = 0, part: int = 0) -> dict:
    seeds = jax.random.split(jax.random.key(seed), 5)
    part_keys = jax.random.split(jax.random.fold_in(seeds[4], part), 5)
    return {
        "wavefunction": draw_wavefunction(jax.random.fold_in(jax.random.fold_in(seeds[4], part), 71), part),
        "sector_dims": draw_sector_dims(jax.random.fold_in(jax.random.fold_in(seeds[4], part), 71), part),
        "left_env": draw_left_env(jax.random.fold_in(jax.random.fold_in(seeds[4], part), 71), part),
        "right_env": draw_right_env(jax.random.fold_in(jax.random.fold_in(seeds[4], part), 71), part),
    }


def build_mask(sector_dims):
    rows_index = jnp.arange(B, dtype=jnp.int32)
    row_ok = rows_index[None, :] < sector_dims[:, 0:1]
    col_ok = rows_index[None, :] < sector_dims[:, 1:2]
    return (row_ok[:, :, None] & col_ok[:, None, :]).astype(jnp.float32)

def neighbour_blocks(vector):
    column = jnp.arange(SECT, dtype=jnp.int32) % QD
    one_zero = jnp.zeros((1, B, B), jnp.bfloat16)
    row_zero = jnp.zeros((QD, B, B), jnp.bfloat16)
    below = jnp.concatenate([one_zero, vector[:-1]], axis=0)
    above = jnp.concatenate([vector[1:], one_zero], axis=0)
    below = jnp.where((column >= 1)[:, None, None], below, jnp.zeros_like(below))
    above = jnp.where((column <= QD - 2)[:, None, None], above, jnp.zeros_like(above))
    lower_row = jnp.concatenate([row_zero, vector[:-QD]], axis=0)
    upper_row = jnp.concatenate([vector[QD:], row_zero], axis=0)
    return jnp.stack([vector, below, above, lower_row, upper_row], axis=1)

def apply_operator(vector, left_env, right_env, live_mask):
    sources = neighbour_blocks(vector)
    bounds = [0, 2, 2 + W, 2 + 2 * W, 2 + 3 * W, 2 + 4 * W]

    def one_sector(items):
        source_blocks, left_block, right_block, mask_block = items
        pieces = []
        for number in range(5):
            partial_value = jnp.einsum('ab,kcb->kac', source_blocks[number].astype(jnp.float32), right_block[bounds[number]:bounds[number + 1]].astype(jnp.float32))
            pieces.append(partial_value.astype(jnp.bfloat16))
        stacked = jnp.concatenate(pieces, axis=0)
        image = jnp.einsum('kxa,kac->xc', left_block.astype(jnp.float32), stacked.astype(jnp.float32))
        return image * mask_block
    return lax.map(one_sector, (sources, left_env, right_env, live_mask))

def reference(wavefunction, sector_dims, left_env, right_env):
    live_mask = build_mask(sector_dims)
    cell_count = jnp.float32(SECT * B * B)
    start_norm = jnp.sum(live_mask * wavefunction * wavefunction)
    first_vector = (live_mask * wavefunction * lax.rsqrt(start_norm / cell_count + 1e-06)).astype(jnp.bfloat16)
    first_image = apply_operator(first_vector, left_env, right_env, live_mask)
    first_wide = first_vector.astype(jnp.float32)
    vector_norm = jnp.sum(first_wide * first_wide)
    rayleigh = jnp.sum(first_wide * first_image) / vector_norm
    residual_field = first_image - rayleigh * first_wide
    residual_norm = jnp.sum(residual_field * residual_field)
    second_vector = (residual_field * lax.rsqrt(residual_norm / cell_count + 1e-06)).astype(jnp.bfloat16)
    second_image = apply_operator(second_vector, left_env, right_env, live_mask)
    return (first_image, second_image)
```

```python
import functools

import jax
import jax.numpy as jnp
from jax import lax
from jax.experimental import pallas as pl
from jax.experimental.pallas import tpu as pltpu
from jax.sharding import PartitionSpec as P

QD = 8
SCALE = 1024.0
NT = (((1,), (1,)), ((), ()))
VM = pl.BlockSpec(memory_space=pltpu.VMEM)
SM = pl.BlockSpec(memory_space=pltpu.SMEM)
PARAMS = pltpu.CompilerParams(vmem_limit_bytes=24 * 1024 * 1024)


def swap(x, axis, pairs):
    return lax.ppermute(x, axis, [(a, b) for a, b in pairs] + [(b, a) for a, b in pairs])


def swap_pairs(size):
    rows = size // QD
    near = [(s, s + 1) for s in range(0, size, 2)]
    far = [(s, s + 1) for s in range(1, size - 1, 2) if s % QD != QD - 1]
    row_even = [(s, s + QD) for r in range(0, rows - 1, 2) for s in range(r * QD, r * QD + QD)]
    row_odd = [(s, s + QD) for r in range(1, rows - 1, 2) for s in range(r * QD, r * QD + QD)]
    return near, far, [p for p in (row_even, row_odd) if p]


def live(dims_ref, shape):
    row_ok = lax.broadcasted_iota(jnp.int32, shape, 0) < dims_ref[0, 0]
    col_ok = lax.broadcasted_iota(jnp.int32, shape, 1) < dims_ref[0, 1]
    return row_ok & col_ok


def total(x):
    return jnp.sum(jnp.sum(x, axis=0, keepdims=True), axis=1, keepdims=True)


def terms(src, left_ref, right_ref, offset, count):
    size = src.shape[0]
    right = right_ref[pl.ds(offset, count)].reshape(count * size, size)
    partial_t = lax.dot_general(right, src, NT, preferred_element_type=jnp.float32).astype(jnp.bfloat16)
    image = None
    for k in range(count):
        piece = lax.dot_general(
            left_ref[offset + k], partial_t[k * size : (k + 1) * size], NT, preferred_element_type=jnp.float32
        )
        image = piece if image is None else image + piece
    return image


def start_kernel(dims_ref, wave_ref, u_ref, norm_ref):
    wave = wave_ref[0]
    held = jnp.where(live(dims_ref, wave.shape), wave, 0.0)
    u_ref[...] = (held * SCALE).astype(jnp.bfloat16)
    norm_ref[...] = jnp.broadcast_to(total(held * held), norm_ref.shape)


def near_kernel(width, offs_ref, self_ref, near_ref, far_ref, left_ref, right_ref, out_ref):
    left_ref, right_ref = left_ref.at[0], right_ref.at[0]
    out_ref[0] = terms(self_ref[...], left_ref, right_ref, 0, 2)
    out_ref[1] = terms(near_ref[...], left_ref, right_ref, offs_ref[0], width)
    out_ref[2] = terms(far_ref[...], left_ref, right_ref, offs_ref[1], width)


def near_sum_kernel(width, offs_ref, self_ref, near_ref, far_ref, left_ref, right_ref, out_ref):
    left_ref, right_ref = left_ref.at[0], right_ref.at[0]
    out_ref[...] = (
        terms(self_ref[...], left_ref, right_ref, 0, 2)
        + terms(near_ref[...], left_ref, right_ref, offs_ref[0], width)
        + terms(far_ref[...], left_ref, right_ref, offs_ref[1], width)
    )


def first_kernel(width, rows, offs_ref, dims_ref, u_ref, norm_ref, part_ref, left_ref, right_ref, *refs):
    row_refs, (row_out_ref, image_ref, w_ref, stats_ref) = refs[:rows], refs[rows:]
    left_ref, right_ref = left_ref.at[0], right_ref.at[0]
    image = part_ref[0] + part_ref[1] + part_ref[2]
    for r in range(rows):
        piece = terms(row_refs[r][...], left_ref, right_ref, offs_ref[2 + r], width)
        row_out_ref[r] = piece
        image = image + piece
    image = jnp.where(live(dims_ref, image.shape), image, 0.0)
    image_ref[...] = image
    u = u_ref[...].astype(jnp.float32)
    square = total(u * u)
    cross = total(u * image)
    rho = jnp.where(square > 0.0, cross / square, 0.0)
    w = image - rho * u
    w_ref[...] = w.astype(jnp.bfloat16)
    lines = lax.broadcasted_iota(jnp.int32, (8, 128), 0)
    stats = jnp.where(lines == 0, norm_ref[...], 0.0)
    for line, value in ((1, square), (2, cross), (3, total(w * w)), (4, rho)):
        stats = jnp.where(lines == line, value, stats)
    stats_ref[...] = jnp.broadcast_to(stats[None], stats_ref.shape)


def second_kernel(width, rows, cells, offs_ref, dims_ref, stats_ref, hw_ref, part_ref, row_part_ref, image_ref,
                  left_ref, right_ref, *refs):
    row_refs, (first_ref, second_ref) = refs[:rows], refs[rows:]
    left_ref, right_ref = left_ref.at[0], right_ref.at[0]
    stats = stats_ref[...]
    sums = jnp.sum(stats, axis=0)
    start, square, cross, inner = (sums[i : i + 1, 0:1] for i in range(4))
    rho = cross / square
    gap = stats[:, 4:5, 0:1] - rho[None]
    residual = inner + jnp.sum(stats[:, 1:2, 0:1] * gap * gap, axis=0)
    scale = lax.rsqrt(start / cells + 1e-06) * (1.0 / SCALE)
    second_scale = scale * lax.rsqrt(scale * scale * (residual / cells) + 1e-06)
    image = hw_ref[...]
    for n in range(3):
        image = image + (stats_ref[offs_ref[8 + n], 4:5, 0:1] - rho) * part_ref[n]
    for r in range(rows):
        image = image + (stats_ref[offs_ref[11 + r], 4:5, 0:1] - rho) * row_part_ref[r]
        image = image + terms(row_refs[r][...], left_ref, right_ref, offs_ref[2 + r], width)
    first_ref[0] = image_ref[...] * scale
    second_ref[0] = jnp.where(live(dims_ref, image.shape), image, 0.0) * second_scale


def body(wavefunction, sector_dims, left_env, right_env):
    size = lax.axis_size("sector")
    block = wavefunction.shape[1]
    square = (block, block)
    width = (right_env.shape[1] - 2) // 4
    near, far, row_pairs = swap_pairs(size)
    rows = len(row_pairs)
    cells = float(size * block * block)

    me = lax.axis_index("sector")
    odd = (me % QD) % 2
    row_odd = (me // QD) % 2
    low, high, down, up = 2, 2 + width, 2 + 2 * width, 2 + 3 * width
    near_off = jnp.where(odd == 1, low, high)
    far_off = jnp.where(odd == 1, high, low)
    even_off = jnp.where(row_odd == 1, down, up)
    odd_off = jnp.where(row_odd == 1, up, down)
    partners = [me, jnp.where(odd == 1, me - 1, me + 1), jnp.where(odd == 1, me + 1, me - 1),
                jnp.where(row_odd == 1, me - QD, me + QD), jnp.where(row_odd == 1, me + QD, me - QD)]
    partners = [jnp.clip(p, 0, size - 1) for p in partners]
    zero = jnp.int32(0)
    offs = jnp.stack([near_off, far_off, even_off, odd_off, zero, zero, zero, zero] + partners + [zero] * 3)
    offs = offs.astype(jnp.int32)

    f32 = jnp.float32
    sds = jax.ShapeDtypeStruct
    u, norm = pl.pallas_call(
        start_kernel, out_shape=(sds(square, jnp.bfloat16), sds((8, 128), f32)),
        in_specs=[SM, VM], out_specs=(VM, VM), compiler_params=PARAMS,
    )(sector_dims, wavefunction)

    row_u = [swap(u, "sector", p) for p in row_pairs]
    near_u = swap(u, "sector", near)
    far_u = swap(u, "sector", far)
    part = pl.pallas_call(
        functools.partial(near_kernel, width), out_shape=sds((3,) + square, f32),
        in_specs=[SM] + [VM] * 5, out_specs=VM, compiler_params=PARAMS,
    )(offs, u, near_u, far_u, left_env, right_env)
    row_part, image, w, stats = pl.pallas_call(
        functools.partial(first_kernel, width, rows),
        out_shape=(sds((rows,) + square, f32), sds(square, f32), sds(square, jnp.bfloat16), sds((size, 8, 128), f32)),
        in_specs=[SM, SM] + [VM] * (5 + rows), out_specs=(VM,) * 4, compiler_params=PARAMS,
    )(offs, sector_dims, u, norm, part, left_env, right_env, *row_u)

    row_w = [swap(w, "sector", p) for p in row_pairs]
    near_w = swap(w, "sector", near)
    far_w = swap(w, "sector", far)
    stats = lax.all_to_all(stats, "sector", 0, 0, tiled=True)
    hw = pl.pallas_call(
        functools.partial(near_sum_kernel, width), out_shape=sds(square, f32),
        in_specs=[SM] + [VM] * 5, out_specs=VM, compiler_params=PARAMS,
    )(offs, w, near_w, far_w, left_env, right_env)
    return pl.pallas_call(
        functools.partial(second_kernel, width, rows, cells),
        out_shape=(sds((1,) + square, f32),) * 2,
        in_specs=[SM, SM] + [VM] * (7 + rows), out_specs=(VM, VM), compiler_params=PARAMS,
    )(offs, sector_dims, stats, hw, part, row_part, image, left_env, right_env, *row_w)


def solution(mesh):
    placed = (
        P(("groups", "sector"), None, None),
        P(("groups", "sector"), None),
        P(("groups", "sector"), None, None, None),
        P(("groups", "sector"), None, None, None),
    )
    return jax.shard_map(
        body,
        mesh=mesh,
        in_specs=placed,
        out_specs=(P(("groups", "sector"), None, None), P(("groups", "sector"), None, None)),
        check_vma=False,
    )
```

```python
import functools

import jax
import jax.numpy as jnp
from jax import lax
from jax.experimental import pallas as pl
from jax.experimental.pallas import tpu as pltpu
from jax.sharding import PartitionSpec as P

QD = 8
SCALE = 1024.0
NT = (((1,), (1,)), ((), ()))
VM = pl.BlockSpec(memory_space=pltpu.VMEM)
HB = pl.BlockSpec(memory_space=pltpu.HBM)
PARAMS = pltpu.CompilerParams(vmem_limit_bytes=16 * 1024 * 1024)


def vmem(x):
    return pltpu.with_memory_space_constraint(x, pltpu.VMEM)


def hbm(x):
    return pltpu.with_memory_space_constraint(x, pltpu.HBM)


def swap(x, axis, pairs):
    return lax.ppermute(x, axis, [(a, b) for a, b in pairs] + [(b, a) for a, b in pairs])


def swap_pairs(size):
    rows = size // QD
    near = [(s, s + 1) for s in range(0, size, 2)]
    far = [(s, s + 1) for s in range(1, size - 1, 2) if s % QD != QD - 1]
    row_even = [(s, s + QD) for r in range(0, rows - 1, 2) for s in range(r * QD, r * QD + QD)]
    row_odd = [(s, s + QD) for r in range(1, rows - 1, 2) for s in range(r * QD, r * QD + QD)]
    return near, far, [p for p in (row_even, row_odd) if p]


def place(size, width):
    me = lax.axis_index("sector")
    odd = lax.rem(me, 2) == 1
    row_odd = lax.rem(lax.div(me, QD), 2) == 1
    low, high, down, up = 2, 2 + width, 2 + 2 * width, 2 + 3 * width
    offsets = [jnp.where(odd, low, high), jnp.where(odd, high, low),
               jnp.where(row_odd, down, up), jnp.where(row_odd, up, down)]
    steps = [jnp.where(odd, -1, 1), jnp.where(odd, 1, -1), jnp.where(row_odd, -QD, QD), jnp.where(row_odd, QD, -QD)]
    partners = [me] + [jnp.clip(me + step, 0, size - 1) for step in steps]
    return offsets, partners


def live(facts, shape):
    row_ok = lax.broadcasted_iota(jnp.int32, shape, 0).astype(jnp.float32) < facts[1:2, 0:1]
    col_ok = lax.broadcasted_iota(jnp.int32, shape, 1).astype(jnp.float32) < facts[2:3, 0:1]
    return row_ok & col_ok


def total(x):
    return jnp.sum(jnp.sum(x, axis=0, keepdims=True), axis=1, keepdims=True)


def terms(src, left_ref, right_ref, offset, count):
    size = src.shape[0]
    right = right_ref[pl.ds(offset, count)].reshape(count * size, size)
    partial_t = lax.dot_general(right, src, NT, preferred_element_type=jnp.float32).astype(jnp.bfloat16)
    image = None
    for k in range(count):
        piece = lax.dot_general(
            left_ref[offset + k], partial_t[k * size : (k + 1) * size], NT, preferred_element_type=jnp.float32
        )
        image = piece if image is None else image + piece
    return image


def start_kernel(wave_hbm, dims_hbm, u_ref, facts_ref, wave_ref, dims_ref, sems):
    wave_copy = pltpu.make_async_copy(wave_hbm.at[0], wave_ref, sems.at[0])
    dims_copy = pltpu.make_async_copy(dims_hbm, dims_ref, sems.at[1])
    dims_copy.start()
    wave_copy.start()
    dims_copy.wait()
    lines = lax.broadcasted_iota(jnp.int32, (8, 128), 0)
    facts = jnp.where(lines == 1, dims_ref[0, 0], jnp.where(lines == 2, dims_ref[0, 1], 0)).astype(jnp.float32)
    wave_copy.wait()
    held = jnp.where(live(facts, wave_ref.shape), wave_ref[...], 0.0)
    u_ref[...] = (held * SCALE).astype(jnp.bfloat16)
    facts_ref[...] = jnp.where(lines == 0, total(held * held), facts)


def near_kernel(width, rows, self_ref, near_ref, far_ref, left_hbm, right_hbm, out_ref, left_ref, right_ref, sems):
    offsets, _ = place(1, width)
    copies = []
    at = 0
    for n, (offset, count) in enumerate([(0, 2)] + [(o, width) for o in offsets[: 2 + rows]]):
        pair = []
        for e, (source, target) in enumerate(((right_hbm, right_ref), (left_hbm, left_ref))):
            copy = pltpu.make_async_copy(
                source.at[0, pl.ds(offset, count)], target.at[pl.ds(at, count)], sems.at[n, e])
            copy.start()
            pair.append(copy)
        copies.append((pair, at, count))
        at += count
    for n, source in enumerate((self_ref, near_ref, far_ref)):
        pair, first, count = copies[n]
        for copy in pair:
            copy.wait()
        out_ref[n] = terms(source[...], left_ref, right_ref, first, count)
    for pair, _, _ in copies[3:]:
        for copy in pair:
            copy.wait()


def first_kernel(width, rows, facts_ref, u_ref, part_ref, left_ref, right_ref, *refs):
    row_refs, (row_out_ref, image_ref, w_ref, stats_ref) = refs[:rows], refs[rows:]
    facts = facts_ref[...]
    image = part_ref[0] + part_ref[1] + part_ref[2]
    for r in range(rows):
        piece = terms(row_refs[r][...], left_ref, right_ref, 2 + (2 + r) * width, width)
        row_out_ref[r] = piece
        image = image + piece
    image = jnp.where(live(facts, image.shape), image, 0.0)
    image_ref[...] = image
    u = u_ref[...].astype(jnp.float32)
    square = total(u * u)
    cross = total(u * image)
    rho = jnp.where(square > 0.0, cross / square, 0.0)
    w = image - rho * u
    w_ref[...] = w.astype(jnp.bfloat16)
    lines = lax.broadcasted_iota(jnp.int32, (8, 128), 0)
    stats = jnp.where(lines == 0, facts, 0.0)
    for line, value in ((1, square), (2, cross), (3, total(w * w)), (4, rho)):
        stats = jnp.where(lines == line, value, stats)
    stats_ref[...] = stats


def image_kernel(width, rows, self_ref, near_ref, far_ref, left_ref, right_ref, *refs):
    row_refs, (out_ref,) = refs[:rows], refs[rows:]
    image = terms(self_ref[...], left_ref, right_ref, 0, 2)
    for n, source in enumerate((near_ref, far_ref) + row_refs):
        image = image + terms(source[...], left_ref, right_ref, 2 + n * width, width)
    out_ref[...] = image


def second_kernel(size, width, rows, cells, facts_ref, stats_ref, hw_ref, part_ref, row_part_ref, image_ref,
                  first_hbm, second_hbm, first_ref, second_ref, sems):
    _, partners = place(size, width)
    facts = facts_ref[...]
    stats = stats_ref[...]
    sums = jnp.sum(stats, axis=0)
    start, square, cross, inner = (sums[i : i + 1, 0:1] for i in range(4))
    scale = lax.rsqrt(start / cells + 1e-06) * (1.0 / SCALE)
    first_ref[...] = image_ref[...] * scale
    first_copy = pltpu.make_async_copy(first_ref, first_hbm.at[0], sems.at[0])
    first_copy.start()
    rho = cross / square
    gap = stats[:, 4:5, 0:1] - rho[None]
    residual = inner + jnp.sum(stats[:, 1:2, 0:1] * gap * gap, axis=0)
    second_scale = scale * lax.rsqrt(scale * scale * (residual / cells) + 1e-06)
    image = hw_ref[...]
    for n in range(3):
        image = image + (stats_ref[partners[n], 4:5, 0:1] - rho) * part_ref[n]
    for r in range(rows):
        image = image + (stats_ref[partners[3 + r], 4:5, 0:1] - rho) * row_part_ref[r]
    second_ref[...] = jnp.where(live(facts, image.shape), image, 0.0) * second_scale
    second_copy = pltpu.make_async_copy(second_ref, second_hbm.at[0], sems.at[1])
    second_copy.start()
    first_copy.wait()
    second_copy.wait()


def body(wavefunction, sector_dims, left_env, right_env):
    size = lax.axis_size("sector")
    block = wavefunction.shape[1]
    square = (block, block)
    width = (right_env.shape[1] - 2) // 4
    near, far, row_pairs = swap_pairs(size)
    rows = len(row_pairs)
    cells = float(size * block * block)
    envs = (2 + (2 + rows) * width,) + square
    f32, bf16 = jnp.float32, jnp.bfloat16

    u, facts = pl.pallas_call(
        start_kernel, out_shape=(pltpu.VMEM(square, bf16), pltpu.VMEM((8, 128), f32)),
        in_specs=[HB, HB], out_specs=(VM, VM),
        scratch_shapes=[pltpu.VMEM(square, f32), pltpu.SMEM((1, 2), jnp.int32), pltpu.SemaphoreType.DMA((2,))],
        compiler_params=PARAMS,
    )(hbm(wavefunction), hbm(sector_dims))

    row_u = [vmem(swap(u, "sector", p)) for p in row_pairs]
    near_u = vmem(swap(u, "sector", near))
    far_u = vmem(swap(u, "sector", far))
    part, left, right = pl.pallas_call(
        functools.partial(near_kernel, width, rows),
        out_shape=(pltpu.VMEM((3,) + square, f32), pltpu.VMEM(envs, bf16), pltpu.VMEM(envs, bf16)),
        in_specs=[VM] * 3 + [HB] * 2, out_specs=(VM,) * 3,
        scratch_shapes=[pltpu.SemaphoreType.DMA((3 + rows, 2))], compiler_params=PARAMS,
    )(vmem(u), near_u, far_u, hbm(left_env), hbm(right_env))
    left, right, part, facts = vmem(left), vmem(right), vmem(part), vmem(facts)
    row_part, image, w, stats = pl.pallas_call(
        functools.partial(first_kernel, width, rows),
        out_shape=(pltpu.VMEM((rows,) + square, f32), pltpu.VMEM(square, f32), pltpu.VMEM(square, bf16),
                   pltpu.VMEM((8, 128), f32)),
        in_specs=[VM] * (5 + rows), out_specs=(VM,) * 4, compiler_params=PARAMS,
    )(facts, vmem(u), part, left, right, *row_u)

    row_w = [vmem(swap(w, "sector", p)) for p in row_pairs]
    near_w = vmem(swap(w, "sector", near))
    far_w = vmem(swap(w, "sector", far))
    stats = lax.all_gather(stats, "sector", axis=0)
    hw = pl.pallas_call(
        functools.partial(image_kernel, width, rows), out_shape=pltpu.VMEM(square, f32),
        in_specs=[VM] * (5 + rows), out_specs=VM, compiler_params=PARAMS,
    )(vmem(w), near_w, far_w, left, right, *row_w)
    return pl.pallas_call(
        functools.partial(second_kernel, size, width, rows, cells),
        out_shape=(jax.ShapeDtypeStruct((1,) + square, f32),) * 2,
        in_specs=[VM] * 6, out_specs=(HB, HB),
        scratch_shapes=[pltpu.VMEM(square, f32), pltpu.VMEM(square, f32), pltpu.SemaphoreType.DMA((2,))],
        compiler_params=PARAMS,
    )(facts, stats, vmem(hw), part, vmem(row_part), vmem(image))


def solution(mesh):
    placed = (
        P(("groups", "sector"), None, None),
        P(("groups", "sector"), None),
        P(("groups", "sector"), None, None, None),
        P(("groups", "sector"), None, None, None),
    )
    return jax.shard_map(
        body,
        mesh=mesh,
        in_specs=placed,
        out_specs=(P(("groups", "sector"), None, None), P(("groups", "sector"), None, None)),
        check_vma=False,
    )
```

```python
import functools

import jax
import jax.numpy as jnp
from jax import lax
from jax.experimental import pallas as pl
from jax.experimental.pallas import tpu as pltpu
from jax.sharding import PartitionSpec as P

QD = 8
SCALE = 1024.0
NT = (((1,), (1,)), ((), ()))
VM = pl.BlockSpec(memory_space=pltpu.VMEM)
HB = pl.BlockSpec(memory_space=pltpu.HBM)
PARAMS = pltpu.CompilerParams(vmem_limit_bytes=16 * 1024 * 1024)


def vmem(x):
    return pltpu.with_memory_space_constraint(x, pltpu.VMEM)


def hbm(x):
    return pltpu.with_memory_space_constraint(x, pltpu.HBM)


def swap(x, axis, pairs):
    to = {a: b for p in pairs for a, b in (p, p[::-1])}
    return lax.ppermute(x, axis, [(s, to.get(s, s)) for s in range(lax.axis_size(axis))])


def swap_pairs(size):
    rows = size // QD
    near = [(s, s + 1) for s in range(0, size, 2)]
    far = [(s, s + 1) for s in range(1, size - 1, 2) if s % QD != QD - 1]
    row_even = [(s, s + QD) for r in range(0, rows - 1, 2) for s in range(r * QD, r * QD + QD)]
    row_odd = [(s, s + QD) for r in range(1, rows - 1, 2) for s in range(r * QD, r * QD + QD)]
    return near, far, [p for p in (row_even, row_odd) if p]


def place(size, width):
    me = lax.axis_index("sector")
    column = lax.rem(me, QD)
    odd = lax.rem(me, 2) == 1
    row_odd = lax.rem(lax.div(me, QD), 2) == 1
    low, high, down, up = 2, 2 + width, 2 + 2 * width, 2 + 3 * width
    offsets = [jnp.where(odd, low, high), jnp.where(odd, high, low),
               jnp.where(row_odd, down, up), jnp.where(row_odd, up, down)]
    partners = [jnp.where(odd, me - 1, me + 1), jnp.where(odd, me + 1, me - 1),
                jnp.where(row_odd, me - QD, me + QD), jnp.where(row_odd, me + QD, me - QD)]
    there = [True, (column != 0) & (column != QD - 1), (partners[2] >= 0) & (partners[2] < size),
             (partners[3] >= 0) & (partners[3] < size)]
    partners = [me] + [jnp.clip(p, 0, size - 1) for p in partners]
    return offsets, partners, there


def live(facts, shape):
    row_ok = lax.broadcasted_iota(jnp.int32, shape, 0).astype(jnp.float32) < facts[1:2, 0:1]
    col_ok = lax.broadcasted_iota(jnp.int32, shape, 1).astype(jnp.float32) < facts[2:3, 0:1]
    return row_ok & col_ok


def total(x):
    return jnp.sum(jnp.sum(x, axis=0, keepdims=True), axis=1, keepdims=True)


def only(there, block):
    return block if there is True else jnp.where(there, block, jnp.zeros_like(block))


def terms(src, left_ref, right_ref, offset, count):
    size = src.shape[0]
    right = right_ref[pl.ds(offset, count)].reshape(count * size, size)
    partial_t = lax.dot_general(right, src, NT, preferred_element_type=jnp.float32).astype(jnp.bfloat16)
    image = None
    for k in range(count):
        piece = lax.dot_general(
            left_ref[offset + k], partial_t[k * size : (k + 1) * size], NT, preferred_element_type=jnp.float32
        )
        image = piece if image is None else image + piece
    return image


def fetch(left_hbm, right_hbm, left_ref, right_ref, sems, spans, first=0):
    copies = []
    at = first
    for n, (offset, count) in enumerate(spans):
        pair = [
            pltpu.make_async_copy(source.at[0, pl.ds(offset, count)], target.at[pl.ds(at, count)], sems.at[n, e])
            for e, (source, target) in enumerate(((right_hbm, right_ref), (left_hbm, left_ref)))
        ]
        for copy in pair:
            copy.start()
        copies.append(pair)
        at += count
    return copies


def start_kernel(wave_hbm, dims_hbm, u_ref, facts_ref, wave_ref, dims_ref, sems):
    wave_copy = pltpu.make_async_copy(wave_hbm.at[0], wave_ref, sems.at[0])
    dims_copy = pltpu.make_async_copy(dims_hbm, dims_ref, sems.at[1])
    dims_copy.start()
    wave_copy.start()
    dims_copy.wait()
    lines = lax.broadcasted_iota(jnp.int32, (8, 128), 0)
    facts = jnp.where(lines == 1, dims_ref[0, 0], jnp.where(lines == 2, dims_ref[0, 1], 0)).astype(jnp.float32)
    wave_copy.wait()
    held = jnp.where(live(facts, wave_ref.shape), wave_ref[...], 0.0)
    u_ref[...] = (held * SCALE).astype(jnp.bfloat16)
    facts_ref[...] = jnp.where(lines == 0, total(held * held), facts)


def near_kernel(size, width, rows, self_ref, near_ref, left_hbm, right_hbm, out_ref, left_ref, right_ref,
                left_own, right_own, sems, later_sems):
    offsets, _, _ = place(size, width)
    own = fetch(left_hbm, right_hbm, left_own, right_own, sems, [(0, 2), (offsets[0], width)])
    later = fetch(left_hbm, right_hbm, left_ref, right_ref, later_sems, [(o, width) for o in offsets[1 : 2 + rows]])
    for n, (source, first, count) in enumerate(((self_ref, 0, 2), (near_ref, 2, width))):
        for copy in own[n]:
            copy.wait()
        out_ref[n] = terms(source[...], left_own, right_own, first, count)
    for pair in later:
        for copy in pair:
            copy.wait()


def first_kernel(size, width, rows, *refs):
    part_ref, facts_ref, u_ref, left_ref, right_ref, far_ref = refs[:6]
    row_refs, (out_ref, image_ref, w_ref, stats_ref) = refs[6 : 6 + rows], refs[6 + rows :]
    _, _, there = place(size, width)
    facts = facts_ref[...]
    image = part_ref[0] + part_ref[1]
    for n, source in enumerate((far_ref,) + row_refs):
        piece = terms(only(there[1 + n], source[...]), left_ref, right_ref, n * width, width)
        out_ref[n] = piece
        image = image + piece
    image = jnp.where(live(facts, image.shape), image, 0.0)
    image_ref[...] = image
    u = u_ref[...].astype(jnp.float32)
    square = total(u * u)
    cross = total(u * image)
    rho = jnp.where(square > 0.0, cross / square, 0.0)
    w = image - rho * u
    w_ref[...] = w.astype(jnp.bfloat16)
    lines = lax.broadcasted_iota(jnp.int32, (8, 128), 0)
    stats = jnp.where(lines == 0, facts, 0.0)
    for line, value in ((1, square), (2, cross), (3, total(w * w)), (4, rho)):
        stats = jnp.where(lines == line, value, stats)
    for n in range(stats_ref.shape[0]):
        stats_ref[n] = stats


def image_kernel(size, width, rows, *refs):
    left_hbm, right_hbm, self_ref, near_ref, far_ref = refs[:5]
    row_refs, (out_ref, left_ref, right_ref, sems) = refs[5 : 5 + rows], refs[5 + rows :]
    offsets, _, there = place(size, width)
    copies = fetch(left_hbm, right_hbm, left_ref, right_ref, sems, [(0, 2)] + [(o, width) for o in offsets[: 2 + rows]])
    image = None
    at = 0
    for n, source in enumerate((self_ref, near_ref, far_ref) + row_refs):
        for copy in copies[n]:
            copy.wait()
        count = width if n else 2
        piece = terms(only(there[n - 1] if n else True, source[...]), left_ref, right_ref, at, count)
        image = piece if image is None else image + piece
        at += count
    out_ref[...] = image


def second_kernel(size, width, rows, cells, facts_ref, stats_ref, hw_ref, near_part_ref, far_part_ref, image_ref,
                  first_hbm, second_hbm, first_ref, second_ref, sems):
    _, partners, _ = place(size, width)
    facts = facts_ref[...]
    stats = stats_ref[...]
    sums = jnp.sum(stats, axis=0)
    start, square, cross, inner = (sums[i : i + 1, 0:1] for i in range(4))
    scale = lax.rsqrt(start / cells + 1e-06) * (1.0 / SCALE)
    first_ref[...] = image_ref[...] * scale
    first_copy = pltpu.make_async_copy(first_ref, first_hbm.at[0], sems.at[0])
    first_copy.start()
    rho = cross / square
    gap = stats[:, 4:5, 0:1] - rho[None]
    residual = inner + jnp.sum(stats[:, 1:2, 0:1] * gap * gap, axis=0)
    second_scale = scale * lax.rsqrt(scale * scale * (residual / cells) + 1e-06)
    image = hw_ref[...]
    for n in range(3 + rows):
        part = near_part_ref[n] if n < 2 else far_part_ref[n - 2]
        image = image + (stats_ref[partners[n], 4:5, 0:1] - rho) * part
    second_ref[...] = jnp.where(live(facts, image.shape), image, 0.0) * second_scale
    second_copy = pltpu.make_async_copy(second_ref, second_hbm.at[0], sems.at[1])
    second_copy.start()
    first_copy.wait()
    second_copy.wait()


def body(wavefunction, sector_dims, left_env, right_env):
    size = lax.axis_size("sector")
    block = wavefunction.shape[1]
    square = (block, block)
    width = (right_env.shape[1] - 2) // 4
    near, far, row_pairs = swap_pairs(size)
    rows = len(row_pairs)
    cells = float(size * block * block)
    later = ((1 + rows) * width,) + square
    own = (2 + width,) + square
    every = (2 + (2 + rows) * width,) + square
    f32, bf16 = jnp.float32, jnp.bfloat16
    dma = pltpu.SemaphoreType.DMA

    u, facts = pl.pallas_call(
        start_kernel, out_shape=(pltpu.VMEM(square, bf16), pltpu.VMEM((8, 128), f32)),
        in_specs=[HB, HB], out_specs=(VM, VM),
        scratch_shapes=[pltpu.VMEM(square, f32), pltpu.SMEM((1, 2), jnp.int32), dma((2,))],
        compiler_params=PARAMS,
    )(hbm(wavefunction), hbm(sector_dims))

    left_env, right_env = hbm(left_env), hbm(right_env)
    row_u = [vmem(swap(u, "sector", p)) for p in row_pairs]
    near_u = vmem(swap(u, "sector", near))
    far_u = vmem(swap(u, "sector", far))
    near_part, left, right = pl.pallas_call(
        functools.partial(near_kernel, size, width, rows),
        out_shape=(pltpu.VMEM((2,) + square, f32), pltpu.VMEM(later, bf16), pltpu.VMEM(later, bf16)),
        in_specs=[VM] * 2 + [HB] * 2, out_specs=(VM,) * 3,
        scratch_shapes=[pltpu.VMEM(own, bf16), pltpu.VMEM(own, bf16), dma((2, 2)), dma((1 + rows, 2))],
        compiler_params=PARAMS,
    )(vmem(u), near_u, left_env, right_env)
    near_part, facts = vmem(near_part), vmem(facts)
    far_part, image, w, stats = pl.pallas_call(
        functools.partial(first_kernel, size, width, rows),
        out_shape=(pltpu.VMEM((1 + rows,) + square, f32), pltpu.VMEM(square, f32), pltpu.VMEM(square, bf16),
                   jax.ShapeDtypeStruct((size, 8, 128), f32)),
        in_specs=[VM] * (6 + rows), out_specs=(VM,) * 4, compiler_params=PARAMS,
    )(near_part, facts, vmem(u), vmem(left), vmem(right), far_u, *row_u)

    row_w = [vmem(swap(w, "sector", p)) for p in row_pairs]
    near_w = vmem(swap(w, "sector", near))
    far_w = vmem(swap(w, "sector", far))
    stats = lax.all_to_all(stats, "sector", 0, 0, tiled=True)
    hw = pl.pallas_call(
        functools.partial(image_kernel, size, width, rows), out_shape=pltpu.VMEM(square, f32),
        in_specs=[HB] * 2 + [VM] * (3 + rows), out_specs=VM,
        scratch_shapes=[pltpu.VMEM(every, bf16), pltpu.VMEM(every, bf16), dma((3 + rows, 2))],
        compiler_params=PARAMS,
    )(left_env, right_env, vmem(w), near_w, far_w, *row_w)
    return pl.pallas_call(
        functools.partial(second_kernel, size, width, rows, cells),
        out_shape=(jax.ShapeDtypeStruct((1,) + square, f32),) * 2,
        in_specs=[VM] * 6, out_specs=(HB, HB),
        scratch_shapes=[pltpu.VMEM(square, f32), pltpu.VMEM(square, f32), dma((2,))],
        compiler_params=PARAMS,
    )(facts, stats, vmem(hw), near_part, vmem(far_part), vmem(image))


def solution(mesh):
    placed = (
        P(("groups", "sector"), None, None),
        P(("groups", "sector"), None),
        P(("groups", "sector"), None, None, None),
        P(("groups", "sector"), None, None, None),
    )
    return jax.shard_map(
        body,
        mesh=mesh,
        in_specs=placed,
        out_specs=(P(("groups", "sector"), None, None), P(("groups", "sector"), None, None)),
        check_vma=False,
    )
```

```python
import functools

import jax
import jax.numpy as jnp
from jax import lax
from jax.experimental import pallas as pl
from jax.experimental.pallas import tpu as pltpu
from jax.sharding import PartitionSpec as P

QD = 8
SCALE = 1024.0
NT = (((1,), (1,)), ((), ()))
VM = pl.BlockSpec(memory_space=pltpu.VMEM)
HB = pl.BlockSpec(memory_space=pltpu.HBM)
AN = pl.BlockSpec(memory_space=pl.ANY)
COST = pl.CostEstimate(flops=1, bytes_accessed=1, transcendentals=0)
LONG = pl.CostEstimate(flops=4000000000, bytes_accessed=1, transcendentals=0)
PARAMS = pltpu.CompilerParams(vmem_limit_bytes=16 * 1024 * 1024)


def vmem(x):
    return pltpu.with_memory_space_constraint(x, pltpu.VMEM)


def hbm(x):
    return pltpu.with_memory_space_constraint(x, pltpu.HBM)


def swap(x, axis, pairs):
    to = {a: b for p in pairs for a, b in (p, p[::-1])}
    return lax.ppermute(x, axis, [(s, to.get(s, s)) for s in range(lax.axis_size(axis))])


def swap_pairs(size):
    rows = size // QD
    near = [(s, s + 1) for s in range(0, size, 2)]
    far = [(s, s + 1) for s in range(1, size - 1, 2) if s % QD != QD - 1]
    row_even = [(s, s + QD) for r in range(0, rows - 1, 2) for s in range(r * QD, r * QD + QD)]
    row_odd = [(s, s + QD) for r in range(1, rows - 1, 2) for s in range(r * QD, r * QD + QD)]
    return near, far, [p for p in (row_even, row_odd) if p]


def place(size, width):
    me = lax.axis_index("sector")
    column = lax.rem(me, QD)
    odd = lax.rem(me, 2) == 1
    row_odd = lax.rem(lax.div(me, QD), 2) == 1
    low, high, down, up = 2, 2 + width, 2 + 2 * width, 2 + 3 * width
    offsets = [jnp.where(odd, low, high), jnp.where(odd, high, low),
               jnp.where(row_odd, down, up), jnp.where(row_odd, up, down)]
    partners = [jnp.where(odd, me - 1, me + 1), jnp.where(odd, me + 1, me - 1),
                jnp.where(row_odd, me - QD, me + QD), jnp.where(row_odd, me + QD, me - QD)]
    there = [True, (column != 0) & (column != QD - 1), (partners[2] >= 0) & (partners[2] < size),
             (partners[3] >= 0) & (partners[3] < size)]
    partners = [me] + [jnp.clip(p, 0, size - 1) for p in partners]
    return offsets, partners, there


def live(facts, shape):
    row_ok = lax.broadcasted_iota(jnp.int32, shape, 0).astype(jnp.float32) < facts[1:2, 0:1]
    col_ok = lax.broadcasted_iota(jnp.int32, shape, 1).astype(jnp.float32) < facts[2:3, 0:1]
    return row_ok & col_ok


def total(x):
    return jnp.sum(jnp.sum(x, axis=0, keepdims=True), axis=1, keepdims=True)


def only(there, block):
    return block if there is True else jnp.where(there, block, jnp.zeros_like(block))


def terms(src, left_ref, right_ref, offset, count):
    size = src.shape[0]
    right = right_ref[pl.ds(offset, count)].reshape(count * size, size)
    partial_t = lax.dot_general(right, src, NT, preferred_element_type=jnp.float32).astype(jnp.bfloat16)
    image = None
    for k in range(count):
        piece = lax.dot_general(
            left_ref[offset + k], partial_t[k * size : (k + 1) * size], NT, preferred_element_type=jnp.float32
        )
        image = piece if image is None else image + piece
    return image


def fetch(left_hbm, right_hbm, left_ref, right_ref, sems, spans):
    copies = []
    at = 0
    for n, (offset, count) in enumerate(spans):
        pair = [
            pltpu.make_async_copy(source.at[0, pl.ds(offset, count)], target.at[pl.ds(at, count)], sems.at[n, e])
            for e, (source, target) in enumerate(((right_hbm, right_ref), (left_hbm, left_ref)))
        ]
        for copy in pair:
            copy.start()
        copies.append(pair)
        at += count
    return copies


def start_kernel(wave_hbm, dims_hbm, u_ref, far_u_ref, facts_ref, wave_ref, dims_ref, sems):
    wave_copy = pltpu.make_async_copy(wave_hbm.at[0], wave_ref, sems.at[0])
    dims_copy = pltpu.make_async_copy(dims_hbm, dims_ref, sems.at[1])
    dims_copy.start()
    wave_copy.start()
    dims_copy.wait()
    lines = lax.broadcasted_iota(jnp.int32, (8, 128), 0)
    facts = jnp.where(lines == 1, dims_ref[0, 0], jnp.where(lines == 2, dims_ref[0, 1], 0)).astype(jnp.float32)
    wave_copy.wait()
    held = jnp.where(live(facts, wave_ref.shape), wave_ref[...], 0.0)
    u_ref[...] = (held * SCALE).astype(jnp.bfloat16)
    far_u_ref[...] = u_ref[...]
    facts_ref[...] = jnp.where(lines == 0, total(held * held), facts)


def near_kernel(size, width, rows, left_hbm, right_hbm, self_ref, near_ref, out_ref, left_ref, right_ref, sems):
    offsets, _, _ = place(size, width)
    copies = fetch(left_hbm, right_hbm, left_ref, right_ref, sems, [(0, 2)] + [(o, width) for o in offsets[: 2 + rows]])
    for n, (source, first, count) in enumerate(((self_ref, 0, 2), (near_ref, 2, width))):
        for copy in copies[n]:
            copy.wait()
        out_ref[n] = terms(source[...], left_ref, right_ref, first, count)
    for pair in copies[2:]:
        for copy in pair:
            copy.wait()


def far_kernel(size, width, left_ref, right_ref, far_ref, out_ref):
    _, _, there = place(size, width)
    out_ref[...] = terms(only(there[1], far_ref[...]), left_ref, right_ref, 2 + width, width)


def first_kernel(size, width, rows, *refs):
    near_part_ref, far_part_ref, facts_ref, u_ref, left_ref, right_ref = refs[:6]
    row_refs, (out_ref, image_ref, w_ref, far_w_ref, stats_ref) = refs[6 : 6 + rows], refs[6 + rows :]
    _, _, there = place(size, width)
    facts = facts_ref[...]
    image = near_part_ref[0] + near_part_ref[1] + far_part_ref[...]
    for r, source in enumerate(row_refs):
        piece = terms(only(there[2 + r], source[...]), left_ref, right_ref, 2 + (2 + r) * width, width)
        out_ref[r] = piece
        image = image + piece
    image = jnp.where(live(facts, image.shape), image, 0.0)
    image_ref[...] = image
    u = u_ref[...].astype(jnp.float32)
    square = total(u * u)
    cross = total(u * image)
    rho = jnp.where(square > 0.0, cross / square, 0.0)
    w = image - rho * u
    for ref in (w_ref, far_w_ref):
        ref[...] = w.astype(jnp.bfloat16)
    lane = lax.broadcasted_iota(jnp.int32, (1, 128), 1)
    record = jnp.zeros((1, 128), jnp.float32)
    for n, value in enumerate((facts[0:1, 0:1], square, cross, total(w * w), rho)):
        record = jnp.where(lane == n, value, record)
    mine = lax.broadcasted_iota(jnp.int32, stats_ref.shape, 0) == lax.axis_index("sector")
    stats_ref[...] = jnp.where(mine, record, 0.0)


def add_kernel(one_ref, other_ref, *refs):
    refs[len(refs) // 2][...] = one_ref[...] + other_ref[...]


def merge(stats, other, held=None):
    extra = [] if held is None else [held]
    out = pl.pallas_call(
        add_kernel, out_shape=[pltpu.VMEM(x.shape, x.dtype) for x in [stats] + extra],
        in_specs=[VM] * 2 + [AN] * len(extra), out_specs=[VM] + [AN] * len(extra),
        input_output_aliases={2: 1} if extra else {}, compiler_params=PARAMS, cost_estimate=COST,
    )(vmem(stats), vmem(other), *map(vmem, extra))
    return out


def pass_kernel(*refs):
    pass


def after(held, first):
    return pl.pallas_call(
        pass_kernel, out_shape=pltpu.VMEM(held.shape, held.dtype), in_specs=[AN] * 2, out_specs=AN,
        input_output_aliases={0: 0}, compiler_params=PARAMS, cost_estimate=COST,
    )(vmem(held), vmem(first))


def image_kernel(size, width, rows, *refs):
    left_ref, right_ref, self_ref, near_ref, far_ref = refs[:5]
    row_refs, (out_ref,) = refs[5 : 5 + rows], refs[5 + rows :]
    _, _, there = place(size, width)
    image = terms(self_ref[...], left_ref, right_ref, 0, 2)
    for n, source in enumerate((near_ref, far_ref) + row_refs):
        image = image + terms(only(there[n], source[...]), left_ref, right_ref, 2 + n * width, width)
    out_ref[...] = image


def second_kernel(size, width, rows, cells, facts_ref, stats_ref, other_stats_ref, hw_ref, near_part_ref, far_part_ref,
                  row_part_ref, image_ref, first_hbm, second_hbm, first_ref, second_ref, sems):
    _, partners, _ = place(size, width)
    facts = facts_ref[...]
    stats = stats_ref[...] + other_stats_ref[...]
    sums = jnp.sum(stats, axis=0, keepdims=True)
    start, square, cross, inner = (sums[:, i : i + 1] for i in range(4))
    scale = lax.rsqrt(start / cells + 1e-06) * (1.0 / SCALE)
    first_ref[...] = image_ref[...] * scale
    first_copy = pltpu.make_async_copy(first_ref, first_hbm.at[0], sems.at[0])
    first_copy.start()
    rho = cross / square
    gap = stats[:, 4:5] - rho
    residual = inner + jnp.sum(stats[:, 1:2] * gap * gap, axis=0, keepdims=True)
    second_scale = scale * lax.rsqrt(scale * scale * (residual / cells) + 1e-06)
    sector = lax.broadcasted_iota(jnp.int32, gap.shape, 0)
    parts = [near_part_ref[0], near_part_ref[1], far_part_ref[...]] + [row_part_ref[r] for r in range(rows)]
    image = hw_ref[...]
    for n, part in enumerate(parts):
        image = image + jnp.sum(jnp.where(sector == partners[n], gap, 0.0), axis=0, keepdims=True) * part
    second_ref[...] = jnp.where(live(facts, image.shape), image, 0.0) * second_scale
    second_copy = pltpu.make_async_copy(second_ref, second_hbm.at[0], sems.at[1])
    second_copy.start()
    first_copy.wait()
    second_copy.wait()


def body(wavefunction, sector_dims, left_env, right_env):
    size = lax.axis_size("sector")
    block = wavefunction.shape[1]
    square = (block, block)
    width = (right_env.shape[1] - 2) // 4
    near, far, row_pairs = swap_pairs(size)
    rows = len(row_pairs)
    cells = float(size * block * block)
    every = (2 + (2 + rows) * width,) + square
    f32, bf16 = jnp.float32, jnp.bfloat16
    dma = pltpu.SemaphoreType.DMA

    u, far_u, facts = pl.pallas_call(
        start_kernel, out_shape=(pltpu.VMEM(square, bf16), pltpu.VMEM(square, bf16), pltpu.VMEM((8, 128), f32)),
        in_specs=[HB, HB], out_specs=(VM,) * 3,
        scratch_shapes=[pltpu.VMEM(square, f32), pltpu.SMEM((1, 2), jnp.int32), dma((2,))],
        compiler_params=PARAMS, cost_estimate=COST,
    )(hbm(wavefunction), hbm(sector_dims))

    left_env, right_env = hbm(left_env), hbm(right_env)
    row_u = [vmem(swap(u, "sector", p)) for p in row_pairs]
    near_u = vmem(swap(u, "sector", near))
    far_u = vmem(swap(after(far_u, near_u), "sector", far))
    near_part, left, right = pl.pallas_call(
        functools.partial(near_kernel, size, width, rows),
        out_shape=(pltpu.VMEM((2,) + square, f32), pltpu.VMEM(every, bf16), pltpu.VMEM(every, bf16)),
        in_specs=[HB] * 2 + [VM] * 2, out_specs=(VM,) * 3, scratch_shapes=[dma((3 + rows, 2))],
        compiler_params=PARAMS, cost_estimate=LONG,
    )(left_env, right_env, vmem(u), near_u)
    near_part, facts, left, right = vmem(near_part), vmem(facts), vmem(left), vmem(right)
    far_part = vmem(pl.pallas_call(
        functools.partial(far_kernel, size, width), out_shape=pltpu.VMEM(square, f32),
        in_specs=[VM] * 3, out_specs=VM, compiler_params=PARAMS, cost_estimate=LONG,
    )(left, right, far_u))
    row_part, image, w, far_w, stats = pl.pallas_call(
        functools.partial(first_kernel, size, width, rows),
        out_shape=(pltpu.VMEM((rows,) + square, f32), pltpu.VMEM(square, f32)) + (pltpu.VMEM(square, bf16),) * 2
        + (pltpu.VMEM((size, 128), f32),),
        in_specs=[VM] * (6 + rows), out_specs=(VM,) * 5, compiler_params=PARAMS, cost_estimate=COST,
    )(near_part, far_part, facts, vmem(u), left, right, *row_u)

    row_w = [vmem(swap(w, "sector", p)) for p in row_pairs]
    near_w = vmem(swap(w, "sector", near))
    step = 1
    while 2 * step < size:
        other = swap(stats, "sector", [(s, s + step) for s in range(size) if not s & step])
        if step == 1:
            stats, far_w = merge(stats, other, far_w)
        else:
            (stats,) = merge(stats, other)
        step *= 2
    other = swap(stats, "sector", [(s, s + step) for s in range(size) if not s & step])
    far_w = vmem(swap(far_w, "sector", far))
    hw = pl.pallas_call(
        functools.partial(image_kernel, size, width, rows), out_shape=pltpu.VMEM(square, f32),
        in_specs=[VM] * (5 + rows), out_specs=VM, compiler_params=PARAMS, cost_estimate=COST,
    )(left, right, vmem(w), near_w, far_w, *row_w)
    return pl.pallas_call(
        functools.partial(second_kernel, size, width, rows, cells),
        out_shape=(jax.ShapeDtypeStruct((1,) + square, f32),) * 2,
        in_specs=[VM] * 8, out_specs=(HB, HB),
        scratch_shapes=[pltpu.VMEM(square, f32), pltpu.VMEM(square, f32), dma((2,))],
        compiler_params=PARAMS, cost_estimate=COST,
    )(facts, vmem(stats), vmem(other), vmem(hw), near_part, far_part, vmem(row_part), vmem(image))


def solution(mesh):
    placed = (
        P(("groups", "sector"), None, None),
        P(("groups", "sector"), None),
        P(("groups", "sector"), None, None, None),
        P(("groups", "sector"), None, None, None),
    )
    return jax.shard_map(
        body,
        mesh=mesh,
        in_specs=placed,
        out_specs=(P(("groups", "sector"), None, None), P(("groups", "sector"), None, None)),
        check_vma=False,
    )
```

```python
import functools

import jax
import jax.numpy as jnp
from jax import lax
from jax.experimental import pallas as pl
from jax.experimental.pallas import tpu as pltpu
from jax.sharding import PartitionSpec as P

QD = 8
SCALE = 1024.0
NT = (((1,), (1,)), ((), ()))
VM = pl.BlockSpec(memory_space=pltpu.VMEM)
HB = pl.BlockSpec(memory_space=pltpu.HBM)
AN = pl.BlockSpec(memory_space=pl.ANY)
COST = pl.CostEstimate(flops=1, bytes_accessed=1, transcendentals=0)
LONG = pl.CostEstimate(flops=4000000000, bytes_accessed=1, transcendentals=0)
PARAMS = pltpu.CompilerParams(vmem_limit_bytes=16 * 1024 * 1024)


def vmem(x):
    return pltpu.with_memory_space_constraint(x, pltpu.VMEM)


def hbm(x):
    return pltpu.with_memory_space_constraint(x, pltpu.HBM)


def swap(x, axis, pairs):
    to = {a: b for p in pairs for a, b in (p, p[::-1])}
    return lax.ppermute(x, axis, [(s, to.get(s, s)) for s in range(lax.axis_size(axis))])


def swap_pairs(size):
    rows = size // QD
    near = [(s, s + 1) for s in range(0, size, 2)]
    far = [(s, s + 1) for s in range(1, size - 1, 2) if s % QD != QD - 1]
    row_even = [(s, s + QD) for r in range(0, rows - 1, 2) for s in range(r * QD, r * QD + QD)]
    row_odd = [(s, s + QD) for r in range(1, rows - 1, 2) for s in range(r * QD, r * QD + QD)]
    return near, far, [p for p in (row_even, row_odd) if p]


def place(size, width):
    me = lax.axis_index("sector")
    column = lax.rem(me, QD)
    odd = lax.rem(me, 2) == 1
    row_odd = lax.rem(lax.div(me, QD), 2) == 1
    low, high, down, up = 2, 2 + width, 2 + 2 * width, 2 + 3 * width
    offsets = [jnp.where(odd, low, high), jnp.where(odd, high, low),
               jnp.where(row_odd, down, up), jnp.where(row_odd, up, down)]
    partners = [jnp.where(odd, me - 1, me + 1), jnp.where(odd, me + 1, me - 1),
                jnp.where(row_odd, me - QD, me + QD), jnp.where(row_odd, me + QD, me - QD)]
    there = [True, (column != 0) & (column != QD - 1), (partners[2] >= 0) & (partners[2] < size),
             (partners[3] >= 0) & (partners[3] < size)]
    partners = [me] + [jnp.clip(p, 0, size - 1) for p in partners]
    return offsets, partners, there


def live(facts, shape):
    row_ok = lax.broadcasted_iota(jnp.int32, shape, 0).astype(jnp.float32) < facts[1:2, 0:1]
    col_ok = lax.broadcasted_iota(jnp.int32, shape, 1).astype(jnp.float32) < facts[2:3, 0:1]
    return row_ok & col_ok


def total(x):
    return jnp.sum(jnp.sum(x, axis=0, keepdims=True), axis=1, keepdims=True)


def only(there, block):
    return block if there is True else jnp.where(there, block, jnp.zeros_like(block))


def terms(src, left_ref, right_ref, offset, count):
    size = src.shape[0]
    right = right_ref[pl.ds(offset, count)].reshape(count * size, size)
    partial_t = lax.dot_general(right, src, NT, preferred_element_type=jnp.float32).astype(jnp.bfloat16)
    image = None
    for k in range(count):
        piece = lax.dot_general(
            left_ref[offset + k], partial_t[k * size : (k + 1) * size], NT, preferred_element_type=jnp.float32
        )
        image = piece if image is None else image + piece
    return image


def fetch(left_hbm, right_hbm, left_ref, right_ref, sems, spans):
    copies = []
    at = 0
    for n, (offset, count) in enumerate(spans):
        pair = [
            pltpu.make_async_copy(source.at[0, pl.ds(offset, count)], target.at[pl.ds(at, count)], sems.at[n, e])
            for e, (source, target) in enumerate(((right_hbm, right_ref), (left_hbm, left_ref)))
        ]
        for copy in pair:
            copy.start()
        copies.append(pair)
        at += count
    return copies


def start_kernel(wave_hbm, dims_hbm, u_ref, far_u_ref, facts_ref, wave_ref, dims_ref, sems):
    wave_copy = pltpu.make_async_copy(wave_hbm.at[0], wave_ref, sems.at[0])
    dims_copy = pltpu.make_async_copy(dims_hbm, dims_ref, sems.at[1])
    dims_copy.start()
    wave_copy.start()
    dims_copy.wait()
    lines = lax.broadcasted_iota(jnp.int32, (8, 128), 0)
    facts = jnp.where(lines == 1, dims_ref[0, 0], jnp.where(lines == 2, dims_ref[0, 1], 0)).astype(jnp.float32)
    wave_copy.wait()
    held = jnp.where(live(facts, wave_ref.shape), wave_ref[...], 0.0)
    u_ref[...] = (held * SCALE).astype(jnp.bfloat16)
    far_u_ref[...] = u_ref[...]
    facts_ref[...] = jnp.where(lines == 0, total(held * held), facts)


def near_kernel(size, width, rows, left_hbm, right_hbm, self_ref, near_ref, out_ref, left_far, right_far, left_row, right_row,
                left_own, right_own, sems, far_sems, row_sems):
    offsets, _, _ = place(size, width)
    own = fetch(left_hbm, right_hbm, left_own, right_own, sems, [(0, 2), (offsets[0], width)])
    later = fetch(left_hbm, right_hbm, left_far, right_far, far_sems, [(offsets[1], width)])
    later += fetch(left_hbm, right_hbm, left_row, right_row, row_sems, [(o, width) for o in offsets[2 : 2 + rows]])
    for n, (source, first, count) in enumerate(((self_ref, 0, 2), (near_ref, 2, width))):
        for copy in own[n]:
            copy.wait()
        out_ref[n] = terms(source[...], left_own, right_own, first, count)
    for pair in later:
        for copy in pair:
            copy.wait()


def far_kernel(size, width, left_ref, right_ref, far_ref, out_ref):
    _, _, there = place(size, width)
    out_ref[...] = terms(only(there[1], far_ref[...]), left_ref, right_ref, 0, width)


def first_kernel(size, width, rows, *refs):
    near_part_ref, far_part_ref, facts_ref, u_ref, left_ref, right_ref = refs[:6]
    row_refs, (out_ref, w_ref, far_w_ref, stats_ref) = refs[6 : 6 + rows], refs[6 + rows :]
    _, _, there = place(size, width)
    facts = facts_ref[...]
    image = near_part_ref[0] + near_part_ref[1] + far_part_ref[...]
    for r, source in enumerate(row_refs):
        piece = terms(only(there[2 + r], source[...]), left_ref, right_ref, r * width, width)
        out_ref[r] = piece
        image = image + piece
    image = jnp.where(live(facts, image.shape), image, 0.0)
    u = u_ref[...].astype(jnp.float32)
    square = total(u * u)
    cross = total(u * image)
    rho = jnp.where(square > 0.0, cross / square, 0.0)
    w = image - rho * u
    for ref in (w_ref, far_w_ref):
        ref[...] = w.astype(jnp.bfloat16)
    lane = lax.broadcasted_iota(jnp.int32, (1, 128), 1)
    record = jnp.zeros((1, 128), jnp.float32)
    for n, value in enumerate((facts[0:1, 0:1], square, cross, total(w * w), rho)):
        record = jnp.where(lane == n, value, record)
    mine = lax.broadcasted_iota(jnp.int32, stats_ref.shape, 0) == lax.rem(lax.axis_index("sector"), 2)
    stats_ref[...] = jnp.where(mine, record, 0.0)


def merge_kernel(one_ref, other_ref, held_in, out_ref, held_out):
    both = one_ref[...] + other_ref[...]
    for n in range(out_ref.shape[0]):
        out_ref[n] = both


def merge(stats, other, copies, held):
    return pl.pallas_call(
        merge_kernel,
        out_shape=(jax.ShapeDtypeStruct((copies,) + stats.shape, stats.dtype), pltpu.VMEM(held.shape, held.dtype)),
        in_specs=[VM] * 2 + [AN], out_specs=(VM, AN), input_output_aliases={2: 1}, compiler_params=PARAMS, cost_estimate=COST,
    )(vmem(stats), vmem(other), vmem(held))


def pass_kernel(*refs):
    pass


def after(held, first):
    return pl.pallas_call(
        pass_kernel, out_shape=pltpu.VMEM(held.shape, held.dtype), in_specs=[AN] * 2, out_specs=AN,
        input_output_aliases={0: 0}, compiler_params=PARAMS, cost_estimate=COST,
    )(vmem(held), vmem(first))


def image_kernel(size, width, rows, left_hbm, right_hbm, left_row, right_row, self_ref, near_ref, far_ref, *refs):
    row_refs, (out_ref, left_own, right_own, sems) = refs[:rows], refs[rows:]
    offsets, _, there = place(size, width)
    own = fetch(left_hbm, right_hbm, left_own, right_own, sems, [(0, 2)] + [(o, width) for o in offsets[:2]])
    image = None
    for r, source in enumerate(row_refs):
        piece = terms(only(there[2 + r], source[...]), left_row, right_row, r * width, width)
        image = piece if image is None else image + piece
    at = 0
    for n, source in enumerate((self_ref, near_ref, far_ref)):
        for copy in own[n]:
            copy.wait()
        count = width if n else 2
        piece = terms(only(there[n - 1] if n else True, source[...]), left_own, right_own, at, count)
        image = piece if image is None else image + piece
        at += count
    out_ref[...] = image


def second_kernel(size, width, rows, cells, facts_ref, stats_ref, hw_ref, near_part_ref, far_part_ref, row_part_ref,
                  first_hbm, second_hbm, first_ref, second_ref, sems):
    _, partners, _ = place(size, width)
    facts = facts_ref[...]
    stats = stats_ref[...]
    sums = jnp.sum(jnp.sum(stats, axis=0), axis=0, keepdims=True)
    start, square, cross, inner = (sums[:, i : i + 1] for i in range(4))
    scale = lax.rsqrt(start / cells + 1e-06) * (1.0 / SCALE)
    parts = [near_part_ref[0], near_part_ref[1], far_part_ref[...]] + [row_part_ref[r] for r in range(rows)]
    cell = live(facts, parts[0].shape)
    first_ref[...] = jnp.where(cell, sum(parts[1:], parts[0]), 0.0) * scale
    first_copy = pltpu.make_async_copy(first_ref, first_hbm.at[0], sems.at[0])
    first_copy.start()
    rho = cross / square
    gap = stats[:, :, 4:5] - rho[None]
    residual = inner + jnp.sum(jnp.sum(stats[:, :, 1:2] * gap * gap, axis=0), axis=0, keepdims=True)
    second_scale = scale * lax.rsqrt(scale * scale * (residual / cells) + 1e-06)
    core = lax.broadcasted_iota(jnp.int32, gap.shape, 1)
    sector = jnp.where(core < 2, 2 * lax.broadcasted_iota(jnp.int32, gap.shape, 0) + core, -1)
    image = hw_ref[...]
    for n, part in enumerate(parts):
        own_gap = jnp.sum(jnp.sum(jnp.where(sector == partners[n], gap, 0.0), axis=0), axis=0, keepdims=True)
        image = image + own_gap * part
    second_ref[...] = jnp.where(cell, image, 0.0) * second_scale
    second_copy = pltpu.make_async_copy(second_ref, second_hbm.at[0], sems.at[1])
    second_copy.start()
    first_copy.wait()
    second_copy.wait()


def body(wavefunction, sector_dims, left_env, right_env):
    size = lax.axis_size("sector")
    block = wavefunction.shape[1]
    square = (block, block)
    width = (right_env.shape[1] - 2) // 4
    near, far, row_pairs = swap_pairs(size)
    rows = len(row_pairs)
    cells = float(size * block * block)
    few, every, side, last = ((n,) + square for n in (2 + width, 2 + 2 * width, width, rows * width))
    f32, bf16 = jnp.float32, jnp.bfloat16
    dma = pltpu.SemaphoreType.DMA

    u, far_u, facts = pl.pallas_call(
        start_kernel, out_shape=(pltpu.VMEM(square, bf16), pltpu.VMEM(square, bf16), pltpu.VMEM((8, 128), f32)),
        in_specs=[HB, HB], out_specs=(VM,) * 3,
        scratch_shapes=[pltpu.VMEM(square, f32), pltpu.SMEM((1, 2), jnp.int32), dma((2,))],
        compiler_params=PARAMS, cost_estimate=COST,
    )(hbm(wavefunction), hbm(sector_dims))

    left_env, right_env = hbm(left_env), hbm(right_env)
    row_u = [vmem(swap(u, "sector", p)) for p in row_pairs]
    near_u = vmem(swap(u, "sector", near))
    far_u = vmem(swap(after(far_u, near_u), "sector", far))
    near_part, left_far, right_far, left_row, right_row = pl.pallas_call(
        functools.partial(near_kernel, size, width, rows),
        out_shape=(pltpu.VMEM((2,) + square, f32),) + (pltpu.VMEM(side, bf16),) * 2 + (pltpu.VMEM(last, bf16),) * 2,
        in_specs=[HB] * 2 + [VM] * 2, out_specs=(VM,) * 5,
        scratch_shapes=[pltpu.VMEM(few, bf16)] * 2 + [dma((2, 2)), dma((1, 2)), dma((rows, 2))],
        compiler_params=PARAMS, cost_estimate=LONG,
    )(left_env, right_env, vmem(u), near_u)
    near_part, facts, left_row, right_row = vmem(near_part), vmem(facts), vmem(left_row), vmem(right_row)
    far_part = vmem(pl.pallas_call(
        functools.partial(far_kernel, size, width), out_shape=pltpu.VMEM(square, f32),
        in_specs=[VM] * 3, out_specs=VM, compiler_params=PARAMS, cost_estimate=LONG,
    )(vmem(left_far), vmem(right_far), far_u))
    row_part, w, far_w, stats = pl.pallas_call(
        functools.partial(first_kernel, size, width, rows),
        out_shape=(pltpu.VMEM((rows,) + square, f32),) + (pltpu.VMEM(square, bf16),) * 2 + (pltpu.VMEM((8, 128), f32),),
        in_specs=[VM] * (6 + rows), out_specs=(VM,) * 4, compiler_params=PARAMS, cost_estimate=COST,
    )(near_part, far_part, facts, vmem(u), left_row, right_row, *row_u)

    row_w = [vmem(swap(w, "sector", p)) for p in row_pairs]
    near_w = vmem(swap(w, "sector", near))
    other = swap(stats, "sector", near)
    stats, far_w = merge(stats, other, size // 2, far_w)
    far_w = vmem(swap(far_w, "sector", far))
    chips = [list(range(0, size, 2)), list(range(1, size, 2))]
    stats = lax.all_to_all(stats, "sector", 0, 0, tiled=True, axis_index_groups=chips)
    hw = pl.pallas_call(
        functools.partial(image_kernel, size, width, rows), out_shape=pltpu.VMEM(square, f32),
        in_specs=[HB] * 2 + [VM] * (5 + rows), out_specs=VM,
        scratch_shapes=[pltpu.VMEM(every, bf16)] * 2 + [dma((3, 2))],
        compiler_params=PARAMS, cost_estimate=COST,
    )(left_env, right_env, left_row, right_row, vmem(w), near_w, far_w, *row_w)
    return pl.pallas_call(
        functools.partial(second_kernel, size, width, rows, cells),
        out_shape=(jax.ShapeDtypeStruct((1,) + square, f32),) * 2,
        in_specs=[VM] * 6, out_specs=(HB, HB),
        scratch_shapes=[pltpu.VMEM(square, f32), pltpu.VMEM(square, f32), dma((2,))],
        compiler_params=PARAMS, cost_estimate=COST,
    )(facts, stats, vmem(hw), near_part, far_part, vmem(row_part))


def solution(mesh):
    placed = (
        P(("groups", "sector"), None, None),
        P(("groups", "sector"), None),
        P(("groups", "sector"), None, None, None),
        P(("groups", "sector"), None, None, None),
    )
    return jax.shard_map(
        body,
        mesh=mesh,
        in_specs=placed,
        out_specs=(P(("groups", "sector"), None, None), P(("groups", "sector"), None, None)),
        check_vma=False,
    )
```

```python
import functools

import jax
import jax.numpy as jnp
from jax import lax
from jax.experimental import pallas as pl
from jax.experimental.pallas import tpu as pltpu
from jax.sharding import PartitionSpec as P

QD = 8
SCALE = 1024.0
COPIES = 16
NT = (((1,), (1,)), ((), ()))
VM = pl.BlockSpec(memory_space=pltpu.VMEM)
HB = pl.BlockSpec(memory_space=pltpu.HBM)
AN = pl.BlockSpec(memory_space=pl.ANY)
COST = pl.CostEstimate(flops=1, bytes_accessed=1, transcendentals=0)
LONG = pl.CostEstimate(flops=4000000000, bytes_accessed=1, transcendentals=0)
PARAMS = pltpu.CompilerParams(vmem_limit_bytes=16 * 1024 * 1024)


def vmem(x):
    return pltpu.with_memory_space_constraint(x, pltpu.VMEM)


def hbm(x):
    return pltpu.with_memory_space_constraint(x, pltpu.HBM)


def swap(x, axis, pairs):
    to = {a: b for p in pairs for a, b in (p, p[::-1])}
    return lax.ppermute(x, axis, [(s, to.get(s, s)) for s in range(lax.axis_size(axis))])


def swap_pairs(size):
    rows = size // QD
    near = [(s, s + 1) for s in range(0, size, 2)]
    far = [(s, s + 1) for s in range(1, size - 1, 2) if s % QD != QD - 1]
    row_even = [(s, s + QD) for r in range(0, rows - 1, 2) for s in range(r * QD, r * QD + QD)]
    row_odd = [(s, s + QD) for r in range(1, rows - 1, 2) for s in range(r * QD, r * QD + QD)]
    return near, far, [p for p in (row_even, row_odd) if p]


def place(size, width):
    me = lax.axis_index("sector")
    column = lax.rem(me, QD)
    odd = lax.rem(me, 2) == 1
    row_odd = lax.rem(lax.div(me, QD), 2) == 1
    low, high, down, up = 2, 2 + width, 2 + 2 * width, 2 + 3 * width
    offsets = [jnp.where(odd, low, high), jnp.where(odd, high, low),
               jnp.where(row_odd, down, up), jnp.where(row_odd, up, down)]
    partners = [jnp.where(odd, me - 1, me + 1), jnp.where(odd, me + 1, me - 1),
                jnp.where(row_odd, me - QD, me + QD), jnp.where(row_odd, me + QD, me - QD)]
    there = [True, (column != 0) & (column != QD - 1), (partners[2] >= 0) & (partners[2] < size),
             (partners[3] >= 0) & (partners[3] < size)]
    partners = [me] + [jnp.clip(p, 0, size - 1) for p in partners]
    return offsets, partners, there


def live(facts, shape):
    row_ok = lax.broadcasted_iota(jnp.int32, shape, 0).astype(jnp.float32) < facts[1:2, 0:1]
    col_ok = lax.broadcasted_iota(jnp.int32, shape, 1).astype(jnp.float32) < facts[2:3, 0:1]
    return row_ok & col_ok


def total(x):
    return jnp.sum(jnp.sum(x, axis=0, keepdims=True), axis=1, keepdims=True)


def only(there, block):
    return block if there is True else jnp.where(there, block, jnp.zeros_like(block))


def terms(src, left_ref, right_ref, offset, count):
    size = src.shape[0]
    right = right_ref[pl.ds(offset, count)].reshape(count * size, size)
    partial_t = lax.dot_general(right, src, NT, preferred_element_type=jnp.float32).astype(jnp.bfloat16)
    image = None
    for k in range(count):
        piece = lax.dot_general(
            left_ref[offset + k], partial_t[k * size : (k + 1) * size], NT, preferred_element_type=jnp.float32
        )
        image = piece if image is None else image + piece
    return image


def fetch(left_hbm, right_hbm, left_ref, right_ref, sems, spans):
    copies = []
    at = 0
    for n, (offset, count) in enumerate(spans):
        pair = [
            pltpu.make_async_copy(source.at[0, pl.ds(offset, count)], target.at[pl.ds(at, count)], sems.at[n, e])
            for e, (source, target) in enumerate(((right_hbm, right_ref), (left_hbm, left_ref)))
        ]
        for copy in pair:
            copy.start()
        copies.append(pair)
        at += count
    return copies


def start_kernel(wave_hbm, dims_hbm, u_ref, far_u_ref, facts_ref, wave_ref, dims_ref, sems):
    wave_copy = pltpu.make_async_copy(wave_hbm.at[0], wave_ref, sems.at[0])
    dims_copy = pltpu.make_async_copy(dims_hbm, dims_ref, sems.at[1])
    dims_copy.start()
    wave_copy.start()
    dims_copy.wait()
    lines = lax.broadcasted_iota(jnp.int32, (8, 128), 0)
    facts = jnp.where(lines == 1, dims_ref[0, 0], jnp.where(lines == 2, dims_ref[0, 1], 0)).astype(jnp.float32)
    wave_copy.wait()
    held = jnp.where(live(facts, wave_ref.shape), wave_ref[...], 0.0)
    u_ref[...] = (held * SCALE).astype(jnp.bfloat16)
    far_u_ref[...] = u_ref[...]
    facts_ref[...] = jnp.where(lines == 0, total(held * held), facts)


def near_kernel(size, width, rows, left_hbm, right_hbm, self_ref, near_ref, out_ref, left_far, right_far, left_row, right_row,
                left_own, right_own, sems, far_sems, row_sems):
    offsets, _, _ = place(size, width)
    own = fetch(left_hbm, right_hbm, left_own, right_own, sems, [(0, 2), (offsets[0], width)])
    later = fetch(left_hbm, right_hbm, left_far, right_far, far_sems, [(offsets[1], width)])
    later += fetch(left_hbm, right_hbm, left_row, right_row, row_sems, [(o, width) for o in offsets[2 : 2 + rows]])
    for n, (source, first, count) in enumerate(((self_ref, 0, 2), (near_ref, 2, width))):
        for copy in own[n]:
            copy.wait()
        out_ref[n] = terms(source[...], left_own, right_own, first, count)
    for pair in later:
        for copy in pair:
            copy.wait()


def far_kernel(size, width, left_ref, right_ref, far_ref, out_ref):
    _, _, there = place(size, width)
    out_ref[...] = terms(only(there[1], far_ref[...]), left_ref, right_ref, 0, width)


def first_kernel(size, width, rows, *refs):
    near_part_ref, far_part_ref, facts_ref, u_ref, left_ref, right_ref = refs[:6]
    row_refs, (out_ref, w_ref, far_w_ref, stats_ref) = refs[6 : 6 + rows], refs[6 + rows :]
    _, _, there = place(size, width)
    facts = facts_ref[...]
    image = near_part_ref[0] + near_part_ref[1] + far_part_ref[...]
    for r, source in enumerate(row_refs):
        piece = terms(only(there[2 + r], source[...]), left_ref, right_ref, r * width, width)
        out_ref[r] = piece
        image = image + piece
    image = jnp.where(live(facts, image.shape), image, 0.0)
    u = u_ref[...].astype(jnp.float32)
    square = total(u * u)
    cross = total(u * image)
    rho = jnp.where(square > 0.0, cross / square, 0.0)
    w = image - rho * u
    for ref in (w_ref, far_w_ref):
        ref[...] = w.astype(jnp.bfloat16)
    lane = lax.broadcasted_iota(jnp.int32, (1, 128), 1)
    record = jnp.zeros((1, 128), jnp.float32)
    for n, value in enumerate((facts[0:1, 0:1], square, cross, total(w * w), rho)):
        record = jnp.where(lane == n, value, record)
    mine = lax.broadcasted_iota(jnp.int32, stats_ref.shape, 0) == 0
    stats_ref[...] = jnp.where(mine, record, 0.0)


def spread_kernel(one_ref, out_ref):
    for n in range(out_ref.shape[0]):
        out_ref[n] = one_ref[...]


def spread(stats, copies):
    return pl.pallas_call(
        spread_kernel, out_shape=jax.ShapeDtypeStruct((copies,) + stats.shape, stats.dtype),
        in_specs=[VM], out_specs=VM, compiler_params=PARAMS, cost_estimate=COST,
    )(vmem(stats))


def pass_kernel(*refs):
    pass


def after(held, first):
    return pl.pallas_call(
        pass_kernel, out_shape=pltpu.VMEM(held.shape, held.dtype), in_specs=[AN] * 2, out_specs=AN,
        input_output_aliases={0: 0}, compiler_params=PARAMS, cost_estimate=COST,
    )(vmem(held), vmem(first))


def image_kernel(size, width, rows, left_hbm, right_hbm, left_row, right_row, self_ref, near_ref, far_ref, *refs):
    row_refs, (out_ref, left_own, right_own, sems) = refs[:rows], refs[rows:]
    offsets, _, there = place(size, width)
    own = fetch(left_hbm, right_hbm, left_own, right_own, sems, [(0, 2)] + [(o, width) for o in offsets[:2]])
    image = None
    for r, source in enumerate(row_refs):
        piece = terms(only(there[2 + r], source[...]), left_row, right_row, r * width, width)
        image = piece if image is None else image + piece
    at = 0
    for n, source in enumerate((self_ref, near_ref, far_ref)):
        for copy in own[n]:
            copy.wait()
        count = width if n else 2
        piece = terms(only(there[n - 1] if n else True, source[...]), left_own, right_own, at, count)
        image = piece if image is None else image + piece
        at += count
    out_ref[...] = image


def second_kernel(size, width, rows, cells, facts_ref, stats_hbm, hw_ref, near_part_ref, far_part_ref, row_part_ref,
                  first_hbm, second_hbm, stats_ref, first_ref, second_ref, sems):
    _, partners, _ = place(size, width)
    stats_copy = pltpu.make_async_copy(stats_hbm.at[:, 0], stats_ref, sems.at[2])
    stats_copy.start()
    facts = facts_ref[...]
    stats_copy.wait()
    stats = stats_ref[...]
    sums = jnp.sum(jnp.sum(stats, axis=0), axis=0, keepdims=True)
    start, square, cross, inner = (sums[:, i : i + 1] for i in range(4))
    scale = lax.rsqrt(start / cells + 1e-06) * (1.0 / SCALE)
    parts = [near_part_ref[0], near_part_ref[1], far_part_ref[...]] + [row_part_ref[r] for r in range(rows)]
    cell = live(facts, parts[0].shape)
    first_ref[...] = jnp.where(cell, sum(parts[1:], parts[0]), 0.0) * scale
    first_copy = pltpu.make_async_copy(first_ref, first_hbm.at[0], sems.at[0])
    first_copy.start()
    rho = cross / square
    gap = stats[:, :, 4:5] - rho[None]
    residual = inner + jnp.sum(jnp.sum(stats[:, :, 1:2] * gap * gap, axis=0), axis=0, keepdims=True)
    second_scale = scale * lax.rsqrt(scale * scale * (residual / cells) + 1e-06)
    line = lax.broadcasted_iota(jnp.int32, gap.shape, 1)
    sector = jnp.where(line == 0, lax.broadcasted_iota(jnp.int32, gap.shape, 0), -1)
    image = hw_ref[...]
    for n, part in enumerate(parts):
        own_gap = jnp.sum(jnp.sum(jnp.where(sector == partners[n], gap, 0.0), axis=0), axis=0, keepdims=True)
        image = image + own_gap * part
    second_ref[...] = jnp.where(cell, image, 0.0) * second_scale
    second_copy = pltpu.make_async_copy(second_ref, second_hbm.at[0], sems.at[1])
    second_copy.start()
    first_copy.wait()
    second_copy.wait()


def body(wavefunction, sector_dims, left_env, right_env):
    size = lax.axis_size("sector")
    block = wavefunction.shape[1]
    square = (block, block)
    width = (right_env.shape[1] - 2) // 4
    near, far, row_pairs = swap_pairs(size)
    rows = len(row_pairs)
    cells = float(size * block * block)
    few, every, side, last = ((n,) + square for n in (2 + width, 2 + 2 * width, width, rows * width))
    f32, bf16 = jnp.float32, jnp.bfloat16
    dma = pltpu.SemaphoreType.DMA

    u, far_u, facts = pl.pallas_call(
        start_kernel, out_shape=(pltpu.VMEM(square, bf16), pltpu.VMEM(square, bf16), pltpu.VMEM((8, 128), f32)),
        in_specs=[HB, HB], out_specs=(VM,) * 3,
        scratch_shapes=[pltpu.VMEM(square, f32), pltpu.SMEM((1, 2), jnp.int32), dma((2,))],
        compiler_params=PARAMS, cost_estimate=COST,
    )(hbm(wavefunction), hbm(sector_dims))

    left_env, right_env = hbm(left_env), hbm(right_env)
    row_u = [vmem(swap(u, "sector", p)) for p in row_pairs]
    near_u = vmem(swap(u, "sector", near))
    far_u = vmem(swap(after(far_u, near_u), "sector", far))
    near_part, left_far, right_far, left_row, right_row = pl.pallas_call(
        functools.partial(near_kernel, size, width, rows),
        out_shape=(pltpu.VMEM((2,) + square, f32),) + (pltpu.VMEM(side, bf16),) * 2 + (pltpu.VMEM(last, bf16),) * 2,
        in_specs=[HB] * 2 + [VM] * 2, out_specs=(VM,) * 5,
        scratch_shapes=[pltpu.VMEM(few, bf16)] * 2 + [dma((2, 2)), dma((1, 2)), dma((rows, 2))],
        compiler_params=PARAMS, cost_estimate=LONG,
    )(left_env, right_env, vmem(u), near_u)
    near_part, facts, left_row, right_row = vmem(near_part), vmem(facts), vmem(left_row), vmem(right_row)
    far_part = vmem(pl.pallas_call(
        functools.partial(far_kernel, size, width), out_shape=pltpu.VMEM(square, f32),
        in_specs=[VM] * 3, out_specs=VM, compiler_params=PARAMS, cost_estimate=LONG,
    )(vmem(left_far), vmem(right_far), far_u))
    row_part, w, far_w, stats = pl.pallas_call(
        functools.partial(first_kernel, size, width, rows),
        out_shape=(pltpu.VMEM((rows,) + square, f32),) + (pltpu.VMEM(square, bf16),) * 2 + (pltpu.VMEM((8, 128), f32),),
        in_specs=[VM] * (6 + rows), out_specs=(VM,) * 4, compiler_params=PARAMS, cost_estimate=COST,
    )(near_part, far_part, facts, vmem(u), left_row, right_row, *row_u)

    row_w = [vmem(swap(w, "sector", p)) for p in row_pairs]
    near_w = vmem(swap(w, "sector", near))
    far_w = vmem(swap(after(far_w, near_w), "sector", far))
    stats = lax.all_gather(spread(stats, COPIES), "sector", axis=0)
    hw = pl.pallas_call(
        functools.partial(image_kernel, size, width, rows), out_shape=pltpu.VMEM(square, f32),
        in_specs=[HB] * 2 + [VM] * (5 + rows), out_specs=VM,
        scratch_shapes=[pltpu.VMEM(every, bf16)] * 2 + [dma((3, 2))],
        compiler_params=PARAMS, cost_estimate=COST,
    )(left_env, right_env, left_row, right_row, vmem(w), near_w, far_w, *row_w)
    return pl.pallas_call(
        functools.partial(second_kernel, size, width, rows, cells),
        out_shape=(jax.ShapeDtypeStruct((1,) + square, f32),) * 2,
        in_specs=[VM, HB] + [VM] * 4, out_specs=(HB, HB),
        scratch_shapes=[pltpu.VMEM((size, 8, 128), f32), pltpu.VMEM(square, f32), pltpu.VMEM(square, f32), dma((3,))],
        compiler_params=PARAMS, cost_estimate=COST,
    )(facts, hbm(stats), vmem(hw), near_part, far_part, vmem(row_part))


def solution(mesh):
    placed = (
        P(("groups", "sector"), None, None),
        P(("groups", "sector"), None),
        P(("groups", "sector"), None, None, None),
        P(("groups", "sector"), None, None, None),
    )
    return jax.shard_map(
        body,
        mesh=mesh,
        in_specs=placed,
        out_specs=(P(("groups", "sector"), None, None), P(("groups", "sector"), None, None)),
        check_vma=False,
    )
```

```python
import functools

import jax
import jax.numpy as jnp
from jax import lax
from jax.experimental import pallas as pl
from jax.experimental.pallas import tpu as pltpu
from jax.sharding import PartitionSpec as P

QD = 8
SCALE = 1024.0
NT = (((1,), (1,)), ((), ()))
VM = pl.BlockSpec(memory_space=pltpu.VMEM)
HB = pl.BlockSpec(memory_space=pltpu.HBM)
COST = pl.CostEstimate(flops=1, bytes_accessed=1, transcendentals=0)
LONG = pl.CostEstimate(flops=4000000000, bytes_accessed=1, transcendentals=0)
PARAMS = pltpu.CompilerParams(vmem_limit_bytes=16 * 1024 * 1024)


def vmem(x):
    return pltpu.with_memory_space_constraint(x, pltpu.VMEM)


def hbm(x):
    return pltpu.with_memory_space_constraint(x, pltpu.HBM)


def call(kernel, out_shape, in_specs, out_specs, scratch=(), cost=COST):
    return pl.pallas_call(
        kernel, out_shape=out_shape, in_specs=in_specs, out_specs=out_specs, scratch_shapes=list(scratch),
        compiler_params=PARAMS, cost_estimate=cost,
    )


def swap(x, axis, pairs):
    to = {a: b for p in pairs for a, b in (p, p[::-1])}
    return lax.ppermute(x, axis, [(s, to.get(s, s)) for s in range(lax.axis_size(axis))])


def swap_pairs(size):
    rows = size // QD
    near = [(s, s + 1) for s in range(0, size, 2)]
    row_even = [(s, s + QD) for r in range(0, rows - 1, 2) for s in range(r * QD, r * QD + QD)]
    row_odd = [(s, s + QD) for r in range(1, rows - 1, 2) for s in range(r * QD, r * QD + QD)]
    return near, [p for p in (row_even, row_odd) if p]


def far_move(near_block, axis):
    hops = [(s, s + 2 if s % 2 == 0 else s - 2) for s in range(lax.axis_size(axis))]
    return lax.ppermute(near_block, axis, [(a, b) for a, b in hops if b >= 0 and a // QD == b // QD])


def place(size, width):
    me = lax.axis_index("sector")
    odd = lax.rem(me, 2) == 1
    row_odd = lax.rem(lax.div(me, QD), 2) == 1
    low, high, down, up = 2, 2 + width, 2 + 2 * width, 2 + 3 * width
    offsets = [jnp.where(odd, low, high), jnp.where(odd, high, low),
               jnp.where(row_odd, down, up), jnp.where(row_odd, up, down)]
    partners = [jnp.where(odd, me - 1, me + 1), jnp.where(odd, me + 1, me - 1),
                jnp.where(row_odd, me - QD, me + QD), jnp.where(row_odd, me + QD, me - QD)]
    there = [True if size // QD % 2 == 0 else (partners[2] >= 0) & (partners[2] < size),
             (partners[3] >= 0) & (partners[3] < size)]
    partners = [me] + [jnp.clip(p, 0, size - 1) for p in partners]
    return offsets, partners, there


def live(facts, shape):
    row_ok = lax.broadcasted_iota(jnp.int32, shape, 0).astype(jnp.float32) < facts[1:2, 0:1]
    col_ok = lax.broadcasted_iota(jnp.int32, shape, 1).astype(jnp.float32) < facts[2:3, 0:1]
    return row_ok & col_ok


def total(x):
    return jnp.sum(jnp.sum(x, axis=0, keepdims=True), axis=1, keepdims=True)


def only(there, block):
    return block if there is True else jnp.where(there, block, jnp.zeros_like(block))


def terms(src, left_ref, right_ref, first, count, copies=None):
    size = src.shape[0]
    image = None
    if copies is None:
        right = right_ref[pl.ds(first, count)].reshape(count * size, size)
        partial_t = lax.dot_general(right, src, NT, preferred_element_type=jnp.float32).astype(jnp.bfloat16)
    for k in range(count):
        if copies is None:
            held = partial_t[k * size : (k + 1) * size]
        else:
            for copy in copies[first + k]:
                copy.wait()
            held = lax.dot_general(right_ref[first + k], src, NT, preferred_element_type=jnp.float32).astype(jnp.bfloat16)
        piece = lax.dot_general(left_ref[first + k], held, NT, preferred_element_type=jnp.float32)
        image = piece if image is None else image + piece
    return image


def fetch(left_hbm, right_hbm, left_ref, right_ref, sems, spans):
    copies = []
    for offset, count in spans:
        for k in range(count):
            at = len(copies)
            pair = [
                pltpu.make_async_copy(source.at[0, pl.ds(offset + k, 1)], target.at[pl.ds(at, 1)], sems.at[at, e])
                for e, (source, target) in enumerate(((right_hbm, right_ref), (left_hbm, left_ref)))
            ]
            for copy in pair:
                copy.start()
            copies.append(pair)
    return copies


def start_kernel(wave_hbm, dims_hbm, u_ref, facts_ref, wave_ref, dims_ref, sems):
    wave_copy = pltpu.make_async_copy(wave_hbm.at[0], wave_ref, sems.at[0])
    dims_copy = pltpu.make_async_copy(dims_hbm, dims_ref, sems.at[1])
    dims_copy.start()
    wave_copy.start()
    dims_copy.wait()
    lines = lax.broadcasted_iota(jnp.int32, (8, 128), 0)
    facts = jnp.where(lines == 1, dims_ref[0, 0], jnp.where(lines == 2, dims_ref[0, 1], 0)).astype(jnp.float32)
    wave_copy.wait()
    held = jnp.where(live(facts, wave_ref.shape), wave_ref[...], 0.0)
    u_ref[...] = (held * SCALE).astype(jnp.bfloat16)
    facts_ref[...] = jnp.where(lines == 0, total(held * held), facts)


def near_kernel(size, width, rows, left_hbm, right_hbm, self_ref, near_ref, out_ref, left_far, right_far, left_row, right_row,
                left_own, right_own, sems, far_sems, row_sems):
    offsets, _, _ = place(size, width)
    own = fetch(left_hbm, right_hbm, left_own, right_own, sems, [(0, 2), (offsets[0], width)])
    later = fetch(left_hbm, right_hbm, left_far, right_far, far_sems, [(offsets[1], width)])
    later += fetch(left_hbm, right_hbm, left_row, right_row, row_sems, [(o, width) for o in offsets[2 : 2 + rows]])
    out_ref[0] = terms(self_ref[...], left_own, right_own, 0, 2, own)
    out_ref[1] = terms(near_ref[...], left_own, right_own, 2, width, own)
    for pair in later:
        for copy in pair:
            copy.wait()


def far_kernel(width, left_ref, right_ref, far_ref, out_ref):
    out_ref[...] = terms(far_ref[...], left_ref, right_ref, 0, width)


def first_kernel(size, width, rows, *refs):
    near_part_ref, far_part_ref, facts_ref, u_ref, left_ref, right_ref = refs[:6]
    row_refs, (out_ref, w_ref, stats_ref) = refs[6 : 6 + rows], refs[6 + rows :]
    _, _, there = place(size, width)
    facts = facts_ref[...]
    image = near_part_ref[0] + near_part_ref[1] + far_part_ref[...]
    for r, source in enumerate(row_refs):
        piece = terms(only(there[r], source[...]), left_ref, right_ref, r * width, width)
        out_ref[r] = piece
        image = image + piece
    image = jnp.where(live(facts, image.shape), image, 0.0)
    u = u_ref[...].astype(jnp.float32)
    square = total(u * u)
    cross = total(u * image)
    rho = jnp.where(square > 0.0, cross / square, 0.0)
    w = image - rho * u
    w_ref[...] = w.astype(jnp.bfloat16)
    lines = lax.broadcasted_iota(jnp.int32, (8, 128), 0)
    stats = jnp.where(lines == 0, facts, 0.0)
    for line, value in ((1, square), (2, cross), (3, total(w * w)), (4, rho)):
        stats = jnp.where(lines == line, value, stats)
    stats_ref[...] = stats


def spread_kernel(one_ref, out_ref):
    for n in range(out_ref.shape[0]):
        out_ref[n] = one_ref[...]


def image_kernel(size, width, rows, left_hbm, right_hbm, left_row, right_row, self_ref, near_ref, far_ref, *refs):
    row_refs, (out_ref, left_own, right_own, sems) = refs[:rows], refs[rows:]
    offsets, _, there = place(size, width)
    own = fetch(left_hbm, right_hbm, left_own, right_own, sems, [(0, 2)] + [(o, width) for o in offsets[:2]])
    image = None
    for r, source in enumerate(row_refs):
        piece = terms(only(there[r], source[...]), left_row, right_row, r * width, width)
        image = piece if image is None else image + piece
    image = image + terms(self_ref[...], left_own, right_own, 0, 2, own)
    image = image + terms(near_ref[...], left_own, right_own, 2, width, own)
    out_ref[...] = image + terms(far_ref[...], left_own, right_own, 2 + width, width, own)


def second_kernel(size, width, rows, cells, facts_ref, stats_ref, hw_ref, near_part_ref, far_part_ref, row_part_ref,
                  first_hbm, second_hbm, first_ref, second_ref, sems):
    _, partners, _ = place(size, width)
    facts = facts_ref[...]
    stats = stats_ref[...]
    sums = jnp.sum(stats, axis=0)
    start, square, cross, inner = (sums[i : i + 1, 0:1] for i in range(4))
    scale = lax.rsqrt(start / cells + 1e-06) * (1.0 / SCALE)
    parts = [near_part_ref[0], near_part_ref[1], far_part_ref[...]] + [row_part_ref[r] for r in range(rows)]
    cell = live(facts, parts[0].shape)
    first_ref[...] = jnp.where(cell, sum(parts[1:], parts[0]), 0.0) * scale
    first_copy = pltpu.make_async_copy(first_ref, first_hbm.at[0], sems.at[0])
    first_copy.start()
    rho = cross / square
    gap = stats[:, 4:5, 0:1] - rho[None]
    residual = inner + jnp.sum(stats[:, 1:2, 0:1] * gap * gap, axis=0)
    second_scale = scale * lax.rsqrt(scale * scale * (residual / cells) + 1e-06)
    image = hw_ref[...]
    for n, part in enumerate(parts):
        image = image + (stats_ref[partners[n], 4:5, 0:1] - rho) * part
    second_ref[...] = jnp.where(cell, image, 0.0) * second_scale
    second_copy = pltpu.make_async_copy(second_ref, second_hbm.at[0], sems.at[1])
    second_copy.start()
    first_copy.wait()
    second_copy.wait()


def body(wavefunction, sector_dims, left_env, right_env):
    size = lax.axis_size("sector")
    block = wavefunction.shape[1]
    square = (block, block)
    width = (right_env.shape[1] - 2) // 4
    near, row_pairs = swap_pairs(size)
    rows = len(row_pairs)
    cells = float(size * block * block)
    few, every, side, last = ((n,) + square for n in (2 + width, 2 + 2 * width, width, rows * width))
    f32, bf16 = jnp.float32, jnp.bfloat16
    dma = pltpu.SemaphoreType.DMA

    u, facts = call(
        start_kernel, (pltpu.VMEM(square, bf16), pltpu.VMEM((8, 128), f32)), [HB, HB], (VM, VM),
        [pltpu.VMEM(square, f32), pltpu.SMEM((1, 2), jnp.int32), dma((2,))],
    )(hbm(wavefunction), hbm(sector_dims))

    left_env, right_env = hbm(left_env), hbm(right_env)
    row_u = [vmem(swap(u, "sector", p)) for p in row_pairs]
    near_u = vmem(swap(u, "sector", near))
    far_u = vmem(far_move(near_u, "sector"))
    near_part, left_far, right_far, left_row, right_row = call(
        functools.partial(near_kernel, size, width, rows),
        (pltpu.VMEM((2,) + square, f32),) + (pltpu.VMEM(side, bf16),) * 2 + (pltpu.VMEM(last, bf16),) * 2,
        [HB] * 2 + [VM] * 2, (VM,) * 5,
        [pltpu.VMEM(few, bf16)] * 2 + [dma((2 + width, 2)), dma((width, 2)), dma((rows * width, 2))], LONG,
    )(left_env, right_env, vmem(u), near_u)
    near_part, facts, left_row, right_row = vmem(near_part), vmem(facts), vmem(left_row), vmem(right_row)
    far_part = vmem(call(
        functools.partial(far_kernel, width), pltpu.VMEM(square, f32), [VM] * 3, VM, cost=LONG,
    )(vmem(left_far), vmem(right_far), far_u))
    row_part, w, stats = call(
        functools.partial(first_kernel, size, width, rows),
        (pltpu.VMEM((rows,) + square, f32), pltpu.VMEM(square, bf16), pltpu.VMEM((8, 128), f32)),
        [VM] * (6 + rows), (VM,) * 3,
    )(near_part, far_part, facts, vmem(u), left_row, right_row, *row_u)

    row_w = [vmem(swap(w, "sector", p)) for p in row_pairs]
    near_w = vmem(swap(w, "sector", near))
    far_w = vmem(far_move(near_w, "sector"))
    stats = call(spread_kernel, jax.ShapeDtypeStruct((size, 8, 128), f32), [VM], VM)(vmem(stats))
    stats = lax.all_to_all(stats, "sector", 0, 0, tiled=True)
    hw = call(
        functools.partial(image_kernel, size, width, rows), pltpu.VMEM(square, f32), [HB] * 2 + [VM] * (5 + rows), VM,
        [pltpu.VMEM(every, bf16)] * 2 + [dma((2 + 2 * width, 2))],
    )(left_env, right_env, left_row, right_row, vmem(w), near_w, far_w, *row_w)
    return call(
        functools.partial(second_kernel, size, width, rows, cells),
        (jax.ShapeDtypeStruct((1,) + square, f32),) * 2, [VM] * 6, (HB, HB),
        [pltpu.VMEM(square, f32)] * 2 + [dma((2,))],
    )(facts, stats, vmem(hw), near_part, far_part, vmem(row_part))


def solution(mesh):
    placed = (
        P(("groups", "sector"), None, None),
        P(("groups", "sector"), None),
        P(("groups", "sector"), None, None, None),
        P(("groups", "sector"), None, None, None),
    )
    return jax.shard_map(
        body,
        mesh=mesh,
        in_specs=placed,
        out_specs=(P(("groups", "sector"), None, None), P(("groups", "sector"), None, None)),
        check_vma=False,
    )
```

```python
import functools

import jax
import jax.numpy as jnp
from jax import lax
from jax.experimental import pallas as pl
from jax.experimental.pallas import tpu as pltpu
from jax.sharding import PartitionSpec as P

QD = 8
SCALE = 1024.0
NT = (((1,), (1,)), ((), ()))
VM = pl.BlockSpec(memory_space=pltpu.VMEM)
HB = pl.BlockSpec(memory_space=pltpu.HBM)
AN = pl.BlockSpec(memory_space=pl.ANY)
COST = pl.CostEstimate(flops=1, bytes_accessed=1, transcendentals=0)
LONG = pl.CostEstimate(flops=4000000000, bytes_accessed=1, transcendentals=0)
PARAMS = pltpu.CompilerParams(vmem_limit_bytes=16 * 1024 * 1024)


def vmem(x):
    return pltpu.with_memory_space_constraint(x, pltpu.VMEM)


def hbm(x):
    return pltpu.with_memory_space_constraint(x, pltpu.HBM)


def call(kernel, out_shape, in_specs, out_specs, scratch=(), cost=COST, aliases={}):
    return pl.pallas_call(
        kernel, out_shape=out_shape, in_specs=in_specs, out_specs=out_specs, scratch_shapes=list(scratch),
        compiler_params=PARAMS, cost_estimate=cost, input_output_aliases=aliases,
    )


def swap(x, axis, pairs):
    to = {a: b for p in pairs for a, b in (p, p[::-1])}
    return lax.ppermute(x, axis, [(s, to.get(s, s)) for s in range(lax.axis_size(axis))])


def swap_pairs(size):
    rows = size // QD
    near = [(s, s + 1) for s in range(0, size, 2)]
    far = [(s, s + 1) for s in range(1, size - 1, 2) if s % QD != QD - 1]
    row_even = [(s, s + QD) for r in range(0, rows - 1, 2) for s in range(r * QD, r * QD + QD)]
    row_odd = [(s, s + QD) for r in range(1, rows - 1, 2) for s in range(r * QD, r * QD + QD)]
    return near, far, [p for p in (row_even, row_odd) if p]


def place(size, width):
    me = lax.axis_index("sector")
    column = lax.rem(me, QD)
    odd = lax.rem(me, 2) == 1
    row_odd = lax.rem(lax.div(me, QD), 2) == 1
    low, high, down, up = 2, 2 + width, 2 + 2 * width, 2 + 3 * width
    offsets = [jnp.where(odd, low, high), jnp.where(odd, high, low),
               jnp.where(row_odd, down, up), jnp.where(row_odd, up, down)]
    partners = [jnp.where(odd, me - 1, me + 1), jnp.where(odd, me + 1, me - 1),
                jnp.where(row_odd, me - QD, me + QD), jnp.where(row_odd, me + QD, me - QD)]
    there = [(column != 0) & (column != QD - 1),
             True if size // QD % 2 == 0 else (partners[2] >= 0) & (partners[2] < size),
             (partners[3] >= 0) & (partners[3] < size)]
    partners = [me] + [jnp.clip(p, 0, size - 1) for p in partners]
    return offsets, partners, there


def live(facts, shape):
    row_ok = lax.broadcasted_iota(jnp.int32, shape, 0).astype(jnp.float32) < facts[1:2, 0:1]
    col_ok = lax.broadcasted_iota(jnp.int32, shape, 1).astype(jnp.float32) < facts[2:3, 0:1]
    return row_ok & col_ok


def total(x):
    return jnp.sum(jnp.sum(x, axis=0, keepdims=True), axis=1, keepdims=True)


def only(there, block):
    return block if there is True else jnp.where(there, block, jnp.zeros_like(block))


def terms(src, left_ref, right_ref, first, count):
    size = src.shape[0]
    right = right_ref[pl.ds(first, count)].reshape(count * size, size)
    partial_t = lax.dot_general(right, src, NT, preferred_element_type=jnp.float32).astype(jnp.bfloat16)
    image = None
    for k in range(count):
        piece = lax.dot_general(
            left_ref[first + k], partial_t[k * size : (k + 1) * size], NT, preferred_element_type=jnp.float32
        )
        image = piece if image is None else image + piece
    return image


def fetch(left_hbm, right_hbm, left_ref, right_ref, sems, spans):
    copies = []
    at = 0
    for n, (offset, count) in enumerate(spans):
        pair = [
            pltpu.make_async_copy(source.at[0, pl.ds(offset, count)], target.at[pl.ds(at, count)], sems.at[n, e])
            for e, (source, target) in enumerate(((right_hbm, right_ref), (left_hbm, left_ref)))
        ]
        for copy in pair:
            copy.start()
        copies.append(pair)
        at += count
    return copies


def finish(copies):
    for copy in copies:
        copy.wait()


def start_kernel(wave_hbm, dims_hbm, u_ref, far_u_ref, facts_ref, wave_ref, dims_ref, sems):
    wave_copy = pltpu.make_async_copy(wave_hbm.at[0], wave_ref, sems.at[0])
    dims_copy = pltpu.make_async_copy(dims_hbm, dims_ref, sems.at[1])
    dims_copy.start()
    wave_copy.start()
    dims_copy.wait()
    lines = lax.broadcasted_iota(jnp.int32, (8, 128), 0)
    facts = jnp.where(lines == 1, dims_ref[0, 0], jnp.where(lines == 2, dims_ref[0, 1], 0)).astype(jnp.float32)
    wave_copy.wait()
    held = jnp.where(live(facts, wave_ref.shape), wave_ref[...], 0.0)
    for ref in (u_ref, far_u_ref):
        ref[...] = (held * SCALE).astype(jnp.bfloat16)
    facts_ref[...] = facts


def pass_kernel(*refs):
    pass


def after(held, first):
    return call(pass_kernel, pltpu.VMEM(held.shape, held.dtype), [AN] * 2, AN, aliases={0: 0})(vmem(held), first)


def near_kernel(size, width, rows, left_hbm, right_hbm, wave_hbm, facts_ref, self_ref, near_ref, out_ref, sums_ref,
                left_far, right_far, left_row, right_row, left_own, right_own, wave_ref, sems, far_sems, row_sems, wave_sem):
    offsets, _, _ = place(size, width)
    wave_copy = pltpu.make_async_copy(wave_hbm.at[0], wave_ref, wave_sem)
    own = fetch(left_hbm, right_hbm, left_own, right_own, sems, [(0, 2), (offsets[0], width)])
    wave_copy.start()
    later = fetch(left_hbm, right_hbm, left_far, right_far, far_sems, [(offsets[1], width)])
    later += fetch(left_hbm, right_hbm, left_row, right_row, row_sems, [(o, width) for o in offsets[2 : 2 + rows]])
    u = self_ref[...].astype(jnp.float32)
    lines = lax.broadcasted_iota(jnp.int32, (8, 128), 0)
    sums = jnp.where(lines == 1, total(u * u), 0.0)
    finish(own[0])
    out_ref[0] = terms(self_ref[...], left_own, right_own, 0, 2)
    finish(own[1])
    out_ref[1] = terms(near_ref[...], left_own, right_own, 2, width)
    wave_copy.wait()
    held = jnp.where(live(facts_ref[...], wave_ref.shape), wave_ref[...], 0.0)
    sums_ref[...] = jnp.where(lines == 0, total(held * held), sums)
    for pair in later:
        finish(pair)


def far_kernel(size, width, left_ref, right_ref, far_ref, out_ref):
    _, _, there = place(size, width)
    out_ref[...] = terms(only(there[0], far_ref[...]), left_ref, right_ref, 0, width)


def first_kernel(size, width, rows, *refs):
    near_part_ref, far_part_ref, facts_ref, sums_ref, u_ref, left_ref, right_ref = refs[:7]
    row_refs, (out_ref, w_ref, far_w_ref, sums_out_ref) = refs[7 : 7 + rows], refs[7 + rows :]
    _, _, there = place(size, width)
    image = near_part_ref[0] + near_part_ref[1] + far_part_ref[...]
    for r, source in enumerate(row_refs):
        piece = terms(only(there[1 + r], source[...]), left_ref, right_ref, r * width, width)
        out_ref[r] = piece
        image = image + piece
    image = jnp.where(live(facts_ref[...], image.shape), image, 0.0)
    u = u_ref[...].astype(jnp.float32)
    square = sums_ref[1:2, 0:1]
    cross = total(u * image)
    rho = jnp.where(square > 0.0, cross / square, 0.0)
    for ref in (w_ref, far_w_ref):
        ref[...] = (image - rho * u).astype(jnp.bfloat16)
    lines = lax.broadcasted_iota(jnp.int32, (8, 128), 0)
    sums_out_ref[...] = jnp.where(lines == 2, cross, jnp.where(lines == 4, rho, sums_ref[...]))


def spread_kernel(sums_ref, w_ref, held_in, out_ref, held_out):
    w = w_ref[...].astype(jnp.float32)
    lines = lax.broadcasted_iota(jnp.int32, (8, 128), 0)
    sums = jnp.where(lines == 3, total(w * w), sums_ref[...])
    for n in range(out_ref.shape[0]):
        out_ref[n] = sums


def image_kernel(size, width, rows, left_hbm, right_hbm, left_row, right_row, self_ref, near_ref, far_ref, *refs):
    row_refs, (out_ref, left_own, right_own, sems) = refs[:rows], refs[rows:]
    offsets, _, there = place(size, width)
    own = fetch(left_hbm, right_hbm, left_own, right_own, sems, [(0, 2)] + [(o, width) for o in offsets[:2]])
    image = None
    for r, source in enumerate(row_refs):
        piece = terms(only(there[1 + r], source[...]), left_row, right_row, r * width, width)
        image = piece if image is None else image + piece
    finish(own[0])
    image = image + terms(self_ref[...], left_own, right_own, 0, 2)
    finish(own[1])
    image = image + terms(near_ref[...], left_own, right_own, 2, width)
    finish(own[2])
    out_ref[...] = image + terms(only(there[0], far_ref[...]), left_own, right_own, 2 + width, width)


def second_kernel(size, width, rows, cells, facts_ref, stats_ref, hw_ref, near_part_ref, far_part_ref, row_part_ref,
                  first_hbm, second_hbm, first_ref, second_ref, sems):
    _, partners, _ = place(size, width)
    facts = facts_ref[...]
    stats = stats_ref[...]
    sums = jnp.sum(stats, axis=0)
    start, square, cross, inner = (sums[i : i + 1, 0:1] for i in range(4))
    scale = lax.rsqrt(start / cells + 1e-06) * (1.0 / SCALE)
    parts = [near_part_ref[0], near_part_ref[1], far_part_ref[...]] + [row_part_ref[r] for r in range(rows)]
    cell = live(facts, parts[0].shape)
    first_ref[...] = jnp.where(cell, sum(parts[1:], parts[0]), 0.0) * scale
    first_copy = pltpu.make_async_copy(first_ref, first_hbm.at[0], sems.at[0])
    first_copy.start()
    rho = cross / square
    gap = stats[:, 4:5, 0:1] - rho[None]
    residual = inner + jnp.sum(stats[:, 1:2, 0:1] * gap * gap, axis=0)
    second_scale = scale * lax.rsqrt(scale * scale * (residual / cells) + 1e-06)
    image = hw_ref[...]
    for n, part in enumerate(parts):
        image = image + (stats_ref[partners[n], 4:5, 0:1] - rho) * part
    second_ref[...] = jnp.where(cell, image, 0.0) * second_scale
    second_copy = pltpu.make_async_copy(second_ref, second_hbm.at[0], sems.at[1])
    second_copy.start()
    first_copy.wait()
    second_copy.wait()


def body(wavefunction, sector_dims, left_env, right_env):
    size = lax.axis_size("sector")
    block = wavefunction.shape[1]
    square = (block, block)
    width = (right_env.shape[1] - 2) // 4
    near, far, row_pairs = swap_pairs(size)
    rows = len(row_pairs)
    cells = float(size * block * block)
    few, every, side, last = ((n,) + square for n in (2 + width, 2 + 2 * width, width, rows * width))
    f32, bf16 = jnp.float32, jnp.bfloat16
    dma = pltpu.SemaphoreType.DMA

    u, far_u, facts = call(
        start_kernel, (pltpu.VMEM(square, bf16),) * 2 + (pltpu.VMEM((8, 128), f32),), [HB, HB], (VM,) * 3,
        [pltpu.VMEM(square, f32), pltpu.SMEM((1, 2), jnp.int32), dma((2,))],
    )(hbm(wavefunction), hbm(sector_dims))

    left_env, right_env = hbm(left_env), hbm(right_env)
    row_u = [vmem(swap(u, "sector", p)) for p in row_pairs]
    near_u = vmem(swap(u, "sector", near))
    far_u = vmem(swap(after(far_u, near_u), "sector", far))
    u, facts = vmem(u), vmem(facts)
    near_part, sums, left_far, right_far, left_row, right_row = call(
        functools.partial(near_kernel, size, width, rows),
        (pltpu.VMEM((2,) + square, f32), pltpu.VMEM((8, 128), f32)) + (pltpu.VMEM(side, bf16),) * 2 + (pltpu.VMEM(last, bf16),) * 2,
        [HB] * 3 + [VM] * 3, (VM,) * 6,
        [pltpu.VMEM(few, bf16)] * 2 + [pltpu.VMEM(square, f32), dma((2, 2)), dma((1, 2)), dma((rows, 2)), dma], LONG,
    )(left_env, right_env, hbm(wavefunction), facts, u, near_u)
    near_part, left_row, right_row = vmem(near_part), vmem(left_row), vmem(right_row)
    far_part = vmem(call(
        functools.partial(far_kernel, size, width), pltpu.VMEM(square, f32), [VM] * 3, VM, cost=LONG,
    )(vmem(left_far), vmem(right_far), far_u))
    row_part, w, far_w, sums = call(
        functools.partial(first_kernel, size, width, rows),
        (pltpu.VMEM((rows,) + square, f32),) + (pltpu.VMEM(square, bf16),) * 2 + (pltpu.VMEM((8, 128), f32),),
        [VM] * (7 + rows), (VM,) * 4,
    )(near_part, far_part, facts, vmem(sums), u, left_row, right_row, *row_u)

    row_w = [vmem(swap(w, "sector", p)) for p in row_pairs]
    near_w = vmem(swap(w, "sector", near))
    w = vmem(w)
    stats, far_w = call(
        spread_kernel, (jax.ShapeDtypeStruct((size, 8, 128), f32), pltpu.VMEM(square, bf16)), [VM] * 2 + [AN], (VM, AN),
        aliases={2: 1},
    )(vmem(sums), w, vmem(far_w))
    far_w = vmem(swap(after(far_w, near_w), "sector", far))
    stats = lax.all_to_all(stats, "sector", 0, 0, tiled=True)
    hw = call(
        functools.partial(image_kernel, size, width, rows), pltpu.VMEM(square, f32), [HB] * 2 + [VM] * (5 + rows), VM,
        [pltpu.VMEM(every, bf16)] * 2 + [dma((3, 2))],
    )(left_env, right_env, left_row, right_row, w, near_w, far_w, *row_w)
    return call(
        functools.partial(second_kernel, size, width, rows, cells),
        (jax.ShapeDtypeStruct((1,) + square, f32),) * 2, [VM] * 6, (HB, HB),
        [pltpu.VMEM(square, f32)] * 2 + [dma((2,))],
    )(facts, stats, vmem(hw), near_part, far_part, vmem(row_part))


def solution(mesh):
    placed = (
        P(("groups", "sector"), None, None),
        P(("groups", "sector"), None),
        P(("groups", "sector"), None, None, None),
        P(("groups", "sector"), None, None, None),
    )
    return jax.shard_map(
        body,
        mesh=mesh,
        in_specs=placed,
        out_specs=(P(("groups", "sector"), None, None), P(("groups", "sector"), None, None)),
        check_vma=False,
    )
```

```python
import functools

import jax
import jax.numpy as jnp
from jax import lax
from jax.experimental import pallas as pl
from jax.experimental.pallas import tpu as pltpu
from jax.sharding import PartitionSpec as P

QD = 8
SCALE = 1024.0
NT = (((1,), (1,)), ((), ()))
VM = pl.BlockSpec(memory_space=pltpu.VMEM)
HB = pl.BlockSpec(memory_space=pltpu.HBM)
AN = pl.BlockSpec(memory_space=pl.ANY)
COST = pl.CostEstimate(flops=1, bytes_accessed=1, transcendentals=0)
LONG = pl.CostEstimate(flops=4000000000, bytes_accessed=1, transcendentals=0)
PARAMS = pltpu.CompilerParams(vmem_limit_bytes=16 * 1024 * 1024)


def vmem(x):
    return pltpu.with_memory_space_constraint(x, pltpu.VMEM)


def hbm(x):
    return pltpu.with_memory_space_constraint(x, pltpu.HBM)


def call(kernel, out_shape, in_specs, out_specs, scratch=(), cost=COST, aliases={}):
    return pl.pallas_call(
        kernel, out_shape=out_shape, in_specs=in_specs, out_specs=out_specs, scratch_shapes=list(scratch),
        compiler_params=PARAMS, cost_estimate=cost, input_output_aliases=aliases,
    )


def swap(x, axis, pairs):
    to = {a: b for p in pairs for a, b in (p, p[::-1])}
    return lax.ppermute(x, axis, [(s, to.get(s, s)) for s in range(lax.axis_size(axis))])


def swap_pairs(size):
    rows = size // QD
    near = [(s, s + 1) for s in range(0, size, 2)]
    far = [(s, s + 1) for s in range(1, size - 1, 2) if s % QD != QD - 1]
    row_even = [(s, s + QD) for r in range(0, rows - 1, 2) for s in range(r * QD, r * QD + QD)]
    row_odd = [(s, s + QD) for r in range(1, rows - 1, 2) for s in range(r * QD, r * QD + QD)]
    return near, far, [p for p in (row_even, row_odd) if p]


def place(size, width):
    me = lax.axis_index("sector")
    column = lax.rem(me, QD)
    odd = lax.rem(me, 2) == 1
    row_odd = lax.rem(lax.div(me, QD), 2) == 1
    low, high, down, up = 2, 2 + width, 2 + 2 * width, 2 + 3 * width
    offsets = [jnp.where(odd, low, high), jnp.where(odd, high, low),
               jnp.where(row_odd, down, up), jnp.where(row_odd, up, down)]
    partners = [jnp.where(odd, me - 1, me + 1), jnp.where(odd, me + 1, me - 1),
                jnp.where(row_odd, me - QD, me + QD), jnp.where(row_odd, me + QD, me - QD)]
    there = [(column != 0) & (column != QD - 1),
             True if size // QD % 2 == 0 else (partners[2] >= 0) & (partners[2] < size),
             (partners[3] >= 0) & (partners[3] < size)]
    partners = [me] + [jnp.clip(p, 0, size - 1) for p in partners]
    return offsets, partners, there


def live(facts, shape):
    row_ok = lax.broadcasted_iota(jnp.int32, shape, 0).astype(jnp.float32) < facts[1:2, 0:1]
    col_ok = lax.broadcasted_iota(jnp.int32, shape, 1).astype(jnp.float32) < facts[2:3, 0:1]
    return row_ok & col_ok


def total(x):
    return jnp.sum(jnp.sum(x, axis=0, keepdims=True), axis=1, keepdims=True)


def only(there, block):
    return block if there is True else jnp.where(there, block, jnp.zeros_like(block))


def terms(src, left_ref, right_ref, first, count):
    size = src.shape[0]
    right = right_ref[pl.ds(first, count)].reshape(count * size, size)
    partial_t = lax.dot_general(right, src, NT, preferred_element_type=jnp.float32).astype(jnp.bfloat16)
    image = None
    for k in range(count):
        piece = lax.dot_general(
            left_ref[first + k], partial_t[k * size : (k + 1) * size], NT, preferred_element_type=jnp.float32
        )
        image = piece if image is None else image + piece
    return image


def fetch(left_hbm, right_hbm, left_ref, right_ref, sems, spans):
    copies = []
    at = 0
    for n, (offset, count) in enumerate(spans):
        pair = [
            pltpu.make_async_copy(source.at[0, pl.ds(offset, count)], target.at[pl.ds(at, count)], sems.at[n, e])
            for e, (source, target) in enumerate(((right_hbm, right_ref), (left_hbm, left_ref)))
        ]
        for copy in pair:
            copy.start()
        copies.append(pair)
        at += count
    return copies


def finish(copies):
    for copy in copies:
        copy.wait()


def start_kernel(wave_hbm, dims_hbm, u_ref, facts_ref, wave_ref, dims_ref, sems):
    wave_copy = pltpu.make_async_copy(wave_hbm.at[0], wave_ref, sems.at[0])
    dims_copy = pltpu.make_async_copy(dims_hbm, dims_ref, sems.at[1])
    dims_copy.start()
    wave_copy.start()
    dims_copy.wait()
    lines = lax.broadcasted_iota(jnp.int32, (8, 128), 0)
    facts = jnp.where(lines == 1, dims_ref[0, 0], jnp.where(lines == 2, dims_ref[0, 1], 0)).astype(jnp.float32)
    wave_copy.wait()
    held = jnp.where(live(facts, wave_ref.shape), wave_ref[...], 0.0)
    u_ref[...] = (held * SCALE).astype(jnp.bfloat16)
    facts_ref[...] = facts


def near_kernel(size, width, rows, left_hbm, right_hbm, wave_hbm, facts_ref, self_ref, near_ref, out_ref, sums_ref,
                left_far, right_far, left_row, right_row, left_own, right_own, wave_ref, sems, far_sems, row_sems, wave_sem):
    offsets, _, _ = place(size, width)
    wave_copy = pltpu.make_async_copy(wave_hbm.at[0], wave_ref, wave_sem)
    own = fetch(left_hbm, right_hbm, left_own, right_own, sems, [(0, 2), (offsets[0], width)])
    wave_copy.start()
    later = fetch(left_hbm, right_hbm, left_far, right_far, far_sems, [(offsets[1], width)])
    later += fetch(left_hbm, right_hbm, left_row, right_row, row_sems, [(o, width) for o in offsets[2 : 2 + rows]])
    u = self_ref[...].astype(jnp.float32)
    lines = lax.broadcasted_iota(jnp.int32, (8, 128), 0)
    sums = jnp.where(lines == 1, total(u * u), 0.0)
    finish(own[0])
    out_ref[0] = terms(self_ref[...], left_own, right_own, 0, 2)
    finish(own[1])
    out_ref[1] = terms(near_ref[...], left_own, right_own, 2, width)
    wave_copy.wait()
    held = jnp.where(live(facts_ref[...], wave_ref.shape), wave_ref[...], 0.0)
    sums_ref[...] = jnp.where(lines == 0, total(held * held), sums)
    for pair in later:
        finish(pair)


def first_kernel(size, width, rows, *refs):
    near_part_ref, facts_ref, sums_ref, u_ref, left_far, right_far, left_row, right_row, far_ref = refs[:9]
    row_refs, (out_ref, w_ref, stats_ref) = refs[9 : 9 + rows], refs[9 + rows :]
    _, _, there = place(size, width)
    out_ref[0] = terms(only(there[0], far_ref[...]), left_far, right_far, 0, width)
    image = near_part_ref[0] + near_part_ref[1] + out_ref[0]
    for r, source in enumerate(row_refs):
        piece = terms(only(there[1 + r], source[...]), left_row, right_row, r * width, width)
        out_ref[1 + r] = piece
        image = image + piece
    image = jnp.where(live(facts_ref[...], image.shape), image, 0.0)
    u = u_ref[...].astype(jnp.float32)
    square = sums_ref[1:2, 0:1]
    cross = total(u * image)
    rho = jnp.where(square > 0.0, cross / square, 0.0)
    w = image - rho * u
    w_ref[...] = w.astype(jnp.bfloat16)
    lines = lax.broadcasted_iota(jnp.int32, (8, 128), 0)
    stats = sums_ref[...]
    for line, value in ((2, cross), (3, total(w * w)), (4, rho)):
        stats = jnp.where(lines == line, value, stats)
    for n in range(stats_ref.shape[0]):
        stats_ref[n] = stats


def image_kernel(size, width, rows, *refs):
    left_hbm, right_hbm, left_row, right_row, self_ref, near_ref, far_ref = refs[:7]
    row_refs, (out_ref, left_own, right_own, sems) = refs[7 : 7 + rows], refs[7 + rows :]
    offsets, _, there = place(size, width)
    own = fetch(left_hbm, right_hbm, left_own, right_own, sems, [(0, 2)] + [(o, width) for o in offsets[:2]])
    image = None
    for r, source in enumerate(row_refs):
        piece = terms(only(there[1 + r], source[...]), left_row, right_row, r * width, width)
        image = piece if image is None else image + piece
    finish(own[0])
    image = image + terms(self_ref[...], left_own, right_own, 0, 2)
    finish(own[1])
    image = image + terms(near_ref[...], left_own, right_own, 2, width)
    finish(own[2])
    out_ref[...] = image + terms(only(there[0], far_ref[...]), left_own, right_own, 2 + width, width)


def second_kernel(size, width, rows, cells, facts_ref, stats_ref, hw_ref, near_part_ref, far_part_ref,
                  first_hbm, second_hbm, first_ref, second_ref, sems):
    _, partners, _ = place(size, width)
    facts = facts_ref[...]
    stats = stats_ref[...]
    sums = jnp.sum(stats, axis=0)
    start, square, cross, inner = (sums[i : i + 1, 0:1] for i in range(4))
    scale = lax.rsqrt(start / cells + 1e-06) * (1.0 / SCALE)
    parts = [near_part_ref[0], near_part_ref[1]] + [far_part_ref[n] for n in range(1 + rows)]
    cell = live(facts, parts[0].shape)
    first_ref[...] = jnp.where(cell, sum(parts[1:], parts[0]), 0.0) * scale
    first_copy = pltpu.make_async_copy(first_ref, first_hbm.at[0], sems.at[0])
    first_copy.start()
    rho = cross / square
    gap = stats[:, 4:5, 0:1] - rho[None]
    residual = inner + jnp.sum(stats[:, 1:2, 0:1] * gap * gap, axis=0)
    second_scale = scale * lax.rsqrt(scale * scale * (residual / cells) + 1e-06)
    image = hw_ref[...]
    for n, part in enumerate(parts):
        image = image + (stats_ref[partners[n], 4:5, 0:1] - rho) * part
    second_ref[...] = jnp.where(cell, image, 0.0) * second_scale
    second_copy = pltpu.make_async_copy(second_ref, second_hbm.at[0], sems.at[1])
    second_copy.start()
    first_copy.wait()
    second_copy.wait()


def body(wavefunction, sector_dims, left_env, right_env):
    size = lax.axis_size("sector")
    block = wavefunction.shape[1]
    square = (block, block)
    width = (right_env.shape[1] - 2) // 4
    near, far, row_pairs = swap_pairs(size)
    rows = len(row_pairs)
    cells = float(size * block * block)
    few, every, side, last = ((n,) + square for n in (2 + width, 2 + 2 * width, width, rows * width))
    f32, bf16 = jnp.float32, jnp.bfloat16
    dma = pltpu.SemaphoreType.DMA

    u, facts = call(
        start_kernel, (pltpu.VMEM(square, bf16), pltpu.VMEM((8, 128), f32)), [HB, HB], (VM,) * 2,
        [pltpu.VMEM(square, f32), pltpu.SMEM((1, 2), jnp.int32), dma((2,))],
    )(hbm(wavefunction), hbm(sector_dims))

    left_env, right_env = hbm(left_env), hbm(right_env)
    row_u = [vmem(swap(u, "sector", p)) for p in row_pairs]
    near_u = vmem(swap(u, "sector", near))
    far_u = vmem(swap(u, "sector", far))
    u, facts = vmem(u), vmem(facts)
    near_part, sums, left_far, right_far, left_row, right_row = call(
        functools.partial(near_kernel, size, width, rows),
        (pltpu.VMEM((2,) + square, f32), pltpu.VMEM((8, 128), f32)) + (pltpu.VMEM(side, bf16),) * 2 + (pltpu.VMEM(last, bf16),) * 2,
        [HB] * 3 + [VM] * 3, (VM,) * 6,
        [pltpu.VMEM(few, bf16)] * 2 + [pltpu.VMEM(square, f32), dma((2, 2)), dma((1, 2)), dma((rows, 2)), dma], LONG,
    )(left_env, right_env, hbm(wavefunction), facts, u, near_u)
    near_part, left_row, right_row = vmem(near_part), vmem(left_row), vmem(right_row)
    far_part, w, stats = call(
        functools.partial(first_kernel, size, width, rows),
        (pltpu.VMEM((1 + rows,) + square, f32), pltpu.VMEM(square, bf16), jax.ShapeDtypeStruct((size, 8, 128), f32)),
        [VM] * (9 + rows), (VM,) * 3,
    )(near_part, facts, vmem(sums), u, vmem(left_far), vmem(right_far), left_row, right_row, far_u, *row_u)

    row_w = [vmem(swap(w, "sector", p)) for p in row_pairs]
    near_w = vmem(swap(w, "sector", near))
    far_w = vmem(swap(w, "sector", far))
    w = vmem(w)
    stats = lax.all_to_all(stats, "sector", 0, 0, tiled=True)
    hw = call(
        functools.partial(image_kernel, size, width, rows), pltpu.VMEM(square, f32), [HB] * 2 + [VM] * (5 + rows), VM,
        [pltpu.VMEM(every, bf16)] * 2 + [dma((3, 2))],
    )(left_env, right_env, left_row, right_row, w, near_w, far_w, *row_w)
    return call(
        functools.partial(second_kernel, size, width, rows, cells),
        (jax.ShapeDtypeStruct((1,) + square, f32),) * 2, [VM] * 5, (HB, HB),
        [pltpu.VMEM(square, f32)] * 2 + [dma((2,))],
    )(facts, stats, vmem(hw), near_part, vmem(far_part))


def solution(mesh):
    placed = (
        P(("groups", "sector"), None, None),
        P(("groups", "sector"), None),
        P(("groups", "sector"), None, None, None),
        P(("groups", "sector"), None, None, None),
    )
    return jax.shard_map(
        body,
        mesh=mesh,
        in_specs=placed,
        out_specs=(P(("groups", "sector"), None, None), P(("groups", "sector"), None, None)),
        check_vma=False,
    )
```

```python
import functools

import jax
import jax.numpy as jnp
from jax import lax
from jax.experimental import pallas as pl
from jax.experimental.pallas import tpu as pltpu
from jax.sharding import PartitionSpec as P

QD = 8
SCALE = 1024.0
NT = (((1,), (1,)), ((), ()))
VM = pl.BlockSpec(memory_space=pltpu.VMEM)
HB = pl.BlockSpec(memory_space=pltpu.HBM)
AN = pl.BlockSpec(memory_space=pl.ANY)
COST = pl.CostEstimate(flops=1, bytes_accessed=1, transcendentals=0)
LONG = pl.CostEstimate(flops=4000000000, bytes_accessed=1, transcendentals=0)
PARAMS = pltpu.CompilerParams(vmem_limit_bytes=16 * 1024 * 1024)


def vmem(x):
    return pltpu.with_memory_space_constraint(x, pltpu.VMEM)


def hbm(x):
    return pltpu.with_memory_space_constraint(x, pltpu.HBM)


def call(kernel, out_shape, in_specs, out_specs, scratch=(), cost=COST, aliases={}):
    return pl.pallas_call(
        kernel, out_shape=out_shape, in_specs=in_specs, out_specs=out_specs, scratch_shapes=list(scratch),
        compiler_params=PARAMS, cost_estimate=cost, input_output_aliases=aliases,
    )


def swap(x, axis, pairs):
    to = {a: b for p in pairs for a, b in (p, p[::-1])}
    return lax.ppermute(x, axis, [(s, to.get(s, s)) for s in range(lax.axis_size(axis))])


def swap_pairs(size):
    rows = size // QD
    near = [(s, s + 1) for s in range(0, size, 2)]
    far = [(s, s + 1 if s % QD != QD - 1 else s + 1 - QD) for s in range(1, size, 2)]
    row_even = [(s, s + QD) for r in range(0, rows - 1, 2) for s in range(r * QD, r * QD + QD)]
    row_odd = [(s, s + QD) for r in range(1, rows - 1, 2) for s in range(r * QD, r * QD + QD)]
    return near, far, [p for p in (row_even, row_odd) if p]


def place(size, width):
    me = lax.axis_index("sector")
    column = lax.rem(me, QD)
    odd = lax.rem(me, 2) == 1
    row_odd = lax.rem(lax.div(me, QD), 2) == 1
    low, high, down, up = 2, 2 + width, 2 + 2 * width, 2 + 3 * width
    offsets = [jnp.where(odd, low, high), jnp.where(odd, high, low),
               jnp.where(row_odd, down, up), jnp.where(row_odd, up, down)]
    partners = [jnp.where(odd, me - 1, me + 1), jnp.where(odd, me + 1, me - 1),
                jnp.where(row_odd, me - QD, me + QD), jnp.where(row_odd, me + QD, me - QD)]
    there = [(column != 0) & (column != QD - 1),
             True if size // QD % 2 == 0 else (partners[2] >= 0) & (partners[2] < size),
             (partners[3] >= 0) & (partners[3] < size)]
    partners = [me] + [jnp.clip(p, 0, size - 1) for p in partners]
    return offsets, partners, there


def live(facts, shape):
    row_ok = lax.broadcasted_iota(jnp.int32, shape, 0).astype(jnp.float32) < facts[1:2, 0:1]
    col_ok = lax.broadcasted_iota(jnp.int32, shape, 1).astype(jnp.float32) < facts[2:3, 0:1]
    return row_ok & col_ok


def total(x):
    return jnp.sum(jnp.sum(x, axis=0, keepdims=True), axis=1, keepdims=True)


def only(there, block):
    return block if there is True else jnp.where(there, block, jnp.zeros_like(block))


def terms(src, left_ref, right_ref, first, count):
    size = src.shape[0]
    right = right_ref[pl.ds(first, count)].reshape(count * size, size)
    partial_t = lax.dot_general(right, src, NT, preferred_element_type=jnp.float32).astype(jnp.bfloat16)
    image = None
    for k in range(count):
        piece = lax.dot_general(
            left_ref[first + k], partial_t[k * size : (k + 1) * size], NT, preferred_element_type=jnp.float32
        )
        image = piece if image is None else image + piece
    return image


def fetch(left_hbm, right_hbm, left_ref, right_ref, sems, spans):
    copies = []
    at = 0
    for n, (offset, count) in enumerate(spans):
        pair = [
            pltpu.make_async_copy(source.at[0, pl.ds(offset, count)], target.at[pl.ds(at, count)], sems.at[n, e])
            for e, (source, target) in enumerate(((right_hbm, right_ref), (left_hbm, left_ref)))
        ]
        for copy in pair:
            copy.start()
        copies.append(pair)
        at += count
    return copies


def finish(copies):
    for copy in copies:
        copy.wait()


def start_kernel(wave_hbm, dims_hbm, u_ref, facts_ref, wave_ref, dims_ref, sems):
    wave_copy = pltpu.make_async_copy(wave_hbm.at[0], wave_ref, sems.at[0])
    dims_copy = pltpu.make_async_copy(dims_hbm, dims_ref, sems.at[1])
    dims_copy.start()
    wave_copy.start()
    dims_copy.wait()
    lines = lax.broadcasted_iota(jnp.int32, (8, 128), 0)
    facts = jnp.where(lines == 1, dims_ref[0, 0], jnp.where(lines == 2, dims_ref[0, 1], 0)).astype(jnp.float32)
    wave_copy.wait()
    held = jnp.where(live(facts, wave_ref.shape), wave_ref[...], 0.0)
    u_ref[...] = (held * SCALE).astype(jnp.bfloat16)
    facts_ref[...] = facts


def near_kernel(size, width, rows, left_hbm, right_hbm, wave_hbm, facts_ref, self_ref, near_ref, out_ref, sums_ref,
                left_far, right_far, left_row, right_row, left_own, right_own, wave_ref, sems, far_sems, row_sems, wave_sem):
    offsets, _, _ = place(size, width)
    wave_copy = pltpu.make_async_copy(wave_hbm.at[0], wave_ref, wave_sem)
    own = fetch(left_hbm, right_hbm, left_own, right_own, sems, [(0, 2), (offsets[0], width)])
    wave_copy.start()
    later = fetch(left_hbm, right_hbm, left_far, right_far, far_sems, [(offsets[1], width)])
    later += fetch(left_hbm, right_hbm, left_row, right_row, row_sems, [(o, width) for o in offsets[2 : 2 + rows]])
    u = self_ref[...].astype(jnp.float32)
    lines = lax.broadcasted_iota(jnp.int32, (8, 128), 0)
    sums = jnp.where(lines == 1, total(u * u), 0.0)
    finish(own[0])
    out_ref[0] = terms(self_ref[...], left_own, right_own, 0, 2)
    finish(own[1])
    out_ref[1] = terms(near_ref[...], left_own, right_own, 2, width)
    wave_copy.wait()
    held = jnp.where(live(facts_ref[...], wave_ref.shape), wave_ref[...], 0.0)
    sums_ref[...] = jnp.where(lines == 0, total(held * held), sums)
    for pair in later:
        finish(pair)


def first_kernel(size, width, rows, *refs):
    near_part_ref, facts_ref, sums_ref, u_ref, left_far, right_far, left_row, right_row, far_ref = refs[:9]
    row_refs, (out_ref, w_ref, stats_ref) = refs[9 : 9 + rows], refs[9 + rows :]
    _, _, there = place(size, width)
    out_ref[0] = terms(only(there[0], far_ref[...]), left_far, right_far, 0, width)
    image = near_part_ref[0] + near_part_ref[1] + out_ref[0]
    for r, source in enumerate(row_refs):
        piece = terms(only(there[1 + r], source[...]), left_row, right_row, r * width, width)
        out_ref[1 + r] = piece
        image = image + piece
    image = jnp.where(live(facts_ref[...], image.shape), image, 0.0)
    u = u_ref[...].astype(jnp.float32)
    square = sums_ref[1:2, 0:1]
    cross = total(u * image)
    rho = jnp.where(square > 0.0, cross / square, 0.0)
    w = image - rho * u
    w_ref[...] = w.astype(jnp.bfloat16)
    lines = lax.broadcasted_iota(jnp.int32, (8, 128), 0)
    stats = sums_ref[...]
    for line, value in ((2, cross), (3, total(w * w)), (4, rho)):
        stats = jnp.where(lines == line, value, stats)
    for n in range(stats_ref.shape[0]):
        stats_ref[n] = stats


def image_kernel(size, width, rows, *refs):
    left_hbm, right_hbm, left_row, right_row, self_ref, near_ref, far_ref = refs[:7]
    row_refs, (out_ref, left_own, right_own, sems) = refs[7 : 7 + rows], refs[7 + rows :]
    offsets, _, there = place(size, width)
    own = fetch(left_hbm, right_hbm, left_own, right_own, sems, [(0, 2)] + [(o, width) for o in offsets[:2]])
    image = None
    for r, source in enumerate(row_refs):
        piece = terms(only(there[1 + r], source[...]), left_row, right_row, r * width, width)
        image = piece if image is None else image + piece
    finish(own[0])
    image = image + terms(self_ref[...], left_own, right_own, 0, 2)
    finish(own[1])
    image = image + terms(near_ref[...], left_own, right_own, 2, width)
    finish(own[2])
    out_ref[...] = image + terms(only(there[0], far_ref[...]), left_own, right_own, 2 + width, width)


def second_kernel(size, width, rows, cells, facts_ref, stats_ref, hw_ref, near_part_ref, far_part_ref,
                  first_hbm, second_hbm, first_ref, second_ref, sems):
    _, partners, _ = place(size, width)
    facts = facts_ref[...]
    stats = stats_ref[...]
    sums = jnp.sum(stats, axis=0)
    start, square, cross, inner = (sums[i : i + 1, 0:1] for i in range(4))
    scale = lax.rsqrt(start / cells + 1e-06) * (1.0 / SCALE)
    parts = [near_part_ref[0], near_part_ref[1]] + [far_part_ref[n] for n in range(1 + rows)]
    cell = live(facts, parts[0].shape)
    first_ref[...] = jnp.where(cell, sum(parts[1:], parts[0]), 0.0) * scale
    first_copy = pltpu.make_async_copy(first_ref, first_hbm.at[0], sems.at[0])
    first_copy.start()
    rho = cross / square
    gap = stats[:, 4:5, 0:1] - rho[None]
    residual = inner + jnp.sum(stats[:, 1:2, 0:1] * gap * gap, axis=0)
    second_scale = scale * lax.rsqrt(scale * scale * (residual / cells) + 1e-06)
    image = hw_ref[...]
    for n, part in enumerate(parts):
        image = image + (stats_ref[partners[n], 4:5, 0:1] - rho) * part
    second_ref[...] = jnp.where(cell, image, 0.0) * second_scale
    second_copy = pltpu.make_async_copy(second_ref, second_hbm.at[0], sems.at[1])
    second_copy.start()
    first_copy.wait()
    second_copy.wait()


def body(wavefunction, sector_dims, left_env, right_env):
    size = lax.axis_size("sector")
    block = wavefunction.shape[1]
    square = (block, block)
    width = (right_env.shape[1] - 2) // 4
    near, far, row_pairs = swap_pairs(size)
    rows = len(row_pairs)
    cells = float(size * block * block)
    few, every, side, last = ((n,) + square for n in (2 + width, 2 + 2 * width, width, rows * width))
    f32, bf16 = jnp.float32, jnp.bfloat16
    dma = pltpu.SemaphoreType.DMA

    u, facts = call(
        start_kernel, (pltpu.VMEM(square, bf16), pltpu.VMEM((8, 128), f32)), [HB, HB], (VM,) * 2,
        [pltpu.VMEM(square, f32), pltpu.SMEM((1, 2), jnp.int32), dma((2,))],
    )(hbm(wavefunction), hbm(sector_dims))

    left_env, right_env = hbm(left_env), hbm(right_env)
    row_u = [vmem(swap(u, "sector", p)) for p in row_pairs]
    near_u = vmem(swap(u, "sector", near))
    far_u = vmem(swap(u, "sector", far))
    u, facts = vmem(u), vmem(facts)
    near_part, sums, left_far, right_far, left_row, right_row = call(
        functools.partial(near_kernel, size, width, rows),
        (pltpu.VMEM((2,) + square, f32), pltpu.VMEM((8, 128), f32)) + (pltpu.VMEM(side, bf16),) * 2 + (pltpu.VMEM(last, bf16),) * 2,
        [HB] * 3 + [VM] * 3, (VM,) * 6,
        [pltpu.VMEM(few, bf16)] * 2 + [pltpu.VMEM(square, f32), dma((2, 2)), dma((1, 2)), dma((rows, 2)), dma], LONG,
    )(left_env, right_env, hbm(wavefunction), facts, u, near_u)
    near_part, left_row, right_row = vmem(near_part), vmem(left_row), vmem(right_row)
    far_part, w, stats = call(
        functools.partial(first_kernel, size, width, rows),
        (pltpu.VMEM((1 + rows,) + square, f32), pltpu.VMEM(square, bf16), jax.ShapeDtypeStruct((size, 8, 128), f32)),
        [VM] * (9 + rows), (VM,) * 3,
    )(near_part, facts, vmem(sums), u, vmem(left_far), vmem(right_far), left_row, right_row, far_u, *row_u)

    row_w = [vmem(swap(w, "sector", p)) for p in row_pairs]
    near_w = vmem(swap(w, "sector", near))
    far_w = vmem(swap(w, "sector", far))
    w = vmem(w)
    stats = lax.all_to_all(stats, "sector", 0, 0, tiled=True)
    hw = call(
        functools.partial(image_kernel, size, width, rows), pltpu.VMEM(square, f32), [HB] * 2 + [VM] * (5 + rows), VM,
        [pltpu.VMEM(every, bf16)] * 2 + [dma((3, 2))],
    )(left_env, right_env, left_row, right_row, w, near_w, far_w, *row_w)
    return call(
        functools.partial(second_kernel, size, width, rows, cells),
        (jax.ShapeDtypeStruct((1,) + square, f32),) * 2, [VM] * 5, (HB, HB),
        [pltpu.VMEM(square, f32)] * 2 + [dma((2,))],
    )(facts, stats, vmem(hw), near_part, vmem(far_part))


def solution(mesh):
    placed = (
        P(("groups", "sector"), None, None),
        P(("groups", "sector"), None),
        P(("groups", "sector"), None, None, None),
        P(("groups", "sector"), None, None, None),
    )
    return jax.shard_map(
        body,
        mesh=mesh,
        in_specs=placed,
        out_specs=(P(("groups", "sector"), None, None), P(("groups", "sector"), None, None)),
        check_vma=False,
    )
```

```python
import functools

import jax
import jax.numpy as jnp
from jax import lax
from jax.experimental import pallas as pl
from jax.experimental.pallas import tpu as pltpu
from jax.sharding import PartitionSpec as P

QD = 8
SCALE = 1024.0
QUARTERS = 4
NT = (((1,), (1,)), ((), ()))
VM = pl.BlockSpec(memory_space=pltpu.VMEM)
HB = pl.BlockSpec(memory_space=pltpu.HBM)
AN = pl.BlockSpec(memory_space=pl.ANY)
COST = pl.CostEstimate(flops=1, bytes_accessed=1, transcendentals=0)
LONG = pl.CostEstimate(flops=4000000000, bytes_accessed=1, transcendentals=0)
PARAMS = pltpu.CompilerParams(vmem_limit_bytes=16 * 1024 * 1024)


def vmem(x):
    return pltpu.with_memory_space_constraint(x, pltpu.VMEM)


def hbm(x):
    return pltpu.with_memory_space_constraint(x, pltpu.HBM)


def call(kernel, out_shape, in_specs, out_specs, scratch=(), cost=COST, aliases={}):
    return pl.pallas_call(
        kernel, out_shape=out_shape, in_specs=in_specs, out_specs=out_specs, scratch_shapes=list(scratch),
        compiler_params=PARAMS, cost_estimate=cost, input_output_aliases=aliases,
    )


def swap(x, axis, pairs):
    to = {a: b for p in pairs for a, b in (p, p[::-1])}
    return lax.ppermute(x, axis, [(s, to.get(s, s)) for s in range(lax.axis_size(axis))])


def swap_pairs(size):
    rows = size // QD
    near = [(s, s + 1) for s in range(0, size, 2)]
    far = [(s, s + 1 if s % QD != QD - 1 else s + 1 - QD) for s in range(1, size, 2)]
    row_even = [(s, s + QD) for r in range(0, rows - 1, 2) for s in range(r * QD, r * QD + QD)]
    row_odd = [(s, s + QD) for r in range(1, rows - 1, 2) for s in range(r * QD, r * QD + QD)]
    return near, far, [p for p in (row_even, row_odd) if p]


def place(size, width):
    me = lax.axis_index("sector")
    column = lax.rem(me, QD)
    odd = lax.rem(me, 2) == 1
    row_odd = lax.rem(lax.div(me, QD), 2) == 1
    low, high, down, up = 2, 2 + width, 2 + 2 * width, 2 + 3 * width
    offsets = [jnp.where(odd, low, high), jnp.where(odd, high, low),
               jnp.where(row_odd, down, up), jnp.where(row_odd, up, down)]
    partners = [jnp.where(odd, me - 1, me + 1), jnp.where(odd, me + 1, me - 1),
                jnp.where(row_odd, me - QD, me + QD), jnp.where(row_odd, me + QD, me - QD)]
    there = [(column != 0) & (column != QD - 1),
             True if size // QD % 2 == 0 else (partners[2] >= 0) & (partners[2] < size),
             (partners[3] >= 0) & (partners[3] < size)]
    partners = [me] + [jnp.clip(p, 0, size - 1) for p in partners]
    return offsets, partners, there


def live(facts, shape):
    row_ok = lax.broadcasted_iota(jnp.int32, shape, 0).astype(jnp.float32) < facts[1:2, 0:1]
    col_ok = lax.broadcasted_iota(jnp.int32, shape, 1).astype(jnp.float32) < facts[2:3, 0:1]
    return row_ok & col_ok


def total(x):
    return jnp.sum(jnp.sum(x, axis=0, keepdims=True), axis=1, keepdims=True)


def only(there, block):
    return block if there is True else jnp.where(there, block, jnp.zeros_like(block))


def terms(src, left_ref, right_ref, first, count):
    size = src.shape[0]
    right = right_ref[pl.ds(first, count)].reshape(count * size, size)
    partial_t = lax.dot_general(right, src, NT, preferred_element_type=jnp.float32).astype(jnp.bfloat16)
    image = None
    for k in range(count):
        piece = lax.dot_general(
            left_ref[first + k], partial_t[k * size : (k + 1) * size], NT, preferred_element_type=jnp.float32
        )
        image = piece if image is None else image + piece
    return image


def fetch(left_hbm, right_hbm, left_ref, right_ref, sems, spans):
    copies = []
    at = 0
    for n, (offset, count) in enumerate(spans):
        pair = [
            pltpu.make_async_copy(source.at[0, pl.ds(offset, count)], target.at[pl.ds(at, count)], sems.at[n, e])
            for e, (source, target) in enumerate(((right_hbm, right_ref), (left_hbm, left_ref)))
        ]
        for copy in pair:
            copy.start()
        copies.append(pair)
        at += count
    return copies


def finish(copies):
    for copy in copies:
        copy.wait()


def start_kernel(wave_hbm, dims_hbm, *refs):
    u_refs, (facts_ref, wave_ref, dims_ref, sems) = refs[:3], refs[3:]
    size = wave_ref.shape[0]
    step = size // QUARTERS
    dims_copy = pltpu.make_async_copy(dims_hbm, dims_ref, sems.at[QUARTERS])
    dims_copy.start()
    copies = [
        pltpu.make_async_copy(wave_hbm.at[0, pl.ds(n * step, step)], wave_ref.at[pl.ds(n * step, step)], sems.at[n])
        for n in range(QUARTERS)
    ]
    for copy in copies:
        copy.start()
    dims_copy.wait()
    row_count, col_count = dims_ref[0, 0], dims_ref[0, 1]
    lines = lax.broadcasted_iota(jnp.int32, (8, 128), 0)
    facts_ref[...] = jnp.where(lines == 1, row_count, jnp.where(lines == 2, col_count, 0)).astype(jnp.float32)
    col_ok = lax.broadcasted_iota(jnp.int32, (step, size), 1) < col_count
    row = lax.broadcasted_iota(jnp.int32, (step, size), 0)
    for n, copy in enumerate(copies):
        copy.wait()
        rows = pl.ds(n * step, step)
        held = jnp.where((row < row_count - n * step) & col_ok, wave_ref[rows], 0.0)
        block = (held * SCALE).astype(jnp.bfloat16)
        for ref in u_refs:
            ref[rows] = block


def pass_kernel(*refs):
    pass


def after(held, first):
    return call(pass_kernel, pltpu.VMEM(held.shape, held.dtype), [AN] * 2, AN, aliases={0: 0})(vmem(held), first)


def near_kernel(size, width, rows, left_hbm, right_hbm, wave_hbm, facts_ref, self_ref, near_ref, out_ref, sums_ref,
                left_far, right_far, left_row, right_row, left_own, right_own, wave_ref, sems, far_sems, row_sems, wave_sem):
    offsets, _, _ = place(size, width)
    wave_copy = pltpu.make_async_copy(wave_hbm.at[0], wave_ref, wave_sem)
    own = fetch(left_hbm, right_hbm, left_own, right_own, sems, [(0, 2), (offsets[0], width)])
    wave_copy.start()
    later = fetch(left_hbm, right_hbm, left_far, right_far, far_sems, [(offsets[1], width)])
    later += fetch(left_hbm, right_hbm, left_row, right_row, row_sems, [(o, width) for o in offsets[2 : 2 + rows]])
    u = self_ref[...].astype(jnp.float32)
    lines = lax.broadcasted_iota(jnp.int32, (8, 128), 0)
    sums = jnp.where(lines == 1, total(u * u), 0.0)
    finish(own[0])
    out_ref[0] = terms(self_ref[...], left_own, right_own, 0, 2)
    finish(own[1])
    out_ref[1] = terms(near_ref[...], left_own, right_own, 2, width)
    wave_copy.wait()
    held = jnp.where(live(facts_ref[...], wave_ref.shape), wave_ref[...], 0.0)
    sums_ref[...] = jnp.where(lines == 0, total(held * held), sums)
    for pair in later:
        finish(pair)


def far_kernel(size, width, left_ref, right_ref, far_ref, out_ref):
    _, _, there = place(size, width)
    out_ref[...] = terms(only(there[0], far_ref[...]), left_ref, right_ref, 0, width)


def first_kernel(size, width, rows, *refs):
    near_part_ref, far_part_ref, facts_ref, sums_ref, u_ref, left_ref, right_ref = refs[:7]
    row_refs, (out_ref, w_ref, near_w_ref, far_w_ref, stats_ref) = refs[7 : 7 + rows], refs[7 + rows :]
    _, _, there = place(size, width)
    image = near_part_ref[0] + near_part_ref[1] + far_part_ref[...]
    for r, source in enumerate(row_refs):
        piece = terms(only(there[1 + r], source[...]), left_ref, right_ref, r * width, width)
        out_ref[r] = piece
        image = image + piece
    image = jnp.where(live(facts_ref[...], image.shape), image, 0.0)
    u = u_ref[...].astype(jnp.float32)
    square = sums_ref[1:2, 0:1]
    cross = total(u * image)
    rho = jnp.where(square > 0.0, cross / square, 0.0)
    w = image - rho * u
    for ref in (w_ref, near_w_ref, far_w_ref):
        ref[...] = w.astype(jnp.bfloat16)
    lines = lax.broadcasted_iota(jnp.int32, (8, 128), 0)
    stats = sums_ref[...]
    for line, value in ((2, cross), (3, total(w * w)), (4, rho)):
        stats = jnp.where(lines == line, value, stats)
    for n in range(stats_ref.shape[0]):
        stats_ref[n] = stats


def image_kernel(size, width, rows, left_hbm, right_hbm, left_row, right_row, self_ref, near_ref, far_ref, *refs):
    row_refs, (out_ref, left_own, right_own, sems) = refs[:rows], refs[rows:]
    offsets, _, there = place(size, width)
    own = fetch(left_hbm, right_hbm, left_own, right_own, sems, [(0, 2)] + [(o, width) for o in offsets[:2]])
    image = None
    for r, source in enumerate(row_refs):
        piece = terms(only(there[1 + r], source[...]), left_row, right_row, r * width, width)
        image = piece if image is None else image + piece
    finish(own[0])
    image = image + terms(self_ref[...], left_own, right_own, 0, 2)
    finish(own[1])
    image = image + terms(near_ref[...], left_own, right_own, 2, width)
    finish(own[2])
    out_ref[...] = image + terms(only(there[0], far_ref[...]), left_own, right_own, 2 + width, width)


def second_kernel(size, width, rows, cells, facts_ref, stats_ref, hw_ref, near_part_ref, far_part_ref, row_part_ref,
                  first_hbm, second_hbm, first_ref, second_ref, sems):
    _, partners, _ = place(size, width)
    facts = facts_ref[...]
    stats = stats_ref[...]
    sums = jnp.sum(stats, axis=0)
    start, square, cross, inner = (sums[i : i + 1, 0:1] for i in range(4))
    scale = lax.rsqrt(start / cells + 1e-06) * (1.0 / SCALE)
    parts = [near_part_ref[0], near_part_ref[1], far_part_ref[...]] + [row_part_ref[r] for r in range(rows)]
    cell = live(facts, parts[0].shape)
    first_ref[...] = jnp.where(cell, sum(parts[1:], parts[0]), 0.0) * scale
    first_copy = pltpu.make_async_copy(first_ref, first_hbm.at[0], sems.at[0])
    first_copy.start()
    rho = cross / square
    gap = stats[:, 4:5, 0:1] - rho[None]
    residual = inner + jnp.sum(stats[:, 1:2, 0:1] * gap * gap, axis=0)
    second_scale = scale * lax.rsqrt(scale * scale * (residual / cells) + 1e-06)
    image = hw_ref[...]
    for n, part in enumerate(parts):
        image = image + (stats_ref[partners[n], 4:5, 0:1] - rho) * part
    second_ref[...] = jnp.where(cell, image, 0.0) * second_scale
    second_copy = pltpu.make_async_copy(second_ref, second_hbm.at[0], sems.at[1])
    second_copy.start()
    first_copy.wait()
    second_copy.wait()


def body(wavefunction, sector_dims, left_env, right_env):
    size = lax.axis_size("sector")
    block = wavefunction.shape[1]
    square = (block, block)
    width = (right_env.shape[1] - 2) // 4
    near, far, row_pairs = swap_pairs(size)
    rows = len(row_pairs)
    cells = float(size * block * block)
    few, every, side, last = ((n,) + square for n in (2 + width, 2 + 2 * width, width, rows * width))
    f32, bf16 = jnp.float32, jnp.bfloat16
    dma = pltpu.SemaphoreType.DMA

    u, near_u, far_u, facts = call(
        start_kernel, (pltpu.VMEM(square, bf16),) * 3 + (pltpu.VMEM((8, 128), f32),), [HB, HB], (VM,) * 4,
        [pltpu.VMEM(square, f32), pltpu.SMEM((1, 2), jnp.int32), dma((QUARTERS + 1,))],
    )(hbm(wavefunction), hbm(sector_dims))

    left_env, right_env = hbm(left_env), hbm(right_env)
    u, facts = vmem(u), vmem(facts)
    row_u = [vmem(swap(u, "sector", p)) for p in row_pairs]
    near_u = vmem(swap(near_u, "sector", near))
    far_u = vmem(swap(after(far_u, near_u), "sector", far))
    near_part, sums, left_far, right_far, left_row, right_row = call(
        functools.partial(near_kernel, size, width, rows),
        (pltpu.VMEM((2,) + square, f32), pltpu.VMEM((8, 128), f32)) + (pltpu.VMEM(side, bf16),) * 2 + (pltpu.VMEM(last, bf16),) * 2,
        [HB] * 3 + [VM] * 3, (VM,) * 6,
        [pltpu.VMEM(few, bf16)] * 2 + [pltpu.VMEM(square, f32), dma((2, 2)), dma((1, 2)), dma((rows, 2)), dma], LONG,
    )(left_env, right_env, hbm(wavefunction), facts, u, near_u)
    near_part, left_row, right_row = vmem(near_part), vmem(left_row), vmem(right_row)
    far_part = vmem(call(
        functools.partial(far_kernel, size, width), pltpu.VMEM(square, f32), [VM] * 3, VM, cost=LONG,
    )(vmem(left_far), vmem(right_far), far_u))
    row_part, w, near_w, far_w, stats = call(
        functools.partial(first_kernel, size, width, rows),
        (pltpu.VMEM((rows,) + square, f32),) + (pltpu.VMEM(square, bf16),) * 3 + (jax.ShapeDtypeStruct((size, 8, 128), f32),),
        [VM] * (7 + rows), (VM,) * 5,
    )(near_part, far_part, facts, vmem(sums), u, left_row, right_row, *row_u)

    w = vmem(w)
    row_w = [vmem(swap(w, "sector", p)) for p in row_pairs]
    near_w = vmem(swap(near_w, "sector", near))
    far_w = vmem(swap(after(far_w, near_w), "sector", far))
    stats = lax.all_to_all(stats, "sector", 0, 0, tiled=True)
    hw = call(
        functools.partial(image_kernel, size, width, rows), pltpu.VMEM(square, f32), [HB] * 2 + [VM] * (5 + rows), VM,
        [pltpu.VMEM(every, bf16)] * 2 + [dma((3, 2))],
    )(left_env, right_env, left_row, right_row, w, near_w, far_w, *row_w)
    return call(
        functools.partial(second_kernel, size, width, rows, cells),
        (jax.ShapeDtypeStruct((1,) + square, f32),) * 2, [VM] * 6, (HB, HB),
        [pltpu.VMEM(square, f32)] * 2 + [dma((2,))],
    )(facts, stats, vmem(hw), near_part, far_part, vmem(row_part))


def solution(mesh):
    placed = (
        P(("groups", "sector"), None, None),
        P(("groups", "sector"), None),
        P(("groups", "sector"), None, None, None),
        P(("groups", "sector"), None, None, None),
    )
    return jax.shard_map(
        body,
        mesh=mesh,
        in_specs=placed,
        out_specs=(P(("groups", "sector"), None, None), P(("groups", "sector"), None, None)),
        check_vma=False,
    )
```

```python
import functools

import jax
import jax.numpy as jnp
from jax import lax
from jax.experimental import pallas as pl
from jax.experimental.pallas import tpu as pltpu
from jax.sharding import PartitionSpec as P

QD = 8
SCALE = 1024.0
QUARTERS = 4
NT = (((1,), (1,)), ((), ()))
VM = pl.BlockSpec(memory_space=pltpu.VMEM)
HB = pl.BlockSpec(memory_space=pltpu.HBM)
AN = pl.BlockSpec(memory_space=pl.ANY)
COST = pl.CostEstimate(flops=1, bytes_accessed=1, transcendentals=0)
LONG = pl.CostEstimate(flops=4000000000, bytes_accessed=1, transcendentals=0)
PARAMS = pltpu.CompilerParams(vmem_limit_bytes=16 * 1024 * 1024)


def vmem(x):
    return pltpu.with_memory_space_constraint(x, pltpu.VMEM)


def hbm(x):
    return pltpu.with_memory_space_constraint(x, pltpu.HBM)


def call(kernel, out_shape, in_specs, out_specs, scratch=(), cost=COST, aliases={}):
    return pl.pallas_call(
        kernel, out_shape=out_shape, in_specs=in_specs, out_specs=out_specs, scratch_shapes=list(scratch),
        compiler_params=PARAMS, cost_estimate=cost, input_output_aliases=aliases,
    )


def swap(x, axis, pairs):
    to = {a: b for p in pairs for a, b in (p, p[::-1])}
    return lax.ppermute(x, axis, [(s, to.get(s, s)) for s in range(lax.axis_size(axis))])


def swap_pairs(size):
    rows = size // QD
    near = [(s, s + 1) for s in range(0, size, 2)]
    row_even = [(s, s + QD) for r in range(0, rows - 1, 2) for s in range(r * QD, r * QD + QD)]
    row_odd = [(s, s + QD) for r in range(1, rows - 1, 2) for s in range(r * QD, r * QD + QD)]
    return near, [p for p in (row_even, row_odd) if p]


def far_swap(x):
    groups, size = lax.axis_size("groups"), lax.axis_size("sector")
    pairs = []
    for g in range(groups):
        for s in range(size):
            if s % QD == 0 or s % QD == QD - 1:
                to, partner = (g ^ 1 if g ^ 1 < groups else g), s
            else:
                to, partner = g, s + 1 if s % 2 else s - 1
            pairs.append((g * size + s, to * size + partner))
    return lax.ppermute(x, ("groups", "sector"), pairs)


def place(size, width):
    me = lax.axis_index("sector")
    column = lax.rem(me, QD)
    odd = lax.rem(me, 2) == 1
    row_odd = lax.rem(lax.div(me, QD), 2) == 1
    low, high, down, up = 2, 2 + width, 2 + 2 * width, 2 + 3 * width
    offsets = [jnp.where(odd, low, high), jnp.where(odd, high, low),
               jnp.where(row_odd, down, up), jnp.where(row_odd, up, down)]
    partners = [jnp.where(odd, me - 1, me + 1), jnp.where(odd, me + 1, me - 1),
                jnp.where(row_odd, me - QD, me + QD), jnp.where(row_odd, me + QD, me - QD)]
    there = [(column != 0) & (column != QD - 1),
             True if size // QD % 2 == 0 else (partners[2] >= 0) & (partners[2] < size),
             (partners[3] >= 0) & (partners[3] < size)]
    partners = [me] + [jnp.clip(p, 0, size - 1) for p in partners]
    return offsets, partners, there


def live(facts, shape):
    row_ok = lax.broadcasted_iota(jnp.int32, shape, 0).astype(jnp.float32) < facts[1:2, 0:1]
    col_ok = lax.broadcasted_iota(jnp.int32, shape, 1).astype(jnp.float32) < facts[2:3, 0:1]
    return row_ok & col_ok


def total(x):
    return jnp.sum(jnp.sum(x, axis=0, keepdims=True), axis=1, keepdims=True)


def only(there, block):
    return block if there is True else jnp.where(there, block, jnp.zeros_like(block))


def terms(src, left_ref, right_ref, first, count):
    size = src.shape[0]
    right = right_ref[pl.ds(first, count)].reshape(count * size, size)
    partial_t = lax.dot_general(right, src, NT, preferred_element_type=jnp.float32).astype(jnp.bfloat16)
    image = None
    for k in range(count):
        piece = lax.dot_general(
            left_ref[first + k], partial_t[k * size : (k + 1) * size], NT, preferred_element_type=jnp.float32
        )
        image = piece if image is None else image + piece
    return image


def fetch(left_hbm, right_hbm, left_ref, right_ref, sems, spans):
    copies = []
    at = 0
    for n, (offset, count) in enumerate(spans):
        pair = [
            pltpu.make_async_copy(source.at[0, pl.ds(offset, count)], target.at[pl.ds(at, count)], sems.at[n, e])
            for e, (source, target) in enumerate(((right_hbm, right_ref), (left_hbm, left_ref)))
        ]
        for copy in pair:
            copy.start()
        copies.append(pair)
        at += count
    return copies


def finish(copies):
    for copy in copies:
        copy.wait()


def start_kernel(wave_hbm, dims_hbm, *refs):
    u_refs, (facts_ref, wave_ref, dims_ref, sems) = refs[:2], refs[2:]
    size = wave_ref.shape[0]
    step = size // QUARTERS
    dims_copy = pltpu.make_async_copy(dims_hbm, dims_ref, sems.at[QUARTERS])
    dims_copy.start()
    copies = [
        pltpu.make_async_copy(wave_hbm.at[0, pl.ds(n * step, step)], wave_ref.at[pl.ds(n * step, step)], sems.at[n])
        for n in range(QUARTERS)
    ]
    for copy in copies:
        copy.start()
    dims_copy.wait()
    row_count, col_count = dims_ref[0, 0], dims_ref[0, 1]
    lines = lax.broadcasted_iota(jnp.int32, (8, 128), 0)
    facts_ref[...] = jnp.where(lines == 1, row_count, jnp.where(lines == 2, col_count, 0)).astype(jnp.float32)
    col_ok = lax.broadcasted_iota(jnp.int32, (step, size), 1) < col_count
    row = lax.broadcasted_iota(jnp.int32, (step, size), 0)
    for n, copy in enumerate(copies):
        copy.wait()
        rows = pl.ds(n * step, step)
        held = jnp.where((row < row_count - n * step) & col_ok, wave_ref[rows], 0.0)
        block = (held * SCALE).astype(jnp.bfloat16)
        for ref in u_refs:
            ref[rows] = block


def pass_kernel(*refs):
    pass


def after(held, first):
    return call(pass_kernel, pltpu.VMEM(held.shape, held.dtype), [AN] * 2, AN, aliases={0: 0})(vmem(held), first)


def near_kernel(size, width, rows, left_hbm, right_hbm, wave_hbm, facts_ref, self_ref, near_ref, out_ref, sums_ref,
                left_far, right_far, left_row, right_row, left_own, right_own, wave_ref, sems, far_sems, row_sems, wave_sem):
    offsets, _, _ = place(size, width)
    wave_copy = pltpu.make_async_copy(wave_hbm.at[0], wave_ref, wave_sem)
    own = fetch(left_hbm, right_hbm, left_own, right_own, sems, [(0, 2), (offsets[0], width)])
    wave_copy.start()
    later = fetch(left_hbm, right_hbm, left_far, right_far, far_sems, [(offsets[1], width)])
    later += fetch(left_hbm, right_hbm, left_row, right_row, row_sems, [(o, width) for o in offsets[2 : 2 + rows]])
    u = self_ref[...].astype(jnp.float32)
    lines = lax.broadcasted_iota(jnp.int32, (8, 128), 0)
    sums = jnp.where(lines == 1, total(u * u), 0.0)
    finish(own[0])
    out_ref[0] = terms(self_ref[...], left_own, right_own, 0, 2)
    finish(own[1])
    out_ref[1] = terms(near_ref[...], left_own, right_own, 2, width)
    wave_copy.wait()
    held = jnp.where(live(facts_ref[...], wave_ref.shape), wave_ref[...], 0.0)
    sums_ref[...] = jnp.where(lines == 0, total(held * held), sums)
    for pair in later:
        finish(pair)


def far_kernel(size, width, left_ref, right_ref, far_ref, out_ref):
    _, _, there = place(size, width)
    out_ref[...] = terms(only(there[0], far_ref[...]), left_ref, right_ref, 0, width)


def first_kernel(size, width, rows, *refs):
    near_part_ref, far_part_ref, facts_ref, sums_ref, u_ref, left_ref, right_ref = refs[:7]
    row_refs, (out_ref, w_ref, stats_ref) = refs[7 : 7 + rows], refs[7 + rows :]
    _, _, there = place(size, width)
    image = near_part_ref[0] + near_part_ref[1] + far_part_ref[...]
    for r, source in enumerate(row_refs):
        piece = terms(only(there[1 + r], source[...]), left_ref, right_ref, r * width, width)
        out_ref[r] = piece
        image = image + piece
    image = jnp.where(live(facts_ref[...], image.shape), image, 0.0)
    u = u_ref[...].astype(jnp.float32)
    square = sums_ref[1:2, 0:1]
    cross = total(u * image)
    rho = jnp.where(square > 0.0, cross / square, 0.0)
    w = image - rho * u
    w_ref[...] = w.astype(jnp.bfloat16)
    lines = lax.broadcasted_iota(jnp.int32, (8, 128), 0)
    stats = sums_ref[...]
    for line, value in ((2, cross), (3, total(w * w)), (4, rho)):
        stats = jnp.where(lines == line, value, stats)
    for n in range(stats_ref.shape[0]):
        stats_ref[n] = stats


def image_kernel(size, width, rows, *refs):
    row_refs, refs = refs[:rows], refs[rows:]
    far_ref, near_ref, self_ref, left_row, right_row, left_hbm, right_hbm, out_ref, left_own, right_own, sems = refs
    _, _, there = place(size, width)
    own = fetch(left_hbm, right_hbm, left_own, right_own, sems, [(0, 2 + width), (2 + width, width)])
    image = None
    for r, source in enumerate(row_refs):
        piece = terms(only(there[1 + r], source[...]), left_row, right_row, r * width, width)
        image = piece if image is None else image + piece
    odd = lax.rem(lax.axis_index("sector"), 2) == 1
    near, far = near_ref[...], only(there[0], far_ref[...])
    finish(own[0])
    image = image + terms(self_ref[...], left_own, right_own, 0, 2)
    image = image + terms(jnp.where(odd, near, far), left_own, right_own, 2, width)
    finish(own[1])
    out_ref[...] = image + terms(jnp.where(odd, far, near), left_own, right_own, 2 + width, width)


def second_kernel(size, width, rows, cells, facts_ref, stats_ref, hw_ref, near_part_ref, far_part_ref, row_part_ref,
                  first_hbm, second_hbm, first_ref, second_ref, sems):
    _, partners, _ = place(size, width)
    facts = facts_ref[...]
    stats = stats_ref[...]
    sums = jnp.sum(stats, axis=0)
    start, square, cross, inner = (sums[i : i + 1, 0:1] for i in range(4))
    scale = lax.rsqrt(start / cells + 1e-06) * (1.0 / SCALE)
    parts = [near_part_ref[0], near_part_ref[1], far_part_ref[...]] + [row_part_ref[r] for r in range(rows)]
    cell = live(facts, parts[0].shape)
    first_ref[...] = jnp.where(cell, sum(parts[1:], parts[0]), 0.0) * scale
    first_copy = pltpu.make_async_copy(first_ref, first_hbm.at[0], sems.at[0])
    first_copy.start()
    rho = cross / square
    gap = stats[:, 4:5, 0:1] - rho[None]
    residual = inner + jnp.sum(stats[:, 1:2, 0:1] * gap * gap, axis=0)
    second_scale = scale * lax.rsqrt(scale * scale * (residual / cells) + 1e-06)
    image = hw_ref[...]
    for n, part in enumerate(parts):
        image = image + (stats_ref[partners[n], 4:5, 0:1] - rho) * part
    second_ref[...] = jnp.where(cell, image, 0.0) * second_scale
    second_copy = pltpu.make_async_copy(second_ref, second_hbm.at[0], sems.at[1])
    second_copy.start()
    first_copy.wait()
    second_copy.wait()


def body(wavefunction, sector_dims, left_env, right_env):
    size = lax.axis_size("sector")
    block = wavefunction.shape[1]
    square = (block, block)
    width = (right_env.shape[1] - 2) // 4
    near, row_pairs = swap_pairs(size)
    rows = len(row_pairs)
    cells = float(size * block * block)
    few, every, side, last = ((n,) + square for n in (2 + width, 2 + 2 * width, width, rows * width))
    f32, bf16 = jnp.float32, jnp.bfloat16
    dma = pltpu.SemaphoreType.DMA

    u, far_u, facts = call(
        start_kernel, (pltpu.VMEM(square, bf16),) * 2 + (pltpu.VMEM((8, 128), f32),), [HB, HB], (VM,) * 3,
        [pltpu.VMEM(square, f32), pltpu.SMEM((1, 2), jnp.int32), dma((QUARTERS + 1,))],
    )(hbm(wavefunction), hbm(sector_dims))

    left_env, right_env = hbm(left_env), hbm(right_env)
    u, facts = vmem(u), vmem(facts)
    row_u = [vmem(swap(u, "sector", p)) for p in row_pairs]
    near_u = vmem(swap(u, "sector", near))
    far_u = vmem(far_swap(after(far_u, near_u)))
    near_part, sums, left_far, right_far, left_row, right_row = call(
        functools.partial(near_kernel, size, width, rows),
        (pltpu.VMEM((2,) + square, f32), pltpu.VMEM((8, 128), f32)) + (pltpu.VMEM(side, bf16),) * 2 + (pltpu.VMEM(last, bf16),) * 2,
        [HB] * 3 + [VM] * 3, (VM,) * 6,
        [pltpu.VMEM(few, bf16)] * 2 + [pltpu.VMEM(square, f32), dma((2, 2)), dma((1, 2)), dma((rows, 2)), dma], LONG,
    )(left_env, right_env, hbm(wavefunction), facts, u, near_u)
    near_part, left_row, right_row = vmem(near_part), vmem(left_row), vmem(right_row)
    far_part = vmem(call(
        functools.partial(far_kernel, size, width), pltpu.VMEM(square, f32), [VM] * 3, VM, cost=LONG,
    )(vmem(left_far), vmem(right_far), far_u))
    row_part, w, stats = call(
        functools.partial(first_kernel, size, width, rows),
        (pltpu.VMEM((rows,) + square, f32),) + (pltpu.VMEM(square, bf16), jax.ShapeDtypeStruct((size, 8, 128), f32)),
        [VM] * (7 + rows), (VM,) * 3,
    )(near_part, far_part, facts, vmem(sums), u, left_row, right_row, *row_u)

    w = vmem(w)
    row_w = [vmem(swap(w, "sector", p)) for p in row_pairs]
    near_w = vmem(swap(w, "sector", near))
    far_w = vmem(far_swap(w))
    stats = lax.all_to_all(stats, "sector", 0, 0, tiled=True)
    hw = call(
        functools.partial(image_kernel, size, width, rows), pltpu.VMEM(square, f32), [VM] * (5 + rows) + [HB] * 2, VM,
        [pltpu.VMEM(every, bf16)] * 2 + [dma((2, 2))],
    )(*row_w, far_w, near_w, w, left_row, right_row, left_env, right_env)
    return call(
        functools.partial(second_kernel, size, width, rows, cells),
        (jax.ShapeDtypeStruct((1,) + square, f32),) * 2, [VM] * 6, (HB, HB),
        [pltpu.VMEM(square, f32)] * 2 + [dma((2,))],
    )(facts, stats, vmem(hw), near_part, far_part, vmem(row_part))


def solution(mesh):
    placed = (
        P(("groups", "sector"), None, None),
        P(("groups", "sector"), None),
        P(("groups", "sector"), None, None, None),
        P(("groups", "sector"), None, None, None),
    )
    return jax.shard_map(
        body,
        mesh=mesh,
        in_specs=placed,
        out_specs=(P(("groups", "sector"), None, None), P(("groups", "sector"), None, None)),
        check_vma=False,
    )
```

```python
import functools

import jax
import jax.numpy as jnp
from jax import lax
from jax.experimental import pallas as pl
from jax.experimental.pallas import tpu as pltpu
from jax.sharding import PartitionSpec as P

QD = 8
SCALE = 1024.0
QUARTERS = 4
NT = (((1,), (1,)), ((), ()))
VM = pl.BlockSpec(memory_space=pltpu.VMEM)
HB = pl.BlockSpec(memory_space=pltpu.HBM)
AN = pl.BlockSpec(memory_space=pl.ANY)
COST = pl.CostEstimate(flops=1, bytes_accessed=1, transcendentals=0)
LONG = pl.CostEstimate(flops=4000000000, bytes_accessed=1, transcendentals=0)
PARAMS = pltpu.CompilerParams(vmem_limit_bytes=16 * 1024 * 1024)


def vmem(x):
    return pltpu.with_memory_space_constraint(x, pltpu.VMEM)


def hbm(x):
    return pltpu.with_memory_space_constraint(x, pltpu.HBM)


def call(kernel, out_shape, in_specs, out_specs, scratch=(), cost=COST, aliases={}):
    return pl.pallas_call(
        kernel, out_shape=out_shape, in_specs=in_specs, out_specs=out_specs, scratch_shapes=list(scratch),
        compiler_params=PARAMS, cost_estimate=cost, input_output_aliases=aliases,
    )


def swap(x, axis, pairs):
    to = {a: b for p in pairs for a, b in (p, p[::-1])}
    return lax.ppermute(x, axis, [(s, to.get(s, s)) for s in range(lax.axis_size(axis))])


def swap_pairs(size):
    rows = size // QD
    near = [(s, s + 1) for s in range(0, size, 2)]
    row_even = [(s, s + QD) for r in range(0, rows - 1, 2) for s in range(r * QD, r * QD + QD)]
    row_odd = [(s, s + QD) for r in range(1, rows - 1, 2) for s in range(r * QD, r * QD + QD)]
    return near, [p for p in (row_even, row_odd) if p]


def far_swap(x):
    groups, size = lax.axis_size("groups"), lax.axis_size("sector")
    pairs = []
    for g in range(groups):
        for s in range(size):
            if s % QD == 0 or s % QD == QD - 1:
                to, partner = (g ^ 1 if g ^ 1 < groups else g), s
            else:
                to, partner = g, s + 1 if s % 2 else s - 1
            pairs.append((g * size + s, to * size + partner))
    return lax.ppermute(x, ("groups", "sector"), pairs)


def place(size, width):
    me = lax.axis_index("sector")
    column = lax.rem(me, QD)
    odd = lax.rem(me, 2) == 1
    row_odd = lax.rem(lax.div(me, QD), 2) == 1
    low, high, down, up = 2, 2 + width, 2 + 2 * width, 2 + 3 * width
    offsets = [jnp.where(odd, low, high), jnp.where(odd, high, low),
               jnp.where(row_odd, down, up), jnp.where(row_odd, up, down)]
    partners = [jnp.where(odd, me - 1, me + 1), jnp.where(odd, me + 1, me - 1),
                jnp.where(row_odd, me - QD, me + QD), jnp.where(row_odd, me + QD, me - QD)]
    there = [(column != 0) & (column != QD - 1),
             True if size // QD % 2 == 0 else (partners[2] >= 0) & (partners[2] < size),
             (partners[3] >= 0) & (partners[3] < size)]
    partners = [me] + [jnp.clip(p, 0, size - 1) for p in partners]
    return offsets, partners, there


def live(facts, shape):
    row_ok = lax.broadcasted_iota(jnp.int32, shape, 0).astype(jnp.float32) < facts[1:2, 0:1]
    col_ok = lax.broadcasted_iota(jnp.int32, shape, 1).astype(jnp.float32) < facts[2:3, 0:1]
    return row_ok & col_ok


def total(x):
    return jnp.sum(jnp.sum(x, axis=0, keepdims=True), axis=1, keepdims=True)


def only(there, block):
    return block if there is True else jnp.where(there, block, jnp.zeros_like(block))


def terms(src, left_ref, right_ref, first, count):
    size = src.shape[0]
    right = right_ref[pl.ds(first, count)].reshape(count * size, size)
    partial_t = lax.dot_general(right, src, NT, preferred_element_type=jnp.float32).astype(jnp.bfloat16)
    image = None
    for k in range(count):
        piece = lax.dot_general(
            left_ref[first + k], partial_t[k * size : (k + 1) * size], NT, preferred_element_type=jnp.float32
        )
        image = piece if image is None else image + piece
    return image


def fetch(left_hbm, right_hbm, left_ref, right_ref, sems, spans):
    copies = []
    at = 0
    for n, (offset, count) in enumerate(spans):
        pair = [
            pltpu.make_async_copy(source.at[0, pl.ds(offset, count)], target.at[pl.ds(at, count)], sems.at[n, e])
            for e, (source, target) in enumerate(((right_hbm, right_ref), (left_hbm, left_ref)))
        ]
        for copy in pair:
            copy.start()
        copies.append(pair)
        at += count
    return copies


def finish(copies):
    for copy in copies:
        copy.wait()


def start_kernel(wave_hbm, dims_hbm, *refs):
    u_refs, (facts_ref, wave_ref, dims_ref, sems) = refs[:2], refs[2:]
    size = wave_ref.shape[0]
    step = size // QUARTERS
    dims_copy = pltpu.make_async_copy(dims_hbm, dims_ref, sems.at[QUARTERS])
    dims_copy.start()
    copies = [
        pltpu.make_async_copy(wave_hbm.at[0, pl.ds(n * step, step)], wave_ref.at[pl.ds(n * step, step)], sems.at[n])
        for n in range(QUARTERS)
    ]
    for copy in copies:
        copy.start()
    dims_copy.wait()
    row_count, col_count = dims_ref[0, 0], dims_ref[0, 1]
    lines = lax.broadcasted_iota(jnp.int32, (8, 128), 0)
    facts_ref[...] = jnp.where(lines == 1, row_count, jnp.where(lines == 2, col_count, 0)).astype(jnp.float32)
    col_ok = lax.broadcasted_iota(jnp.int32, (step, size), 1) < col_count
    row = lax.broadcasted_iota(jnp.int32, (step, size), 0)
    for n, copy in enumerate(copies):
        copy.wait()
        rows = pl.ds(n * step, step)
        held = jnp.where((row < row_count - n * step) & col_ok, wave_ref[rows], 0.0)
        block = (held * SCALE).astype(jnp.bfloat16)
        for ref in u_refs:
            ref[rows] = block


def pass_kernel(*refs):
    pass


def after(held, first):
    return call(pass_kernel, pltpu.VMEM(held.shape, held.dtype), [AN] * 2, AN, aliases={0: 0})(vmem(held), first)


def near_kernel(size, width, rows, left_hbm, right_hbm, wave_hbm, facts_ref, self_ref, near_ref, out_ref, sums_ref,
                left_far, right_far, left_row, right_row, left_own, right_own, wave_ref, sems, far_sems, row_sems, wave_sem):
    offsets, _, _ = place(size, width)
    wave_copy = pltpu.make_async_copy(wave_hbm.at[0], wave_ref, wave_sem)
    own = fetch(left_hbm, right_hbm, left_own, right_own, sems, [(0, 2), (offsets[0], width)])
    wave_copy.start()
    later = fetch(left_hbm, right_hbm, left_far, right_far, far_sems, [(offsets[1], width)])
    later += fetch(left_hbm, right_hbm, left_row, right_row, row_sems, [(o, width) for o in offsets[2 : 2 + rows]])
    u = self_ref[...].astype(jnp.float32)
    lines = lax.broadcasted_iota(jnp.int32, (8, 128), 0)
    sums = jnp.where(lines == 1, total(u * u), 0.0)
    finish(own[0])
    out_ref[0] = terms(self_ref[...], left_own, right_own, 0, 2)
    finish(own[1])
    out_ref[1] = terms(near_ref[...], left_own, right_own, 2, width)
    wave_copy.wait()
    held = jnp.where(live(facts_ref[...], wave_ref.shape), wave_ref[...], 0.0)
    sums_ref[...] = jnp.where(lines == 0, total(held * held), sums)
    for pair in later:
        finish(pair)


def far_kernel(size, width, left_ref, right_ref, far_ref, out_ref):
    _, _, there = place(size, width)
    out_ref[...] = terms(only(there[0], far_ref[...]), left_ref, right_ref, 0, width)


def first_kernel(size, width, rows, *refs):
    near_part_ref, far_part_ref, facts_ref, sums_ref, u_ref, left_ref, right_ref = refs[:7]
    row_refs, (out_ref, w_ref, stats_ref) = refs[7 : 7 + rows], refs[7 + rows :]
    _, _, there = place(size, width)
    image = near_part_ref[0] + near_part_ref[1] + far_part_ref[...]
    for r, source in enumerate(row_refs):
        piece = terms(only(there[1 + r], source[...]), left_ref, right_ref, r * width, width)
        out_ref[r] = piece
        image = image + piece
    image = jnp.where(live(facts_ref[...], image.shape), image, 0.0)
    u = u_ref[...].astype(jnp.float32)
    square = sums_ref[1:2, 0:1]
    cross = total(u * image)
    rho = jnp.where(square > 0.0, cross / square, 0.0)
    w = image - rho * u
    w_ref[...] = w.astype(jnp.bfloat16)
    lane = lax.broadcasted_iota(jnp.int32, (1, 128), 1)
    stats = jnp.zeros((1, 128), jnp.float32)
    for n, value in enumerate((sums_ref[0:1, 0:1], square, cross, total(w * w), rho)):
        stats = jnp.where(lane == n, value, stats)
    for n in range(stats_ref.shape[0]):
        stats_ref[n] = stats


def image_kernel(size, width, rows, *refs):
    row_refs, refs = refs[:rows], refs[rows:]
    far_ref, near_ref, self_ref, left_row, right_row, left_hbm, right_hbm, out_ref, left_own, right_own, sems = refs
    _, _, there = place(size, width)
    own = fetch(left_hbm, right_hbm, left_own, right_own, sems, [(0, 2 + width), (2 + width, width)])
    image = None
    for r, source in enumerate(row_refs):
        piece = terms(only(there[1 + r], source[...]), left_row, right_row, r * width, width)
        image = piece if image is None else image + piece
    odd = lax.rem(lax.axis_index("sector"), 2) == 1
    near, far = near_ref[...], only(there[0], far_ref[...])
    finish(own[0])
    image = image + terms(self_ref[...], left_own, right_own, 0, 2)
    image = image + terms(jnp.where(odd, near, far), left_own, right_own, 2, width)
    finish(own[1])
    out_ref[...] = image + terms(jnp.where(odd, far, near), left_own, right_own, 2 + width, width)


def second_kernel(size, width, rows, cells, facts_ref, stats_ref, hw_ref, near_part_ref, far_part_ref, row_part_ref,
                  first_hbm, second_hbm, first_ref, second_ref, sems):
    _, partners, _ = place(size, width)
    facts = facts_ref[...]
    stats = stats_ref[:, 0, :]
    sums = jnp.sum(stats, axis=0, keepdims=True)
    start, square, cross, inner = (sums[:, i : i + 1] for i in range(4))
    scale = lax.rsqrt(start / cells + 1e-06) * (1.0 / SCALE)
    parts = [near_part_ref[0], near_part_ref[1], far_part_ref[...]] + [row_part_ref[r] for r in range(rows)]
    cell = live(facts, parts[0].shape)
    first_ref[...] = jnp.where(cell, sum(parts[1:], parts[0]), 0.0) * scale
    first_copy = pltpu.make_async_copy(first_ref, first_hbm.at[0], sems.at[0])
    first_copy.start()
    rho = cross / square
    gap = stats[:, 4:5] - rho
    residual = inner + jnp.sum(stats[:, 1:2] * gap * gap, axis=0, keepdims=True)
    second_scale = scale * lax.rsqrt(scale * scale * (residual / cells) + 1e-06)
    image = hw_ref[...]
    for n, part in enumerate(parts):
        image = image + (stats_ref[partners[n], :, 4:5] - rho) * part
    second_ref[...] = jnp.where(cell, image, 0.0) * second_scale
    second_copy = pltpu.make_async_copy(second_ref, second_hbm.at[0], sems.at[1])
    second_copy.start()
    first_copy.wait()
    second_copy.wait()


def body(wavefunction, sector_dims, left_env, right_env):
    size = lax.axis_size("sector")
    block = wavefunction.shape[1]
    square = (block, block)
    width = (right_env.shape[1] - 2) // 4
    near, row_pairs = swap_pairs(size)
    rows = len(row_pairs)
    cells = float(size * block * block)
    few, every, side, last = ((n,) + square for n in (2 + width, 2 + 2 * width, width, rows * width))
    f32, bf16 = jnp.float32, jnp.bfloat16
    dma = pltpu.SemaphoreType.DMA

    u, far_u, facts = call(
        start_kernel, (pltpu.VMEM(square, bf16),) * 2 + (pltpu.VMEM((8, 128), f32),), [HB, HB], (VM,) * 3,
        [pltpu.VMEM(square, f32), pltpu.SMEM((1, 2), jnp.int32), dma((QUARTERS + 1,))],
    )(hbm(wavefunction), hbm(sector_dims))

    left_env, right_env = hbm(left_env), hbm(right_env)
    u, facts = vmem(u), vmem(facts)
    row_u = [vmem(swap(u, "sector", p)) for p in row_pairs]
    near_u = vmem(swap(u, "sector", near))
    far_u = vmem(far_swap(after(far_u, near_u)))
    near_part, sums, left_far, right_far, left_row, right_row = call(
        functools.partial(near_kernel, size, width, rows),
        (pltpu.VMEM((2,) + square, f32), pltpu.VMEM((8, 128), f32)) + (pltpu.VMEM(side, bf16),) * 2 + (pltpu.VMEM(last, bf16),) * 2,
        [HB] * 3 + [VM] * 3, (VM,) * 6,
        [pltpu.VMEM(few, bf16)] * 2 + [pltpu.VMEM(square, f32), dma((2, 2)), dma((1, 2)), dma((rows, 2)), dma], LONG,
    )(left_env, right_env, hbm(wavefunction), facts, u, near_u)
    near_part, left_row, right_row = vmem(near_part), vmem(left_row), vmem(right_row)
    far_part = vmem(call(
        functools.partial(far_kernel, size, width), pltpu.VMEM(square, f32), [VM] * 3, VM, cost=LONG,
    )(vmem(left_far), vmem(right_far), far_u))
    row_part, w, stats = call(
        functools.partial(first_kernel, size, width, rows),
        (pltpu.VMEM((rows,) + square, f32),) + (pltpu.VMEM(square, bf16), jax.ShapeDtypeStruct((size, 1, 128), f32)),
        [VM] * (7 + rows), (VM,) * 3,
    )(near_part, far_part, facts, vmem(sums), u, left_row, right_row, *row_u)

    w = vmem(w)
    row_w = [vmem(swap(w, "sector", p)) for p in row_pairs]
    near_w = vmem(swap(w, "sector", near))
    far_w = vmem(far_swap(w))
    stats = lax.all_to_all(stats, "sector", 0, 0, tiled=True)
    hw = call(
        functools.partial(image_kernel, size, width, rows), pltpu.VMEM(square, f32), [VM] * (5 + rows) + [HB] * 2, VM,
        [pltpu.VMEM(every, bf16)] * 2 + [dma((2, 2))],
    )(*row_w, far_w, near_w, w, left_row, right_row, left_env, right_env)
    return call(
        functools.partial(second_kernel, size, width, rows, cells),
        (jax.ShapeDtypeStruct((1,) + square, f32),) * 2, [VM] * 6, (HB, HB),
        [pltpu.VMEM(square, f32)] * 2 + [dma((2,))],
    )(facts, stats, vmem(hw), near_part, far_part, vmem(row_part))


def solution(mesh):
    placed = (
        P(("groups", "sector"), None, None),
        P(("groups", "sector"), None),
        P(("groups", "sector"), None, None, None),
        P(("groups", "sector"), None, None, None),
    )
    return jax.shard_map(
        body,
        mesh=mesh,
        in_specs=placed,
        out_specs=(P(("groups", "sector"), None, None), P(("groups", "sector"), None, None)),
        check_vma=False,
    )
```

```python
import functools

import jax
import jax.numpy as jnp
from jax import lax
from jax.experimental import pallas as pl
from jax.experimental.pallas import tpu as pltpu
from jax.sharding import PartitionSpec as P

QD = 8
SCALE = 1024.0
QUARTERS = 4
NT = (((1,), (1,)), ((), ()))
VM = pl.BlockSpec(memory_space=pltpu.VMEM)
HB = pl.BlockSpec(memory_space=pltpu.HBM)
AN = pl.BlockSpec(memory_space=pl.ANY)
COST = pl.CostEstimate(flops=1, bytes_accessed=1, transcendentals=0)
LONG = pl.CostEstimate(flops=4000000000, bytes_accessed=1, transcendentals=0)
PARAMS = pltpu.CompilerParams(vmem_limit_bytes=16 * 1024 * 1024)


def vmem(x):
    return pltpu.with_memory_space_constraint(x, pltpu.VMEM)


def hbm(x):
    return pltpu.with_memory_space_constraint(x, pltpu.HBM)


def call(kernel, out_shape, in_specs, out_specs, scratch=(), cost=COST, aliases={}):
    return pl.pallas_call(
        kernel, out_shape=out_shape, in_specs=in_specs, out_specs=out_specs, scratch_shapes=list(scratch),
        compiler_params=PARAMS, cost_estimate=cost, input_output_aliases=aliases,
    )


def swap(x, axis, pairs):
    to = {a: b for p in pairs for a, b in (p, p[::-1])}
    return lax.ppermute(x, axis, [(s, to.get(s, s)) for s in range(lax.axis_size(axis))])


def swap_pairs(size):
    rows = size // QD
    near = [(s, s + 1) for s in range(0, size, 2)]
    row_even = [(s, s + QD) for r in range(0, rows - 1, 2) for s in range(r * QD, r * QD + QD)]
    row_odd = [(s, s + QD) for r in range(1, rows - 1, 2) for s in range(r * QD, r * QD + QD)]
    return near, [p for p in (row_even, row_odd) if p]


def far_swap(x):
    groups, size = lax.axis_size("groups"), lax.axis_size("sector")
    pairs = []
    for g in range(groups):
        for s in range(size):
            if s % QD == 0 or s % QD == QD - 1:
                to, partner = (g ^ 1 if g ^ 1 < groups else g), s
            else:
                to, partner = g, s + 1 if s % 2 else s - 1
            pairs.append((g * size + s, to * size + partner))
    return lax.ppermute(x, ("groups", "sector"), pairs)


def place(size, width):
    me = lax.axis_index("sector")
    column = lax.rem(me, QD)
    odd = lax.rem(me, 2) == 1
    row_odd = lax.rem(lax.div(me, QD), 2) == 1
    low, high, down, up = 2, 2 + width, 2 + 2 * width, 2 + 3 * width
    offsets = [jnp.where(odd, low, high), jnp.where(odd, high, low),
               jnp.where(row_odd, down, up), jnp.where(row_odd, up, down)]
    partners = [jnp.where(odd, me - 1, me + 1), jnp.where(odd, me + 1, me - 1),
                jnp.where(row_odd, me - QD, me + QD), jnp.where(row_odd, me + QD, me - QD)]
    there = [(column != 0) & (column != QD - 1),
             True if size // QD % 2 == 0 else (partners[2] >= 0) & (partners[2] < size),
             (partners[3] >= 0) & (partners[3] < size)]
    partners = [me] + [jnp.clip(p, 0, size - 1) for p in partners]
    return offsets, partners, there


def live(facts, shape):
    row_ok = lax.broadcasted_iota(jnp.int32, shape, 0).astype(jnp.float32) < facts[1:2, 0:1]
    col_ok = lax.broadcasted_iota(jnp.int32, shape, 1).astype(jnp.float32) < facts[2:3, 0:1]
    return row_ok & col_ok


def total(x):
    return jnp.sum(jnp.sum(x, axis=0, keepdims=True), axis=1, keepdims=True)


def only(there, block):
    return block if there is True else jnp.where(there, block, jnp.zeros_like(block))


def terms(src, left_ref, right_ref, first, count):
    size = src.shape[0]
    right = right_ref[pl.ds(first, count)].reshape(count * size, size)
    partial_t = lax.dot_general(right, src, NT, preferred_element_type=jnp.float32).astype(jnp.bfloat16)
    image = None
    for k in range(count):
        piece = lax.dot_general(
            left_ref[first + k], partial_t[k * size : (k + 1) * size], NT, preferred_element_type=jnp.float32
        )
        image = piece if image is None else image + piece
    return image


def fetch(left_hbm, right_hbm, left_ref, right_ref, sems, spans):
    copies = []
    at = 0
    for n, (offset, count) in enumerate(spans):
        pair = [
            pltpu.make_async_copy(source.at[0, pl.ds(offset, count)], target.at[pl.ds(at, count)], sems.at[n, e])
            for e, (source, target) in enumerate(((right_hbm, right_ref), (left_hbm, left_ref)))
        ]
        for copy in pair:
            copy.start()
        copies.append(pair)
        at += count
    return copies


def finish(copies):
    for copy in copies:
        copy.wait()


def start_kernel(wave_hbm, dims_hbm, *refs):
    u_refs, (facts_ref, wave_ref, dims_ref, sems) = refs[:2], refs[2:]
    size = wave_ref.shape[0]
    step = size // QUARTERS
    dims_copy = pltpu.make_async_copy(dims_hbm, dims_ref, sems.at[QUARTERS])
    dims_copy.start()
    copies = [
        pltpu.make_async_copy(wave_hbm.at[0, pl.ds(n * step, step)], wave_ref.at[pl.ds(n * step, step)], sems.at[n])
        for n in range(QUARTERS)
    ]
    for copy in copies:
        copy.start()
    dims_copy.wait()
    row_count, col_count = dims_ref[0, 0], dims_ref[0, 1]
    lines = lax.broadcasted_iota(jnp.int32, (8, 128), 0)
    facts_ref[...] = jnp.where(lines == 1, row_count, jnp.where(lines == 2, col_count, 0)).astype(jnp.float32)
    col_ok = lax.broadcasted_iota(jnp.int32, (step, size), 1) < col_count
    row = lax.broadcasted_iota(jnp.int32, (step, size), 0)
    for n, copy in enumerate(copies):
        copy.wait()
        rows = pl.ds(n * step, step)
        held = jnp.where((row < row_count - n * step) & col_ok, wave_ref[rows], 0.0)
        block = (held * SCALE).astype(jnp.bfloat16)
        for ref in u_refs:
            ref[rows] = block


def pass_kernel(*refs):
    pass


def after(held, first):
    return call(pass_kernel, pltpu.VMEM(held.shape, held.dtype), [AN] * 2, AN, aliases={0: 0})(vmem(held), first)


def near_kernel(size, width, rows, left_hbm, right_hbm, wave_hbm, facts_ref, self_ref, near_ref, out_ref, sums_ref,
                left_far, right_far, left_row, right_row, left_own, right_own, wave_ref, sems, far_sems, row_sems, wave_sem):
    offsets, _, _ = place(size, width)
    wave_copy = pltpu.make_async_copy(wave_hbm.at[0], wave_ref, wave_sem)
    own = fetch(left_hbm, right_hbm, left_own, right_own, sems, [(0, 2), (offsets[0], width)])
    wave_copy.start()
    later = fetch(left_hbm, right_hbm, left_far, right_far, far_sems, [(offsets[1], width)])
    later += fetch(left_hbm, right_hbm, left_row, right_row, row_sems, [(o, width) for o in offsets[2 : 2 + rows]])
    u = self_ref[...].astype(jnp.float32)
    lines = lax.broadcasted_iota(jnp.int32, (8, 128), 0)
    sums = jnp.where(lines == 1, total(u * u), 0.0)
    finish(own[0])
    out_ref[0] = terms(self_ref[...], left_own, right_own, 0, 2)
    finish(own[1])
    out_ref[1] = terms(near_ref[...], left_own, right_own, 2, width)
    wave_copy.wait()
    held = jnp.where(live(facts_ref[...], wave_ref.shape), wave_ref[...], 0.0)
    sums_ref[...] = jnp.where(lines == 0, total(held * held), sums)
    for pair in later:
        finish(pair)


def far_kernel(size, width, left_ref, right_ref, far_ref, out_ref):
    _, _, there = place(size, width)
    out_ref[...] = terms(only(there[0], far_ref[...]), left_ref, right_ref, 0, width)


def first_kernel(size, width, rows, *refs):
    near_part_ref, far_part_ref, facts_ref, sums_ref, u_ref, left_ref, right_ref = refs[:7]
    row_refs, (out_ref, w_ref, stats_ref) = refs[7 : 7 + rows], refs[7 + rows :]
    _, _, there = place(size, width)
    image = near_part_ref[0] + near_part_ref[1] + far_part_ref[...]
    for r, source in enumerate(row_refs):
        piece = terms(only(there[1 + r], source[...]), left_ref, right_ref, r * width, width)
        out_ref[r] = piece
        image = image + piece
    image = jnp.where(live(facts_ref[...], image.shape), image, 0.0)
    u = u_ref[...].astype(jnp.float32)
    square = sums_ref[1:2, 0:1]
    cross = total(u * image)
    rho = jnp.where(square > 0.0, cross / square, 0.0)
    w = image - rho * u
    w_ref[...] = w.astype(jnp.bfloat16)
    lane = lax.broadcasted_iota(jnp.int32, (1, 128), 1)
    stats = jnp.zeros((1, 128), jnp.float32)
    for n, value in enumerate((sums_ref[0:1, 0:1], square, cross, total(w * w), rho)):
        stats = jnp.where(lane == n, value, stats)
    for n in range(stats_ref.shape[0]):
        stats_ref[n] = stats


def image_kernel(size, width, rows, *refs):
    near_ref, far_ref, refs = refs[0], refs[1], refs[2:]
    row_refs, refs = refs[:rows], refs[rows:]
    self_ref, left_row, right_row, left_hbm, right_hbm, out_ref, left_own, right_own, sems = refs
    _, _, there = place(size, width)
    own = fetch(left_hbm, right_hbm, left_own, right_own, sems, [(0, 2 + width), (2 + width, width)])
    image = None
    for r, source in enumerate(row_refs):
        piece = terms(only(there[1 + r], source[...]), left_row, right_row, r * width, width)
        image = piece if image is None else image + piece
    odd = lax.rem(lax.axis_index("sector"), 2) == 1
    near, far = near_ref[...], only(there[0], far_ref[...])
    finish(own[0])
    image = image + terms(self_ref[...], left_own, right_own, 0, 2)
    image = image + terms(jnp.where(odd, near, far), left_own, right_own, 2, width)
    finish(own[1])
    out_ref[...] = image + terms(jnp.where(odd, far, near), left_own, right_own, 2 + width, width)


def second_kernel(size, width, rows, cells, facts_ref, stats_ref, hw_ref, near_part_ref, far_part_ref, row_part_ref,
                  first_hbm, second_hbm, first_ref, second_ref, sems):
    _, partners, _ = place(size, width)
    facts = facts_ref[...]
    stats = stats_ref[:, 0, :]
    sums = jnp.sum(stats, axis=0, keepdims=True)
    start, square, cross, inner = (sums[:, i : i + 1] for i in range(4))
    scale = lax.rsqrt(start / cells + 1e-06) * (1.0 / SCALE)
    parts = [near_part_ref[0], near_part_ref[1], far_part_ref[...]] + [row_part_ref[r] for r in range(rows)]
    cell = live(facts, parts[0].shape)
    first_ref[...] = jnp.where(cell, sum(parts[1:], parts[0]), 0.0) * scale
    first_copy = pltpu.make_async_copy(first_ref, first_hbm.at[0], sems.at[0])
    first_copy.start()
    rho = cross / square
    gap = stats[:, 4:5] - rho
    residual = inner + jnp.sum(stats[:, 1:2] * gap * gap, axis=0, keepdims=True)
    second_scale = scale * lax.rsqrt(scale * scale * (residual / cells) + 1e-06)
    image = hw_ref[...]
    for n, part in enumerate(parts):
        image = image + (stats_ref[partners[n], :, 4:5] - rho) * part
    second_ref[...] = jnp.where(cell, image, 0.0) * second_scale
    second_copy = pltpu.make_async_copy(second_ref, second_hbm.at[0], sems.at[1])
    second_copy.start()
    first_copy.wait()
    second_copy.wait()


def body(wavefunction, sector_dims, left_env, right_env):
    size = lax.axis_size("sector")
    block = wavefunction.shape[1]
    square = (block, block)
    width = (right_env.shape[1] - 2) // 4
    near, row_pairs = swap_pairs(size)
    rows = len(row_pairs)
    cells = float(size * block * block)
    few, every, side, last = ((n,) + square for n in (2 + width, 2 + 2 * width, width, rows * width))
    f32, bf16 = jnp.float32, jnp.bfloat16
    dma = pltpu.SemaphoreType.DMA

    u, far_u, facts = call(
        start_kernel, (pltpu.VMEM(square, bf16),) * 2 + (pltpu.VMEM((8, 128), f32),), [HB, HB], (VM,) * 3,
        [pltpu.VMEM(square, f32), pltpu.SMEM((1, 2), jnp.int32), dma((QUARTERS + 1,))],
    )(hbm(wavefunction), hbm(sector_dims))

    left_env, right_env = hbm(left_env), hbm(right_env)
    u, facts = vmem(u), vmem(facts)
    row_u = [vmem(swap(u, "sector", p)) for p in row_pairs]
    near_u = vmem(swap(u, "sector", near))
    far_u = vmem(far_swap(after(far_u, near_u)))
    near_part, sums, left_far, right_far, left_row, right_row = call(
        functools.partial(near_kernel, size, width, rows),
        (pltpu.VMEM((2,) + square, f32), pltpu.VMEM((8, 128), f32)) + (pltpu.VMEM(side, bf16),) * 2 + (pltpu.VMEM(last, bf16),) * 2,
        [HB] * 3 + [VM] * 3, (VM,) * 6,
        [pltpu.VMEM(few, bf16)] * 2 + [pltpu.VMEM(square, f32), dma((2, 2)), dma((1, 2)), dma((rows, 2)), dma], LONG,
    )(left_env, right_env, hbm(wavefunction), facts, u, near_u)
    near_part, left_row, right_row = vmem(near_part), vmem(left_row), vmem(right_row)
    far_part = vmem(call(
        functools.partial(far_kernel, size, width), pltpu.VMEM(square, f32), [VM] * 3, VM, cost=LONG,
    )(vmem(left_far), vmem(right_far), far_u))
    row_part, w, stats = call(
        functools.partial(first_kernel, size, width, rows),
        (pltpu.VMEM((rows,) + square, f32),) + (pltpu.VMEM(square, bf16), jax.ShapeDtypeStruct((size, 1, 128), f32)),
        [VM] * (7 + rows), (VM,) * 3,
    )(near_part, far_part, facts, vmem(sums), u, left_row, right_row, *row_u)

    w = vmem(w)
    row_w = [vmem(swap(w, "sector", p)) for p in row_pairs]
    near_w = vmem(swap(w, "sector", near))
    far_w = vmem(far_swap(w))
    stats = lax.all_to_all(stats, "sector", 0, 0, tiled=True)
    hw = call(
        functools.partial(image_kernel, size, width, rows), pltpu.VMEM(square, f32), [VM] * (5 + rows) + [HB] * 2, VM,
        [pltpu.VMEM(every, bf16)] * 2 + [dma((2, 2))],
    )(near_w, far_w, *row_w, w, left_row, right_row, left_env, right_env)
    return call(
        functools.partial(second_kernel, size, width, rows, cells),
        (jax.ShapeDtypeStruct((1,) + square, f32),) * 2, [VM] * 6, (HB, HB),
        [pltpu.VMEM(square, f32)] * 2 + [dma((2,))],
    )(facts, stats, vmem(hw), near_part, far_part, vmem(row_part))


def solution(mesh):
    placed = (
        P(("groups", "sector"), None, None),
        P(("groups", "sector"), None),
        P(("groups", "sector"), None, None, None),
        P(("groups", "sector"), None, None, None),
    )
    return jax.shard_map(
        body,
        mesh=mesh,
        in_specs=placed,
        out_specs=(P(("groups", "sector"), None, None), P(("groups", "sector"), None, None)),
        check_vma=False,
    )
```

```python
import functools

import jax
import jax.numpy as jnp
from jax import lax
from jax.experimental import pallas as pl
from jax.experimental.pallas import tpu as pltpu
from jax.sharding import PartitionSpec as P

QD = 8
SCALE = 1024.0
QUARTERS = 4
NT = (((1,), (1,)), ((), ()))
VM = pl.BlockSpec(memory_space=pltpu.VMEM)
HB = pl.BlockSpec(memory_space=pltpu.HBM)
AN = pl.BlockSpec(memory_space=pl.ANY)
COST = pl.CostEstimate(flops=1, bytes_accessed=1, transcendentals=0)
LONG = pl.CostEstimate(flops=4000000000, bytes_accessed=1, transcendentals=0)
PARAMS = pltpu.CompilerParams(vmem_limit_bytes=16 * 1024 * 1024)


def vmem(x):
    return pltpu.with_memory_space_constraint(x, pltpu.VMEM)


def hbm(x):
    return pltpu.with_memory_space_constraint(x, pltpu.HBM)


def call(kernel, out_shape, in_specs, out_specs, scratch=(), cost=COST, aliases={}):
    return pl.pallas_call(
        kernel, out_shape=out_shape, in_specs=in_specs, out_specs=out_specs, scratch_shapes=list(scratch),
        compiler_params=PARAMS, cost_estimate=cost, input_output_aliases=aliases,
    )


def swap(x, axis, pairs):
    to = {a: b for p in pairs for a, b in (p, p[::-1])}
    return lax.ppermute(x, axis, [(s, to.get(s, s)) for s in range(lax.axis_size(axis))])


def swap_pairs(size):
    rows = size // QD
    near = [(s, s + 1) for s in range(0, size, 2)]
    row_even = [(s, s + QD) for r in range(0, rows - 1, 2) for s in range(r * QD, r * QD + QD)]
    row_odd = [(s, s + QD) for r in range(1, rows - 1, 2) for s in range(r * QD, r * QD + QD)]
    return near, [p for p in (row_even, row_odd) if p]


def far_swap(x):
    groups, size = lax.axis_size("groups"), lax.axis_size("sector")
    pairs = []
    for g in range(groups):
        for s in range(size):
            if s % QD == 0 or s % QD == QD - 1:
                to, partner = (g ^ 1 if g ^ 1 < groups else g), s
            else:
                to, partner = g, s + 1 if s % 2 else s - 1
            pairs.append((g * size + s, to * size + partner))
    return lax.ppermute(x, ("groups", "sector"), pairs)


def place(size, width):
    me = lax.axis_index("sector")
    column = lax.rem(me, QD)
    odd = lax.rem(me, 2) == 1
    row_odd = lax.rem(lax.div(me, QD), 2) == 1
    low, high, down, up = 2, 2 + width, 2 + 2 * width, 2 + 3 * width
    offsets = [jnp.where(odd, low, high), jnp.where(odd, high, low),
               jnp.where(row_odd, down, up), jnp.where(row_odd, up, down)]
    partners = [jnp.where(odd, me - 1, me + 1), jnp.where(odd, me + 1, me - 1),
                jnp.where(row_odd, me - QD, me + QD), jnp.where(row_odd, me + QD, me - QD)]
    there = [(column != 0) & (column != QD - 1),
             True if size // QD % 2 == 0 else (partners[2] >= 0) & (partners[2] < size),
             (partners[3] >= 0) & (partners[3] < size)]
    partners = [me] + [jnp.clip(p, 0, size - 1) for p in partners]
    return offsets, partners, there


def live(facts, shape):
    row_ok = lax.broadcasted_iota(jnp.int32, shape, 0).astype(jnp.float32) < facts[1:2, 0:1]
    col_ok = lax.broadcasted_iota(jnp.int32, shape, 1).astype(jnp.float32) < facts[2:3, 0:1]
    return row_ok & col_ok


def total(x):
    return jnp.sum(jnp.sum(x, axis=0, keepdims=True), axis=1, keepdims=True)


def only(there, block):
    return block if there is True else jnp.where(there, block, jnp.zeros_like(block))


def terms(src, left_ref, right_ref, first, count):
    size = src.shape[0]
    right = right_ref[pl.ds(first, count)].reshape(count * size, size)
    partial_t = lax.dot_general(right, src, NT, preferred_element_type=jnp.float32).astype(jnp.bfloat16)
    image = None
    for k in range(count):
        piece = lax.dot_general(
            left_ref[first + k], partial_t[k * size : (k + 1) * size], NT, preferred_element_type=jnp.float32
        )
        image = piece if image is None else image + piece
    return image


def fetch(left_hbm, right_hbm, left_ref, right_ref, sems, spans):
    copies = []
    at = 0
    for n, (offset, count) in enumerate(spans):
        pair = [
            pltpu.make_async_copy(source.at[0, pl.ds(offset, count)], target.at[pl.ds(at, count)], sems.at[n, e])
            for e, (source, target) in enumerate(((right_hbm, right_ref), (left_hbm, left_ref)))
        ]
        for copy in pair:
            copy.start()
        copies.append(pair)
        at += count
    return copies


def finish(copies):
    for copy in copies:
        copy.wait()


def start_kernel(wave_hbm, dims_hbm, *refs):
    u_refs, (facts_ref, wave_ref, dims_ref, sems) = refs[:2], refs[2:]
    size = wave_ref.shape[0]
    step = size // QUARTERS
    dims_copy = pltpu.make_async_copy(dims_hbm, dims_ref, sems.at[QUARTERS])
    dims_copy.start()
    copies = [
        pltpu.make_async_copy(wave_hbm.at[0, pl.ds(n * step, step)], wave_ref.at[pl.ds(n * step, step)], sems.at[n])
        for n in range(QUARTERS)
    ]
    for copy in copies:
        copy.start()
    dims_copy.wait()
    row_count, col_count = dims_ref[0, 0], dims_ref[0, 1]
    lines = lax.broadcasted_iota(jnp.int32, (8, 128), 0)
    facts_ref[...] = jnp.where(lines == 1, row_count, jnp.where(lines == 2, col_count, 0)).astype(jnp.float32)
    col_ok = lax.broadcasted_iota(jnp.int32, (step, size), 1) < col_count
    row = lax.broadcasted_iota(jnp.int32, (step, size), 0)
    for n, copy in enumerate(copies):
        copy.wait()
        rows = pl.ds(n * step, step)
        held = jnp.where((row < row_count - n * step) & col_ok, wave_ref[rows], 0.0)
        block = (held * SCALE).astype(jnp.bfloat16)
        for ref in u_refs:
            ref[rows] = block


def pass_kernel(*refs):
    pass


def after(held, first):
    return call(pass_kernel, pltpu.VMEM(held.shape, held.dtype), [AN] * 2, AN, aliases={0: 0})(vmem(held), first)


def near_kernel(size, width, rows, left_hbm, right_hbm, wave_hbm, facts_ref, self_ref, near_ref, out_ref, sums_ref,
                left_far, right_far, left_row, right_row, left_own, right_own, wave_ref, sems, far_sems, row_sems, wave_sem):
    offsets, _, _ = place(size, width)
    wave_copy = pltpu.make_async_copy(wave_hbm.at[0], wave_ref, wave_sem)
    own = fetch(left_hbm, right_hbm, left_own, right_own, sems, [(0, 2), (offsets[0], width)])
    wave_copy.start()
    later = fetch(left_hbm, right_hbm, left_far, right_far, far_sems, [(offsets[1], width)])
    later += fetch(left_hbm, right_hbm, left_row, right_row, row_sems, [(o, width) for o in offsets[2 : 2 + rows]])
    u = self_ref[...].astype(jnp.float32)
    lines = lax.broadcasted_iota(jnp.int32, (8, 128), 0)
    sums = jnp.where(lines == 1, total(u * u), 0.0)
    finish(own[0])
    out_ref[0] = terms(self_ref[...], left_own, right_own, 0, 2)
    finish(own[1])
    out_ref[1] = terms(near_ref[...], left_own, right_own, 2, width)
    wave_copy.wait()
    held = jnp.where(live(facts_ref[...], wave_ref.shape), wave_ref[...], 0.0)
    sums_ref[...] = jnp.where(lines == 0, total(held * held), sums)
    for pair in later:
        finish(pair)


def far_kernel(size, width, left_ref, right_ref, far_ref, out_ref):
    _, _, there = place(size, width)
    out_ref[...] = terms(only(there[0], far_ref[...]), left_ref, right_ref, 0, width)


def first_kernel(size, width, rows, *refs):
    near_part_ref, far_part_ref, facts_ref, sums_ref, u_ref, left_ref, right_ref = refs[:7]
    row_refs, (out_ref, w_ref, far_w_ref, sums_out_ref) = refs[7 : 7 + rows], refs[7 + rows :]
    _, _, there = place(size, width)
    image = near_part_ref[0] + near_part_ref[1] + far_part_ref[...]
    for r, source in enumerate(row_refs):
        piece = terms(only(there[1 + r], source[...]), left_ref, right_ref, r * width, width)
        out_ref[r] = piece
        image = image + piece
    image = jnp.where(live(facts_ref[...], image.shape), image, 0.0)
    u = u_ref[...].astype(jnp.float32)
    square = sums_ref[1:2, 0:1]
    cross = total(u * image)
    rho = jnp.where(square > 0.0, cross / square, 0.0)
    for ref in (w_ref, far_w_ref):
        ref[...] = (image - rho * u).astype(jnp.bfloat16)
    lines = lax.broadcasted_iota(jnp.int32, (8, 128), 0)
    sums_out_ref[...] = jnp.where(lines == 2, cross, jnp.where(lines == 4, rho, sums_ref[...]))


def numbers_kernel(sums_ref, w_ref, out_ref):
    w = w_ref[...].astype(jnp.float32)
    values = [sums_ref[n : n + 1, 0:1] for n in range(5)]
    values[3] = total(w * w)
    lane = lax.broadcasted_iota(jnp.int32, (1, 128), 1)
    numbers = jnp.zeros((1, 128), jnp.float32)
    for n, value in enumerate(values):
        numbers = jnp.where(lane == n, value, numbers)
    for n in range(out_ref.shape[0]):
        out_ref[n] = numbers


def image_kernel(size, width, rows, *refs):
    row_refs, refs = refs[:rows], refs[rows:]
    far_ref, near_ref, self_ref, left_row, right_row, left_hbm, right_hbm, out_ref, left_own, right_own, sems = refs
    _, _, there = place(size, width)
    own = fetch(left_hbm, right_hbm, left_own, right_own, sems, [(0, 2 + width), (2 + width, width)])
    image = None
    for r, source in enumerate(row_refs):
        piece = terms(only(there[1 + r], source[...]), left_row, right_row, r * width, width)
        image = piece if image is None else image + piece
    odd = lax.rem(lax.axis_index("sector"), 2) == 1
    near, far = near_ref[...], only(there[0], far_ref[...])
    finish(own[0])
    image = image + terms(self_ref[...], left_own, right_own, 0, 2)
    image = image + terms(jnp.where(odd, near, far), left_own, right_own, 2, width)
    finish(own[1])
    out_ref[...] = image + terms(jnp.where(odd, far, near), left_own, right_own, 2 + width, width)


def second_kernel(size, width, rows, cells, facts_ref, stats_ref, hw_ref, near_part_ref, far_part_ref, row_part_ref,
                  first_hbm, second_hbm, first_ref, second_ref, sems):
    _, partners, _ = place(size, width)
    facts = facts_ref[...]
    stats = stats_ref[:, 0, :]
    sums = jnp.sum(stats, axis=0, keepdims=True)
    start, square, cross, inner = (sums[:, i : i + 1] for i in range(4))
    scale = lax.rsqrt(start / cells + 1e-06) * (1.0 / SCALE)
    parts = [near_part_ref[0], near_part_ref[1], far_part_ref[...]] + [row_part_ref[r] for r in range(rows)]
    cell = live(facts, parts[0].shape)
    first_ref[...] = jnp.where(cell, sum(parts[1:], parts[0]), 0.0) * scale
    first_copy = pltpu.make_async_copy(first_ref, first_hbm.at[0], sems.at[0])
    first_copy.start()
    rho = cross / square
    gap = stats[:, 4:5] - rho
    residual = inner + jnp.sum(stats[:, 1:2] * gap * gap, axis=0, keepdims=True)
    second_scale = scale * lax.rsqrt(scale * scale * (residual / cells) + 1e-06)
    image = hw_ref[...]
    for n, part in enumerate(parts):
        image = image + (stats_ref[partners[n], :, 4:5] - rho) * part
    second_ref[...] = jnp.where(cell, image, 0.0) * second_scale
    second_copy = pltpu.make_async_copy(second_ref, second_hbm.at[0], sems.at[1])
    second_copy.start()
    first_copy.wait()
    second_copy.wait()


def body(wavefunction, sector_dims, left_env, right_env):
    size = lax.axis_size("sector")
    block = wavefunction.shape[1]
    square = (block, block)
    width = (right_env.shape[1] - 2) // 4
    near, row_pairs = swap_pairs(size)
    rows = len(row_pairs)
    cells = float(size * block * block)
    few, every, side, last = ((n,) + square for n in (2 + width, 2 + 2 * width, width, rows * width))
    f32, bf16 = jnp.float32, jnp.bfloat16
    dma = pltpu.SemaphoreType.DMA

    u, far_u, facts = call(
        start_kernel, (pltpu.VMEM(square, bf16),) * 2 + (pltpu.VMEM((8, 128), f32),), [HB, HB], (VM,) * 3,
        [pltpu.VMEM(square, f32), pltpu.SMEM((1, 2), jnp.int32), dma((QUARTERS + 1,))],
    )(hbm(wavefunction), hbm(sector_dims))

    left_env, right_env = hbm(left_env), hbm(right_env)
    u, facts = vmem(u), vmem(facts)
    row_u = [vmem(swap(u, "sector", p)) for p in row_pairs]
    near_u = vmem(swap(u, "sector", near))
    far_u = vmem(far_swap(after(far_u, near_u)))
    near_part, sums, left_far, right_far, left_row, right_row = call(
        functools.partial(near_kernel, size, width, rows),
        (pltpu.VMEM((2,) + square, f32), pltpu.VMEM((8, 128), f32)) + (pltpu.VMEM(side, bf16),) * 2 + (pltpu.VMEM(last, bf16),) * 2,
        [HB] * 3 + [VM] * 3, (VM,) * 6,
        [pltpu.VMEM(few, bf16)] * 2 + [pltpu.VMEM(square, f32), dma((2, 2)), dma((1, 2)), dma((rows, 2)), dma], LONG,
    )(left_env, right_env, hbm(wavefunction), facts, u, near_u)
    near_part, left_row, right_row = vmem(near_part), vmem(left_row), vmem(right_row)
    far_part = vmem(call(
        functools.partial(far_kernel, size, width), pltpu.VMEM(square, f32), [VM] * 3, VM, cost=LONG,
    )(vmem(left_far), vmem(right_far), far_u))
    row_part, w, far_w, sums = call(
        functools.partial(first_kernel, size, width, rows),
        (pltpu.VMEM((rows,) + square, f32),) + (pltpu.VMEM(square, bf16),) * 2 + (pltpu.VMEM((8, 128), f32),),
        [VM] * (7 + rows), (VM,) * 4,
    )(near_part, far_part, facts, vmem(sums), u, left_row, right_row, *row_u)

    w = vmem(w)
    row_w = [vmem(swap(w, "sector", p)) for p in row_pairs]
    near_w = vmem(swap(w, "sector", near))
    far_w = vmem(far_swap(after(far_w, near_w)))
    stats = call(numbers_kernel, jax.ShapeDtypeStruct((size, 1, 128), f32), [VM] * 2, VM)(vmem(sums), w)
    stats = lax.all_to_all(stats, "sector", 0, 0, tiled=True)
    hw = call(
        functools.partial(image_kernel, size, width, rows), pltpu.VMEM(square, f32), [VM] * (5 + rows) + [HB] * 2, VM,
        [pltpu.VMEM(every, bf16)] * 2 + [dma((2, 2))],
    )(*row_w, far_w, near_w, w, left_row, right_row, left_env, right_env)
    return call(
        functools.partial(second_kernel, size, width, rows, cells),
        (jax.ShapeDtypeStruct((1,) + square, f32),) * 2, [VM] * 6, (HB, HB),
        [pltpu.VMEM(square, f32)] * 2 + [dma((2,))],
    )(facts, stats, vmem(hw), near_part, far_part, vmem(row_part))


def solution(mesh):
    placed = (
        P(("groups", "sector"), None, None),
        P(("groups", "sector"), None),
        P(("groups", "sector"), None, None, None),
        P(("groups", "sector"), None, None, None),
    )
    return jax.shard_map(
        body,
        mesh=mesh,
        in_specs=placed,
        out_specs=(P(("groups", "sector"), None, None), P(("groups", "sector"), None, None)),
        check_vma=False,
    )
```

```python
import functools

import jax
import jax.numpy as jnp
from jax import lax
from jax.experimental import pallas as pl
from jax.experimental.pallas import tpu as pltpu
from jax.sharding import PartitionSpec as P

QD = 8
SCALE = 1024.0
QUARTERS = 4
NT = (((1,), (1,)), ((), ()))
VM = pl.BlockSpec(memory_space=pltpu.VMEM)
HB = pl.BlockSpec(memory_space=pltpu.HBM)
AN = pl.BlockSpec(memory_space=pl.ANY)
COST = pl.CostEstimate(flops=1, bytes_accessed=1, transcendentals=0)
LONG = pl.CostEstimate(flops=4000000000, bytes_accessed=1, transcendentals=0)
PARAMS = pltpu.CompilerParams(vmem_limit_bytes=16 * 1024 * 1024)


def vmem(x):
    return pltpu.with_memory_space_constraint(x, pltpu.VMEM)


def hbm(x):
    return pltpu.with_memory_space_constraint(x, pltpu.HBM)


def call(kernel, out_shape, in_specs, out_specs, scratch=(), cost=COST, aliases={}):
    return pl.pallas_call(
        kernel, out_shape=out_shape, in_specs=in_specs, out_specs=out_specs, scratch_shapes=list(scratch),
        compiler_params=PARAMS, cost_estimate=cost, input_output_aliases=aliases,
    )


def swap(x, axis, pairs):
    to = {a: b for p in pairs for a, b in (p, p[::-1])}
    return lax.ppermute(x, axis, [(s, to.get(s, s)) for s in range(lax.axis_size(axis))])


def swap_pairs(size):
    rows = size // QD
    near = [(s, s + 1) for s in range(0, size, 2)]
    row_even = [(s, s + QD) for r in range(0, rows - 1, 2) for s in range(r * QD, r * QD + QD)]
    row_odd = [(s, s + QD) for r in range(1, rows - 1, 2) for s in range(r * QD, r * QD + QD)]
    return near, [p for p in (row_even, row_odd) if p]


def far_swap(x):
    groups, size = lax.axis_size("groups"), lax.axis_size("sector")
    pairs = []
    for g in range(groups):
        for s in range(size):
            if s % QD == 0 or s % QD == QD - 1:
                to, partner = (g ^ 1 if g ^ 1 < groups else g), s
            else:
                to, partner = g, s + 1 if s % 2 else s - 1
            pairs.append((g * size + s, to * size + partner))
    return lax.ppermute(x, ("groups", "sector"), pairs)


def place(size, width):
    me = lax.axis_index("sector")
    column = lax.rem(me, QD)
    odd = lax.rem(me, 2) == 1
    row_odd = lax.rem(lax.div(me, QD), 2) == 1
    low, high, down, up = 2, 2 + width, 2 + 2 * width, 2 + 3 * width
    offsets = [jnp.where(odd, low, high), jnp.where(odd, high, low),
               jnp.where(row_odd, down, up), jnp.where(row_odd, up, down)]
    partners = [jnp.where(odd, me - 1, me + 1), jnp.where(odd, me + 1, me - 1),
                jnp.where(row_odd, me - QD, me + QD), jnp.where(row_odd, me + QD, me - QD)]
    there = [(column != 0) & (column != QD - 1),
             True if size // QD % 2 == 0 else (partners[2] >= 0) & (partners[2] < size),
             (partners[3] >= 0) & (partners[3] < size)]
    partners = [me] + [jnp.clip(p, 0, size - 1) for p in partners]
    return offsets, partners, there


def live(facts, shape):
    row_ok = lax.broadcasted_iota(jnp.int32, shape, 0).astype(jnp.float32) < facts[1:2, 0:1]
    col_ok = lax.broadcasted_iota(jnp.int32, shape, 1).astype(jnp.float32) < facts[2:3, 0:1]
    return row_ok & col_ok


def total(x):
    return jnp.sum(jnp.sum(x, axis=0, keepdims=True), axis=1, keepdims=True)


def only(there, block):
    return block if there is True else jnp.where(there, block, jnp.zeros_like(block))


def terms(src, left_ref, right_ref, first, count):
    size = src.shape[0]
    right = right_ref[pl.ds(first, count)].reshape(count * size, size)
    partial_t = lax.dot_general(right, src, NT, preferred_element_type=jnp.float32).astype(jnp.bfloat16)
    image = None
    for k in range(count):
        piece = lax.dot_general(
            left_ref[first + k], partial_t[k * size : (k + 1) * size], NT, preferred_element_type=jnp.float32
        )
        image = piece if image is None else image + piece
    return image


def fetch(left_hbm, right_hbm, left_ref, right_ref, sems, spans):
    copies = []
    at = 0
    for n, (offset, count) in enumerate(spans):
        pair = [
            pltpu.make_async_copy(source.at[0, pl.ds(offset, count)], target.at[pl.ds(at, count)], sems.at[n, e])
            for e, (source, target) in enumerate(((right_hbm, right_ref), (left_hbm, left_ref)))
        ]
        for copy in pair:
            copy.start()
        copies.append(pair)
        at += count
    return copies


def finish(copies):
    for copy in copies:
        copy.wait()


def start_kernel(wave_hbm, dims_hbm, *refs):
    u_refs, (facts_ref, wave_ref, dims_ref, sems) = refs[:2], refs[2:]
    size = wave_ref.shape[0]
    step = size // QUARTERS
    dims_copy = pltpu.make_async_copy(dims_hbm, dims_ref, sems.at[QUARTERS])
    dims_copy.start()
    copies = [
        pltpu.make_async_copy(wave_hbm.at[0, pl.ds(n * step, step)], wave_ref.at[pl.ds(n * step, step)], sems.at[n])
        for n in range(QUARTERS)
    ]
    for copy in copies:
        copy.start()
    dims_copy.wait()
    row_count, col_count = dims_ref[0, 0], dims_ref[0, 1]
    lines = lax.broadcasted_iota(jnp.int32, (8, 128), 0)
    facts_ref[...] = jnp.where(lines == 1, row_count, jnp.where(lines == 2, col_count, 0)).astype(jnp.float32)
    col_ok = lax.broadcasted_iota(jnp.int32, (step, size), 1) < col_count
    row = lax.broadcasted_iota(jnp.int32, (step, size), 0)
    for n, copy in enumerate(copies):
        copy.wait()
        rows = pl.ds(n * step, step)
        held = jnp.where((row < row_count - n * step) & col_ok, wave_ref[rows], 0.0)
        block = (held * SCALE).astype(jnp.bfloat16)
        for ref in u_refs:
            ref[rows] = block


def pass_kernel(*refs):
    pass


def after(held, first):
    return call(pass_kernel, pltpu.VMEM(held.shape, held.dtype), [AN] * 2, AN, aliases={0: 0})(vmem(held), first)


def near_kernel(size, width, rows, left_hbm, right_hbm, wave_hbm, facts_ref, self_ref, near_ref, out_ref, sums_ref,
                left_far, right_far, left_row, right_row, left_own, right_own, wave_ref, sems, far_sems, row_sems, wave_sem):
    offsets, _, _ = place(size, width)
    wave_copy = pltpu.make_async_copy(wave_hbm.at[0], wave_ref, wave_sem)
    own = fetch(left_hbm, right_hbm, left_own, right_own, sems, [(0, 2), (offsets[0], width)])
    wave_copy.start()
    later = fetch(left_hbm, right_hbm, left_far, right_far, far_sems, [(offsets[1], width)])
    later += fetch(left_hbm, right_hbm, left_row, right_row, row_sems, [(o, width) for o in offsets[2 : 2 + rows]])
    u = self_ref[...].astype(jnp.float32)
    lines = lax.broadcasted_iota(jnp.int32, (8, 128), 0)
    sums = jnp.where(lines == 1, total(u * u), 0.0)
    finish(own[0])
    out_ref[0] = terms(self_ref[...], left_own, right_own, 0, 2)
    finish(own[1])
    out_ref[1] = terms(near_ref[...], left_own, right_own, 2, width)
    wave_copy.wait()
    held = jnp.where(live(facts_ref[...], wave_ref.shape), wave_ref[...], 0.0)
    sums_ref[...] = jnp.where(lines == 0, total(held * held), sums)
    for pair in later:
        finish(pair)


def far_kernel(size, width, left_ref, right_ref, far_ref, out_ref):
    _, _, there = place(size, width)
    out_ref[...] = terms(only(there[0], far_ref[...]), left_ref, right_ref, 0, width)


def first_kernel(size, width, rows, *refs):
    near_part_ref, far_part_ref, facts_ref, sums_ref, u_ref, left_ref, right_ref = refs[:7]
    row_refs, (out_ref, w_ref, sums_out_ref, numbers_hbm, numbers_ref, sem) = refs[7 : 7 + rows], refs[7 + rows :]
    _, _, there = place(size, width)
    image = near_part_ref[0] + near_part_ref[1] + far_part_ref[...]
    for r, source in enumerate(row_refs):
        piece = terms(only(there[1 + r], source[...]), left_ref, right_ref, r * width, width)
        out_ref[r] = piece
        image = image + piece
    image = jnp.where(live(facts_ref[...], image.shape), image, 0.0)
    u = u_ref[...].astype(jnp.float32)
    square = sums_ref[1:2, 0:1]
    cross = total(u * image)
    rho = jnp.where(square > 0.0, cross / square, 0.0)
    w_ref[...] = (image - rho * u).astype(jnp.bfloat16)
    lines = lax.broadcasted_iota(jnp.int32, (8, 128), 0)
    sums = jnp.where(lines == 2, cross, jnp.where(lines == 4, rho, sums_ref[...]))
    sums_out_ref[...] = sums

    @pl.when(even_row())
    def _():
        write_numbers(sums, w_ref, numbers_hbm, numbers_ref, sem)


def even_row():
    return lax.rem(lax.div(lax.axis_index("sector"), QD), 2) == 0


def write_numbers(sums, w_ref, numbers_hbm, numbers_ref, sem):
    w = w_ref[...].astype(jnp.float32)
    values = [sums[n : n + 1, 0:1] for n in range(5)]
    values[3] = total(w * w)
    lane = lax.broadcasted_iota(jnp.int32, (1, 128), 1)
    numbers = jnp.zeros((1, 128), jnp.float32)
    for n, value in enumerate(values):
        numbers = jnp.where(lane == n, value, numbers)
    for n in range(numbers_ref.shape[0]):
        numbers_ref[n] = numbers
    copy = pltpu.make_async_copy(numbers_ref, numbers_hbm, sem)
    copy.start()
    copy.wait()


def numbers_kernel(held_hbm, sums_ref, w_ref, numbers_hbm, numbers_ref, sem):
    @pl.when(jnp.logical_not(even_row()))
    def _():
        write_numbers(sums_ref[...], w_ref, numbers_hbm, numbers_ref, sem)


def image_kernel(size, width, rows, *refs):
    row_refs, refs = refs[:rows], refs[rows:]
    far_ref, near_ref, self_ref, left_row, right_row, left_hbm, right_hbm, out_ref, left_own, right_own, sems = refs
    _, _, there = place(size, width)
    own = fetch(left_hbm, right_hbm, left_own, right_own, sems, [(0, 2 + width), (2 + width, width)])
    image = None
    for r, source in enumerate(row_refs):
        piece = terms(only(there[1 + r], source[...]), left_row, right_row, r * width, width)
        image = piece if image is None else image + piece
    odd = lax.rem(lax.axis_index("sector"), 2) == 1
    near, far = near_ref[...], only(there[0], far_ref[...])
    finish(own[0])
    image = image + terms(self_ref[...], left_own, right_own, 0, 2)
    image = image + terms(jnp.where(odd, near, far), left_own, right_own, 2, width)
    finish(own[1])
    out_ref[...] = image + terms(jnp.where(odd, far, near), left_own, right_own, 2 + width, width)


def second_kernel(size, width, rows, cells, facts_ref, stats_ref, hw_ref, near_part_ref, far_part_ref, row_part_ref,
                  first_hbm, second_hbm, first_ref, second_ref, sems):
    _, partners, _ = place(size, width)
    facts = facts_ref[...]
    stats = stats_ref[:, 0, :]
    sums = jnp.sum(stats, axis=0, keepdims=True)
    start, square, cross, inner = (sums[:, i : i + 1] for i in range(4))
    scale = lax.rsqrt(start / cells + 1e-06) * (1.0 / SCALE)
    parts = [near_part_ref[0], near_part_ref[1], far_part_ref[...]] + [row_part_ref[r] for r in range(rows)]
    cell = live(facts, parts[0].shape)
    first_ref[...] = jnp.where(cell, sum(parts[1:], parts[0]), 0.0) * scale
    first_copy = pltpu.make_async_copy(first_ref, first_hbm.at[0], sems.at[0])
    first_copy.start()
    rho = cross / square
    gap = stats[:, 4:5] - rho
    residual = inner + jnp.sum(stats[:, 1:2] * gap * gap, axis=0, keepdims=True)
    second_scale = scale * lax.rsqrt(scale * scale * (residual / cells) + 1e-06)
    image = hw_ref[...]
    for n, part in enumerate(parts):
        image = image + (stats_ref[partners[n], :, 4:5] - rho) * part
    second_ref[...] = jnp.where(cell, image, 0.0) * second_scale
    second_copy = pltpu.make_async_copy(second_ref, second_hbm.at[0], sems.at[1])
    second_copy.start()
    first_copy.wait()
    second_copy.wait()


def body(wavefunction, sector_dims, left_env, right_env):
    size = lax.axis_size("sector")
    block = wavefunction.shape[1]
    square = (block, block)
    width = (right_env.shape[1] - 2) // 4
    near, row_pairs = swap_pairs(size)
    rows = len(row_pairs)
    cells = float(size * block * block)
    few, every, side, last = ((n,) + square for n in (2 + width, 2 + 2 * width, width, rows * width))
    f32, bf16 = jnp.float32, jnp.bfloat16
    dma = pltpu.SemaphoreType.DMA

    u, far_u, facts = call(
        start_kernel, (pltpu.VMEM(square, bf16),) * 2 + (pltpu.VMEM((8, 128), f32),), [HB, HB], (VM,) * 3,
        [pltpu.VMEM(square, f32), pltpu.SMEM((1, 2), jnp.int32), dma((QUARTERS + 1,))],
    )(hbm(wavefunction), hbm(sector_dims))

    left_env, right_env = hbm(left_env), hbm(right_env)
    u, facts = vmem(u), vmem(facts)
    row_u = [vmem(swap(u, "sector", p)) for p in row_pairs]
    near_u = vmem(swap(u, "sector", near))
    far_u = vmem(far_swap(after(far_u, near_u)))
    near_part, sums, left_far, right_far, left_row, right_row = call(
        functools.partial(near_kernel, size, width, rows),
        (pltpu.VMEM((2,) + square, f32), pltpu.VMEM((8, 128), f32)) + (pltpu.VMEM(side, bf16),) * 2 + (pltpu.VMEM(last, bf16),) * 2,
        [HB] * 3 + [VM] * 3, (VM,) * 6,
        [pltpu.VMEM(few, bf16)] * 2 + [pltpu.VMEM(square, f32), dma((2, 2)), dma((1, 2)), dma((rows, 2)), dma], LONG,
    )(left_env, right_env, hbm(wavefunction), facts, u, near_u)
    near_part, left_row, right_row = vmem(near_part), vmem(left_row), vmem(right_row)
    far_part = vmem(call(
        functools.partial(far_kernel, size, width), pltpu.VMEM(square, f32), [VM] * 3, VM, cost=LONG,
    )(vmem(left_far), vmem(right_far), far_u))
    table = pltpu.HBM((size, 1, 128), f32)
    table_scratch = [pltpu.VMEM((size, 1, 128), f32), dma]
    row_part, w, sums, stats = call(
        functools.partial(first_kernel, size, width, rows),
        (pltpu.VMEM((rows,) + square, f32), pltpu.VMEM(square, bf16), pltpu.VMEM((8, 128), f32), table),
        [VM] * (7 + rows), (VM,) * 3 + (HB,), table_scratch,
    )(near_part, far_part, facts, vmem(sums), u, left_row, right_row, *row_u)

    w = vmem(w)
    row_w = [vmem(swap(w, "sector", p)) for p in row_pairs]
    near_w = vmem(swap(w, "sector", near))
    far_w = vmem(far_swap(w))
    stats = call(numbers_kernel, table, [HB] + [VM] * 2, HB, table_scratch, aliases={0: 0})(hbm(stats), vmem(sums), w)
    stats = lax.all_to_all(stats, "sector", 0, 0, tiled=True)
    hw = call(
        functools.partial(image_kernel, size, width, rows), pltpu.VMEM(square, f32), [VM] * (5 + rows) + [HB] * 2, VM,
        [pltpu.VMEM(every, bf16)] * 2 + [dma((2, 2))],
    )(*row_w, far_w, near_w, w, left_row, right_row, left_env, right_env)
    return call(
        functools.partial(second_kernel, size, width, rows, cells),
        (jax.ShapeDtypeStruct((1,) + square, f32),) * 2, [VM] * 6, (HB, HB),
        [pltpu.VMEM(square, f32)] * 2 + [dma((2,))],
    )(facts, stats, vmem(hw), near_part, far_part, vmem(row_part))


def solution(mesh):
    placed = (
        P(("groups", "sector"), None, None),
        P(("groups", "sector"), None),
        P(("groups", "sector"), None, None, None),
        P(("groups", "sector"), None, None, None),
    )
    return jax.shard_map(
        body,
        mesh=mesh,
        in_specs=placed,
        out_specs=(P(("groups", "sector"), None, None), P(("groups", "sector"), None, None)),
        check_vma=False,
    )
```

```python
import functools

import jax
import jax.numpy as jnp
from jax import lax
from jax.experimental import pallas as pl
from jax.experimental.pallas import tpu as pltpu
from jax.sharding import PartitionSpec as P

QD = 8
SCALE = 1024.0
QUARTERS = 4
NT = (((1,), (1,)), ((), ()))
VM = pl.BlockSpec(memory_space=pltpu.VMEM)
HB = pl.BlockSpec(memory_space=pltpu.HBM)
AN = pl.BlockSpec(memory_space=pl.ANY)
COST = pl.CostEstimate(flops=1, bytes_accessed=1, transcendentals=0)
LONG = pl.CostEstimate(flops=4000000000, bytes_accessed=1, transcendentals=0)
PARAMS = pltpu.CompilerParams(vmem_limit_bytes=16 * 1024 * 1024)


def vmem(x):
    return pltpu.with_memory_space_constraint(x, pltpu.VMEM)


def hbm(x):
    return pltpu.with_memory_space_constraint(x, pltpu.HBM)


def call(kernel, out_shape, in_specs, out_specs, scratch=(), cost=COST, aliases={}):
    return pl.pallas_call(
        kernel, out_shape=out_shape, in_specs=in_specs, out_specs=out_specs, scratch_shapes=list(scratch),
        compiler_params=PARAMS, cost_estimate=cost, input_output_aliases=aliases,
    )


def swap(x, axis, pairs):
    to = {a: b for p in pairs for a, b in (p, p[::-1])}
    return lax.ppermute(x, axis, [(s, to.get(s, s)) for s in range(lax.axis_size(axis))])


def swap_pairs(size):
    rows = size // QD
    near = [(s, s + 1) for s in range(0, size, 2)]
    row_even = [(s, s + QD) for r in range(0, rows - 1, 2) for s in range(r * QD, r * QD + QD)]
    row_odd = [(s, s + QD) for r in range(1, rows - 1, 2) for s in range(r * QD, r * QD + QD)]
    return near, [p for p in (row_even, row_odd) if p]


def far_swap(x):
    groups, size = lax.axis_size("groups"), lax.axis_size("sector")
    pairs = []
    for g in range(groups):
        for s in range(size):
            if s % QD == 0 or s % QD == QD - 1:
                to, partner = (g ^ 1 if g ^ 1 < groups else g), s
            else:
                to, partner = g, s + 1 if s % 2 else s - 1
            pairs.append((g * size + s, to * size + partner))
    return lax.ppermute(x, ("groups", "sector"), pairs)


def place(size, width):
    me = lax.axis_index("sector")
    column = lax.rem(me, QD)
    odd = lax.rem(me, 2) == 1
    row_odd = lax.rem(lax.div(me, QD), 2) == 1
    low, high, down, up = 2, 2 + width, 2 + 2 * width, 2 + 3 * width
    offsets = [jnp.where(odd, low, high), jnp.where(odd, high, low),
               jnp.where(row_odd, down, up), jnp.where(row_odd, up, down)]
    partners = [jnp.where(odd, me - 1, me + 1), jnp.where(odd, me + 1, me - 1),
                jnp.where(row_odd, me - QD, me + QD), jnp.where(row_odd, me + QD, me - QD)]
    there = [(column != 0) & (column != QD - 1),
             True if size // QD % 2 == 0 else (partners[2] >= 0) & (partners[2] < size),
             (partners[3] >= 0) & (partners[3] < size)]
    partners = [me] + [jnp.clip(p, 0, size - 1) for p in partners]
    return offsets, partners, there


def live(facts, shape):
    row_ok = lax.broadcasted_iota(jnp.int32, shape, 0).astype(jnp.float32) < facts[1:2, 0:1]
    col_ok = lax.broadcasted_iota(jnp.int32, shape, 1).astype(jnp.float32) < facts[2:3, 0:1]
    return row_ok & col_ok


def total(x):
    return jnp.sum(jnp.sum(x, axis=0, keepdims=True), axis=1, keepdims=True)


def only(there, block):
    return block if there is True else jnp.where(there, block, jnp.zeros_like(block))


def terms(src, left_ref, right_ref, first, count):
    size = src.shape[0]
    right = right_ref[pl.ds(first, count)].reshape(count * size, size)
    partial_t = lax.dot_general(right, src, NT, preferred_element_type=jnp.float32).astype(jnp.bfloat16)
    image = None
    for k in range(count):
        piece = lax.dot_general(
            left_ref[first + k], partial_t[k * size : (k + 1) * size], NT, preferred_element_type=jnp.float32
        )
        image = piece if image is None else image + piece
    return image


def fetch(left_hbm, right_hbm, left_ref, right_ref, sems, spans):
    copies = []
    at = 0
    for n, (offset, count) in enumerate(spans):
        pair = [
            pltpu.make_async_copy(source.at[0, pl.ds(offset, count)], target.at[pl.ds(at, count)], sems.at[n, e])
            for e, (source, target) in enumerate(((right_hbm, right_ref), (left_hbm, left_ref)))
        ]
        for copy in pair:
            copy.start()
        copies.append(pair)
        at += count
    return copies


def finish(copies):
    for copy in copies:
        copy.wait()


def start_kernel(wave_hbm, dims_hbm, *refs):
    u_refs, (facts_ref, wave_ref, dims_ref, sems) = refs[:2], refs[2:]
    size = wave_ref.shape[0]
    step = size // QUARTERS
    dims_copy = pltpu.make_async_copy(dims_hbm, dims_ref, sems.at[QUARTERS])
    dims_copy.start()
    copies = [
        pltpu.make_async_copy(wave_hbm.at[0, pl.ds(n * step, step)], wave_ref.at[pl.ds(n * step, step)], sems.at[n])
        for n in range(QUARTERS)
    ]
    for copy in copies:
        copy.start()
    dims_copy.wait()
    row_count, col_count = dims_ref[0, 0], dims_ref[0, 1]
    lines = lax.broadcasted_iota(jnp.int32, (8, 128), 0)
    facts_ref[...] = jnp.where(lines == 1, row_count, jnp.where(lines == 2, col_count, 0)).astype(jnp.float32)
    col_ok = lax.broadcasted_iota(jnp.int32, (step, size), 1) < col_count
    row = lax.broadcasted_iota(jnp.int32, (step, size), 0)
    for n, copy in enumerate(copies):
        copy.wait()
        rows = pl.ds(n * step, step)
        held = jnp.where((row < row_count - n * step) & col_ok, wave_ref[rows], 0.0)
        block = (held * SCALE).astype(jnp.bfloat16)
        for ref in u_refs:
            ref[rows] = block


def pass_kernel(*refs):
    pass


def after(held, first):
    return call(pass_kernel, pltpu.VMEM(held.shape, held.dtype), [AN] * 2, AN, aliases={0: 0})(vmem(held), first)


def near_kernel(size, width, rows, left_hbm, right_hbm, wave_hbm, facts_ref, self_ref, near_ref, out_ref, sums_ref,
                left_far, right_far, left_row, right_row, left_own, right_own, wave_ref, sems, far_sems, row_sems, wave_sem):
    offsets, _, _ = place(size, width)
    wave_copy = pltpu.make_async_copy(wave_hbm.at[0], wave_ref, wave_sem)
    own = fetch(left_hbm, right_hbm, left_own, right_own, sems, [(0, 2), (offsets[0], width)])
    wave_copy.start()
    later = fetch(left_hbm, right_hbm, left_far, right_far, far_sems, [(offsets[1], width)])
    later += fetch(left_hbm, right_hbm, left_row, right_row, row_sems, [(o, width) for o in offsets[2 : 2 + rows]])
    u = self_ref[...].astype(jnp.float32)
    lines = lax.broadcasted_iota(jnp.int32, (8, 128), 0)
    sums = jnp.where(lines == 1, total(u * u), 0.0)
    finish(own[0])
    out_ref[0] = terms(self_ref[...], left_own, right_own, 0, 2)
    finish(own[1])
    out_ref[1] = terms(near_ref[...], left_own, right_own, 2, width)
    wave_copy.wait()
    held = jnp.where(live(facts_ref[...], wave_ref.shape), wave_ref[...], 0.0)
    sums_ref[...] = jnp.where(lines == 0, total(held * held), sums)
    for pair in later:
        finish(pair)


def far_kernel(size, width, left_ref, right_ref, near_part_ref, u_ref, sums_ref, far_ref, out_ref, sums_out_ref):
    _, _, there = place(size, width)
    part = terms(only(there[0], far_ref[...]), left_ref, right_ref, 0, width)
    out_ref[...] = part
    sums = sums_ref[...]
    square = sums[1:2, 0:1]
    cross = total(u_ref[...].astype(jnp.float32) * (near_part_ref[0] + near_part_ref[1] + part))
    lines = lax.broadcasted_iota(jnp.int32, (8, 128), 0)
    sums_out_ref[...] = jnp.where(lines == 2, jnp.where(square > 0.0, cross / square, 0.0), sums)


def first_kernel(size, width, rows, *refs):
    near_part_ref, far_part_ref, facts_ref, sums_ref, u_ref, left_ref, right_ref = refs[:7]
    row_refs, (out_ref, w_ref, numbers_hbm, numbers_ref, sem) = refs[7 : 7 + rows], refs[7 + rows :]
    _, _, there = place(size, width)
    image = near_part_ref[0] + near_part_ref[1] + far_part_ref[...]
    for r, source in enumerate(row_refs):
        piece = terms(only(there[1 + r], source[...]), left_ref, right_ref, r * width, width)
        out_ref[r] = piece
        image = image + piece
    u = u_ref[...].astype(jnp.float32)
    start, square, guess = (sums_ref[n : n + 1, 0:1] for n in range(3))
    rough = jnp.where(live(facts_ref[...], image.shape), image - guess * u, 0.0)
    along, inner = total(u * rough), total(rough * rough)
    shift = jnp.where(square > 0.0, along / square, 0.0)
    rho = guess + shift
    lane = lax.broadcasted_iota(jnp.int32, (1, 128), 1)
    numbers = jnp.zeros((1, 128), jnp.float32)
    for n, value in enumerate((start, square, rho * square, jnp.maximum(inner - shift * along, 0.0), rho)):
        numbers = jnp.where(lane == n, value, numbers)
    for n in range(numbers_ref.shape[0]):
        numbers_ref[n] = numbers
    copy = pltpu.make_async_copy(numbers_ref, numbers_hbm, sem)
    copy.start()
    w_ref[...] = (rough - shift * u).astype(jnp.bfloat16)
    copy.wait()


def image_kernel(size, width, rows, *refs):
    row_refs, refs = refs[:rows], refs[rows:]
    far_ref, near_ref, self_ref, left_row, right_row, left_hbm, right_hbm, out_ref, left_own, right_own, sems = refs
    _, _, there = place(size, width)
    own = fetch(left_hbm, right_hbm, left_own, right_own, sems, [(0, 2 + width), (2 + width, width)])
    image = None
    for r, source in enumerate(row_refs):
        piece = terms(only(there[1 + r], source[...]), left_row, right_row, r * width, width)
        image = piece if image is None else image + piece
    odd = lax.rem(lax.axis_index("sector"), 2) == 1
    near, far = near_ref[...], only(there[0], far_ref[...])
    finish(own[0])
    image = image + terms(self_ref[...], left_own, right_own, 0, 2)
    image = image + terms(jnp.where(odd, near, far), left_own, right_own, 2, width)
    finish(own[1])
    out_ref[...] = image + terms(jnp.where(odd, far, near), left_own, right_own, 2 + width, width)


def second_kernel(size, width, rows, cells, facts_ref, stats_ref, hw_ref, near_part_ref, far_part_ref, row_part_ref,
                  first_hbm, second_hbm, first_ref, second_ref, sems):
    _, partners, _ = place(size, width)
    facts = facts_ref[...]
    stats = stats_ref[:, 0, :]
    sums = jnp.sum(stats, axis=0, keepdims=True)
    start, square, cross, inner = (sums[:, i : i + 1] for i in range(4))
    scale = lax.rsqrt(start / cells + 1e-06) * (1.0 / SCALE)
    parts = [near_part_ref[0], near_part_ref[1], far_part_ref[...]] + [row_part_ref[r] for r in range(rows)]
    cell = live(facts, parts[0].shape)
    first_ref[...] = jnp.where(cell, sum(parts[1:], parts[0]), 0.0) * scale
    first_copy = pltpu.make_async_copy(first_ref, first_hbm.at[0], sems.at[0])
    first_copy.start()
    rho = cross / square
    gap = stats[:, 4:5] - rho
    residual = inner + jnp.sum(stats[:, 1:2] * gap * gap, axis=0, keepdims=True)
    second_scale = scale * lax.rsqrt(scale * scale * (residual / cells) + 1e-06)
    image = hw_ref[...]
    for n, part in enumerate(parts):
        image = image + (stats_ref[partners[n], :, 4:5] - rho) * part
    second_ref[...] = jnp.where(cell, image, 0.0) * second_scale
    second_copy = pltpu.make_async_copy(second_ref, second_hbm.at[0], sems.at[1])
    second_copy.start()
    first_copy.wait()
    second_copy.wait()


def body(wavefunction, sector_dims, left_env, right_env):
    size = lax.axis_size("sector")
    block = wavefunction.shape[1]
    square = (block, block)
    width = (right_env.shape[1] - 2) // 4
    near, row_pairs = swap_pairs(size)
    rows = len(row_pairs)
    cells = float(size * block * block)
    few, every, side, last = ((n,) + square for n in (2 + width, 2 + 2 * width, width, rows * width))
    f32, bf16 = jnp.float32, jnp.bfloat16
    dma = pltpu.SemaphoreType.DMA

    u, far_u, facts = call(
        start_kernel, (pltpu.VMEM(square, bf16),) * 2 + (pltpu.VMEM((8, 128), f32),), [HB, HB], (VM,) * 3,
        [pltpu.VMEM(square, f32), pltpu.SMEM((1, 2), jnp.int32), dma((QUARTERS + 1,))],
    )(hbm(wavefunction), hbm(sector_dims))

    left_env, right_env = hbm(left_env), hbm(right_env)
    u, facts = vmem(u), vmem(facts)
    row_u = [vmem(swap(u, "sector", p)) for p in row_pairs]
    near_u = vmem(swap(u, "sector", near))
    far_u = vmem(far_swap(after(far_u, near_u)))
    near_part, sums, left_far, right_far, left_row, right_row = call(
        functools.partial(near_kernel, size, width, rows),
        (pltpu.VMEM((2,) + square, f32), pltpu.VMEM((8, 128), f32)) + (pltpu.VMEM(side, bf16),) * 2 + (pltpu.VMEM(last, bf16),) * 2,
        [HB] * 3 + [VM] * 3, (VM,) * 6,
        [pltpu.VMEM(few, bf16)] * 2 + [pltpu.VMEM(square, f32), dma((2, 2)), dma((1, 2)), dma((rows, 2)), dma], LONG,
    )(left_env, right_env, hbm(wavefunction), facts, u, near_u)
    near_part, left_row, right_row = vmem(near_part), vmem(left_row), vmem(right_row)
    far_part, sums = call(
        functools.partial(far_kernel, size, width), (pltpu.VMEM(square, f32), pltpu.VMEM((8, 128), f32)),
        [VM] * 6, (VM,) * 2, cost=LONG,
    )(vmem(left_far), vmem(right_far), near_part, u, vmem(sums), far_u)
    far_part = vmem(far_part)
    row_part, w, stats = call(
        functools.partial(first_kernel, size, width, rows),
        (pltpu.VMEM((rows,) + square, f32), pltpu.VMEM(square, bf16), pltpu.HBM((size, 1, 128), f32)),
        [VM] * (7 + rows), (VM, VM, HB), [pltpu.VMEM((size, 1, 128), f32), dma],
    )(near_part, far_part, facts, vmem(sums), u, left_row, right_row, *row_u)

    w = vmem(w)
    row_w = [vmem(swap(w, "sector", p)) for p in row_pairs]
    near_w = vmem(swap(w, "sector", near))
    far_w = vmem(far_swap(w))
    stats = lax.all_to_all(stats, "sector", 0, 0, tiled=True)
    hw = call(
        functools.partial(image_kernel, size, width, rows), pltpu.VMEM(square, f32), [VM] * (5 + rows) + [HB] * 2, VM,
        [pltpu.VMEM(every, bf16)] * 2 + [dma((2, 2))],
    )(*row_w, far_w, near_w, w, left_row, right_row, left_env, right_env)
    return call(
        functools.partial(second_kernel, size, width, rows, cells),
        (jax.ShapeDtypeStruct((1,) + square, f32),) * 2, [VM] * 6, (HB, HB),
        [pltpu.VMEM(square, f32)] * 2 + [dma((2,))],
    )(facts, stats, vmem(hw), near_part, far_part, vmem(row_part))


def solution(mesh):
    placed = (
        P(("groups", "sector"), None, None),
        P(("groups", "sector"), None),
        P(("groups", "sector"), None, None, None),
        P(("groups", "sector"), None, None, None),
    )
    return jax.shard_map(
        body,
        mesh=mesh,
        in_specs=placed,
        out_specs=(P(("groups", "sector"), None, None), P(("groups", "sector"), None, None)),
        check_vma=False,
    )
```

```python
import functools

import jax
import jax.numpy as jnp
from jax import lax
from jax.experimental import pallas as pl
from jax.experimental.pallas import tpu as pltpu
from jax.sharding import PartitionSpec as P

QD = 8
SCALE = 1024.0
QUARTERS = 4
NT = (((1,), (1,)), ((), ()))
VM = pl.BlockSpec(memory_space=pltpu.VMEM)
HB = pl.BlockSpec(memory_space=pltpu.HBM)
AN = pl.BlockSpec(memory_space=pl.ANY)
COST = pl.CostEstimate(flops=1, bytes_accessed=1, transcendentals=0)
LONG = pl.CostEstimate(flops=4000000000, bytes_accessed=1, transcendentals=0)
PARAMS = pltpu.CompilerParams(vmem_limit_bytes=16 * 1024 * 1024)


def vmem(x):
    return pltpu.with_memory_space_constraint(x, pltpu.VMEM)


def hbm(x):
    return pltpu.with_memory_space_constraint(x, pltpu.HBM)


def call(kernel, out_shape, in_specs, out_specs, scratch=(), cost=COST, aliases={}):
    return pl.pallas_call(
        kernel, out_shape=out_shape, in_specs=in_specs, out_specs=out_specs, scratch_shapes=list(scratch),
        compiler_params=PARAMS, cost_estimate=cost, input_output_aliases=aliases,
    )


def swap(x, axis, pairs):
    to = {a: b for p in pairs for a, b in (p, p[::-1])}
    return lax.ppermute(x, axis, [(s, to.get(s, s)) for s in range(lax.axis_size(axis))])


def swap_pairs(size):
    rows = size // QD
    near = [(s, s + 1) for s in range(0, size, 2)]
    row_even = [(s, s + QD) for r in range(0, rows - 1, 2) for s in range(r * QD, r * QD + QD)]
    row_odd = [(s, s + QD) for r in range(1, rows - 1, 2) for s in range(r * QD, r * QD + QD)]
    return near, [p for p in (row_even, row_odd) if p]


def far_swap(x):
    groups, size = lax.axis_size("groups"), lax.axis_size("sector")
    pairs = []
    for g in range(groups):
        for s in range(size):
            if s % QD == 0 or s % QD == QD - 1:
                to, partner = (g ^ 1 if g ^ 1 < groups else g), s
            else:
                to, partner = g, s + 1 if s % 2 else s - 1
            pairs.append((g * size + s, to * size + partner))
    return lax.ppermute(x, ("groups", "sector"), pairs)


def place(size, width):
    me = lax.axis_index("sector")
    column = lax.rem(me, QD)
    odd = lax.rem(me, 2) == 1
    row_odd = lax.rem(lax.div(me, QD), 2) == 1
    low, high, down, up = 2, 2 + width, 2 + 2 * width, 2 + 3 * width
    offsets = [jnp.where(odd, low, high), jnp.where(odd, high, low),
               jnp.where(row_odd, down, up), jnp.where(row_odd, up, down)]
    partners = [jnp.where(odd, me - 1, me + 1), jnp.where(odd, me + 1, me - 1),
                jnp.where(row_odd, me - QD, me + QD), jnp.where(row_odd, me + QD, me - QD)]
    there = [(column != 0) & (column != QD - 1),
             True if size // QD % 2 == 0 else (partners[2] >= 0) & (partners[2] < size),
             (partners[3] >= 0) & (partners[3] < size)]
    partners = [me] + [jnp.clip(p, 0, size - 1) for p in partners]
    return offsets, partners, there


def live(facts, shape):
    row_ok = lax.broadcasted_iota(jnp.int32, shape, 0).astype(jnp.float32) < facts[1:2, 0:1]
    col_ok = lax.broadcasted_iota(jnp.int32, shape, 1).astype(jnp.float32) < facts[2:3, 0:1]
    return row_ok & col_ok


def total(x):
    return jnp.sum(jnp.sum(x, axis=0, keepdims=True), axis=1, keepdims=True)


def only(there, block):
    return block if there is True else jnp.where(there, block, jnp.zeros_like(block))


def terms(src, left_ref, right_ref, first, count):
    size = src.shape[0]
    right = right_ref[pl.ds(first, count)].reshape(count * size, size)
    partial_t = lax.dot_general(right, src, NT, preferred_element_type=jnp.float32).astype(jnp.bfloat16)
    left = jnp.concatenate([left_ref[first + k] for k in range(count)], axis=1)
    partial_t = jnp.concatenate([partial_t[k * size : (k + 1) * size] for k in range(count)], axis=1)
    return lax.dot_general(left, partial_t, NT, preferred_element_type=jnp.float32)


def fetch(left_hbm, right_hbm, left_ref, right_ref, sems, spans):
    copies = []
    at = 0
    for n, (offset, count) in enumerate(spans):
        pair = [
            pltpu.make_async_copy(source.at[0, pl.ds(offset, count)], target.at[pl.ds(at, count)], sems.at[n, e])
            for e, (source, target) in enumerate(((right_hbm, right_ref), (left_hbm, left_ref)))
        ]
        for copy in pair:
            copy.start()
        copies.append(pair)
        at += count
    return copies


def finish(copies):
    for copy in copies:
        copy.wait()


def start_kernel(wave_hbm, dims_hbm, *refs):
    u_refs, (facts_ref, wave_ref, dims_ref, sems) = refs[:2], refs[2:]
    size = wave_ref.shape[0]
    step = size // QUARTERS
    dims_copy = pltpu.make_async_copy(dims_hbm, dims_ref, sems.at[QUARTERS])
    dims_copy.start()
    copies = [
        pltpu.make_async_copy(wave_hbm.at[0, pl.ds(n * step, step)], wave_ref.at[pl.ds(n * step, step)], sems.at[n])
        for n in range(QUARTERS)
    ]
    for copy in copies:
        copy.start()
    dims_copy.wait()
    row_count, col_count = dims_ref[0, 0], dims_ref[0, 1]
    lines = lax.broadcasted_iota(jnp.int32, (8, 128), 0)
    facts_ref[...] = jnp.where(lines == 1, row_count, jnp.where(lines == 2, col_count, 0)).astype(jnp.float32)
    col_ok = lax.broadcasted_iota(jnp.int32, (step, size), 1) < col_count
    row = lax.broadcasted_iota(jnp.int32, (step, size), 0)
    for n, copy in enumerate(copies):
        copy.wait()
        rows = pl.ds(n * step, step)
        held = jnp.where((row < row_count - n * step) & col_ok, wave_ref[rows], 0.0)
        block = (held * SCALE).astype(jnp.bfloat16)
        for ref in u_refs:
            ref[rows] = block


def pass_kernel(*refs):
    pass


def after(held, first):
    return call(pass_kernel, pltpu.VMEM(held.shape, held.dtype), [AN] * 2, AN, aliases={0: 0})(vmem(held), first)


def near_kernel(size, width, rows, left_hbm, right_hbm, wave_hbm, facts_ref, self_ref, near_ref, out_ref, sums_ref,
                left_far, right_far, left_row, right_row, left_own, right_own, wave_ref, sems, far_sems, row_sems, wave_sem):
    offsets, _, _ = place(size, width)
    wave_copy = pltpu.make_async_copy(wave_hbm.at[0], wave_ref, wave_sem)
    own = fetch(left_hbm, right_hbm, left_own, right_own, sems, [(0, 2), (offsets[0], width)])
    wave_copy.start()
    later = fetch(left_hbm, right_hbm, left_far, right_far, far_sems, [(offsets[1], width)])
    later += fetch(left_hbm, right_hbm, left_row, right_row, row_sems, [(o, width) for o in offsets[2 : 2 + rows]])
    u = self_ref[...].astype(jnp.float32)
    lines = lax.broadcasted_iota(jnp.int32, (8, 128), 0)
    sums = jnp.where(lines == 1, total(u * u), 0.0)
    finish(own[0])
    out_ref[0] = terms(self_ref[...], left_own, right_own, 0, 2)
    finish(own[1])
    out_ref[1] = terms(near_ref[...], left_own, right_own, 2, width)
    wave_copy.wait()
    held = jnp.where(live(facts_ref[...], wave_ref.shape), wave_ref[...], 0.0)
    sums_ref[...] = jnp.where(lines == 0, total(held * held), sums)
    for pair in later:
        finish(pair)


def far_kernel(size, width, left_ref, right_ref, far_ref, out_ref):
    _, _, there = place(size, width)
    out_ref[...] = terms(only(there[0], far_ref[...]), left_ref, right_ref, 0, width)


def first_kernel(size, width, rows, *refs):
    near_part_ref, far_part_ref, facts_ref, sums_ref, u_ref, left_ref, right_ref = refs[:7]
    row_refs, (out_ref, w_ref, stats_ref) = refs[7 : 7 + rows], refs[7 + rows :]
    _, _, there = place(size, width)
    image = near_part_ref[0] + near_part_ref[1] + far_part_ref[...]
    for r, source in enumerate(row_refs):
        piece = terms(only(there[1 + r], source[...]), left_ref, right_ref, r * width, width)
        out_ref[r] = piece
        image = image + piece
    image = jnp.where(live(facts_ref[...], image.shape), image, 0.0)
    u = u_ref[...].astype(jnp.float32)
    square = sums_ref[1:2, 0:1]
    cross = total(u * image)
    rho = jnp.where(square > 0.0, cross / square, 0.0)
    w = image - rho * u
    w_ref[...] = w.astype(jnp.bfloat16)
    lane = lax.broadcasted_iota(jnp.int32, (1, 128), 1)
    stats = jnp.zeros((1, 128), jnp.float32)
    for n, value in enumerate((sums_ref[0:1, 0:1], square, cross, total(w * w), rho)):
        stats = jnp.where(lane == n, value, stats)
    for n in range(stats_ref.shape[0]):
        stats_ref[n] = stats


def image_kernel(size, width, rows, *refs):
    row_refs, refs = refs[:rows], refs[rows:]
    far_ref, near_ref, self_ref, left_row, right_row, left_hbm, right_hbm, out_ref, left_own, right_own, sems = refs
    _, _, there = place(size, width)
    own = fetch(left_hbm, right_hbm, left_own, right_own, sems, [(0, 2 + width), (2 + width, width)])
    image = None
    for r, source in enumerate(row_refs):
        piece = terms(only(there[1 + r], source[...]), left_row, right_row, r * width, width)
        image = piece if image is None else image + piece
    odd = lax.rem(lax.axis_index("sector"), 2) == 1
    near, far = near_ref[...], only(there[0], far_ref[...])
    finish(own[0])
    image = image + terms(self_ref[...], left_own, right_own, 0, 2)
    image = image + terms(jnp.where(odd, near, far), left_own, right_own, 2, width)
    finish(own[1])
    out_ref[...] = image + terms(jnp.where(odd, far, near), left_own, right_own, 2 + width, width)


def second_kernel(size, width, rows, cells, facts_ref, stats_ref, hw_ref, near_part_ref, far_part_ref, row_part_ref,
                  first_hbm, second_hbm, first_ref, second_ref, sems):
    _, partners, _ = place(size, width)
    facts = facts_ref[...]
    stats = stats_ref[:, 0, :]
    sums = jnp.sum(stats, axis=0, keepdims=True)
    start, square, cross, inner = (sums[:, i : i + 1] for i in range(4))
    scale = lax.rsqrt(start / cells + 1e-06) * (1.0 / SCALE)
    parts = [near_part_ref[0], near_part_ref[1], far_part_ref[...]] + [row_part_ref[r] for r in range(rows)]
    cell = live(facts, parts[0].shape)
    first_ref[...] = jnp.where(cell, sum(parts[1:], parts[0]), 0.0) * scale
    first_copy = pltpu.make_async_copy(first_ref, first_hbm.at[0], sems.at[0])
    first_copy.start()
    rho = cross / square
    gap = stats[:, 4:5] - rho
    residual = inner + jnp.sum(stats[:, 1:2] * gap * gap, axis=0, keepdims=True)
    second_scale = scale * lax.rsqrt(scale * scale * (residual / cells) + 1e-06)
    image = hw_ref[...]
    for n, part in enumerate(parts):
        image = image + (stats_ref[partners[n], :, 4:5] - rho) * part
    second_ref[...] = jnp.where(cell, image, 0.0) * second_scale
    second_copy = pltpu.make_async_copy(second_ref, second_hbm.at[0], sems.at[1])
    second_copy.start()
    first_copy.wait()
    second_copy.wait()


def body(wavefunction, sector_dims, left_env, right_env):
    size = lax.axis_size("sector")
    block = wavefunction.shape[1]
    square = (block, block)
    width = (right_env.shape[1] - 2) // 4
    near, row_pairs = swap_pairs(size)
    rows = len(row_pairs)
    cells = float(size * block * block)
    few, every, side, last = ((n,) + square for n in (2 + width, 2 + 2 * width, width, rows * width))
    f32, bf16 = jnp.float32, jnp.bfloat16
    dma = pltpu.SemaphoreType.DMA

    u, far_u, facts = call(
        start_kernel, (pltpu.VMEM(square, bf16),) * 2 + (pltpu.VMEM((8, 128), f32),), [HB, HB], (VM,) * 3,
        [pltpu.VMEM(square, f32), pltpu.SMEM((1, 2), jnp.int32), dma((QUARTERS + 1,))],
    )(hbm(wavefunction), hbm(sector_dims))

    left_env, right_env = hbm(left_env), hbm(right_env)
    u, facts = vmem(u), vmem(facts)
    row_u = [vmem(swap(u, "sector", p)) for p in row_pairs]
    near_u = vmem(swap(u, "sector", near))
    far_u = vmem(far_swap(after(far_u, near_u)))
    near_part, sums, left_far, right_far, left_row, right_row = call(
        functools.partial(near_kernel, size, width, rows),
        (pltpu.VMEM((2,) + square, f32), pltpu.VMEM((8, 128), f32)) + (pltpu.VMEM(side, bf16),) * 2 + (pltpu.VMEM(last, bf16),) * 2,
        [HB] * 3 + [VM] * 3, (VM,) * 6,
        [pltpu.VMEM(few, bf16)] * 2 + [pltpu.VMEM(square, f32), dma((2, 2)), dma((1, 2)), dma((rows, 2)), dma], LONG,
    )(left_env, right_env, hbm(wavefunction), facts, u, near_u)
    near_part, left_row, right_row = vmem(near_part), vmem(left_row), vmem(right_row)
    far_part = vmem(call(
        functools.partial(far_kernel, size, width), pltpu.VMEM(square, f32), [VM] * 3, VM, cost=LONG,
    )(vmem(left_far), vmem(right_far), far_u))
    row_part, w, stats = call(
        functools.partial(first_kernel, size, width, rows),
        (pltpu.VMEM((rows,) + square, f32),) + (pltpu.VMEM(square, bf16), jax.ShapeDtypeStruct((size, 1, 128), f32)),
        [VM] * (7 + rows), (VM,) * 3,
    )(near_part, far_part, facts, vmem(sums), u, left_row, right_row, *row_u)

    w = vmem(w)
    row_w = [vmem(swap(w, "sector", p)) for p in row_pairs]
    near_w = vmem(swap(w, "sector", near))
    far_w = vmem(far_swap(w))
    stats = lax.all_to_all(stats, "sector", 0, 0, tiled=True)
    hw = call(
        functools.partial(image_kernel, size, width, rows), pltpu.VMEM(square, f32), [VM] * (5 + rows) + [HB] * 2, VM,
        [pltpu.VMEM(every, bf16)] * 2 + [dma((2, 2))],
    )(*row_w, far_w, near_w, w, left_row, right_row, left_env, right_env)
    return call(
        functools.partial(second_kernel, size, width, rows, cells),
        (jax.ShapeDtypeStruct((1,) + square, f32),) * 2, [VM] * 6, (HB, HB),
        [pltpu.VMEM(square, f32)] * 2 + [dma((2,))],
    )(facts, stats, vmem(hw), near_part, far_part, vmem(row_part))


def solution(mesh):
    placed = (
        P(("groups", "sector"), None, None),
        P(("groups", "sector"), None),
        P(("groups", "sector"), None, None, None),
        P(("groups", "sector"), None, None, None),
    )
    return jax.shard_map(
        body,
        mesh=mesh,
        in_specs=placed,
        out_specs=(P(("groups", "sector"), None, None), P(("groups", "sector"), None, None)),
        check_vma=False,
    )
```

```python
import functools

import jax
import jax.numpy as jnp
from jax import lax
from jax.experimental import pallas as pl
from jax.experimental.pallas import tpu as pltpu
from jax.sharding import PartitionSpec as P

QD = 8
SCALE = 1024.0
QUARTERS = 4
NT = (((1,), (1,)), ((), ()))
VM = pl.BlockSpec(memory_space=pltpu.VMEM)
HB = pl.BlockSpec(memory_space=pltpu.HBM)
AN = pl.BlockSpec(memory_space=pl.ANY)
COST = pl.CostEstimate(flops=1, bytes_accessed=1, transcendentals=0)
LONG = pl.CostEstimate(flops=4000000000, bytes_accessed=1, transcendentals=0)
PARAMS = pltpu.CompilerParams(vmem_limit_bytes=16 * 1024 * 1024)


def vmem(x):
    return pltpu.with_memory_space_constraint(x, pltpu.VMEM)


def hbm(x):
    return pltpu.with_memory_space_constraint(x, pltpu.HBM)


def call(kernel, out_shape, in_specs, out_specs, scratch=(), cost=COST, aliases={}):
    return pl.pallas_call(
        kernel, out_shape=out_shape, in_specs=in_specs, out_specs=out_specs, scratch_shapes=list(scratch),
        compiler_params=PARAMS, cost_estimate=cost, input_output_aliases=aliases,
    )


def swap(x, axis, pairs):
    to = {a: b for p in pairs for a, b in (p, p[::-1])}
    return lax.ppermute(x, axis, [(s, to.get(s, s)) for s in range(lax.axis_size(axis))])


def swap_pairs(size):
    rows = size // QD
    near = [(s, s + 1) for s in range(0, size, 2)]
    row_even = [(s, s + QD) for r in range(0, rows - 1, 2) for s in range(r * QD, r * QD + QD)]
    row_odd = [(s, s + QD) for r in range(1, rows - 1, 2) for s in range(r * QD, r * QD + QD)]
    return near, [p for p in (row_even, row_odd) if p]


def far_swap(x):
    groups, size = lax.axis_size("groups"), lax.axis_size("sector")
    pairs = []
    for g in range(groups):
        for s in range(size):
            if s % QD == 0 or s % QD == QD - 1:
                to, partner = (g ^ 1 if g ^ 1 < groups else g), s
            else:
                to, partner = g, s + 1 if s % 2 else s - 1
            pairs.append((g * size + s, to * size + partner))
    return lax.ppermute(x, ("groups", "sector"), pairs)


def place(size, width):
    me = lax.axis_index("sector")
    column = lax.rem(me, QD)
    odd = lax.rem(me, 2) == 1
    row_odd = lax.rem(lax.div(me, QD), 2) == 1
    low, high, down, up = 2, 2 + width, 2 + 2 * width, 2 + 3 * width
    offsets = [jnp.where(odd, low, high), jnp.where(odd, high, low),
               jnp.where(row_odd, down, up), jnp.where(row_odd, up, down)]
    partners = [jnp.where(odd, me - 1, me + 1), jnp.where(odd, me + 1, me - 1),
                jnp.where(row_odd, me - QD, me + QD), jnp.where(row_odd, me + QD, me - QD)]
    there = [(column != 0) & (column != QD - 1),
             True if size // QD % 2 == 0 else (partners[2] >= 0) & (partners[2] < size),
             (partners[3] >= 0) & (partners[3] < size)]
    partners = [me] + [jnp.clip(p, 0, size - 1) for p in partners]
    return offsets, partners, there


def live(facts, shape):
    row_ok = lax.broadcasted_iota(jnp.int32, shape, 0).astype(jnp.float32) < facts[1:2, 0:1]
    col_ok = lax.broadcasted_iota(jnp.int32, shape, 1).astype(jnp.float32) < facts[2:3, 0:1]
    return row_ok & col_ok


def total(x):
    return jnp.sum(jnp.sum(x, axis=0, keepdims=True), axis=1, keepdims=True)


def only(there, block):
    return block if there is True else jnp.where(there, block, jnp.zeros_like(block))


def terms(src, left_ref, right_ref, first, count):
    size = src.shape[0]
    right = right_ref[pl.ds(first, count)].reshape(count * size, size)
    partial_t = lax.dot_general(right, src, NT, preferred_element_type=jnp.float32).astype(jnp.bfloat16)
    left = jnp.concatenate([left_ref[first + k] for k in range(count)], axis=1)
    partial_t = jnp.concatenate([partial_t[k * size : (k + 1) * size] for k in range(count)], axis=1)
    return lax.dot_general(left, partial_t, NT, preferred_element_type=jnp.float32)


def fetch(left_hbm, right_hbm, left_ref, right_ref, sems, spans):
    copies = []
    at = 0
    for n, (offset, count) in enumerate(spans):
        pair = [
            pltpu.make_async_copy(source.at[0, pl.ds(offset, count)], target.at[pl.ds(at, count)], sems.at[n, e])
            for e, (source, target) in enumerate(((right_hbm, right_ref), (left_hbm, left_ref)))
        ]
        for copy in pair:
            copy.start()
        copies.append(pair)
        at += count
    return copies


def finish(copies):
    for copy in copies:
        copy.wait()


def start_kernel(wave_hbm, dims_hbm, *refs):
    u_refs, (facts_ref, wave_ref, dims_ref, sems) = refs[:2], refs[2:]
    size = wave_ref.shape[0]
    step = size // QUARTERS
    dims_copy = pltpu.make_async_copy(dims_hbm, dims_ref, sems.at[QUARTERS])
    dims_copy.start()
    copies = [
        pltpu.make_async_copy(wave_hbm.at[0, pl.ds(n * step, step)], wave_ref.at[pl.ds(n * step, step)], sems.at[n])
        for n in range(QUARTERS)
    ]
    for copy in copies:
        copy.start()
    dims_copy.wait()
    row_count, col_count = dims_ref[0, 0], dims_ref[0, 1]
    lines = lax.broadcasted_iota(jnp.int32, (8, 128), 0)
    facts_ref[...] = jnp.where(lines == 1, row_count, jnp.where(lines == 2, col_count, 0)).astype(jnp.float32)
    col_ok = lax.broadcasted_iota(jnp.int32, (step, size), 1) < col_count
    row = lax.broadcasted_iota(jnp.int32, (step, size), 0)
    for n, copy in enumerate(copies):
        copy.wait()
        rows = pl.ds(n * step, step)
        held = jnp.where((row < row_count - n * step) & col_ok, wave_ref[rows], 0.0)
        block = (held * SCALE).astype(jnp.bfloat16)
        for ref in u_refs:
            ref[rows] = block


def pass_kernel(*refs):
    pass


def after(held, first):
    return call(pass_kernel, pltpu.VMEM(held.shape, held.dtype), [AN] * 2, AN, aliases={0: 0})(vmem(held), first)


def near_kernel(size, width, rows, left_hbm, right_hbm, wave_hbm, facts_ref, self_ref, near_ref, out_ref, sums_ref,
                left_far, right_far, left_row, right_row, left_own, right_own, wave_ref, sems, far_sems, row_sems, wave_sem):
    offsets, _, _ = place(size, width)
    wave_copy = pltpu.make_async_copy(wave_hbm.at[0], wave_ref, wave_sem)
    own = fetch(left_hbm, right_hbm, left_own, right_own, sems, [(0, 2), (offsets[0], width)])
    wave_copy.start()
    later = fetch(left_hbm, right_hbm, left_far, right_far, far_sems, [(offsets[1], width)])
    later += fetch(left_hbm, right_hbm, left_row, right_row, row_sems, [(o, width) for o in offsets[2 : 2 + rows]])
    u = self_ref[...].astype(jnp.float32)
    lines = lax.broadcasted_iota(jnp.int32, (8, 128), 0)
    sums = jnp.where(lines == 1, total(u * u), 0.0)
    finish(own[0])
    out_ref[0] = terms(self_ref[...], left_own, right_own, 0, 2)
    finish(own[1])
    out_ref[1] = terms(near_ref[...], left_own, right_own, 2, width)
    wave_copy.wait()
    held = jnp.where(live(facts_ref[...], wave_ref.shape), wave_ref[...], 0.0)
    sums_ref[...] = jnp.where(lines == 0, total(held * held), sums)
    for pair in later:
        finish(pair)


def far_kernel(size, width, left_ref, right_ref, far_ref, out_ref):
    _, _, there = place(size, width)
    out_ref[...] = terms(only(there[0], far_ref[...]), left_ref, right_ref, 0, width)


def first_kernel(size, width, rows, *refs):
    near_part_ref, far_part_ref, facts_ref, sums_ref, u_ref, left_ref, right_ref = refs[:7]
    row_refs, (out_ref, w_ref, far_w_ref, sums_out_ref, numbers_hbm, numbers_ref, sem) = refs[7 : 7 + rows], refs[7 + rows :]
    _, _, there = place(size, width)
    image = near_part_ref[0] + near_part_ref[1] + far_part_ref[...]
    for r, source in enumerate(row_refs):
        piece = terms(only(there[1 + r], source[...]), left_ref, right_ref, r * width, width)
        out_ref[r] = piece
        image = image + piece
    image = jnp.where(live(facts_ref[...], image.shape), image, 0.0)
    u = u_ref[...].astype(jnp.float32)
    square = sums_ref[1:2, 0:1]
    cross = total(u * image)
    rho = jnp.where(square > 0.0, cross / square, 0.0)
    for ref in (w_ref, far_w_ref):
        ref[...] = (image - rho * u).astype(jnp.bfloat16)
    lines = lax.broadcasted_iota(jnp.int32, (8, 128), 0)
    sums = jnp.where(lines == 2, cross, jnp.where(lines == 4, rho, sums_ref[...]))
    sums_out_ref[...] = sums

    @pl.when(even_row())
    def _():
        write_numbers(sums, w_ref, numbers_hbm, numbers_ref, sem)


def even_row():
    return lax.rem(lax.div(lax.axis_index("sector"), QD), 2) == 0


def write_numbers(sums, w_ref, numbers_hbm, numbers_ref, sem):
    w = w_ref[...].astype(jnp.float32)
    values = [sums[n : n + 1, 0:1] for n in range(5)]
    values[3] = total(w * w)
    lane = lax.broadcasted_iota(jnp.int32, (1, 128), 1)
    numbers = jnp.zeros((1, 128), jnp.float32)
    for n, value in enumerate(values):
        numbers = jnp.where(lane == n, value, numbers)
    for n in range(numbers_ref.shape[0]):
        numbers_ref[n] = numbers
    copy = pltpu.make_async_copy(numbers_ref, numbers_hbm, sem)
    copy.start()
    copy.wait()


def numbers_kernel(held_hbm, sums_ref, w_ref, far_w_in, near_w, numbers_hbm, far_w_out, numbers_ref, sem):
    @pl.when(jnp.logical_not(even_row()))
    def _():
        write_numbers(sums_ref[...], w_ref, numbers_hbm, numbers_ref, sem)


def image_kernel(size, width, rows, *refs):
    row_refs, refs = refs[:rows], refs[rows:]
    far_ref, near_ref, self_ref, left_row, right_row, left_hbm, right_hbm, out_ref, left_own, right_own, sems = refs
    _, _, there = place(size, width)
    own = fetch(left_hbm, right_hbm, left_own, right_own, sems, [(0, 2 + width), (2 + width, width)])
    image = None
    for r, source in enumerate(row_refs):
        piece = terms(only(there[1 + r], source[...]), left_row, right_row, r * width, width)
        image = piece if image is None else image + piece
    odd = lax.rem(lax.axis_index("sector"), 2) == 1
    near, far = near_ref[...], only(there[0], far_ref[...])
    finish(own[0])
    image = image + terms(self_ref[...], left_own, right_own, 0, 2)
    image = image + terms(jnp.where(odd, near, far), left_own, right_own, 2, width)
    finish(own[1])
    out_ref[...] = image + terms(jnp.where(odd, far, near), left_own, right_own, 2 + width, width)


def second_kernel(size, width, rows, cells, facts_ref, stats_ref, hw_ref, near_part_ref, far_part_ref, row_part_ref,
                  first_hbm, second_hbm, first_ref, second_ref, sems):
    _, partners, _ = place(size, width)
    facts = facts_ref[...]
    stats = stats_ref[:, 0, :]
    sums = jnp.sum(stats, axis=0, keepdims=True)
    start, square, cross, inner = (sums[:, i : i + 1] for i in range(4))
    scale = lax.rsqrt(start / cells + 1e-06) * (1.0 / SCALE)
    parts = [near_part_ref[0], near_part_ref[1], far_part_ref[...]] + [row_part_ref[r] for r in range(rows)]
    cell = live(facts, parts[0].shape)
    first_ref[...] = jnp.where(cell, sum(parts[1:], parts[0]), 0.0) * scale
    first_copy = pltpu.make_async_copy(first_ref, first_hbm.at[0], sems.at[0])
    first_copy.start()
    rho = cross / square
    gap = stats[:, 4:5] - rho
    residual = inner + jnp.sum(stats[:, 1:2] * gap * gap, axis=0, keepdims=True)
    second_scale = scale * lax.rsqrt(scale * scale * (residual / cells) + 1e-06)
    image = hw_ref[...]
    for n, part in enumerate(parts):
        image = image + (stats_ref[partners[n], :, 4:5] - rho) * part
    second_ref[...] = jnp.where(cell, image, 0.0) * second_scale
    second_copy = pltpu.make_async_copy(second_ref, second_hbm.at[0], sems.at[1])
    second_copy.start()
    first_copy.wait()
    second_copy.wait()


def body(wavefunction, sector_dims, left_env, right_env):
    size = lax.axis_size("sector")
    block = wavefunction.shape[1]
    square = (block, block)
    width = (right_env.shape[1] - 2) // 4
    near, row_pairs = swap_pairs(size)
    rows = len(row_pairs)
    cells = float(size * block * block)
    few, every, side, last = ((n,) + square for n in (2 + width, 2 + 2 * width, width, rows * width))
    f32, bf16 = jnp.float32, jnp.bfloat16
    dma = pltpu.SemaphoreType.DMA

    u, far_u, facts = call(
        start_kernel, (pltpu.VMEM(square, bf16),) * 2 + (pltpu.VMEM((8, 128), f32),), [HB, HB], (VM,) * 3,
        [pltpu.VMEM(square, f32), pltpu.SMEM((1, 2), jnp.int32), dma((QUARTERS + 1,))],
    )(hbm(wavefunction), hbm(sector_dims))

    left_env, right_env = hbm(left_env), hbm(right_env)
    u, facts = vmem(u), vmem(facts)
    row_u = [vmem(swap(u, "sector", p)) for p in row_pairs]
    near_u = vmem(swap(u, "sector", near))
    far_u = vmem(far_swap(after(far_u, near_u)))
    near_part, sums, left_far, right_far, left_row, right_row = call(
        functools.partial(near_kernel, size, width, rows),
        (pltpu.VMEM((2,) + square, f32), pltpu.VMEM((8, 128), f32)) + (pltpu.VMEM(side, bf16),) * 2 + (pltpu.VMEM(last, bf16),) * 2,
        [HB] * 3 + [VM] * 3, (VM,) * 6,
        [pltpu.VMEM(few, bf16)] * 2 + [pltpu.VMEM(square, f32), dma((2, 2)), dma((1, 2)), dma((rows, 2)), dma], LONG,
    )(left_env, right_env, hbm(wavefunction), facts, u, near_u)
    near_part, left_row, right_row = vmem(near_part), vmem(left_row), vmem(right_row)
    far_part = vmem(call(
        functools.partial(far_kernel, size, width), pltpu.VMEM(square, f32), [VM] * 3, VM, cost=LONG,
    )(vmem(left_far), vmem(right_far), far_u))
    table = pltpu.HBM((size, 1, 128), f32)
    table_scratch = [pltpu.VMEM((size, 1, 128), f32), dma]
    row_part, w, far_w, sums, stats = call(
        functools.partial(first_kernel, size, width, rows),
        (pltpu.VMEM((rows,) + square, f32),) + (pltpu.VMEM(square, bf16),) * 2 + (pltpu.VMEM((8, 128), f32), table),
        [VM] * (7 + rows), (VM,) * 4 + (HB,), table_scratch,
    )(near_part, far_part, facts, vmem(sums), u, left_row, right_row, *row_u)

    w = vmem(w)
    row_w = [vmem(swap(w, "sector", p)) for p in row_pairs]
    near_w = vmem(swap(w, "sector", near))
    stats, far_w = call(
        numbers_kernel, (table, pltpu.VMEM(square, bf16)), [HB] + [VM] * 2 + [AN] * 2, (HB, AN), table_scratch, aliases={0: 0, 3: 1},
    )(hbm(stats), vmem(sums), w, vmem(far_w), near_w)
    far_w = vmem(far_swap(far_w))
    stats = lax.all_to_all(stats, "sector", 0, 0, tiled=True)
    hw = call(
        functools.partial(image_kernel, size, width, rows), pltpu.VMEM(square, f32), [VM] * (5 + rows) + [HB] * 2, VM,
        [pltpu.VMEM(every, bf16)] * 2 + [dma((2, 2))],
    )(*row_w, far_w, near_w, w, left_row, right_row, left_env, right_env)
    return call(
        functools.partial(second_kernel, size, width, rows, cells),
        (jax.ShapeDtypeStruct((1,) + square, f32),) * 2, [VM] * 6, (HB, HB),
        [pltpu.VMEM(square, f32)] * 2 + [dma((2,))],
    )(facts, stats, vmem(hw), near_part, far_part, vmem(row_part))


def solution(mesh):
    placed = (
        P(("groups", "sector"), None, None),
        P(("groups", "sector"), None),
        P(("groups", "sector"), None, None, None),
        P(("groups", "sector"), None, None, None),
    )
    return jax.shard_map(
        body,
        mesh=mesh,
        in_specs=placed,
        out_specs=(P(("groups", "sector"), None, None), P(("groups", "sector"), None, None)),
        check_vma=False,
    )
```

```python
import functools

import jax
import jax.numpy as jnp
from jax import lax
from jax.experimental import pallas as pl
from jax.experimental.pallas import tpu as pltpu
from jax.sharding import PartitionSpec as P

QD = 8
SCALE = 1024.0
QUARTERS = 4
NT = (((1,), (1,)), ((), ()))
VM = pl.BlockSpec(memory_space=pltpu.VMEM)
HB = pl.BlockSpec(memory_space=pltpu.HBM)
AN = pl.BlockSpec(memory_space=pl.ANY)
COST = pl.CostEstimate(flops=1, bytes_accessed=1, transcendentals=0)
LONG = pl.CostEstimate(flops=4000000000, bytes_accessed=1, transcendentals=0)
PARAMS = pltpu.CompilerParams(vmem_limit_bytes=16 * 1024 * 1024)


def vmem(x):
    return pltpu.with_memory_space_constraint(x, pltpu.VMEM)


def hbm(x):
    return pltpu.with_memory_space_constraint(x, pltpu.HBM)


def call(kernel, out_shape, in_specs, out_specs, scratch=(), cost=COST, aliases={}):
    return pl.pallas_call(
        kernel, out_shape=out_shape, in_specs=in_specs, out_specs=out_specs, scratch_shapes=list(scratch),
        compiler_params=PARAMS, cost_estimate=cost, input_output_aliases=aliases,
    )


def swap(x, axis, pairs):
    to = {a: b for p in pairs for a, b in (p, p[::-1])}
    return lax.ppermute(x, axis, [(s, to.get(s, s)) for s in range(lax.axis_size(axis))])


def swap_pairs(size):
    rows = size // QD
    near = [(s, s + 1) for s in range(0, size, 2)]
    row_even = [(s, s + QD) for r in range(0, rows - 1, 2) for s in range(r * QD, r * QD + QD)]
    row_odd = [(s, s + QD) for r in range(1, rows - 1, 2) for s in range(r * QD, r * QD + QD)]
    return near, [p for p in (row_even, row_odd) if p]


def far_swap(x):
    groups, size = lax.axis_size("groups"), lax.axis_size("sector")
    pairs = []
    for g in range(groups):
        for s in range(size):
            if s % QD == 0 or s % QD == QD - 1:
                to, partner = (g ^ 1 if g ^ 1 < groups else g), s
            else:
                to, partner = g, s + 1 if s % 2 else s - 1
            pairs.append((g * size + s, to * size + partner))
    return lax.ppermute(x, ("groups", "sector"), pairs)


def place(size, width):
    me = lax.axis_index("sector")
    column = lax.rem(me, QD)
    odd = lax.rem(me, 2) == 1
    row_odd = lax.rem(lax.div(me, QD), 2) == 1
    low, high, down, up = 2, 2 + width, 2 + 2 * width, 2 + 3 * width
    offsets = [jnp.where(odd, low, high), jnp.where(odd, high, low),
               jnp.where(row_odd, down, up), jnp.where(row_odd, up, down)]
    partners = [jnp.where(odd, me - 1, me + 1), jnp.where(odd, me + 1, me - 1),
                jnp.where(row_odd, me - QD, me + QD), jnp.where(row_odd, me + QD, me - QD)]
    there = [(column != 0) & (column != QD - 1),
             True if size // QD % 2 == 0 else (partners[2] >= 0) & (partners[2] < size),
             (partners[3] >= 0) & (partners[3] < size)]
    partners = [me] + [jnp.clip(p, 0, size - 1) for p in partners]
    return offsets, partners, there


def live(facts, shape):
    row_ok = lax.broadcasted_iota(jnp.int32, shape, 0).astype(jnp.float32) < facts[1:2, 0:1]
    col_ok = lax.broadcasted_iota(jnp.int32, shape, 1).astype(jnp.float32) < facts[2:3, 0:1]
    return row_ok & col_ok


def total(x):
    return jnp.sum(jnp.sum(x, axis=0, keepdims=True), axis=1, keepdims=True)


def only(there, block):
    return block if there is True else jnp.where(there, block, jnp.zeros_like(block))


def terms(src, left_ref, right_ref, first, count):
    size = src.shape[0]
    right = right_ref[pl.ds(first, count)].reshape(count * size, size)
    partial_t = lax.dot_general(right, src, NT, preferred_element_type=jnp.float32).astype(jnp.bfloat16)
    left = jnp.concatenate([left_ref[first + k] for k in range(count)], axis=1)
    partial_t = jnp.concatenate([partial_t[k * size : (k + 1) * size] for k in range(count)], axis=1)
    return lax.dot_general(left, partial_t, NT, preferred_element_type=jnp.float32)


def fetch(left_hbm, right_hbm, left_ref, right_ref, sems, spans):
    copies = []
    at = 0
    for n, (offset, count) in enumerate(spans):
        pair = [
            pltpu.make_async_copy(source.at[0, pl.ds(offset, count)], target.at[pl.ds(at, count)], sems.at[n, e])
            for e, (source, target) in enumerate(((right_hbm, right_ref), (left_hbm, left_ref)))
        ]
        for copy in pair:
            copy.start()
        copies.append(pair)
        at += count
    return copies


def finish(copies):
    for copy in copies:
        copy.wait()


def start_kernel(wave_hbm, dims_hbm, *refs):
    u_refs, (facts_ref, wave_ref, dims_ref, sems) = refs[:2], refs[2:]
    size = wave_ref.shape[0]
    step = size // QUARTERS
    dims_copy = pltpu.make_async_copy(dims_hbm, dims_ref, sems.at[QUARTERS])
    dims_copy.start()
    copies = [
        pltpu.make_async_copy(wave_hbm.at[0, pl.ds(n * step, step)], wave_ref.at[pl.ds(n * step, step)], sems.at[n])
        for n in range(QUARTERS)
    ]
    for copy in copies:
        copy.start()
    dims_copy.wait()
    row_count, col_count = dims_ref[0, 0], dims_ref[0, 1]
    lines = lax.broadcasted_iota(jnp.int32, (8, 128), 0)
    facts_ref[...] = jnp.where(lines == 1, row_count, jnp.where(lines == 2, col_count, 0)).astype(jnp.float32)
    col_ok = lax.broadcasted_iota(jnp.int32, (step, size), 1) < col_count
    row = lax.broadcasted_iota(jnp.int32, (step, size), 0)
    for n, copy in enumerate(copies):
        copy.wait()
        rows = pl.ds(n * step, step)
        held = jnp.where((row < row_count - n * step) & col_ok, wave_ref[rows], 0.0)
        block = (held * SCALE).astype(jnp.bfloat16)
        for ref in u_refs:
            ref[rows] = block


def pass_kernel(*refs):
    pass


def after(held, first):
    return call(pass_kernel, pltpu.VMEM(held.shape, held.dtype), [AN] * 2, AN, aliases={0: 0})(vmem(held), first)


def near_kernel(size, width, rows, left_hbm, right_hbm, wave_hbm, facts_ref, self_ref, near_ref, out_ref, sums_ref,
                left_far, right_far, left_row, right_row, left_own, right_own, wave_ref, sems, far_sems, row_sems, wave_sem):
    offsets, _, _ = place(size, width)
    wave_copy = pltpu.make_async_copy(wave_hbm.at[0], wave_ref, wave_sem)
    own = fetch(left_hbm, right_hbm, left_own, right_own, sems, [(0, 2), (offsets[0], width)])
    wave_copy.start()
    later = fetch(left_hbm, right_hbm, left_far, right_far, far_sems, [(offsets[1], width)])
    later += fetch(left_hbm, right_hbm, left_row, right_row, row_sems, [(o, width) for o in offsets[2 : 2 + rows]])
    u = self_ref[...].astype(jnp.float32)
    lines = lax.broadcasted_iota(jnp.int32, (8, 128), 0)
    sums = jnp.where(lines == 1, total(u * u), 0.0)
    finish(own[0])
    out_ref[0] = terms(self_ref[...], left_own, right_own, 0, 2)
    finish(own[1])
    out_ref[1] = terms(near_ref[...], left_own, right_own, 2, width)
    wave_copy.wait()
    held = jnp.where(live(facts_ref[...], wave_ref.shape), wave_ref[...], 0.0)
    sums_ref[...] = jnp.where(lines == 0, total(held * held), sums)
    for pair in later:
        finish(pair)


def far_kernel(size, width, left_ref, right_ref, far_ref, out_ref):
    _, _, there = place(size, width)
    out_ref[...] = terms(only(there[0], far_ref[...]), left_ref, right_ref, 0, width)


def first_kernel(size, width, rows, *refs):
    near_part_ref, far_part_ref, facts_ref, sums_ref, u_ref, left_ref, right_ref = refs[:7]
    row_refs, (out_ref, w_ref, stats_ref) = refs[7 : 7 + rows], refs[7 + rows :]
    _, _, there = place(size, width)
    image = near_part_ref[0] + near_part_ref[1] + far_part_ref[...]
    for r, source in enumerate(row_refs):
        piece = terms(only(there[1 + r], source[...]), left_ref, right_ref, r * width, width)
        out_ref[r] = piece
        image = image + piece
    image = jnp.where(live(facts_ref[...], image.shape), image, 0.0)
    u = u_ref[...].astype(jnp.float32)
    square = sums_ref[1:2, 0:1]
    cross = total(u * image)
    rho = jnp.where(square > 0.0, cross / square, 0.0)
    w = image - rho * u
    w_ref[...] = w.astype(jnp.bfloat16)
    lane = lax.broadcasted_iota(jnp.int32, (1, 128), 1)
    stats = jnp.zeros((1, 128), jnp.float32)
    for n, value in enumerate((sums_ref[0:1, 0:1], square, cross, total(w * w), rho)):
        stats = jnp.where(lane == n, value, stats)
    for n in range(stats_ref.shape[0]):
        stats_ref[n] = stats


def image_kernel(size, width, rows, *refs):
    row_refs, refs = refs[:rows], refs[rows:]
    near_ref, far_ref, self_ref, left_row, right_row, left_hbm, right_hbm, out_ref, left_own, right_own, sems = refs
    _, _, there = place(size, width)
    own = fetch(left_hbm, right_hbm, left_own, right_own, sems, [(0, 2 + width), (2 + width, width)])
    image = None
    for r, source in enumerate(row_refs):
        piece = terms(only(there[1 + r], source[...]), left_row, right_row, r * width, width)
        image = piece if image is None else image + piece
    odd = lax.rem(lax.axis_index("sector"), 2) == 1
    near, far = near_ref[...], only(there[0], far_ref[...])
    finish(own[0])
    image = image + terms(self_ref[...], left_own, right_own, 0, 2)
    image = image + terms(jnp.where(odd, near, far), left_own, right_own, 2, width)
    finish(own[1])
    out_ref[...] = image + terms(jnp.where(odd, far, near), left_own, right_own, 2 + width, width)


def second_kernel(size, width, rows, cells, facts_ref, stats_ref, hw_ref, near_part_ref, far_part_ref, row_part_ref,
                  first_hbm, second_hbm, first_ref, second_ref, sems):
    _, partners, _ = place(size, width)
    facts = facts_ref[...]
    stats = stats_ref[:, 0, :]
    sums = jnp.sum(stats, axis=0, keepdims=True)
    start, square, cross, inner = (sums[:, i : i + 1] for i in range(4))
    scale = lax.rsqrt(start / cells + 1e-06) * (1.0 / SCALE)
    parts = [near_part_ref[0], near_part_ref[1], far_part_ref[...]] + [row_part_ref[r] for r in range(rows)]
    cell = live(facts, parts[0].shape)
    first_ref[...] = jnp.where(cell, sum(parts[1:], parts[0]), 0.0) * scale
    first_copy = pltpu.make_async_copy(first_ref, first_hbm.at[0], sems.at[0])
    first_copy.start()
    rho = cross / square
    gap = stats[:, 4:5] - rho
    residual = inner + jnp.sum(stats[:, 1:2] * gap * gap, axis=0, keepdims=True)
    second_scale = scale * lax.rsqrt(scale * scale * (residual / cells) + 1e-06)
    image = hw_ref[...]
    for n, part in enumerate(parts):
        image = image + (stats_ref[partners[n], :, 4:5] - rho) * part
    second_ref[...] = jnp.where(cell, image, 0.0) * second_scale
    second_copy = pltpu.make_async_copy(second_ref, second_hbm.at[0], sems.at[1])
    second_copy.start()
    first_copy.wait()
    second_copy.wait()


def body(wavefunction, sector_dims, left_env, right_env):
    size = lax.axis_size("sector")
    block = wavefunction.shape[1]
    square = (block, block)
    width = (right_env.shape[1] - 2) // 4
    near, row_pairs = swap_pairs(size)
    rows = len(row_pairs)
    cells = float(size * block * block)
    few, every, side, last = ((n,) + square for n in (2 + width, 2 + 2 * width, width, rows * width))
    f32, bf16 = jnp.float32, jnp.bfloat16
    dma = pltpu.SemaphoreType.DMA

    u, far_u, facts = call(
        start_kernel, (pltpu.VMEM(square, bf16),) * 2 + (pltpu.VMEM((8, 128), f32),), [HB, HB], (VM,) * 3,
        [pltpu.VMEM(square, f32), pltpu.SMEM((1, 2), jnp.int32), dma((QUARTERS + 1,))],
    )(hbm(wavefunction), hbm(sector_dims))

    left_env, right_env = hbm(left_env), hbm(right_env)
    u, facts = vmem(u), vmem(facts)
    row_u = [vmem(swap(u, "sector", p)) for p in row_pairs]
    near_u = vmem(swap(u, "sector", near))
    far_u = vmem(far_swap(after(far_u, near_u)))
    near_part, sums, left_far, right_far, left_row, right_row = call(
        functools.partial(near_kernel, size, width, rows),
        (pltpu.VMEM((2,) + square, f32), pltpu.VMEM((8, 128), f32)) + (pltpu.VMEM(side, bf16),) * 2 + (pltpu.VMEM(last, bf16),) * 2,
        [HB] * 3 + [VM] * 3, (VM,) * 6,
        [pltpu.VMEM(few, bf16)] * 2 + [pltpu.VMEM(square, f32), dma((2, 2)), dma((1, 2)), dma((rows, 2)), dma], LONG,
    )(left_env, right_env, hbm(wavefunction), facts, u, near_u)
    near_part, left_row, right_row = vmem(near_part), vmem(left_row), vmem(right_row)
    far_part = vmem(call(
        functools.partial(far_kernel, size, width), pltpu.VMEM(square, f32), [VM] * 3, VM, cost=LONG,
    )(vmem(left_far), vmem(right_far), far_u))
    row_part, w, stats = call(
        functools.partial(first_kernel, size, width, rows),
        (pltpu.VMEM((rows,) + square, f32),) + (pltpu.VMEM(square, bf16), jax.ShapeDtypeStruct((size, 1, 128), f32)),
        [VM] * (7 + rows), (VM,) * 3,
    )(near_part, far_part, facts, vmem(sums), u, left_row, right_row, *row_u)

    w = vmem(w)
    row_w = [vmem(swap(w, "sector", p)) for p in row_pairs]
    near_w = vmem(swap(w, "sector", near))
    far_w = vmem(far_swap(w))
    stats = lax.all_to_all(stats, "sector", 0, 0, tiled=True)
    hw = call(
        functools.partial(image_kernel, size, width, rows), pltpu.VMEM(square, f32), [VM] * (5 + rows) + [HB] * 2, VM,
        [pltpu.VMEM(every, bf16)] * 2 + [dma((2, 2))],
    )(*row_w, near_w, far_w, w, left_row, right_row, left_env, right_env)
    return call(
        functools.partial(second_kernel, size, width, rows, cells),
        (jax.ShapeDtypeStruct((1,) + square, f32),) * 2, [VM] * 6, (HB, HB),
        [pltpu.VMEM(square, f32)] * 2 + [dma((2,))],
    )(facts, stats, vmem(hw), near_part, far_part, vmem(row_part))


def solution(mesh):
    placed = (
        P(("groups", "sector"), None, None),
        P(("groups", "sector"), None),
        P(("groups", "sector"), None, None, None),
        P(("groups", "sector"), None, None, None),
    )
    return jax.shard_map(
        body,
        mesh=mesh,
        in_specs=placed,
        out_specs=(P(("groups", "sector"), None, None), P(("groups", "sector"), None, None)),
        check_vma=False,
    )
```

```python
import functools

import jax
import jax.numpy as jnp
from jax import lax
from jax.experimental import pallas as pl
from jax.experimental.pallas import tpu as pltpu
from jax.sharding import PartitionSpec as P

QD = 8
SCALE = 1024.0
QUARTERS = 4
NT = (((1,), (1,)), ((), ()))
VM = pl.BlockSpec(memory_space=pltpu.VMEM)
HB = pl.BlockSpec(memory_space=pltpu.HBM)
AN = pl.BlockSpec(memory_space=pl.ANY)
COST = pl.CostEstimate(flops=1, bytes_accessed=1, transcendentals=0)
LONG = pl.CostEstimate(flops=4000000000, bytes_accessed=1, transcendentals=0)
PARAMS = pltpu.CompilerParams(vmem_limit_bytes=16 * 1024 * 1024)


def vmem(x):
    return pltpu.with_memory_space_constraint(x, pltpu.VMEM)


def hbm(x):
    return pltpu.with_memory_space_constraint(x, pltpu.HBM)


def call(kernel, out_shape, in_specs, out_specs, scratch=(), cost=COST, aliases={}):
    return pl.pallas_call(
        kernel, out_shape=out_shape, in_specs=in_specs, out_specs=out_specs, scratch_shapes=list(scratch),
        compiler_params=PARAMS, cost_estimate=cost, input_output_aliases=aliases,
    )


def swap(x, axis, pairs):
    to = {a: b for p in pairs for a, b in (p, p[::-1])}
    return lax.ppermute(x, axis, [(s, to.get(s, s)) for s in range(lax.axis_size(axis))])


def swap_pairs(size):
    rows = size // QD
    near = [(s, s + 1) for s in range(0, size, 2)]
    row_even = [(s, s + QD) for r in range(0, rows - 1, 2) for s in range(r * QD, r * QD + QD)]
    row_odd = [(s, s + QD) for r in range(1, rows - 1, 2) for s in range(r * QD, r * QD + QD)]
    return near, [p for p in (row_even, row_odd) if p]


def far_swap(x):
    groups, size = lax.axis_size("groups"), lax.axis_size("sector")
    pairs = []
    for g in range(groups):
        for s in range(size):
            if s % QD == 0 or s % QD == QD - 1:
                to, partner = (g ^ 1 if g ^ 1 < groups else g), s
            else:
                to, partner = g, s + 1 if s % 2 else s - 1
            pairs.append((g * size + s, to * size + partner))
    return lax.ppermute(x, ("groups", "sector"), pairs)


def place(size, width):
    me = lax.axis_index("sector")
    column = lax.rem(me, QD)
    odd = lax.rem(me, 2) == 1
    row_odd = lax.rem(lax.div(me, QD), 2) == 1
    low, high, down, up = 2, 2 + width, 2 + 2 * width, 2 + 3 * width
    offsets = [jnp.where(odd, low, high), jnp.where(odd, high, low),
               jnp.where(row_odd, down, up), jnp.where(row_odd, up, down)]
    partners = [jnp.where(odd, me - 1, me + 1), jnp.where(odd, me + 1, me - 1),
                jnp.where(row_odd, me - QD, me + QD), jnp.where(row_odd, me + QD, me - QD)]
    there = [(column != 0) & (column != QD - 1),
             True if size // QD % 2 == 0 else (partners[2] >= 0) & (partners[2] < size),
             (partners[3] >= 0) & (partners[3] < size)]
    partners = [me] + [jnp.clip(p, 0, size - 1) for p in partners]
    return offsets, partners, there


def live(facts, shape):
    row_ok = lax.broadcasted_iota(jnp.int32, shape, 0).astype(jnp.float32) < facts[1:2, 0:1]
    col_ok = lax.broadcasted_iota(jnp.int32, shape, 1).astype(jnp.float32) < facts[2:3, 0:1]
    return row_ok & col_ok


def total(x):
    return jnp.sum(jnp.sum(x, axis=0, keepdims=True), axis=1, keepdims=True)


def only(there, block):
    return block if there is True else jnp.where(there, block, jnp.zeros_like(block))


def terms(src, left_ref, right_ref, first, count):
    size = src.shape[0]
    right = right_ref[pl.ds(first, count)].reshape(count * size, size)
    partial_t = lax.dot_general(right, src, NT, preferred_element_type=jnp.float32).astype(jnp.bfloat16)
    left = jnp.concatenate([left_ref[first + k] for k in range(count)], axis=1)
    partial_t = jnp.concatenate([partial_t[k * size : (k + 1) * size] for k in range(count)], axis=1)
    return lax.dot_general(left, partial_t, NT, preferred_element_type=jnp.float32)


def fetch(left_hbm, right_hbm, left_ref, right_ref, sems, spans):
    copies = []
    at = 0
    for n, (offset, count) in enumerate(spans):
        pair = [
            pltpu.make_async_copy(source.at[0, pl.ds(offset, count)], target.at[pl.ds(at, count)], sems.at[n, e])
            for e, (source, target) in enumerate(((right_hbm, right_ref), (left_hbm, left_ref)))
        ]
        for copy in pair:
            copy.start()
        copies.append(pair)
        at += count
    return copies


def finish(copies):
    for copy in copies:
        copy.wait()


def start_kernel(wave_hbm, dims_hbm, *refs):
    u_refs, (facts_ref, wave_ref, dims_ref, sems) = refs[:2], refs[2:]
    size = wave_ref.shape[0]
    step = size // QUARTERS
    dims_copy = pltpu.make_async_copy(dims_hbm, dims_ref, sems.at[QUARTERS])
    dims_copy.start()
    copies = [
        pltpu.make_async_copy(wave_hbm.at[0, pl.ds(n * step, step)], wave_ref.at[pl.ds(n * step, step)], sems.at[n])
        for n in range(QUARTERS)
    ]
    for copy in copies:
        copy.start()
    dims_copy.wait()
    row_count, col_count = dims_ref[0, 0], dims_ref[0, 1]
    lines = lax.broadcasted_iota(jnp.int32, (8, 128), 0)
    facts_ref[...] = jnp.where(lines == 1, row_count, jnp.where(lines == 2, col_count, 0)).astype(jnp.float32)
    col_ok = lax.broadcasted_iota(jnp.int32, (step, size), 1) < col_count
    row = lax.broadcasted_iota(jnp.int32, (step, size), 0)
    for n, copy in enumerate(copies):
        copy.wait()
        rows = pl.ds(n * step, step)
        held = jnp.where((row < row_count - n * step) & col_ok, wave_ref[rows], 0.0)
        block = (held * SCALE).astype(jnp.bfloat16)
        for ref in u_refs:
            ref[rows] = block


def pass_kernel(*refs):
    pass


def after(held, first):
    return call(pass_kernel, pltpu.VMEM(held.shape, held.dtype), [AN] * 2, AN, aliases={0: 0})(vmem(held), first)


def near_kernel(size, width, rows, left_hbm, right_hbm, wave_hbm, facts_ref, self_ref, near_ref, out_ref, sums_ref,
                left_far, right_far, left_row, right_row, left_own, right_own, wave_ref, sems, far_sems, row_sems, wave_sem):
    offsets, _, _ = place(size, width)
    wave_copy = pltpu.make_async_copy(wave_hbm.at[0], wave_ref, wave_sem)
    own = fetch(left_hbm, right_hbm, left_own, right_own, sems, [(0, 2), (offsets[0], width)])
    wave_copy.start()
    later = fetch(left_hbm, right_hbm, left_far, right_far, far_sems, [(offsets[1], width)])
    later += fetch(left_hbm, right_hbm, left_row, right_row, row_sems, [(o, width) for o in offsets[2 : 2 + rows]])
    u = self_ref[...].astype(jnp.float32)
    lines = lax.broadcasted_iota(jnp.int32, (8, 128), 0)
    sums = jnp.where(lines == 1, total(u * u), 0.0)
    finish(own[0])
    out_ref[0] = terms(self_ref[...], left_own, right_own, 0, 2)
    finish(own[1])
    out_ref[1] = terms(near_ref[...], left_own, right_own, 2, width)
    wave_copy.wait()
    held = jnp.where(live(facts_ref[...], wave_ref.shape), wave_ref[...], 0.0)
    sums_ref[...] = jnp.where(lines == 0, total(held * held), sums)
    for pair in later:
        finish(pair)


def far_kernel(size, width, left_ref, right_ref, far_ref, out_ref):
    _, _, there = place(size, width)
    out_ref[...] = terms(only(there[0], far_ref[...]), left_ref, right_ref, 0, width)


def first_kernel(size, width, rows, *refs):
    near_part_ref, far_part_ref, facts_ref, sums_ref, u_ref, left_ref, right_ref = refs[:7]
    row_refs, (out_ref, w_ref, far_w_ref, line_ref) = refs[7 : 7 + rows], refs[7 + rows :]
    _, _, there = place(size, width)
    image = near_part_ref[0] + near_part_ref[1] + far_part_ref[...]
    for r, source in enumerate(row_refs):
        piece = terms(only(there[1 + r], source[...]), left_ref, right_ref, r * width, width)
        out_ref[r] = piece
        image = image + piece
    image = jnp.where(live(facts_ref[...], image.shape), image, 0.0)
    u = u_ref[...].astype(jnp.float32)
    square = sums_ref[1:2, 0:1]
    cross = total(u * image)
    rho = jnp.where(square > 0.0, cross / square, 0.0)
    w = image - rho * u
    for ref in (w_ref, far_w_ref):
        ref[...] = w.astype(jnp.bfloat16)
    lane = lax.broadcasted_iota(jnp.int32, (1, 128), 1) - 8 * lax.rem(lax.axis_index("sector"), 2)
    line = jnp.zeros((1, 128), jnp.float32)
    for n, value in enumerate((sums_ref[0:1, 0:1], square, cross, total(w * w), rho)):
        line = jnp.where(lane == n, value, line)
    line_ref[...] = jnp.broadcast_to(line, line_ref.shape)


def merge_kernel(one_ref, other_ref, held_in, out_ref, held_out):
    line = one_ref[0:1] + other_ref[0:1]
    for n in range(out_ref.shape[0]):
        out_ref[n] = line


def image_kernel(size, width, rows, *refs):
    row_refs, refs = refs[:rows], refs[rows:]
    far_ref, near_ref, self_ref, left_row, right_row, left_hbm, right_hbm, out_ref, left_own, right_own, sems = refs
    _, _, there = place(size, width)
    own = fetch(left_hbm, right_hbm, left_own, right_own, sems, [(0, 2 + width), (2 + width, width)])
    image = None
    for r, source in enumerate(row_refs):
        piece = terms(only(there[1 + r], source[...]), left_row, right_row, r * width, width)
        image = piece if image is None else image + piece
    odd = lax.rem(lax.axis_index("sector"), 2) == 1
    near, far = near_ref[...], only(there[0], far_ref[...])
    finish(own[0])
    image = image + terms(self_ref[...], left_own, right_own, 0, 2)
    image = image + terms(jnp.where(odd, near, far), left_own, right_own, 2, width)
    finish(own[1])
    out_ref[...] = image + terms(jnp.where(odd, far, near), left_own, right_own, 2 + width, width)


def second_kernel(size, width, rows, cells, facts_ref, stats_ref, hw_ref, near_part_ref, far_part_ref, row_part_ref,
                  first_hbm, second_hbm, first_ref, second_ref, sems):
    _, partners, _ = place(size, width)
    facts = facts_ref[...]
    stats = stats_ref[:, 0, :]
    sums = jnp.sum(stats, axis=0, keepdims=True)
    start, square, cross, inner = (sums[:, i : i + 1] + sums[:, i + 8 : i + 9] for i in range(4))
    scale = lax.rsqrt(start / cells + 1e-06) * (1.0 / SCALE)
    parts = [near_part_ref[0], near_part_ref[1], far_part_ref[...]] + [row_part_ref[r] for r in range(rows)]
    cell = live(facts, parts[0].shape)
    first_ref[...] = jnp.where(cell, sum(parts[1:], parts[0]), 0.0) * scale
    first_copy = pltpu.make_async_copy(first_ref, first_hbm.at[0], sems.at[0])
    first_copy.start()
    rho = cross / square
    gaps = [stats[:, 8 * core + 4 : 8 * core + 5] - rho for core in range(2)]
    spread = [stats[:, 8 * core + 1 : 8 * core + 2] * gap * gap for core, gap in enumerate(gaps)]
    residual = inner + jnp.sum(spread[0] + spread[1], axis=0, keepdims=True)
    second_scale = scale * lax.rsqrt(scale * scale * (residual / cells) + 1e-06)
    image = hw_ref[...]
    for n, part in enumerate(parts):
        chip, core = lax.div(partners[n], 2), lax.rem(partners[n], 2)
        line = stats_ref[chip]
        image = image + (jnp.where(core == 0, line[:, 4:5], line[:, 12:13]) - rho) * part
    second_ref[...] = jnp.where(cell, image, 0.0) * second_scale
    second_copy = pltpu.make_async_copy(second_ref, second_hbm.at[0], sems.at[1])
    second_copy.start()
    first_copy.wait()
    second_copy.wait()


def body(wavefunction, sector_dims, left_env, right_env):
    size = lax.axis_size("sector")
    block = wavefunction.shape[1]
    square = (block, block)
    width = (right_env.shape[1] - 2) // 4
    near, row_pairs = swap_pairs(size)
    rows = len(row_pairs)
    cells = float(size * block * block)
    few, every, side, last = ((n,) + square for n in (2 + width, 2 + 2 * width, width, rows * width))
    f32, bf16 = jnp.float32, jnp.bfloat16
    dma = pltpu.SemaphoreType.DMA

    u, far_u, facts = call(
        start_kernel, (pltpu.VMEM(square, bf16),) * 2 + (pltpu.VMEM((8, 128), f32),), [HB, HB], (VM,) * 3,
        [pltpu.VMEM(square, f32), pltpu.SMEM((1, 2), jnp.int32), dma((QUARTERS + 1,))],
    )(hbm(wavefunction), hbm(sector_dims))

    left_env, right_env = hbm(left_env), hbm(right_env)
    u, facts = vmem(u), vmem(facts)
    row_u = [vmem(swap(u, "sector", p)) for p in row_pairs]
    near_u = vmem(swap(u, "sector", near))
    far_u = vmem(far_swap(after(far_u, near_u)))
    near_part, sums, left_far, right_far, left_row, right_row = call(
        functools.partial(near_kernel, size, width, rows),
        (pltpu.VMEM((2,) + square, f32), pltpu.VMEM((8, 128), f32)) + (pltpu.VMEM(side, bf16),) * 2 + (pltpu.VMEM(last, bf16),) * 2,
        [HB] * 3 + [VM] * 3, (VM,) * 6,
        [pltpu.VMEM(few, bf16)] * 2 + [pltpu.VMEM(square, f32), dma((2, 2)), dma((1, 2)), dma((rows, 2)), dma], LONG,
    )(left_env, right_env, hbm(wavefunction), facts, u, near_u)
    near_part, left_row, right_row = vmem(near_part), vmem(left_row), vmem(right_row)
    far_part = vmem(call(
        functools.partial(far_kernel, size, width), pltpu.VMEM(square, f32), [VM] * 3, VM, cost=LONG,
    )(vmem(left_far), vmem(right_far), far_u))
    row_part, w, far_w, line = call(
        functools.partial(first_kernel, size, width, rows),
        (pltpu.VMEM((rows,) + square, f32),) + (pltpu.VMEM(square, bf16),) * 2 + (pltpu.VMEM((8, 128), f32),),
        [VM] * (7 + rows), (VM,) * 4,
    )(near_part, far_part, facts, vmem(sums), u, left_row, right_row, *row_u)

    w = vmem(w)
    row_w = [vmem(swap(w, "sector", p)) for p in row_pairs]
    near_w = vmem(swap(w, "sector", near))
    line = vmem(line)
    stats, far_w = call(
        merge_kernel, (jax.ShapeDtypeStruct((size // 2, 1, 128), f32), pltpu.VMEM(square, bf16)), [VM] * 2 + [AN], (VM, AN),
        aliases={2: 1},
    )(line, vmem(swap(line, "sector", near)), vmem(far_w))
    far_w = vmem(far_swap(far_w))
    chips = [list(range(core, size, 2)) for core in range(2)]
    stats = lax.all_to_all(stats, "sector", 0, 0, tiled=True, axis_index_groups=chips)
    hw = call(
        functools.partial(image_kernel, size, width, rows), pltpu.VMEM(square, f32), [VM] * (5 + rows) + [HB] * 2, VM,
        [pltpu.VMEM(every, bf16)] * 2 + [dma((2, 2))],
    )(*row_w, far_w, near_w, w, left_row, right_row, left_env, right_env)
    return call(
        functools.partial(second_kernel, size, width, rows, cells),
        (jax.ShapeDtypeStruct((1,) + square, f32),) * 2, [VM] * 6, (HB, HB),
        [pltpu.VMEM(square, f32)] * 2 + [dma((2,))],
    )(facts, stats, vmem(hw), near_part, far_part, vmem(row_part))


def solution(mesh):
    placed = (
        P(("groups", "sector"), None, None),
        P(("groups", "sector"), None),
        P(("groups", "sector"), None, None, None),
        P(("groups", "sector"), None, None, None),
    )
    return jax.shard_map(
        body,
        mesh=mesh,
        in_specs=placed,
        out_specs=(P(("groups", "sector"), None, None), P(("groups", "sector"), None, None)),
        check_vma=False,
    )
```

```python
import functools

import jax
import jax.numpy as jnp
from jax import lax
from jax.experimental import pallas as pl
from jax.experimental.pallas import tpu as pltpu
from jax.sharding import PartitionSpec as P

QD = 8
SCALE = 1024.0
QUARTERS = 4
HALVES = 2
NT = (((1,), (1,)), ((), ()))
VM = pl.BlockSpec(memory_space=pltpu.VMEM)
HB = pl.BlockSpec(memory_space=pltpu.HBM)
AN = pl.BlockSpec(memory_space=pl.ANY)
COST = pl.CostEstimate(flops=1, bytes_accessed=1, transcendentals=0)
LONG = pl.CostEstimate(flops=4000000000, bytes_accessed=1, transcendentals=0)
PARAMS = pltpu.CompilerParams(vmem_limit_bytes=16 * 1024 * 1024)


def vmem(x):
    return pltpu.with_memory_space_constraint(x, pltpu.VMEM)


def hbm(x):
    return pltpu.with_memory_space_constraint(x, pltpu.HBM)


def call(kernel, out_shape, in_specs, out_specs, scratch=(), cost=COST, aliases={}):
    return pl.pallas_call(
        kernel, out_shape=out_shape, in_specs=in_specs, out_specs=out_specs, scratch_shapes=list(scratch),
        compiler_params=PARAMS, cost_estimate=cost, input_output_aliases=aliases,
    )


def swap(x, axis, pairs):
    to = {a: b for p in pairs for a, b in (p, p[::-1])}
    return lax.ppermute(x, axis, [(s, to.get(s, s)) for s in range(lax.axis_size(axis))])


def swap_pairs(size):
    rows = size // QD
    near = [(s, s + 1) for s in range(0, size, 2)]
    row_even = [(s, s + QD) for r in range(0, rows - 1, 2) for s in range(r * QD, r * QD + QD)]
    row_odd = [(s, s + QD) for r in range(1, rows - 1, 2) for s in range(r * QD, r * QD + QD)]
    return near, [p for p in (row_even, row_odd) if p]


def far_swap(x):
    groups, size = lax.axis_size("groups"), lax.axis_size("sector")
    pairs = []
    for g in range(groups):
        for s in range(size):
            if s % QD == 0 or s % QD == QD - 1:
                to, partner = (g ^ 1 if g ^ 1 < groups else g), s
            else:
                to, partner = g, s + 1 if s % 2 else s - 1
            pairs.append((g * size + s, to * size + partner))
    return lax.ppermute(x, ("groups", "sector"), pairs)


def place(size, width):
    me = lax.axis_index("sector")
    column = lax.rem(me, QD)
    odd = lax.rem(me, 2) == 1
    row_odd = lax.rem(lax.div(me, QD), 2) == 1
    low, high, down, up = 2, 2 + width, 2 + 2 * width, 2 + 3 * width
    offsets = [jnp.where(odd, low, high), jnp.where(odd, high, low),
               jnp.where(row_odd, down, up), jnp.where(row_odd, up, down)]
    partners = [jnp.where(odd, me - 1, me + 1), jnp.where(odd, me + 1, me - 1),
                jnp.where(row_odd, me - QD, me + QD), jnp.where(row_odd, me + QD, me - QD)]
    there = [(column != 0) & (column != QD - 1),
             True if size // QD % 2 == 0 else (partners[2] >= 0) & (partners[2] < size),
             (partners[3] >= 0) & (partners[3] < size)]
    partners = [me] + [jnp.clip(p, 0, size - 1) for p in partners]
    return offsets, partners, there


def live(facts, shape):
    row_ok = lax.broadcasted_iota(jnp.int32, shape, 0).astype(jnp.float32) < facts[1:2, 0:1]
    col_ok = lax.broadcasted_iota(jnp.int32, shape, 1).astype(jnp.float32) < facts[2:3, 0:1]
    return row_ok & col_ok


def total(x):
    return jnp.sum(jnp.sum(x, axis=0, keepdims=True), axis=1, keepdims=True)


def only(there, block):
    return block if there is True else jnp.where(there, block, jnp.zeros_like(block))


def terms(src, left_ref, right_ref, first, count):
    size = src.shape[0]
    right = right_ref[pl.ds(first, count)].reshape(count * size, size)
    partial_t = lax.dot_general(right, src, NT, preferred_element_type=jnp.float32).astype(jnp.bfloat16)
    left = jnp.concatenate([left_ref[first + k] for k in range(count)], axis=1)
    partial_t = jnp.concatenate([partial_t[k * size : (k + 1) * size] for k in range(count)], axis=1)
    return lax.dot_general(left, partial_t, NT, preferred_element_type=jnp.float32)


def fetch(left_hbm, right_hbm, left_ref, right_ref, sems, spans):
    copies = []
    at = 0
    for n, (offset, count) in enumerate(spans):
        pair = [
            pltpu.make_async_copy(source.at[0, pl.ds(offset, count)], target.at[pl.ds(at, count)], sems.at[n, e])
            for e, (source, target) in enumerate(((right_hbm, right_ref), (left_hbm, left_ref)))
        ]
        for copy in pair:
            copy.start()
        copies.append(pair)
        at += count
    return copies


def finish(copies):
    for copy in copies:
        copy.wait()


def start_kernel(wave_hbm, dims_hbm, *refs):
    u_refs, (facts_ref, wave_ref, dims_ref, sems) = refs[:2], refs[2:]
    size = wave_ref.shape[0]
    step = size // QUARTERS
    dims_copy = pltpu.make_async_copy(dims_hbm, dims_ref, sems.at[QUARTERS])
    dims_copy.start()
    copies = [
        pltpu.make_async_copy(wave_hbm.at[0, pl.ds(n * step, step)], wave_ref.at[pl.ds(n * step, step)], sems.at[n])
        for n in range(QUARTERS)
    ]
    for copy in copies:
        copy.start()
    dims_copy.wait()
    row_count, col_count = dims_ref[0, 0], dims_ref[0, 1]
    lines = lax.broadcasted_iota(jnp.int32, (8, 128), 0)
    facts_ref[...] = jnp.where(lines == 1, row_count, jnp.where(lines == 2, col_count, 0)).astype(jnp.float32)
    col_ok = lax.broadcasted_iota(jnp.int32, (step, size), 1) < col_count
    row = lax.broadcasted_iota(jnp.int32, (step, size), 0)
    for n, copy in enumerate(copies):
        copy.wait()
        rows = pl.ds(n * step, step)
        held = jnp.where((row < row_count - n * step) & col_ok, wave_ref[rows], 0.0)
        block = (held * SCALE).astype(jnp.bfloat16)
        for ref in u_refs:
            ref[rows] = block


def pass_kernel(*refs):
    pass


def after(held, first):
    return call(pass_kernel, pltpu.VMEM(held.shape, held.dtype), [AN] * 2, AN, aliases={0: 0})(vmem(held), first)


def near_kernel(size, width, rows, left_hbm, right_hbm, wave_hbm, facts_ref, self_ref, near_ref, out_ref, sums_ref,
                left_far, right_far, left_row, right_row, left_own, right_own, wave_ref, sems, far_sems, row_sems, wave_sem):
    offsets, _, _ = place(size, width)
    wave_copy = pltpu.make_async_copy(wave_hbm.at[0], wave_ref, wave_sem)
    own = fetch(left_hbm, right_hbm, left_own, right_own, sems, [(0, 2), (offsets[0], width)])
    wave_copy.start()
    later = fetch(left_hbm, right_hbm, left_far, right_far, far_sems, [(offsets[1], width)])
    later += fetch(left_hbm, right_hbm, left_row, right_row, row_sems, [(o, width) for o in offsets[2 : 2 + rows]])
    u = self_ref[...].astype(jnp.float32)
    lines = lax.broadcasted_iota(jnp.int32, (8, 128), 0)
    sums = jnp.where(lines == 1, total(u * u), 0.0)
    finish(own[0])
    out_ref[0] = terms(self_ref[...], left_own, right_own, 0, 2)
    finish(own[1])
    out_ref[1] = terms(near_ref[...], left_own, right_own, 2, width)
    wave_copy.wait()
    held = jnp.where(live(facts_ref[...], wave_ref.shape), wave_ref[...], 0.0)
    sums_ref[...] = jnp.where(lines == 0, total(held * held), sums)
    for pair in later:
        finish(pair)


def far_kernel(size, width, left_ref, right_ref, near_part_ref, far_ref, out_ref, sum_ref):
    _, _, there = place(size, width)
    part = terms(only(there[0], far_ref[...]), left_ref, right_ref, 0, width)
    out_ref[...] = part
    sum_ref[...] = near_part_ref[0] + near_part_ref[1] + part


def first_kernel(size, width, rows, *refs):
    part_ref, facts_ref, sums_ref, u_ref, left_ref, right_ref = refs[:6]
    row_refs, (out_ref, w_ref, stats_ref) = refs[6 : 6 + rows], refs[6 + rows :]
    _, _, there = place(size, width)
    image = part_ref[...]
    for r, source in enumerate(row_refs):
        piece = terms(only(there[1 + r], source[...]), left_ref, right_ref, r * width, width)
        out_ref[r] = piece
        image = image + piece
    image = jnp.where(live(facts_ref[...], image.shape), image, 0.0)
    u = u_ref[...].astype(jnp.float32)
    square = sums_ref[1:2, 0:1]
    cross = total(u * image)
    rho = jnp.where(square > 0.0, cross / square, 0.0)
    w = image - rho * u
    w_ref[...] = w.astype(jnp.bfloat16)
    lane = lax.broadcasted_iota(jnp.int32, (1, 128), 1)
    stats = jnp.zeros((1, 128), jnp.float32)
    for n, value in enumerate((sums_ref[0:1, 0:1], square, cross, total(w * w), rho)):
        stats = jnp.where(lane == n, value, stats)
    for n in range(stats_ref.shape[0]):
        stats_ref[n] = stats


def image_kernel(size, width, rows, *refs):
    row_refs, refs = refs[:rows], refs[rows:]
    far_ref, near_ref, self_ref, left_row, right_row, left_hbm, right_hbm, out_ref, left_own, right_own, sems = refs
    _, _, there = place(size, width)
    own = fetch(left_hbm, right_hbm, left_own, right_own, sems, [(0, 2 + width), (2 + width, width)])
    image = None
    for r, source in enumerate(row_refs):
        piece = terms(only(there[1 + r], source[...]), left_row, right_row, r * width, width)
        image = piece if image is None else image + piece
    odd = lax.rem(lax.axis_index("sector"), 2) == 1
    near, far = near_ref[...], only(there[0], far_ref[...])
    finish(own[0])
    image = image + terms(self_ref[...], left_own, right_own, 0, 2)
    image = image + terms(jnp.where(odd, near, far), left_own, right_own, 2, width)
    finish(own[1])
    out_ref[...] = image + terms(jnp.where(odd, far, near), left_own, right_own, 2 + width, width)


def second_kernel(size, width, rows, cells, facts_ref, stats_ref, hw_ref, near_part_ref, far_part_ref, row_part_ref,
                  first_hbm, second_hbm, first_ref, second_ref, sems):
    _, partners, _ = place(size, width)
    facts = facts_ref[...]
    stats = stats_ref[:, 0, :]
    sums = jnp.sum(stats, axis=0, keepdims=True)
    start, square, cross, inner = (sums[:, i : i + 1] for i in range(4))
    scale = lax.rsqrt(start / cells + 1e-06) * (1.0 / SCALE)
    rho = cross / square
    gap = stats[:, 4:5] - rho
    residual = inner + jnp.sum(stats[:, 1:2] * gap * gap, axis=0, keepdims=True)
    second_scale = scale * lax.rsqrt(scale * scale * (residual / cells) + 1e-06)
    gaps = [stats_ref[partner, :, 4:5] - rho for partner in partners[: 3 + rows]]
    block = hw_ref.shape[0]
    step = block // HALVES
    col_ok = lax.broadcasted_iota(jnp.int32, (step, block), 1).astype(jnp.float32) < facts[2:3, 0:1]
    row = lax.broadcasted_iota(jnp.int32, (step, block), 0).astype(jnp.float32)
    copies = []
    for n in range(HALVES):
        lines = pl.ds(n * step, step)
        parts = [near_part_ref[0, lines], near_part_ref[1, lines], far_part_ref[lines]]
        parts += [row_part_ref[r, lines] for r in range(rows)]
        cell = (row + n * step < facts[1:2, 0:1]) & col_ok
        image = hw_ref[lines]
        for gap, part in zip(gaps, parts):
            image = image + gap * part
        second_ref[lines] = jnp.where(cell, image, 0.0) * second_scale
        first_ref[lines] = jnp.where(cell, sum(parts[1:], parts[0]), 0.0) * scale
        for e, (source, target) in enumerate(((second_ref, second_hbm), (first_ref, first_hbm))):
            copies.append(pltpu.make_async_copy(source.at[lines], target.at[0, lines], sems.at[n, e]))
            copies[-1].start()
    finish(copies)


def body(wavefunction, sector_dims, left_env, right_env):
    size = lax.axis_size("sector")
    block = wavefunction.shape[1]
    square = (block, block)
    width = (right_env.shape[1] - 2) // 4
    near, row_pairs = swap_pairs(size)
    rows = len(row_pairs)
    cells = float(size * block * block)
    few, every, side, last = ((n,) + square for n in (2 + width, 2 + 2 * width, width, rows * width))
    f32, bf16 = jnp.float32, jnp.bfloat16
    dma = pltpu.SemaphoreType.DMA

    u, far_u, facts = call(
        start_kernel, (pltpu.VMEM(square, bf16),) * 2 + (pltpu.VMEM((8, 128), f32),), [HB, HB], (VM,) * 3,
        [pltpu.VMEM(square, f32), pltpu.SMEM((1, 2), jnp.int32), dma((QUARTERS + 1,))],
    )(hbm(wavefunction), hbm(sector_dims))

    left_env, right_env = hbm(left_env), hbm(right_env)
    u, facts = vmem(u), vmem(facts)
    row_u = [vmem(swap(u, "sector", p)) for p in row_pairs]
    near_u = vmem(swap(u, "sector", near))
    far_u = vmem(far_swap(after(far_u, near_u)))
    near_part, sums, left_far, right_far, left_row, right_row = call(
        functools.partial(near_kernel, size, width, rows),
        (pltpu.VMEM((2,) + square, f32), pltpu.VMEM((8, 128), f32)) + (pltpu.VMEM(side, bf16),) * 2 + (pltpu.VMEM(last, bf16),) * 2,
        [HB] * 3 + [VM] * 3, (VM,) * 6,
        [pltpu.VMEM(few, bf16)] * 2 + [pltpu.VMEM(square, f32), dma((2, 2)), dma((1, 2)), dma((rows, 2)), dma], LONG,
    )(left_env, right_env, hbm(wavefunction), facts, u, near_u)
    near_part, left_row, right_row = vmem(near_part), vmem(left_row), vmem(right_row)
    far_part, part = call(
        functools.partial(far_kernel, size, width), (pltpu.VMEM(square, f32),) * 2, [VM] * 4, (VM,) * 2, cost=LONG,
    )(vmem(left_far), vmem(right_far), near_part, far_u)
    far_part = vmem(far_part)
    row_part, w, stats = call(
        functools.partial(first_kernel, size, width, rows),
        (pltpu.VMEM((rows,) + square, f32), pltpu.VMEM(square, bf16), jax.ShapeDtypeStruct((size, 1, 128), f32)),
        [VM] * (6 + rows), (VM,) * 3,
    )(vmem(part), facts, vmem(sums), u, left_row, right_row, *row_u)

    w = vmem(w)
    row_w = [vmem(swap(w, "sector", p)) for p in row_pairs]
    near_w = vmem(swap(w, "sector", near))
    far_w = vmem(far_swap(w))
    stats = lax.all_to_all(stats, "sector", 0, 0, tiled=True)
    hw = call(
        functools.partial(image_kernel, size, width, rows), pltpu.VMEM(square, f32), [VM] * (5 + rows) + [HB] * 2, VM,
        [pltpu.VMEM(every, bf16)] * 2 + [dma((2, 2))],
    )(*row_w, far_w, near_w, w, left_row, right_row, left_env, right_env)
    return call(
        functools.partial(second_kernel, size, width, rows, cells),
        (jax.ShapeDtypeStruct((1,) + square, f32),) * 2, [VM] * 6, (HB, HB),
        [pltpu.VMEM(square, f32)] * 2 + [dma((HALVES, 2))],
    )(facts, stats, vmem(hw), near_part, far_part, vmem(row_part))


def solution(mesh):
    placed = (
        P(("groups", "sector"), None, None),
        P(("groups", "sector"), None),
        P(("groups", "sector"), None, None, None),
        P(("groups", "sector"), None, None, None),
    )
    return jax.shard_map(
        body,
        mesh=mesh,
        in_specs=placed,
        out_specs=(P(("groups", "sector"), None, None), P(("groups", "sector"), None, None)),
        check_vma=False,
    )
```

```python
import functools

import jax
import jax.numpy as jnp
from jax import lax
from jax.experimental import pallas as pl
from jax.experimental.pallas import tpu as pltpu
from jax.sharding import PartitionSpec as P

QD = 8
SCALE = 1024.0
QUARTERS = 4
HALVES = 2
NT = (((1,), (1,)), ((), ()))
VM = pl.BlockSpec(memory_space=pltpu.VMEM)
HB = pl.BlockSpec(memory_space=pltpu.HBM)
AN = pl.BlockSpec(memory_space=pl.ANY)
COST = pl.CostEstimate(flops=1, bytes_accessed=1, transcendentals=0)
LONG = pl.CostEstimate(flops=4000000000, bytes_accessed=1, transcendentals=0)
PARAMS = pltpu.CompilerParams(vmem_limit_bytes=16 * 1024 * 1024)


def vmem(x):
    return pltpu.with_memory_space_constraint(x, pltpu.VMEM)


def hbm(x):
    return pltpu.with_memory_space_constraint(x, pltpu.HBM)


def call(kernel, out_shape, in_specs, out_specs, scratch=(), cost=COST, aliases={}):
    return pl.pallas_call(
        kernel, out_shape=out_shape, in_specs=in_specs, out_specs=out_specs, scratch_shapes=list(scratch),
        compiler_params=PARAMS, cost_estimate=cost, input_output_aliases=aliases,
    )


def swap(x, axis, pairs):
    to = {a: b for p in pairs for a, b in (p, p[::-1])}
    return lax.ppermute(x, axis, [(s, to.get(s, s)) for s in range(lax.axis_size(axis))])


def swap_pairs(size):
    rows = size // QD
    near = [(s, s + 1) for s in range(0, size, 2)]
    row_even = [(s, s + QD) for r in range(0, rows - 1, 2) for s in range(r * QD, r * QD + QD)]
    row_odd = [(s, s + QD) for r in range(1, rows - 1, 2) for s in range(r * QD, r * QD + QD)]
    return near, [p for p in (row_even, row_odd) if p]


def far_swap(x):
    groups, size = lax.axis_size("groups"), lax.axis_size("sector")
    pairs = []
    for g in range(groups):
        for s in range(size):
            if s % QD == 0 or s % QD == QD - 1:
                to, partner = (g ^ 1 if g ^ 1 < groups else g), s
            else:
                to, partner = g, s + 1 if s % 2 else s - 1
            pairs.append((g * size + s, to * size + partner))
    return lax.ppermute(x, ("groups", "sector"), pairs)


def place(size, width):
    me = lax.axis_index("sector")
    column = lax.rem(me, QD)
    odd = lax.rem(me, 2) == 1
    row_odd = lax.rem(lax.div(me, QD), 2) == 1
    low, high, down, up = 2, 2 + width, 2 + 2 * width, 2 + 3 * width
    offsets = [jnp.where(odd, low, high), jnp.where(odd, high, low),
               jnp.where(row_odd, down, up), jnp.where(row_odd, up, down)]
    partners = [jnp.where(odd, me - 1, me + 1), jnp.where(odd, me + 1, me - 1),
                jnp.where(row_odd, me - QD, me + QD), jnp.where(row_odd, me + QD, me - QD)]
    there = [(column != 0) & (column != QD - 1),
             True if size // QD % 2 == 0 else (partners[2] >= 0) & (partners[2] < size),
             (partners[3] >= 0) & (partners[3] < size)]
    partners = [me] + [jnp.clip(p, 0, size - 1) for p in partners]
    return offsets, partners, there


def live(facts, shape):
    row_ok = lax.broadcasted_iota(jnp.int32, shape, 0).astype(jnp.float32) < facts[1:2, 0:1]
    col_ok = lax.broadcasted_iota(jnp.int32, shape, 1).astype(jnp.float32) < facts[2:3, 0:1]
    return row_ok & col_ok


def total(x):
    return jnp.sum(jnp.sum(x, axis=0, keepdims=True), axis=1, keepdims=True)


def only(there, block):
    return block if there is True else jnp.where(there, block, jnp.zeros_like(block))


def terms(src, left_ref, right_ref, first, count):
    size = src.shape[0]
    right = right_ref[pl.ds(first, count)].reshape(count * size, size)
    partial_t = lax.dot_general(right, src, NT, preferred_element_type=jnp.float32).astype(jnp.bfloat16)
    left = jnp.concatenate([left_ref[first + k] for k in range(count)], axis=1)
    partial_t = jnp.concatenate([partial_t[k * size : (k + 1) * size] for k in range(count)], axis=1)
    return lax.dot_general(left, partial_t, NT, preferred_element_type=jnp.float32)


def fetch(left_hbm, right_hbm, left_ref, right_ref, sems, spans, start=True):
    copies = []
    at = 0
    for n, (offset, count) in enumerate(spans):
        pair = [
            pltpu.make_async_copy(source.at[0, pl.ds(offset, count)], target.at[pl.ds(at, count)], sems.at[n, e])
            for e, (source, target) in enumerate(((right_hbm, right_ref), (left_hbm, left_ref)))
        ]
        for copy in pair if start else ():
            copy.start()
        copies.append(pair)
        at += count
    return copies


def finish(copies):
    for copy in copies:
        copy.wait()


def start_kernel(wave_hbm, dims_hbm, *refs):
    u_refs, (facts_ref, wave_ref, dims_ref, sems) = refs[:2], refs[2:]
    size = wave_ref.shape[0]
    step = size // QUARTERS
    dims_copy = pltpu.make_async_copy(dims_hbm, dims_ref, sems.at[QUARTERS])
    dims_copy.start()
    copies = [
        pltpu.make_async_copy(wave_hbm.at[0, pl.ds(n * step, step)], wave_ref.at[pl.ds(n * step, step)], sems.at[n])
        for n in range(QUARTERS)
    ]
    for copy in copies:
        copy.start()
    dims_copy.wait()
    row_count, col_count = dims_ref[0, 0], dims_ref[0, 1]
    lines = lax.broadcasted_iota(jnp.int32, (8, 128), 0)
    facts_ref[...] = jnp.where(lines == 1, row_count, jnp.where(lines == 2, col_count, 0)).astype(jnp.float32)
    col_ok = lax.broadcasted_iota(jnp.int32, (step, size), 1) < col_count
    row = lax.broadcasted_iota(jnp.int32, (step, size), 0)
    for n, copy in enumerate(copies):
        copy.wait()
        rows = pl.ds(n * step, step)
        held = jnp.where((row < row_count - n * step) & col_ok, wave_ref[rows], 0.0)
        block = (held * SCALE).astype(jnp.bfloat16)
        for ref in u_refs:
            ref[rows] = block


def pass_kernel(*refs):
    pass


def after(held, first):
    return call(pass_kernel, pltpu.VMEM(held.shape, held.dtype), [AN] * 2, AN, aliases={0: 0})(vmem(held), first)


def near_kernel(size, width, rows, left_hbm, right_hbm, wave_hbm, facts_ref, self_ref, near_ref, out_ref, sums_ref,
                left_far, right_far, left_row, right_row, left_own, right_own, wave_ref, sems, far_sems, row_sems, wave_sem):
    offsets, _, _ = place(size, width)
    wave_copy = pltpu.make_async_copy(wave_hbm.at[0], wave_ref, wave_sem)
    own = fetch(left_hbm, right_hbm, left_own, right_own, sems, [(0, 2), (offsets[0], width)])
    wave_copy.start()
    later = fetch(left_hbm, right_hbm, left_far, right_far, far_sems, [(offsets[1], width)])
    later += fetch(left_hbm, right_hbm, left_row, right_row, row_sems, [(o, width) for o in offsets[2 : 2 + rows]])
    u = self_ref[...].astype(jnp.float32)
    lines = lax.broadcasted_iota(jnp.int32, (8, 128), 0)
    sums = jnp.where(lines == 1, total(u * u), 0.0)
    finish(own[0])
    out_ref[0] = terms(self_ref[...], left_own, right_own, 0, 2)
    finish(own[1])
    out_ref[1] = terms(near_ref[...], left_own, right_own, 2, width)
    wave_copy.wait()
    held = jnp.where(live(facts_ref[...], wave_ref.shape), wave_ref[...], 0.0)
    sums_ref[...] = jnp.where(lines == 0, total(held * held), sums)
    for pair in later:
        finish(pair)


def far_kernel(size, width, left_ref, right_ref, near_part_ref, far_ref, out_ref, sum_ref):
    _, _, there = place(size, width)
    part = terms(only(there[0], far_ref[...]), left_ref, right_ref, 0, width)
    out_ref[...] = part
    sum_ref[...] = near_part_ref[0] + near_part_ref[1] + part


def first_kernel(size, width, rows, *refs):
    part_ref, facts_ref, sums_ref, u_ref, left_ref, right_ref = refs[:6]
    row_refs, (out_ref, w_ref, stats_ref) = refs[6 : 6 + rows], refs[6 + rows :]
    _, _, there = place(size, width)
    image = part_ref[...]
    for r, source in enumerate(row_refs):
        piece = terms(only(there[1 + r], source[...]), left_ref, right_ref, r * width, width)
        out_ref[r] = piece
        image = image + piece
    image = jnp.where(live(facts_ref[...], image.shape), image, 0.0)
    u = u_ref[...].astype(jnp.float32)
    square = sums_ref[1:2, 0:1]
    cross = total(u * image)
    rho = jnp.where(square > 0.0, cross / square, 0.0)
    w = image - rho * u
    w_ref[...] = w.astype(jnp.bfloat16)
    lane = lax.broadcasted_iota(jnp.int32, (1, 128), 1)
    stats = jnp.zeros((1, 128), jnp.float32)
    for n, value in enumerate((sums_ref[0:1, 0:1], square, cross, total(w * w), rho)):
        stats = jnp.where(lane == n, value, stats)
    for n in range(stats_ref.shape[0]):
        stats_ref[n] = stats


def image_kernel(size, width, rows, *refs):
    row_refs, refs = refs[:rows], refs[rows:]
    far_ref, near_ref, self_ref, left_row, right_row, left_hbm, right_hbm, out_ref, left_own, right_own, sems = refs
    _, _, there = place(size, width)
    own = fetch(left_hbm, right_hbm, left_own, right_own, sems, [(0, 2 + width), (2 + width, width)], False)
    image = None
    for r, source in enumerate(row_refs):
        piece = terms(only(there[1 + r], source[...]), left_row, right_row, r * width, width)
        image = piece if image is None else image + piece
    out_ref[...] = image

    @pl.when(lax.axis_index("sector") >= 0)
    def _():
        for pair in own:
            for copy in pair:
                copy.start()

    odd = lax.rem(lax.axis_index("sector"), 2) == 1
    near, far = near_ref[...], only(there[0], far_ref[...])
    finish(own[0])
    image = out_ref[...] + terms(self_ref[...], left_own, right_own, 0, 2)
    image = image + terms(jnp.where(odd, near, far), left_own, right_own, 2, width)
    finish(own[1])
    out_ref[...] = image + terms(jnp.where(odd, far, near), left_own, right_own, 2 + width, width)


def second_kernel(size, width, rows, cells, facts_ref, stats_ref, hw_ref, near_part_ref, far_part_ref, row_part_ref,
                  first_hbm, second_hbm, first_ref, second_ref, sems):
    _, partners, _ = place(size, width)
    facts = facts_ref[...]
    stats = stats_ref[:, 0, :]
    sums = jnp.sum(stats, axis=0, keepdims=True)
    start, square, cross, inner = (sums[:, i : i + 1] for i in range(4))
    scale = lax.rsqrt(start / cells + 1e-06) * (1.0 / SCALE)
    rho = cross / square
    gap = stats[:, 4:5] - rho
    residual = inner + jnp.sum(stats[:, 1:2] * gap * gap, axis=0, keepdims=True)
    second_scale = scale * lax.rsqrt(scale * scale * (residual / cells) + 1e-06)
    gaps = [stats_ref[partner, :, 4:5] - rho for partner in partners[: 3 + rows]]
    block = hw_ref.shape[0]
    step = block // HALVES
    col_ok = lax.broadcasted_iota(jnp.int32, (step, block), 1).astype(jnp.float32) < facts[2:3, 0:1]
    row = lax.broadcasted_iota(jnp.int32, (step, block), 0).astype(jnp.float32)
    copies = []
    for n in range(HALVES):
        lines = pl.ds(n * step, step)
        parts = [near_part_ref[0, lines], near_part_ref[1, lines], far_part_ref[lines]]
        parts += [row_part_ref[r, lines] for r in range(rows)]
        cell = (row + n * step < facts[1:2, 0:1]) & col_ok
        image = hw_ref[lines]
        for gap, part in zip(gaps, parts):
            image = image + gap * part
        second_ref[lines] = jnp.where(cell, image, 0.0) * second_scale
        first_ref[lines] = jnp.where(cell, sum(parts[1:], parts[0]), 0.0) * scale
        for e, (source, target) in enumerate(((second_ref, second_hbm), (first_ref, first_hbm))):
            copies.append(pltpu.make_async_copy(source.at[lines], target.at[0, lines], sems.at[n, e]))
            copies[-1].start()
    finish(copies)


def body(wavefunction, sector_dims, left_env, right_env):
    size = lax.axis_size("sector")
    block = wavefunction.shape[1]
    square = (block, block)
    width = (right_env.shape[1] - 2) // 4
    near, row_pairs = swap_pairs(size)
    rows = len(row_pairs)
    cells = float(size * block * block)
    few, every, side, last = ((n,) + square for n in (2 + width, 2 + 2 * width, width, rows * width))
    f32, bf16 = jnp.float32, jnp.bfloat16
    dma = pltpu.SemaphoreType.DMA

    u, far_u, facts = call(
        start_kernel, (pltpu.VMEM(square, bf16),) * 2 + (pltpu.VMEM((8, 128), f32),), [HB, HB], (VM,) * 3,
        [pltpu.VMEM(square, f32), pltpu.SMEM((1, 2), jnp.int32), dma((QUARTERS + 1,))],
    )(hbm(wavefunction), hbm(sector_dims))

    left_env, right_env = hbm(left_env), hbm(right_env)
    u, facts = vmem(u), vmem(facts)
    row_u = [vmem(swap(u, "sector", p)) for p in row_pairs]
    near_u = vmem(swap(u, "sector", near))
    far_u = vmem(far_swap(after(far_u, near_u)))
    near_part, sums, left_far, right_far, left_row, right_row = call(
        functools.partial(near_kernel, size, width, rows),
        (pltpu.VMEM((2,) + square, f32), pltpu.VMEM((8, 128), f32)) + (pltpu.VMEM(side, bf16),) * 2 + (pltpu.VMEM(last, bf16),) * 2,
        [HB] * 3 + [VM] * 3, (VM,) * 6,
        [pltpu.VMEM(few, bf16)] * 2 + [pltpu.VMEM(square, f32), dma((2, 2)), dma((1, 2)), dma((rows, 2)), dma], LONG,
    )(left_env, right_env, hbm(wavefunction), facts, u, near_u)
    near_part, left_row, right_row = vmem(near_part), vmem(left_row), vmem(right_row)
    far_part, part = call(
        functools.partial(far_kernel, size, width), (pltpu.VMEM(square, f32),) * 2, [VM] * 4, (VM,) * 2, cost=LONG,
    )(vmem(left_far), vmem(right_far), near_part, far_u)
    far_part = vmem(far_part)
    row_part, w, stats = call(
        functools.partial(first_kernel, size, width, rows),
        (pltpu.VMEM((rows,) + square, f32), pltpu.VMEM(square, bf16), jax.ShapeDtypeStruct((size, 1, 128), f32)),
        [VM] * (6 + rows), (VM,) * 3,
    )(vmem(part), facts, vmem(sums), u, left_row, right_row, *row_u)

    w = vmem(w)
    row_w = [vmem(swap(w, "sector", p)) for p in row_pairs]
    near_w = vmem(swap(w, "sector", near))
    far_w = vmem(far_swap(w))
    stats = lax.all_to_all(stats, "sector", 0, 0, tiled=True)
    hw = call(
        functools.partial(image_kernel, size, width, rows), pltpu.VMEM(square, f32), [VM] * (5 + rows) + [HB] * 2, VM,
        [pltpu.VMEM(every, bf16)] * 2 + [dma((2, 2))],
    )(*row_w, far_w, near_w, w, left_row, right_row, left_env, right_env)
    return call(
        functools.partial(second_kernel, size, width, rows, cells),
        (jax.ShapeDtypeStruct((1,) + square, f32),) * 2, [VM] * 6, (HB, HB),
        [pltpu.VMEM(square, f32)] * 2 + [dma((HALVES, 2))],
    )(facts, stats, vmem(hw), near_part, far_part, vmem(row_part))


def solution(mesh):
    placed = (
        P(("groups", "sector"), None, None),
        P(("groups", "sector"), None),
        P(("groups", "sector"), None, None, None),
        P(("groups", "sector"), None, None, None),
    )
    return jax.shard_map(
        body,
        mesh=mesh,
        in_specs=placed,
        out_specs=(P(("groups", "sector"), None, None), P(("groups", "sector"), None, None)),
        check_vma=False,
    )
```

```python
import functools

import jax
import jax.numpy as jnp
from jax import lax
from jax.experimental import pallas as pl
from jax.experimental.pallas import tpu as pltpu
from jax.sharding import PartitionSpec as P

QD = 8
SCALE = 1024.0
QUARTERS = 4
HALVES = 2
NT = (((1,), (1,)), ((), ()))
VM = pl.BlockSpec(memory_space=pltpu.VMEM)
HB = pl.BlockSpec(memory_space=pltpu.HBM)
AN = pl.BlockSpec(memory_space=pl.ANY)
COST = pl.CostEstimate(flops=1, bytes_accessed=1, transcendentals=0)
LONG = pl.CostEstimate(flops=4000000000, bytes_accessed=1, transcendentals=0)
PARAMS = pltpu.CompilerParams(vmem_limit_bytes=16 * 1024 * 1024)


def vmem(x):
    return pltpu.with_memory_space_constraint(x, pltpu.VMEM)


def hbm(x):
    return pltpu.with_memory_space_constraint(x, pltpu.HBM)


def call(kernel, out_shape, in_specs, out_specs, scratch=(), cost=COST, aliases={}):
    return pl.pallas_call(
        kernel, out_shape=out_shape, in_specs=in_specs, out_specs=out_specs, scratch_shapes=list(scratch),
        compiler_params=PARAMS, cost_estimate=cost, input_output_aliases=aliases,
    )


def swap(x, axis, pairs):
    to = {a: b for p in pairs for a, b in (p, p[::-1])}
    return lax.ppermute(x, axis, [(s, to.get(s, s)) for s in range(lax.axis_size(axis))])


def swap_pairs(size):
    rows = size // QD
    near = [(s, s + 1) for s in range(0, size, 2)]
    row_even = [(s, s + QD) for r in range(0, rows - 1, 2) for s in range(r * QD, r * QD + QD)]
    row_odd = [(s, s + QD) for r in range(1, rows - 1, 2) for s in range(r * QD, r * QD + QD)]
    return near, [p for p in (row_even, row_odd) if p]


def far_swap(x):
    groups, size = lax.axis_size("groups"), lax.axis_size("sector")
    pairs = []
    for g in range(groups):
        for s in range(size):
            if s % QD == 0 or s % QD == QD - 1:
                to, partner = (g ^ 1 if g ^ 1 < groups else g), s
            else:
                to, partner = g, s + 1 if s % 2 else s - 1
            pairs.append((g * size + s, to * size + partner))
    return lax.ppermute(x, ("groups", "sector"), pairs)


def place(size, width):
    me = lax.axis_index("sector")
    column = lax.rem(me, QD)
    odd = lax.rem(me, 2) == 1
    row_odd = lax.rem(lax.div(me, QD), 2) == 1
    low, high, down, up = 2, 2 + width, 2 + 2 * width, 2 + 3 * width
    offsets = [jnp.where(odd, low, high), jnp.where(odd, high, low),
               jnp.where(row_odd, down, up), jnp.where(row_odd, up, down)]
    partners = [jnp.where(odd, me - 1, me + 1), jnp.where(odd, me + 1, me - 1),
                jnp.where(row_odd, me - QD, me + QD), jnp.where(row_odd, me + QD, me - QD)]
    there = [(column != 0) & (column != QD - 1),
             True if size // QD % 2 == 0 else (partners[2] >= 0) & (partners[2] < size),
             (partners[3] >= 0) & (partners[3] < size)]
    partners = [me] + [jnp.clip(p, 0, size - 1) for p in partners]
    return offsets, partners, there


def live(facts, shape):
    row_ok = lax.broadcasted_iota(jnp.int32, shape, 0).astype(jnp.float32) < facts[1:2, 0:1]
    col_ok = lax.broadcasted_iota(jnp.int32, shape, 1).astype(jnp.float32) < facts[2:3, 0:1]
    return row_ok & col_ok


def total(x):
    return jnp.sum(jnp.sum(x, axis=0, keepdims=True), axis=1, keepdims=True)


def only(there, block):
    return block if there is True else jnp.where(there, block, jnp.zeros_like(block))


def terms(src, left_ref, right_ref, first, count):
    size = src.shape[0]
    right = right_ref[pl.ds(first, count)].reshape(count * size, size)
    partial_t = lax.dot_general(right, src, NT, preferred_element_type=jnp.float32).astype(jnp.bfloat16)
    left = jnp.concatenate([left_ref[first + k] for k in range(count)], axis=1)
    partial_t = jnp.concatenate([partial_t[k * size : (k + 1) * size] for k in range(count)], axis=1)
    return lax.dot_general(left, partial_t, NT, preferred_element_type=jnp.float32)


def fetch(left_hbm, right_hbm, left_ref, right_ref, sems, spans):
    copies = []
    at = 0
    for n, (offset, count) in enumerate(spans):
        pair = [
            pltpu.make_async_copy(source.at[0, pl.ds(offset, count)], target.at[pl.ds(at, count)], sems.at[n, e])
            for e, (source, target) in enumerate(((right_hbm, right_ref), (left_hbm, left_ref)))
        ]
        for copy in pair:
            copy.start()
        copies.append(pair)
        at += count
    return copies


def finish(copies):
    for copy in copies:
        copy.wait()


def start_kernel(wave_hbm, dims_hbm, *refs):
    u_refs, (facts_ref, wave_ref, dims_ref, sems) = refs[:2], refs[2:]
    size = wave_ref.shape[0]
    step = size // QUARTERS
    dims_copy = pltpu.make_async_copy(dims_hbm, dims_ref, sems.at[QUARTERS])
    dims_copy.start()
    copies = [
        pltpu.make_async_copy(wave_hbm.at[0, pl.ds(n * step, step)], wave_ref.at[pl.ds(n * step, step)], sems.at[n])
        for n in range(QUARTERS)
    ]
    for copy in copies:
        copy.start()
    dims_copy.wait()
    row_count, col_count = dims_ref[0, 0], dims_ref[0, 1]
    lines = lax.broadcasted_iota(jnp.int32, (8, 128), 0)
    facts_ref[...] = jnp.where(lines == 1, row_count, jnp.where(lines == 2, col_count, 0)).astype(jnp.float32)
    col_ok = lax.broadcasted_iota(jnp.int32, (step, size), 1) < col_count
    row = lax.broadcasted_iota(jnp.int32, (step, size), 0)
    for n, copy in enumerate(copies):
        copy.wait()
        rows = pl.ds(n * step, step)
        held = jnp.where((row < row_count - n * step) & col_ok, wave_ref[rows], 0.0)
        block = (held * SCALE).astype(jnp.bfloat16)
        for ref in u_refs:
            ref[rows] = block


def pass_kernel(*refs):
    pass


def after(held, first):
    return call(pass_kernel, pltpu.VMEM(held.shape, held.dtype), [AN] * 2, AN, aliases={0: 0})(vmem(held), first)


def near_kernel(size, width, rows, left_hbm, right_hbm, wave_hbm, facts_ref, self_ref, near_ref, out_ref, sums_ref,
                left_own, right_own, left_far, right_far, left_row, right_row, wave_ref, sems, far_sems, row_sems, wave_sem):
    offsets, _, _ = place(size, width)
    wave_copy = pltpu.make_async_copy(wave_hbm.at[0], wave_ref, wave_sem)
    own = fetch(left_hbm, right_hbm, left_own, right_own, sems, [(0, 2), (offsets[0], width)])
    wave_copy.start()
    later = fetch(left_hbm, right_hbm, left_far, right_far, far_sems, [(offsets[1], width)])
    later += fetch(left_hbm, right_hbm, left_row, right_row, row_sems, [(o, width) for o in offsets[2 : 2 + rows]])
    u = self_ref[...].astype(jnp.float32)
    lines = lax.broadcasted_iota(jnp.int32, (8, 128), 0)
    sums = jnp.where(lines == 1, total(u * u), 0.0)
    finish(own[0])
    out_ref[0] = terms(self_ref[...], left_own, right_own, 0, 2)
    finish(own[1])
    out_ref[1] = terms(near_ref[...], left_own, right_own, 2, width)
    wave_copy.wait()
    held = jnp.where(live(facts_ref[...], wave_ref.shape), wave_ref[...], 0.0)
    sums_ref[...] = jnp.where(lines == 0, total(held * held), sums)
    for pair in later:
        finish(pair)


def far_kernel(size, width, left_ref, right_ref, near_part_ref, far_ref, out_ref, sum_ref):
    _, _, there = place(size, width)
    part = terms(only(there[0], far_ref[...]), left_ref, right_ref, 0, width)
    out_ref[...] = part
    sum_ref[...] = near_part_ref[0] + near_part_ref[1] + part


def first_kernel(size, width, rows, *refs):
    part_ref, facts_ref, sums_ref, u_ref, left_ref, right_ref = refs[:6]
    row_refs, (out_ref, w_ref, stats_ref) = refs[6 : 6 + rows], refs[6 + rows :]
    _, _, there = place(size, width)
    image = part_ref[...]
    for r, source in enumerate(row_refs):
        piece = terms(only(there[1 + r], source[...]), left_ref, right_ref, r * width, width)
        out_ref[r] = piece
        image = image + piece
    image = jnp.where(live(facts_ref[...], image.shape), image, 0.0)
    u = u_ref[...].astype(jnp.float32)
    square = sums_ref[1:2, 0:1]
    cross = total(u * image)
    rho = jnp.where(square > 0.0, cross / square, 0.0)
    w = image - rho * u
    w_ref[...] = w.astype(jnp.bfloat16)
    lane = lax.broadcasted_iota(jnp.int32, (1, 128), 1)
    stats = jnp.zeros((1, 128), jnp.float32)
    for n, value in enumerate((sums_ref[0:1, 0:1], square, cross, total(w * w), rho)):
        stats = jnp.where(lane == n, value, stats)
    for n in range(stats_ref.shape[0]):
        stats_ref[n] = stats


def image_kernel(size, width, rows, *refs):
    near_ref, far_ref, refs = refs[0], refs[1], refs[2:]
    row_refs, refs = refs[:rows], refs[rows:]
    self_ref, left_row, right_row, left_far, right_far, left_own, right_own, _, out_ref = refs
    _, _, there = place(size, width)
    image = terms(self_ref[...], left_own, right_own, 0, 2)
    image = image + terms(near_ref[...], left_own, right_own, 2, width)
    image = image + terms(only(there[0], far_ref[...]), left_far, right_far, 0, width)
    for r, source in enumerate(row_refs):
        image = image + terms(only(there[1 + r], source[...]), left_row, right_row, r * width, width)
    out_ref[...] = image


def second_kernel(size, width, rows, cells, facts_ref, stats_ref, hw_ref, near_part_ref, far_part_ref, row_part_ref,
                  first_hbm, second_hbm, first_ref, second_ref, sems):
    _, partners, _ = place(size, width)
    facts = facts_ref[...]
    stats = stats_ref[:, 0, :]
    sums = jnp.sum(stats, axis=0, keepdims=True)
    start, square, cross, inner = (sums[:, i : i + 1] for i in range(4))
    scale = lax.rsqrt(start / cells + 1e-06) * (1.0 / SCALE)
    rho = cross / square
    gap = stats[:, 4:5] - rho
    residual = inner + jnp.sum(stats[:, 1:2] * gap * gap, axis=0, keepdims=True)
    second_scale = scale * lax.rsqrt(scale * scale * (residual / cells) + 1e-06)
    gaps = [stats_ref[partner, :, 4:5] - rho for partner in partners[: 3 + rows]]
    block = hw_ref.shape[0]
    step = block // HALVES
    col_ok = lax.broadcasted_iota(jnp.int32, (step, block), 1).astype(jnp.float32) < facts[2:3, 0:1]
    row = lax.broadcasted_iota(jnp.int32, (step, block), 0).astype(jnp.float32)
    copies = []
    for n in range(HALVES):
        lines = pl.ds(n * step, step)
        parts = [near_part_ref[0, lines], near_part_ref[1, lines], far_part_ref[lines]]
        parts += [row_part_ref[r, lines] for r in range(rows)]
        cell = (row + n * step < facts[1:2, 0:1]) & col_ok
        image = hw_ref[lines]
        for gap, part in zip(gaps, parts):
            image = image + gap * part
        second_ref[lines] = jnp.where(cell, image, 0.0) * second_scale
        first_ref[lines] = jnp.where(cell, sum(parts[1:], parts[0]), 0.0) * scale
        for e, (source, target) in enumerate(((second_ref, second_hbm), (first_ref, first_hbm))):
            copies.append(pltpu.make_async_copy(source.at[lines], target.at[0, lines], sems.at[n, e]))
            copies[-1].start()
    finish(copies)


def body(wavefunction, sector_dims, left_env, right_env):
    size = lax.axis_size("sector")
    block = wavefunction.shape[1]
    square = (block, block)
    width = (right_env.shape[1] - 2) // 4
    near, row_pairs = swap_pairs(size)
    rows = len(row_pairs)
    cells = float(size * block * block)
    few, side, last = ((n,) + square for n in (2 + width, width, rows * width))
    f32, bf16 = jnp.float32, jnp.bfloat16
    dma = pltpu.SemaphoreType.DMA

    u, far_u, facts = call(
        start_kernel, (pltpu.VMEM(square, bf16),) * 2 + (pltpu.VMEM((8, 128), f32),), [HB, HB], (VM,) * 3,
        [pltpu.VMEM(square, f32), pltpu.SMEM((1, 2), jnp.int32), dma((QUARTERS + 1,))],
    )(hbm(wavefunction), hbm(sector_dims))

    left_env, right_env = hbm(left_env), hbm(right_env)
    u, facts = vmem(u), vmem(facts)
    row_u = [vmem(swap(u, "sector", p)) for p in row_pairs]
    near_u = vmem(swap(u, "sector", near))
    far_u = vmem(far_swap(after(far_u, near_u)))
    near_part, sums, left_own, right_own, left_far, right_far, left_row, right_row = call(
        functools.partial(near_kernel, size, width, rows),
        (pltpu.VMEM((2,) + square, f32), pltpu.VMEM((8, 128), f32))
        + (pltpu.VMEM(few, bf16),) * 2 + (pltpu.VMEM(side, bf16),) * 2 + (pltpu.VMEM(last, bf16),) * 2,
        [HB] * 3 + [VM] * 3, (VM,) * 8,
        [pltpu.VMEM(square, f32), dma((2, 2)), dma((1, 2)), dma((rows, 2)), dma], LONG,
    )(left_env, right_env, hbm(wavefunction), facts, u, near_u)
    near_part, left_row, right_row = vmem(near_part), vmem(left_row), vmem(right_row)
    left_own, right_own, left_far, right_far = map(vmem, (left_own, right_own, left_far, right_far))
    far_part, part = call(
        functools.partial(far_kernel, size, width), (pltpu.VMEM(square, f32),) * 2, [VM] * 4, (VM,) * 2, cost=LONG,
    )(left_far, right_far, near_part, far_u)
    far_part = vmem(far_part)
    row_part, w, stats = call(
        functools.partial(first_kernel, size, width, rows),
        (pltpu.VMEM((rows,) + square, f32), pltpu.VMEM(square, bf16), jax.ShapeDtypeStruct((size, 1, 128), f32)),
        [VM] * (6 + rows), (VM,) * 3,
    )(vmem(part), facts, vmem(sums), u, left_row, right_row, *row_u)

    w = vmem(w)
    row_w = [vmem(swap(w, "sector", p)) for p in row_pairs]
    near_w = vmem(swap(w, "sector", near))
    far_w = vmem(far_swap(w))
    stats = lax.all_to_all(stats, "sector", 0, 0, tiled=True)
    hw = call(
        functools.partial(image_kernel, size, width, rows), pltpu.VMEM(square, f32), [VM] * (9 + rows) + [AN], VM,
    )(near_w, far_w, *row_w, w, left_row, right_row, left_far, right_far, left_own, right_own, stats)
    return call(
        functools.partial(second_kernel, size, width, rows, cells),
        (jax.ShapeDtypeStruct((1,) + square, f32),) * 2, [VM] * 6, (HB, HB),
        [pltpu.VMEM(square, f32)] * 2 + [dma((HALVES, 2))],
    )(facts, stats, vmem(hw), near_part, far_part, vmem(row_part))


def solution(mesh):
    placed = (
        P(("groups", "sector"), None, None),
        P(("groups", "sector"), None),
        P(("groups", "sector"), None, None, None),
        P(("groups", "sector"), None, None, None),
    )
    return jax.shard_map(
        body,
        mesh=mesh,
        in_specs=placed,
        out_specs=(P(("groups", "sector"), None, None), P(("groups", "sector"), None, None)),
        check_vma=False,
    )
```

```python
import functools

import jax
import jax.numpy as jnp
from jax import lax
from jax.experimental import pallas as pl
from jax.experimental.pallas import tpu as pltpu
from jax.sharding import PartitionSpec as P

QD = 8
SCALE = 1024.0
QUARTERS = 4
HALVES = 2
NT = (((1,), (1,)), ((), ()))
VM = pl.BlockSpec(memory_space=pltpu.VMEM)
HB = pl.BlockSpec(memory_space=pltpu.HBM)
AN = pl.BlockSpec(memory_space=pl.ANY)
COST = pl.CostEstimate(flops=1, bytes_accessed=1, transcendentals=0)
LONG = pl.CostEstimate(flops=4000000000, bytes_accessed=1, transcendentals=0)
PARAMS = pltpu.CompilerParams(vmem_limit_bytes=16 * 1024 * 1024)


def vmem(x):
    return pltpu.with_memory_space_constraint(x, pltpu.VMEM)


def hbm(x):
    return pltpu.with_memory_space_constraint(x, pltpu.HBM)


def call(kernel, out_shape, in_specs, out_specs, scratch=(), cost=COST, aliases={}):
    return pl.pallas_call(
        kernel, out_shape=out_shape, in_specs=in_specs, out_specs=out_specs, scratch_shapes=list(scratch),
        compiler_params=PARAMS, cost_estimate=cost, input_output_aliases=aliases,
    )


def swap(x, axis, pairs):
    to = {a: b for p in pairs for a, b in (p, p[::-1])}
    return lax.ppermute(x, axis, [(s, to.get(s, s)) for s in range(lax.axis_size(axis))])


def swap_pairs(size):
    rows = size // QD
    near = [(s, s + 1) for s in range(0, size, 2)]
    row_even = [(s, s + QD) for r in range(0, rows - 1, 2) for s in range(r * QD, r * QD + QD)]
    row_odd = [(s, s + QD) for r in range(1, rows - 1, 2) for s in range(r * QD, r * QD + QD)]
    return near, [p for p in (row_even, row_odd) if p]


def far_swap(x):
    groups, size = lax.axis_size("groups"), lax.axis_size("sector")
    pairs = []
    for g in range(groups):
        for s in range(size):
            if s % QD == 0 or s % QD == QD - 1:
                to, partner = (g ^ 1 if g ^ 1 < groups else g), s
            else:
                to, partner = g, s + 1 if s % 2 else s - 1
            pairs.append((g * size + s, to * size + partner))
    return lax.ppermute(x, ("groups", "sector"), pairs)


def place(size, width):
    me = lax.axis_index("sector")
    column = lax.rem(me, QD)
    odd = lax.rem(me, 2) == 1
    row_odd = lax.rem(lax.div(me, QD), 2) == 1
    low, high, down, up = 2, 2 + width, 2 + 2 * width, 2 + 3 * width
    offsets = [jnp.where(odd, low, high), jnp.where(odd, high, low),
               jnp.where(row_odd, down, up), jnp.where(row_odd, up, down)]
    partners = [jnp.where(odd, me - 1, me + 1), jnp.where(odd, me + 1, me - 1),
                jnp.where(row_odd, me - QD, me + QD), jnp.where(row_odd, me + QD, me - QD)]
    there = [(column != 0) & (column != QD - 1),
             True if size // QD % 2 == 0 else (partners[2] >= 0) & (partners[2] < size),
             (partners[3] >= 0) & (partners[3] < size)]
    partners = [me] + [jnp.clip(p, 0, size - 1) for p in partners]
    return offsets, partners, there


def live(facts, shape):
    row_ok = lax.broadcasted_iota(jnp.int32, shape, 0).astype(jnp.float32) < facts[1:2, 0:1]
    col_ok = lax.broadcasted_iota(jnp.int32, shape, 1).astype(jnp.float32) < facts[2:3, 0:1]
    return row_ok & col_ok


def total(x):
    return jnp.sum(jnp.sum(x, axis=0, keepdims=True), axis=1, keepdims=True)


def only(there, block):
    return block if there is True else jnp.where(there, block, jnp.zeros_like(block))


def terms(src, left_ref, right_ref, first, count):
    size = src.shape[0]
    right = right_ref[pl.ds(first, count)].reshape(count * size, size)
    partial_t = lax.dot_general(right, src, NT, preferred_element_type=jnp.float32).astype(jnp.bfloat16)
    left = jnp.concatenate([left_ref[first + k] for k in range(count)], axis=1)
    partial_t = jnp.concatenate([partial_t[k * size : (k + 1) * size] for k in range(count)], axis=1)
    return lax.dot_general(left, partial_t, NT, preferred_element_type=jnp.float32)


def fetch(left_hbm, right_hbm, left_ref, right_ref, sems, spans):
    copies = []
    at = 0
    for n, (offset, count) in enumerate(spans):
        pair = [
            pltpu.make_async_copy(source.at[0, pl.ds(offset, count)], target.at[pl.ds(at, count)], sems.at[n, e])
            for e, (source, target) in enumerate(((right_hbm, right_ref), (left_hbm, left_ref)))
        ]
        for copy in pair:
            copy.start()
        copies.append(pair)
        at += count
    return copies


def finish(copies):
    for copy in copies:
        copy.wait()


def start_kernel(wave_hbm, dims_hbm, *refs):
    u_refs, (facts_ref, wave_ref, dims_ref, sems) = refs[:2], refs[2:]
    size = wave_ref.shape[0]
    step = size // QUARTERS
    dims_copy = pltpu.make_async_copy(dims_hbm, dims_ref, sems.at[QUARTERS])
    dims_copy.start()
    copies = [
        pltpu.make_async_copy(wave_hbm.at[0, pl.ds(n * step, step)], wave_ref.at[pl.ds(n * step, step)], sems.at[n])
        for n in range(QUARTERS)
    ]
    for copy in copies:
        copy.start()
    dims_copy.wait()
    row_count, col_count = dims_ref[0, 0], dims_ref[0, 1]
    lines = lax.broadcasted_iota(jnp.int32, (8, 128), 0)
    facts_ref[...] = jnp.where(lines == 1, row_count, jnp.where(lines == 2, col_count, 0)).astype(jnp.float32)
    col_ok = lax.broadcasted_iota(jnp.int32, (step, size), 1) < col_count
    row = lax.broadcasted_iota(jnp.int32, (step, size), 0)
    for n, copy in enumerate(copies):
        copy.wait()
        rows = pl.ds(n * step, step)
        held = jnp.where((row < row_count - n * step) & col_ok, wave_ref[rows], 0.0)
        block = (held * SCALE).astype(jnp.bfloat16)
        for ref in u_refs:
            ref[rows] = block


def pass_kernel(*refs):
    pass


def after(held, first):
    return call(pass_kernel, pltpu.VMEM(held.shape, held.dtype), [AN] * 2, AN, aliases={0: 0})(vmem(held), first)


def near_kernel(size, width, rows, left_hbm, right_hbm, wave_hbm, facts_ref, self_ref, near_ref, out_ref, sums_ref,
                left_far, right_far, left_row, right_row, left_own, right_own, wave_ref, sems, far_sems, row_sems, wave_sem):
    offsets, _, _ = place(size, width)
    wave_copy = pltpu.make_async_copy(wave_hbm.at[0], wave_ref, wave_sem)
    own = fetch(left_hbm, right_hbm, left_own, right_own, sems, [(0, 2), (offsets[0], width)])
    wave_copy.start()
    later = fetch(left_hbm, right_hbm, left_far, right_far, far_sems, [(offsets[1], width)])
    later += fetch(left_hbm, right_hbm, left_row, right_row, row_sems, [(o, width) for o in offsets[2 : 2 + rows]])
    u = self_ref[...].astype(jnp.float32)
    lines = lax.broadcasted_iota(jnp.int32, (8, 128), 0)
    sums = jnp.where(lines == 1, total(u * u), 0.0)
    finish(own[0])
    out_ref[0] = terms(self_ref[...], left_own, right_own, 0, 2)
    finish(own[1])
    out_ref[1] = terms(near_ref[...], left_own, right_own, 2, width)
    wave_copy.wait()
    held = jnp.where(live(facts_ref[...], wave_ref.shape), wave_ref[...], 0.0)
    sums_ref[...] = jnp.where(lines == 0, total(held * held), sums)
    for pair in later:
        finish(pair)


def far_kernel(size, width, left_ref, right_ref, near_part_ref, far_ref, out_ref, sum_ref):
    _, _, there = place(size, width)
    part = terms(only(there[0], far_ref[...]), left_ref, right_ref, 0, width)
    out_ref[...] = part
    sum_ref[...] = near_part_ref[0] + near_part_ref[1] + part


def first_kernel(size, width, rows, *refs):
    part_ref, facts_ref, sums_ref, u_ref, left_ref, right_ref = refs[:6]
    row_refs, (out_ref, w_ref, stats_ref) = refs[6 : 6 + rows], refs[6 + rows :]
    _, _, there = place(size, width)
    image = part_ref[...]
    for r, source in enumerate(row_refs):
        piece = terms(only(there[1 + r], source[...]), left_ref, right_ref, r * width, width)
        out_ref[r] = piece
        image = image + piece
    image = jnp.where(live(facts_ref[...], image.shape), image, 0.0)
    u = u_ref[...].astype(jnp.float32)
    square = sums_ref[1:2, 0:1]
    cross = total(u * image)
    rho = jnp.where(square > 0.0, cross / square, 0.0)
    w = image - rho * u
    w_ref[...] = w.astype(jnp.bfloat16)
    lane = lax.broadcasted_iota(jnp.int32, (1, 128), 1)
    stats = jnp.zeros((1, 128), jnp.float32)
    for n, value in enumerate((sums_ref[0:1, 0:1], square, cross, total(w * w), rho)):
        stats = jnp.where(lane == n, value, stats)
    for n in range(stats_ref.shape[0]):
        stats_ref[n] = stats


def image_kernel(size, width, near_ref, far_ref, self_ref, left_hbm, right_hbm, out_ref, left_own, right_own, sems):
    _, _, there = place(size, width)
    own = fetch(left_hbm, right_hbm, left_own, right_own, sems, [(0, 2 + width), (2 + width, width)])
    odd = lax.rem(lax.axis_index("sector"), 2) == 1
    near, far = near_ref[...], only(there[0], far_ref[...])
    finish(own[0])
    image = terms(self_ref[...], left_own, right_own, 0, 2)
    image = image + terms(jnp.where(odd, near, far), left_own, right_own, 2, width)
    finish(own[1])
    out_ref[...] = image + terms(jnp.where(odd, far, near), left_own, right_own, 2 + width, width)


def row_kernel(size, width, rows, part_ref, left_row, right_row, *refs):
    row_refs, (out_ref,) = refs[:rows], refs[rows:]
    _, _, there = place(size, width)
    image = part_ref[...]
    for r, source in enumerate(row_refs):
        image = image + terms(only(there[1 + r], source[...]), left_row, right_row, r * width, width)
    out_ref[...] = image


def second_kernel(size, width, rows, cells, facts_ref, stats_ref, hw_ref, near_part_ref, far_part_ref, row_part_ref,
                  first_hbm, second_hbm, first_ref, second_ref, sems):
    _, partners, _ = place(size, width)
    facts = facts_ref[...]
    stats = stats_ref[:, 0, :]
    sums = jnp.sum(stats, axis=0, keepdims=True)
    start, square, cross, inner = (sums[:, i : i + 1] for i in range(4))
    scale = lax.rsqrt(start / cells + 1e-06) * (1.0 / SCALE)
    rho = cross / square
    gap = stats[:, 4:5] - rho
    residual = inner + jnp.sum(stats[:, 1:2] * gap * gap, axis=0, keepdims=True)
    second_scale = scale * lax.rsqrt(scale * scale * (residual / cells) + 1e-06)
    gaps = [stats_ref[partner, :, 4:5] - rho for partner in partners[: 3 + rows]]
    block = hw_ref.shape[0]
    step = block // HALVES
    col_ok = lax.broadcasted_iota(jnp.int32, (step, block), 1).astype(jnp.float32) < facts[2:3, 0:1]
    row = lax.broadcasted_iota(jnp.int32, (step, block), 0).astype(jnp.float32)
    copies = []
    for n in range(HALVES):
        lines = pl.ds(n * step, step)
        parts = [near_part_ref[0, lines], near_part_ref[1, lines], far_part_ref[lines]]
        parts += [row_part_ref[r, lines] for r in range(rows)]
        cell = (row + n * step < facts[1:2, 0:1]) & col_ok
        image = hw_ref[lines]
        for gap, part in zip(gaps, parts):
            image = image + gap * part
        second_ref[lines] = jnp.where(cell, image, 0.0) * second_scale
        first_ref[lines] = jnp.where(cell, sum(parts[1:], parts[0]), 0.0) * scale
        for e, (source, target) in enumerate(((second_ref, second_hbm), (first_ref, first_hbm))):
            copies.append(pltpu.make_async_copy(source.at[lines], target.at[0, lines], sems.at[n, e]))
            copies[-1].start()
    finish(copies)


def body(wavefunction, sector_dims, left_env, right_env):
    size = lax.axis_size("sector")
    block = wavefunction.shape[1]
    square = (block, block)
    width = (right_env.shape[1] - 2) // 4
    near, row_pairs = swap_pairs(size)
    rows = len(row_pairs)
    cells = float(size * block * block)
    few, every, side, last = ((n,) + square for n in (2 + width, 2 + 2 * width, width, rows * width))
    f32, bf16 = jnp.float32, jnp.bfloat16
    dma = pltpu.SemaphoreType.DMA

    u, far_u, facts = call(
        start_kernel, (pltpu.VMEM(square, bf16),) * 2 + (pltpu.VMEM((8, 128), f32),), [HB, HB], (VM,) * 3,
        [pltpu.VMEM(square, f32), pltpu.SMEM((1, 2), jnp.int32), dma((QUARTERS + 1,))],
    )(hbm(wavefunction), hbm(sector_dims))

    left_env, right_env = hbm(left_env), hbm(right_env)
    u, facts = vmem(u), vmem(facts)
    row_u = [vmem(swap(u, "sector", p)) for p in row_pairs]
    near_u = vmem(swap(u, "sector", near))
    far_u = vmem(far_swap(after(far_u, near_u)))
    near_part, sums, left_far, right_far, left_row, right_row = call(
        functools.partial(near_kernel, size, width, rows),
        (pltpu.VMEM((2,) + square, f32), pltpu.VMEM((8, 128), f32)) + (pltpu.VMEM(side, bf16),) * 2 + (pltpu.VMEM(last, bf16),) * 2,
        [HB] * 3 + [VM] * 3, (VM,) * 6,
        [pltpu.VMEM(few, bf16)] * 2 + [pltpu.VMEM(square, f32), dma((2, 2)), dma((1, 2)), dma((rows, 2)), dma], LONG,
    )(left_env, right_env, hbm(wavefunction), facts, u, near_u)
    near_part, left_row, right_row = vmem(near_part), vmem(left_row), vmem(right_row)
    far_part, part = call(
        functools.partial(far_kernel, size, width), (pltpu.VMEM(square, f32),) * 2, [VM] * 4, (VM,) * 2, cost=LONG,
    )(vmem(left_far), vmem(right_far), near_part, far_u)
    far_part = vmem(far_part)
    row_part, w, stats = call(
        functools.partial(first_kernel, size, width, rows),
        (pltpu.VMEM((rows,) + square, f32), pltpu.VMEM(square, bf16), jax.ShapeDtypeStruct((size, 1, 128), f32)),
        [VM] * (6 + rows), (VM,) * 3,
    )(vmem(part), facts, vmem(sums), u, left_row, right_row, *row_u)

    w = vmem(w)
    row_w = [vmem(swap(w, "sector", p)) for p in row_pairs]
    near_w = vmem(swap(w, "sector", near))
    far_w = vmem(far_swap(w))
    stats = lax.all_to_all(stats, "sector", 0, 0, tiled=True)
    hw = call(
        functools.partial(image_kernel, size, width), pltpu.VMEM(square, f32), [VM] * 3 + [HB] * 2, VM,
        [pltpu.VMEM(every, bf16)] * 2 + [dma((2, 2))],
    )(near_w, far_w, w, left_env, right_env)
    hw = call(
        functools.partial(row_kernel, size, width, rows), pltpu.VMEM(square, f32), [VM] * (3 + rows), VM,
    )(vmem(hw), left_row, right_row, *row_w)
    return call(
        functools.partial(second_kernel, size, width, rows, cells),
        (jax.ShapeDtypeStruct((1,) + square, f32),) * 2, [VM] * 6, (HB, HB),
        [pltpu.VMEM(square, f32)] * 2 + [dma((HALVES, 2))],
    )(facts, stats, vmem(hw), near_part, far_part, vmem(row_part))


def solution(mesh):
    placed = (
        P(("groups", "sector"), None, None),
        P(("groups", "sector"), None),
        P(("groups", "sector"), None, None, None),
        P(("groups", "sector"), None, None, None),
    )
    return jax.shard_map(
        body,
        mesh=mesh,
        in_specs=placed,
        out_specs=(P(("groups", "sector"), None, None), P(("groups", "sector"), None, None)),
        check_vma=False,
    )
```

```python
import functools

import jax
import jax.numpy as jnp
from jax import lax
from jax.experimental import pallas as pl
from jax.experimental.pallas import tpu as pltpu
from jax.sharding import PartitionSpec as P

QD = 8
SCALE = 1024.0
QUARTERS = 4
HALVES = 2
NT = (((1,), (1,)), ((), ()))
VM = pl.BlockSpec(memory_space=pltpu.VMEM)
HB = pl.BlockSpec(memory_space=pltpu.HBM)
AN = pl.BlockSpec(memory_space=pl.ANY)
COST = pl.CostEstimate(flops=1, bytes_accessed=1, transcendentals=0)
LONG = pl.CostEstimate(flops=4000000000, bytes_accessed=1, transcendentals=0)
PARAMS = pltpu.CompilerParams(vmem_limit_bytes=16 * 1024 * 1024)


def vmem(x):
    return pltpu.with_memory_space_constraint(x, pltpu.VMEM)


def hbm(x):
    return pltpu.with_memory_space_constraint(x, pltpu.HBM)


def call(kernel, out_shape, in_specs, out_specs, scratch=(), cost=COST, aliases={}):
    return pl.pallas_call(
        kernel, out_shape=out_shape, in_specs=in_specs, out_specs=out_specs, scratch_shapes=list(scratch),
        compiler_params=PARAMS, cost_estimate=cost, input_output_aliases=aliases,
    )


def swap(x, axis, pairs):
    to = {a: b for p in pairs for a, b in (p, p[::-1])}
    return lax.ppermute(x, axis, [(s, to.get(s, s)) for s in range(lax.axis_size(axis))])


def swap_pairs(size):
    rows = size // QD
    near = [(s, s + 1) for s in range(0, size, 2)]
    row_even = [(s, s + QD) for r in range(0, rows - 1, 2) for s in range(r * QD, r * QD + QD)]
    row_odd = [(s, s + QD) for r in range(1, rows - 1, 2) for s in range(r * QD, r * QD + QD)]
    return near, [p for p in (row_even, row_odd) if p]


def far_swap(x, across):
    groups, size = lax.axis_size("groups"), lax.axis_size("sector")
    pairs = []
    for g in range(groups):
        for s in range(size):
            end = s % QD == 0 or s % QD == QD - 1
            if end and across:
                to, partner = (g ^ 1 if g ^ 1 < groups else g), s
            elif end:
                to, partner = g, s + QD - 1 if s % QD == 0 else s + 1 - QD
            else:
                to, partner = g, s + 1 if s % 2 else s - 1
            pairs.append((g * size + s, to * size + partner))
    return lax.ppermute(x, ("groups", "sector"), pairs)


def place(size, width):
    me = lax.axis_index("sector")
    column = lax.rem(me, QD)
    odd = lax.rem(me, 2) == 1
    row_odd = lax.rem(lax.div(me, QD), 2) == 1
    low, high, down, up = 2, 2 + width, 2 + 2 * width, 2 + 3 * width
    offsets = [jnp.where(odd, low, high), jnp.where(odd, high, low),
               jnp.where(row_odd, down, up), jnp.where(row_odd, up, down)]
    partners = [jnp.where(odd, me - 1, me + 1), jnp.where(odd, me + 1, me - 1),
                jnp.where(row_odd, me - QD, me + QD), jnp.where(row_odd, me + QD, me - QD)]
    there = [(column != 0) & (column != QD - 1),
             True if size // QD % 2 == 0 else (partners[2] >= 0) & (partners[2] < size),
             (partners[3] >= 0) & (partners[3] < size)]
    partners = [me] + [jnp.clip(p, 0, size - 1) for p in partners]
    return offsets, partners, there


def live(facts, shape):
    row_ok = lax.broadcasted_iota(jnp.int32, shape, 0).astype(jnp.float32) < facts[1:2, 0:1]
    col_ok = lax.broadcasted_iota(jnp.int32, shape, 1).astype(jnp.float32) < facts[2:3, 0:1]
    return row_ok & col_ok


def total(x):
    return jnp.sum(jnp.sum(x, axis=0, keepdims=True), axis=1, keepdims=True)


def only(there, block):
    return block if there is True else jnp.where(there, block, jnp.zeros_like(block))


def terms(src, left_ref, right_ref, first, count):
    size = src.shape[0]
    right = right_ref[pl.ds(first, count)].reshape(count * size, size)
    partial_t = lax.dot_general(right, src, NT, preferred_element_type=jnp.float32).astype(jnp.bfloat16)
    left = jnp.concatenate([left_ref[first + k] for k in range(count)], axis=1)
    partial_t = jnp.concatenate([partial_t[k * size : (k + 1) * size] for k in range(count)], axis=1)
    return lax.dot_general(left, partial_t, NT, preferred_element_type=jnp.float32)


def fetch(left_hbm, right_hbm, left_ref, right_ref, sems, spans):
    copies = []
    at = 0
    for n, (offset, count) in enumerate(spans):
        pair = [
            pltpu.make_async_copy(source.at[0, pl.ds(offset, count)], target.at[pl.ds(at, count)], sems.at[n, e])
            for e, (source, target) in enumerate(((right_hbm, right_ref), (left_hbm, left_ref)))
        ]
        for copy in pair:
            copy.start()
        copies.append(pair)
        at += count
    return copies


def finish(copies):
    for copy in copies:
        copy.wait()


def start_kernel(wave_hbm, dims_hbm, *refs):
    u_refs, (facts_ref, wave_ref, dims_ref, sems) = refs[:2], refs[2:]
    size = wave_ref.shape[0]
    step = size // QUARTERS
    dims_copy = pltpu.make_async_copy(dims_hbm, dims_ref, sems.at[QUARTERS])
    dims_copy.start()
    copies = [
        pltpu.make_async_copy(wave_hbm.at[0, pl.ds(n * step, step)], wave_ref.at[pl.ds(n * step, step)], sems.at[n])
        for n in range(QUARTERS)
    ]
    for copy in copies:
        copy.start()
    dims_copy.wait()
    row_count, col_count = dims_ref[0, 0], dims_ref[0, 1]
    lines = lax.broadcasted_iota(jnp.int32, (8, 128), 0)
    facts_ref[...] = jnp.where(lines == 1, row_count, jnp.where(lines == 2, col_count, 0)).astype(jnp.float32)
    col_ok = lax.broadcasted_iota(jnp.int32, (step, size), 1) < col_count
    row = lax.broadcasted_iota(jnp.int32, (step, size), 0)
    for n, copy in enumerate(copies):
        copy.wait()
        rows = pl.ds(n * step, step)
        held = jnp.where((row < row_count - n * step) & col_ok, wave_ref[rows], 0.0)
        block = (held * SCALE).astype(jnp.bfloat16)
        for ref in u_refs:
            ref[rows] = block


def pass_kernel(*refs):
    pass


def after(held, first):
    return call(pass_kernel, pltpu.VMEM(held.shape, held.dtype), [AN] * 2, AN, aliases={0: 0})(vmem(held), first)


def near_kernel(size, width, rows, left_hbm, right_hbm, wave_hbm, facts_ref, self_ref, near_ref, out_ref, sums_ref,
                left_far, right_far, left_row, right_row, left_own, right_own, wave_ref, sems, far_sems, row_sems, wave_sem):
    offsets, _, _ = place(size, width)
    wave_copy = pltpu.make_async_copy(wave_hbm.at[0], wave_ref, wave_sem)
    own = fetch(left_hbm, right_hbm, left_own, right_own, sems, [(0, 2), (offsets[0], width)])
    wave_copy.start()
    later = fetch(left_hbm, right_hbm, left_far, right_far, far_sems, [(offsets[1], width)])
    later += fetch(left_hbm, right_hbm, left_row, right_row, row_sems, [(o, width) for o in offsets[2 : 2 + rows]])
    u = self_ref[...].astype(jnp.float32)
    lines = lax.broadcasted_iota(jnp.int32, (8, 128), 0)
    sums = jnp.where(lines == 1, total(u * u), 0.0)
    finish(own[0])
    out_ref[0] = terms(self_ref[...], left_own, right_own, 0, 2)
    finish(own[1])
    out_ref[1] = terms(near_ref[...], left_own, right_own, 2, width)
    wave_copy.wait()
    held = jnp.where(live(facts_ref[...], wave_ref.shape), wave_ref[...], 0.0)
    sums_ref[...] = jnp.where(lines == 0, total(held * held), sums)
    for pair in later:
        finish(pair)


def far_kernel(size, width, left_ref, right_ref, near_part_ref, far_ref, out_ref, sum_ref):
    _, _, there = place(size, width)
    part = terms(only(there[0], far_ref[...]), left_ref, right_ref, 0, width)
    out_ref[...] = part
    sum_ref[...] = near_part_ref[0] + near_part_ref[1] + part


def first_kernel(size, width, rows, *refs):
    part_ref, facts_ref, sums_ref, u_ref, left_ref, right_ref = refs[:6]
    row_refs, (out_ref, w_ref, stats_ref) = refs[6 : 6 + rows], refs[6 + rows :]
    _, _, there = place(size, width)
    image = part_ref[...]
    for r, source in enumerate(row_refs):
        piece = terms(only(there[1 + r], source[...]), left_ref, right_ref, r * width, width)
        out_ref[r] = piece
        image = image + piece
    image = jnp.where(live(facts_ref[...], image.shape), image, 0.0)
    u = u_ref[...].astype(jnp.float32)
    square = sums_ref[1:2, 0:1]
    cross = total(u * image)
    rho = jnp.where(square > 0.0, cross / square, 0.0)
    w = image - rho * u
    w_ref[...] = w.astype(jnp.bfloat16)
    lane = lax.broadcasted_iota(jnp.int32, (1, 128), 1)
    stats = jnp.zeros((1, 128), jnp.float32)
    for n, value in enumerate((sums_ref[0:1, 0:1], square, cross, total(w * w), rho)):
        stats = jnp.where(lane == n, value, stats)
    for n in range(stats_ref.shape[0]):
        stats_ref[n] = stats


def image_kernel(size, width, near_ref, far_ref, self_ref, left_hbm, right_hbm, out_ref, left_own, right_own, sems):
    _, _, there = place(size, width)
    own = fetch(left_hbm, right_hbm, left_own, right_own, sems, [(0, 2 + width), (2 + width, width)])
    odd = lax.rem(lax.axis_index("sector"), 2) == 1
    near, far = near_ref[...], only(there[0], far_ref[...])
    finish(own[0])
    image = terms(self_ref[...], left_own, right_own, 0, 2)
    image = image + terms(jnp.where(odd, near, far), left_own, right_own, 2, width)
    finish(own[1])
    out_ref[...] = image + terms(jnp.where(odd, far, near), left_own, right_own, 2 + width, width)


def row_kernel(size, width, rows, part_ref, left_row, right_row, *refs):
    row_refs, (out_ref,) = refs[:rows], refs[rows:]
    _, _, there = place(size, width)
    image = part_ref[...]
    for r, source in enumerate(row_refs):
        image = image + terms(only(there[1 + r], source[...]), left_row, right_row, r * width, width)
    out_ref[...] = image


def second_kernel(size, width, rows, cells, facts_ref, stats_ref, hw_ref, near_part_ref, far_part_ref, row_part_ref,
                  first_hbm, second_hbm, first_ref, second_ref, sems):
    _, partners, _ = place(size, width)
    facts = facts_ref[...]
    stats = stats_ref[:, 0, :]
    sums = jnp.sum(stats, axis=0, keepdims=True)
    start, square, cross, inner = (sums[:, i : i + 1] for i in range(4))
    scale = lax.rsqrt(start / cells + 1e-06) * (1.0 / SCALE)
    rho = cross / square
    gap = stats[:, 4:5] - rho
    residual = inner + jnp.sum(stats[:, 1:2] * gap * gap, axis=0, keepdims=True)
    second_scale = scale * lax.rsqrt(scale * scale * (residual / cells) + 1e-06)
    gaps = [stats_ref[partner, :, 4:5] - rho for partner in partners[: 3 + rows]]
    block = hw_ref.shape[0]
    step = block // HALVES
    col_ok = lax.broadcasted_iota(jnp.int32, (step, block), 1).astype(jnp.float32) < facts[2:3, 0:1]
    row = lax.broadcasted_iota(jnp.int32, (step, block), 0).astype(jnp.float32)
    copies = []
    for n in range(HALVES):
        lines = pl.ds(n * step, step)
        parts = [near_part_ref[0, lines], near_part_ref[1, lines], far_part_ref[lines]]
        parts += [row_part_ref[r, lines] for r in range(rows)]
        cell = (row + n * step < facts[1:2, 0:1]) & col_ok
        image = hw_ref[lines]
        for gap, part in zip(gaps, parts):
            image = image + gap * part
        second_ref[lines] = jnp.where(cell, image, 0.0) * second_scale
        first_ref[lines] = jnp.where(cell, sum(parts[1:], parts[0]), 0.0) * scale
        for e, (source, target) in enumerate(((second_ref, second_hbm), (first_ref, first_hbm))):
            copies.append(pltpu.make_async_copy(source.at[lines], target.at[0, lines], sems.at[n, e]))
            copies[-1].start()
    finish(copies)


def body(wavefunction, sector_dims, left_env, right_env):
    size = lax.axis_size("sector")
    block = wavefunction.shape[1]
    square = (block, block)
    width = (right_env.shape[1] - 2) // 4
    near, row_pairs = swap_pairs(size)
    rows = len(row_pairs)
    cells = float(size * block * block)
    few, every, side, last = ((n,) + square for n in (2 + width, 2 + 2 * width, width, rows * width))
    f32, bf16 = jnp.float32, jnp.bfloat16
    dma = pltpu.SemaphoreType.DMA

    u, far_u, facts = call(
        start_kernel, (pltpu.VMEM(square, bf16),) * 2 + (pltpu.VMEM((8, 128), f32),), [HB, HB], (VM,) * 3,
        [pltpu.VMEM(square, f32), pltpu.SMEM((1, 2), jnp.int32), dma((QUARTERS + 1,))],
    )(hbm(wavefunction), hbm(sector_dims))

    left_env, right_env = hbm(left_env), hbm(right_env)
    u, facts = vmem(u), vmem(facts)
    row_u = [vmem(swap(u, "sector", p)) for p in row_pairs]
    near_u = vmem(swap(u, "sector", near))
    far_u = vmem(far_swap(after(far_u, near_u), True))
    near_part, sums, left_far, right_far, left_row, right_row = call(
        functools.partial(near_kernel, size, width, rows),
        (pltpu.VMEM((2,) + square, f32), pltpu.VMEM((8, 128), f32)) + (pltpu.VMEM(side, bf16),) * 2 + (pltpu.VMEM(last, bf16),) * 2,
        [HB] * 3 + [VM] * 3, (VM,) * 6,
        [pltpu.VMEM(few, bf16)] * 2 + [pltpu.VMEM(square, f32), dma((2, 2)), dma((1, 2)), dma((rows, 2)), dma], LONG,
    )(left_env, right_env, hbm(wavefunction), facts, u, near_u)
    near_part, left_row, right_row = vmem(near_part), vmem(left_row), vmem(right_row)
    far_part, part = call(
        functools.partial(far_kernel, size, width), (pltpu.VMEM(square, f32),) * 2, [VM] * 4, (VM,) * 2, cost=LONG,
    )(vmem(left_far), vmem(right_far), near_part, far_u)
    far_part = vmem(far_part)
    row_part, w, stats = call(
        functools.partial(first_kernel, size, width, rows),
        (pltpu.VMEM((rows,) + square, f32), pltpu.VMEM(square, bf16), jax.ShapeDtypeStruct((size, 1, 128), f32)),
        [VM] * (6 + rows), (VM,) * 3,
    )(vmem(part), facts, vmem(sums), u, left_row, right_row, *row_u)

    w = vmem(w)
    row_w = [vmem(swap(w, "sector", p)) for p in row_pairs]
    near_w = vmem(swap(w, "sector", near))
    far_w = vmem(far_swap(w, False))
    stats = lax.all_to_all(stats, "sector", 0, 0, tiled=True)
    hw = call(
        functools.partial(image_kernel, size, width), pltpu.VMEM(square, f32), [VM] * 3 + [HB] * 2, VM,
        [pltpu.VMEM(every, bf16)] * 2 + [dma((2, 2))],
    )(near_w, far_w, w, left_env, right_env)
    hw = call(
        functools.partial(row_kernel, size, width, rows), pltpu.VMEM(square, f32), [VM] * (3 + rows), VM,
    )(vmem(hw), left_row, right_row, *row_w)
    return call(
        functools.partial(second_kernel, size, width, rows, cells),
        (jax.ShapeDtypeStruct((1,) + square, f32),) * 2, [VM] * 6, (HB, HB),
        [pltpu.VMEM(square, f32)] * 2 + [dma((HALVES, 2))],
    )(facts, stats, vmem(hw), near_part, far_part, vmem(row_part))


def solution(mesh):
    placed = (
        P(("groups", "sector"), None, None),
        P(("groups", "sector"), None),
        P(("groups", "sector"), None, None, None),
        P(("groups", "sector"), None, None, None),
    )
    return jax.shard_map(
        body,
        mesh=mesh,
        in_specs=placed,
        out_specs=(P(("groups", "sector"), None, None), P(("groups", "sector"), None, None)),
        check_vma=False,
    )
```

```python
import functools

import jax
import jax.numpy as jnp
from jax import lax
from jax.experimental import pallas as pl
from jax.experimental.pallas import tpu as pltpu
from jax.sharding import PartitionSpec as P

QD = 8
SCALE = 1024.0
QUARTERS = 4
HALVES = 2
NT = (((1,), (1,)), ((), ()))
VM = pl.BlockSpec(memory_space=pltpu.VMEM)
HB = pl.BlockSpec(memory_space=pltpu.HBM)
AN = pl.BlockSpec(memory_space=pl.ANY)
COST = pl.CostEstimate(flops=1, bytes_accessed=1, transcendentals=0)
LONG = pl.CostEstimate(flops=4000000000, bytes_accessed=1, transcendentals=0)
PARAMS = pltpu.CompilerParams(vmem_limit_bytes=16 * 1024 * 1024)


def vmem(x):
    return pltpu.with_memory_space_constraint(x, pltpu.VMEM)


def hbm(x):
    return pltpu.with_memory_space_constraint(x, pltpu.HBM)


def call(kernel, out_shape, in_specs, out_specs, scratch=(), cost=COST, aliases={}):
    return pl.pallas_call(
        kernel, out_shape=out_shape, in_specs=in_specs, out_specs=out_specs, scratch_shapes=list(scratch),
        compiler_params=PARAMS, cost_estimate=cost, input_output_aliases=aliases,
    )


def swap(x, axis, pairs):
    to = {a: b for p in pairs for a, b in (p, p[::-1])}
    return lax.ppermute(x, axis, [(s, to.get(s, s)) for s in range(lax.axis_size(axis))])


def swap_pairs(size):
    rows = size // QD
    near = [(s, s + 1) for s in range(0, size, 2)]
    row_even = [(s, s + QD) for r in range(0, rows - 1, 2) for s in range(r * QD, r * QD + QD)]
    row_odd = [(s, s + QD) for r in range(1, rows - 1, 2) for s in range(r * QD, r * QD + QD)]
    return near, [p for p in (row_even, row_odd) if p]


def far_swap(x):
    groups, size = lax.axis_size("groups"), lax.axis_size("sector")
    pairs = []
    for g in range(groups):
        for s in range(size):
            if s % QD == 0 or s % QD == QD - 1:
                to, partner = (g ^ 1 if g ^ 1 < groups else g), s
            else:
                to, partner = g, s + 1 if s % 2 else s - 1
            pairs.append((g * size + s, to * size + partner))
    return lax.ppermute(x, ("groups", "sector"), pairs)


def place(size, width):
    me = lax.axis_index("sector")
    column = lax.rem(me, QD)
    odd = lax.rem(me, 2) == 1
    row_odd = lax.rem(lax.div(me, QD), 2) == 1
    low, high, down, up = 2, 2 + width, 2 + 2 * width, 2 + 3 * width
    offsets = [jnp.where(odd, low, high), jnp.where(odd, high, low),
               jnp.where(row_odd, down, up), jnp.where(row_odd, up, down)]
    partners = [jnp.where(odd, me - 1, me + 1), jnp.where(odd, me + 1, me - 1),
                jnp.where(row_odd, me - QD, me + QD), jnp.where(row_odd, me + QD, me - QD)]
    there = [(column != 0) & (column != QD - 1),
             True if size // QD % 2 == 0 else (partners[2] >= 0) & (partners[2] < size),
             (partners[3] >= 0) & (partners[3] < size)]
    partners = [me] + [jnp.clip(p, 0, size - 1) for p in partners]
    return offsets, partners, there


def live(facts, shape):
    row_ok = lax.broadcasted_iota(jnp.int32, shape, 0).astype(jnp.float32) < facts[1:2, 0:1]
    col_ok = lax.broadcasted_iota(jnp.int32, shape, 1).astype(jnp.float32) < facts[2:3, 0:1]
    return row_ok & col_ok


def total(x):
    return jnp.sum(jnp.sum(x, axis=0, keepdims=True), axis=1, keepdims=True)


def only(there, block):
    return block if there is True else jnp.where(there, block, jnp.zeros_like(block))


def terms(src, left_ref, right_ref, first, count):
    size = src.shape[0]
    right = right_ref[pl.ds(first, count)].reshape(count * size, size)
    partial_t = lax.dot_general(right, src, NT, preferred_element_type=jnp.float32).astype(jnp.bfloat16)
    left = jnp.concatenate([left_ref[first + k] for k in range(count)], axis=1)
    partial_t = jnp.concatenate([partial_t[k * size : (k + 1) * size] for k in range(count)], axis=1)
    return lax.dot_general(left, partial_t, NT, preferred_element_type=jnp.float32)


def fetch(left_hbm, right_hbm, left_ref, right_ref, sems, spans):
    copies = []
    at = 0
    for n, (offset, count) in enumerate(spans):
        pair = [
            pltpu.make_async_copy(source.at[0, pl.ds(offset, count)], target.at[pl.ds(at, count)], sems.at[n, e])
            for e, (source, target) in enumerate(((right_hbm, right_ref), (left_hbm, left_ref)))
        ]
        for copy in pair:
            copy.start()
        copies.append(pair)
        at += count
    return copies


def finish(copies):
    for copy in copies:
        copy.wait()


def start_kernel(wave_hbm, dims_hbm, *refs):
    u_refs, (facts_ref, wave_ref, dims_ref, sems) = refs[:2], refs[2:]
    size = wave_ref.shape[0]
    step = size // QUARTERS
    dims_copy = pltpu.make_async_copy(dims_hbm, dims_ref, sems.at[QUARTERS])
    dims_copy.start()
    copies = [
        pltpu.make_async_copy(wave_hbm.at[0, pl.ds(n * step, step)], wave_ref.at[pl.ds(n * step, step)], sems.at[n])
        for n in range(QUARTERS)
    ]
    for copy in copies:
        copy.start()
    dims_copy.wait()
    row_count, col_count = dims_ref[0, 0], dims_ref[0, 1]
    lines = lax.broadcasted_iota(jnp.int32, (8, 128), 0)
    facts_ref[...] = jnp.where(lines == 1, row_count, jnp.where(lines == 2, col_count, 0)).astype(jnp.float32)
    col_ok = lax.broadcasted_iota(jnp.int32, (step, size), 1) < col_count
    row = lax.broadcasted_iota(jnp.int32, (step, size), 0)
    for n, copy in enumerate(copies):
        copy.wait()
        rows = pl.ds(n * step, step)
        held = jnp.where((row < row_count - n * step) & col_ok, wave_ref[rows], 0.0)
        block = (held * SCALE).astype(jnp.bfloat16)
        for ref in u_refs:
            ref[rows] = block


def pass_kernel(*refs):
    pass


def after(held, first):
    return call(pass_kernel, pltpu.VMEM(held.shape, held.dtype), [AN] * 2, AN, aliases={0: 0})(vmem(held), first)


def near_kernel(size, width, rows, left_hbm, right_hbm, wave_hbm, facts_ref, self_ref, near_ref, out_ref, sums_ref,
                left_far, right_far, left_row, right_row, left_own, right_own, wave_ref, sems, far_sems, row_sems, wave_sem):
    offsets, _, _ = place(size, width)
    wave_copy = pltpu.make_async_copy(wave_hbm.at[0], wave_ref, wave_sem)
    own = fetch(left_hbm, right_hbm, left_own, right_own, sems, [(0, 2), (offsets[0], width)])
    wave_copy.start()
    later = fetch(left_hbm, right_hbm, left_far, right_far, far_sems, [(offsets[1], width)])
    later += fetch(left_hbm, right_hbm, left_row, right_row, row_sems, [(o, width) for o in offsets[2 : 2 + rows]])
    u = self_ref[...].astype(jnp.float32)
    lines = lax.broadcasted_iota(jnp.int32, (8, 128), 0)
    sums = jnp.where(lines == 1, total(u * u), 0.0)
    finish(own[0])
    out_ref[0] = terms(self_ref[...], left_own, right_own, 0, 2)
    finish(own[1])
    out_ref[1] = terms(near_ref[...], left_own, right_own, 2, width)
    wave_copy.wait()
    held = jnp.where(live(facts_ref[...], wave_ref.shape), wave_ref[...], 0.0)
    sums_ref[...] = jnp.where(lines == 0, total(held * held), sums)
    for pair in later:
        finish(pair)


def far_kernel(size, width, left_ref, right_ref, near_part_ref, far_ref, out_ref, sum_ref):
    _, _, there = place(size, width)
    part = terms(only(there[0], far_ref[...]), left_ref, right_ref, 0, width)
    out_ref[...] = part
    sum_ref[...] = near_part_ref[0] + near_part_ref[1] + part


def first_kernel(size, width, rows, *refs):
    part_ref, facts_ref, sums_ref, u_ref, left_ref, right_ref = refs[:6]
    row_refs, (out_ref, w_ref, sums_out_ref, numbers_hbm, numbers_ref, sem) = refs[6 : 6 + rows], refs[6 + rows :]
    _, _, there = place(size, width)
    image = part_ref[...]
    for r, source in enumerate(row_refs):
        piece = terms(only(there[1 + r], source[...]), left_ref, right_ref, r * width, width)
        out_ref[r] = piece
        image = image + piece
    image = jnp.where(live(facts_ref[...], image.shape), image, 0.0)
    u = u_ref[...].astype(jnp.float32)
    square = sums_ref[1:2, 0:1]
    cross = total(u * image)
    rho = jnp.where(square > 0.0, cross / square, 0.0)
    w_ref[...] = (image - rho * u).astype(jnp.bfloat16)
    lines = lax.broadcasted_iota(jnp.int32, (8, 128), 0)
    sums = jnp.where(lines == 2, cross, jnp.where(lines == 4, rho, sums_ref[...]))
    sums_out_ref[...] = sums

    @pl.when(even_row())
    def _():
        write_numbers(sums, w_ref, numbers_hbm, numbers_ref, sem)


def even_row():
    return lax.rem(lax.div(lax.axis_index("sector"), QD), 2) == 0


def write_numbers(sums, w_ref, numbers_hbm, numbers_ref, sem):
    w = w_ref[...].astype(jnp.float32)
    values = [sums[n : n + 1, 0:1] for n in range(5)]
    values[3] = total(w * w)
    lane = lax.broadcasted_iota(jnp.int32, (1, 128), 1)
    numbers = jnp.zeros((1, 128), jnp.float32)
    for n, value in enumerate(values):
        numbers = jnp.where(lane == n, value, numbers)
    for n in range(numbers_ref.shape[0]):
        numbers_ref[n] = numbers
    copy = pltpu.make_async_copy(numbers_ref, numbers_hbm, sem)
    copy.start()
    copy.wait()


def numbers_kernel(held_hbm, sums_ref, w_ref, numbers_hbm, numbers_ref, sem):
    @pl.when(jnp.logical_not(even_row()))
    def _():
        write_numbers(sums_ref[...], w_ref, numbers_hbm, numbers_ref, sem)


def image_kernel(size, width, near_ref, far_ref, self_ref, left_hbm, right_hbm, out_ref, left_own, right_own, sems):
    _, _, there = place(size, width)
    own = fetch(left_hbm, right_hbm, left_own, right_own, sems, [(0, 2 + width), (2 + width, width)])
    odd = lax.rem(lax.axis_index("sector"), 2) == 1
    near, far = near_ref[...], only(there[0], far_ref[...])
    finish(own[0])
    image = terms(self_ref[...], left_own, right_own, 0, 2)
    image = image + terms(jnp.where(odd, near, far), left_own, right_own, 2, width)
    finish(own[1])
    out_ref[...] = image + terms(jnp.where(odd, far, near), left_own, right_own, 2 + width, width)


def row_kernel(size, width, rows, part_ref, left_row, right_row, *refs):
    row_refs, (out_ref,) = refs[:rows], refs[rows:]
    _, _, there = place(size, width)
    image = part_ref[...]
    for r, source in enumerate(row_refs):
        image = image + terms(only(there[1 + r], source[...]), left_row, right_row, r * width, width)
    out_ref[...] = image


def second_kernel(size, width, rows, cells, facts_ref, stats_ref, hw_ref, near_part_ref, far_part_ref, row_part_ref,
                  first_hbm, second_hbm, first_ref, second_ref, sems):
    _, partners, _ = place(size, width)
    facts = facts_ref[...]
    stats = stats_ref[:, 0, :]
    sums = jnp.sum(stats, axis=0, keepdims=True)
    start, square, cross, inner = (sums[:, i : i + 1] for i in range(4))
    scale = lax.rsqrt(start / cells + 1e-06) * (1.0 / SCALE)
    rho = cross / square
    gap = stats[:, 4:5] - rho
    residual = inner + jnp.sum(stats[:, 1:2] * gap * gap, axis=0, keepdims=True)
    second_scale = scale * lax.rsqrt(scale * scale * (residual / cells) + 1e-06)
    gaps = [stats_ref[partner, :, 4:5] - rho for partner in partners[: 3 + rows]]
    block = hw_ref.shape[0]
    step = block // HALVES
    col_ok = lax.broadcasted_iota(jnp.int32, (step, block), 1).astype(jnp.float32) < facts[2:3, 0:1]
    row = lax.broadcasted_iota(jnp.int32, (step, block), 0).astype(jnp.float32)
    copies = []
    for n in range(HALVES):
        lines = pl.ds(n * step, step)
        parts = [near_part_ref[0, lines], near_part_ref[1, lines], far_part_ref[lines]]
        parts += [row_part_ref[r, lines] for r in range(rows)]
        cell = (row + n * step < facts[1:2, 0:1]) & col_ok
        image = hw_ref[lines]
        for gap, part in zip(gaps, parts):
            image = image + gap * part
        second_ref[lines] = jnp.where(cell, image, 0.0) * second_scale
        first_ref[lines] = jnp.where(cell, sum(parts[1:], parts[0]), 0.0) * scale
        for e, (source, target) in enumerate(((second_ref, second_hbm), (first_ref, first_hbm))):
            copies.append(pltpu.make_async_copy(source.at[lines], target.at[0, lines], sems.at[n, e]))
            copies[-1].start()
    finish(copies)


def body(wavefunction, sector_dims, left_env, right_env):
    size = lax.axis_size("sector")
    block = wavefunction.shape[1]
    square = (block, block)
    width = (right_env.shape[1] - 2) // 4
    near, row_pairs = swap_pairs(size)
    rows = len(row_pairs)
    cells = float(size * block * block)
    few, every, side, last = ((n,) + square for n in (2 + width, 2 + 2 * width, width, rows * width))
    f32, bf16 = jnp.float32, jnp.bfloat16
    dma = pltpu.SemaphoreType.DMA

    u, far_u, facts = call(
        start_kernel, (pltpu.VMEM(square, bf16),) * 2 + (pltpu.VMEM((8, 128), f32),), [HB, HB], (VM,) * 3,
        [pltpu.VMEM(square, f32), pltpu.SMEM((1, 2), jnp.int32), dma((QUARTERS + 1,))],
    )(hbm(wavefunction), hbm(sector_dims))

    left_env, right_env = hbm(left_env), hbm(right_env)
    u, facts = vmem(u), vmem(facts)
    row_u = [vmem(swap(u, "sector", p)) for p in row_pairs]
    near_u = vmem(swap(u, "sector", near))
    far_u = vmem(far_swap(after(far_u, near_u)))
    near_part, sums, left_far, right_far, left_row, right_row = call(
        functools.partial(near_kernel, size, width, rows),
        (pltpu.VMEM((2,) + square, f32), pltpu.VMEM((8, 128), f32)) + (pltpu.VMEM(side, bf16),) * 2 + (pltpu.VMEM(last, bf16),) * 2,
        [HB] * 3 + [VM] * 3, (VM,) * 6,
        [pltpu.VMEM(few, bf16)] * 2 + [pltpu.VMEM(square, f32), dma((2, 2)), dma((1, 2)), dma((rows, 2)), dma], LONG,
    )(left_env, right_env, hbm(wavefunction), facts, u, near_u)
    near_part, left_row, right_row = vmem(near_part), vmem(left_row), vmem(right_row)
    far_part, part = call(
        functools.partial(far_kernel, size, width), (pltpu.VMEM(square, f32),) * 2, [VM] * 4, (VM,) * 2, cost=LONG,
    )(vmem(left_far), vmem(right_far), near_part, far_u)
    far_part = vmem(far_part)
    table = pltpu.HBM((size, 1, 128), f32)
    table_scratch = [pltpu.VMEM((size, 1, 128), f32), dma]
    row_part, w, sums, stats = call(
        functools.partial(first_kernel, size, width, rows),
        (pltpu.VMEM((rows,) + square, f32), pltpu.VMEM(square, bf16), pltpu.VMEM((8, 128), f32), table),
        [VM] * (6 + rows), (VM,) * 3 + (HB,), table_scratch,
    )(vmem(part), facts, vmem(sums), u, left_row, right_row, *row_u)

    w = vmem(w)
    row_w = [vmem(swap(w, "sector", p)) for p in row_pairs]
    near_w = vmem(swap(w, "sector", near))
    far_w = vmem(far_swap(w))
    stats = call(numbers_kernel, table, [HB] + [VM] * 2, HB, table_scratch, aliases={0: 0})(hbm(stats), vmem(sums), w)
    stats = lax.all_to_all(stats, "sector", 0, 0, tiled=True)
    hw = call(
        functools.partial(image_kernel, size, width), pltpu.VMEM(square, f32), [VM] * 3 + [HB] * 2, VM,
        [pltpu.VMEM(every, bf16)] * 2 + [dma((2, 2))],
    )(near_w, far_w, w, left_env, right_env)
    hw = call(
        functools.partial(row_kernel, size, width, rows), pltpu.VMEM(square, f32), [VM] * (3 + rows), VM,
    )(vmem(hw), left_row, right_row, *row_w)
    return call(
        functools.partial(second_kernel, size, width, rows, cells),
        (jax.ShapeDtypeStruct((1,) + square, f32),) * 2, [VM] * 6, (HB, HB),
        [pltpu.VMEM(square, f32)] * 2 + [dma((HALVES, 2))],
    )(facts, stats, vmem(hw), near_part, far_part, vmem(row_part))


def solution(mesh):
    placed = (
        P(("groups", "sector"), None, None),
        P(("groups", "sector"), None),
        P(("groups", "sector"), None, None, None),
        P(("groups", "sector"), None, None, None),
    )
    return jax.shard_map(
        body,
        mesh=mesh,
        in_specs=placed,
        out_specs=(P(("groups", "sector"), None, None), P(("groups", "sector"), None, None)),
        check_vma=False,
    )
```

```python
import functools

import jax
import jax.numpy as jnp
from jax import lax
from jax.experimental import pallas as pl
from jax.experimental.pallas import tpu as pltpu
from jax.sharding import PartitionSpec as P

QD = 8
SCALE = 1024.0
QUARTERS = 2
HALVES = 2
NT = (((1,), (1,)), ((), ()))
VM = pl.BlockSpec(memory_space=pltpu.VMEM)
HB = pl.BlockSpec(memory_space=pltpu.HBM)
AN = pl.BlockSpec(memory_space=pl.ANY)
COST = pl.CostEstimate(flops=1, bytes_accessed=1, transcendentals=0)
LONG = pl.CostEstimate(flops=4000000000, bytes_accessed=1, transcendentals=0)
PARAMS = pltpu.CompilerParams(vmem_limit_bytes=16 * 1024 * 1024)


def vmem(x):
    return pltpu.with_memory_space_constraint(x, pltpu.VMEM)


def hbm(x):
    return pltpu.with_memory_space_constraint(x, pltpu.HBM)


def call(kernel, out_shape, in_specs, out_specs, scratch=(), cost=COST, aliases={}):
    return pl.pallas_call(
        kernel, out_shape=out_shape, in_specs=in_specs, out_specs=out_specs, scratch_shapes=list(scratch),
        compiler_params=PARAMS, cost_estimate=cost, input_output_aliases=aliases,
    )


def swap(x, axis, pairs):
    to = {a: b for p in pairs for a, b in (p, p[::-1])}
    return lax.ppermute(x, axis, [(s, to.get(s, s)) for s in range(lax.axis_size(axis))])


def swap_pairs(size):
    rows = size // QD
    near = [(s, s + 1) for s in range(0, size, 2)]
    row_even = [(s, s + QD) for r in range(0, rows - 1, 2) for s in range(r * QD, r * QD + QD)]
    row_odd = [(s, s + QD) for r in range(1, rows - 1, 2) for s in range(r * QD, r * QD + QD)]
    return near, [p for p in (row_even, row_odd) if p]


def far_swap(x):
    groups, size = lax.axis_size("groups"), lax.axis_size("sector")
    pairs = []
    for g in range(groups):
        for s in range(size):
            if s % QD == 0 or s % QD == QD - 1:
                to, partner = (g ^ 1 if g ^ 1 < groups else g), s
            else:
                to, partner = g, s + 1 if s % 2 else s - 1
            pairs.append((g * size + s, to * size + partner))
    return lax.ppermute(x, ("groups", "sector"), pairs)


def place(size, width):
    me = lax.axis_index("sector")
    column = lax.rem(me, QD)
    odd = lax.rem(me, 2) == 1
    row_odd = lax.rem(lax.div(me, QD), 2) == 1
    low, high, down, up = 2, 2 + width, 2 + 2 * width, 2 + 3 * width
    offsets = [jnp.where(odd, low, high), jnp.where(odd, high, low),
               jnp.where(row_odd, down, up), jnp.where(row_odd, up, down)]
    partners = [jnp.where(odd, me - 1, me + 1), jnp.where(odd, me + 1, me - 1),
                jnp.where(row_odd, me - QD, me + QD), jnp.where(row_odd, me + QD, me - QD)]
    there = [(column != 0) & (column != QD - 1),
             True if size // QD % 2 == 0 else (partners[2] >= 0) & (partners[2] < size),
             (partners[3] >= 0) & (partners[3] < size)]
    partners = [me] + [jnp.clip(p, 0, size - 1) for p in partners]
    return offsets, partners, there


def live(facts, shape):
    row_ok = lax.broadcasted_iota(jnp.int32, shape, 0).astype(jnp.float32) < facts[1:2, 0:1]
    col_ok = lax.broadcasted_iota(jnp.int32, shape, 1).astype(jnp.float32) < facts[2:3, 0:1]
    return row_ok & col_ok


def total(x):
    return jnp.sum(jnp.sum(x, axis=0, keepdims=True), axis=1, keepdims=True)


def only(there, block):
    return block if there is True else jnp.where(there, block, jnp.zeros_like(block))


def terms(src, left_ref, right_ref, first, count):
    size = src.shape[0]
    right = right_ref[pl.ds(first, count)].reshape(count * size, size)
    partial_t = lax.dot_general(right, src, NT, preferred_element_type=jnp.float32).astype(jnp.bfloat16)
    left = jnp.concatenate([left_ref[first + k] for k in range(count)], axis=1)
    partial_t = jnp.concatenate([partial_t[k * size : (k + 1) * size] for k in range(count)], axis=1)
    return lax.dot_general(left, partial_t, NT, preferred_element_type=jnp.float32)


def fetch(left_hbm, right_hbm, left_ref, right_ref, sems, spans):
    copies = []
    at = 0
    for n, (offset, count) in enumerate(spans):
        pair = [
            pltpu.make_async_copy(source.at[0, pl.ds(offset, count)], target.at[pl.ds(at, count)], sems.at[n, e])
            for e, (source, target) in enumerate(((right_hbm, right_ref), (left_hbm, left_ref)))
        ]
        for copy in pair:
            copy.start()
        copies.append(pair)
        at += count
    return copies


def finish(copies):
    for copy in copies:
        copy.wait()


def start_kernel(wave_hbm, dims_hbm, *refs):
    u_refs, (facts_ref, wave_ref, dims_ref, sems) = refs[:2], refs[2:]
    size = wave_ref.shape[0]
    step = size // QUARTERS
    dims_copy = pltpu.make_async_copy(dims_hbm, dims_ref, sems.at[QUARTERS])
    dims_copy.start()
    copies = [
        pltpu.make_async_copy(wave_hbm.at[0, pl.ds(n * step, step)], wave_ref.at[pl.ds(n * step, step)], sems.at[n])
        for n in range(QUARTERS)
    ]
    for copy in copies:
        copy.start()
    dims_copy.wait()
    row_count, col_count = dims_ref[0, 0], dims_ref[0, 1]
    lines = lax.broadcasted_iota(jnp.int32, (8, 128), 0)
    facts_ref[...] = jnp.where(lines == 1, row_count, jnp.where(lines == 2, col_count, 0)).astype(jnp.float32)
    col_ok = lax.broadcasted_iota(jnp.int32, (step, size), 1) < col_count
    row = lax.broadcasted_iota(jnp.int32, (step, size), 0)
    for n, copy in enumerate(copies):
        copy.wait()
        rows = pl.ds(n * step, step)
        held = jnp.where((row < row_count - n * step) & col_ok, wave_ref[rows], 0.0)
        block = (held * SCALE).astype(jnp.bfloat16)
        for ref in u_refs:
            ref[rows] = block


def pass_kernel(*refs):
    pass


def after(held, first):
    return call(pass_kernel, pltpu.VMEM(held.shape, held.dtype), [AN] * 2, AN, aliases={0: 0})(vmem(held), first)


def near_kernel(size, width, rows, left_hbm, right_hbm, wave_hbm, facts_ref, self_ref, near_ref, out_ref, sums_ref,
                left_far, right_far, left_row, right_row, left_own, right_own, wave_ref, sems, far_sems, row_sems, wave_sem):
    offsets, _, _ = place(size, width)
    wave_copy = pltpu.make_async_copy(wave_hbm.at[0], wave_ref, wave_sem)
    own = fetch(left_hbm, right_hbm, left_own, right_own, sems, [(0, 2), (offsets[0], width)])
    wave_copy.start()
    later = fetch(left_hbm, right_hbm, left_far, right_far, far_sems, [(offsets[1], width)])
    later += fetch(left_hbm, right_hbm, left_row, right_row, row_sems, [(o, width) for o in offsets[2 : 2 + rows]])
    u = self_ref[...].astype(jnp.float32)
    lines = lax.broadcasted_iota(jnp.int32, (8, 128), 0)
    sums = jnp.where(lines == 1, total(u * u), 0.0)
    finish(own[0])
    out_ref[0] = terms(self_ref[...], left_own, right_own, 0, 2)
    finish(own[1])
    out_ref[1] = terms(near_ref[...], left_own, right_own, 2, width)
    wave_copy.wait()
    held = jnp.where(live(facts_ref[...], wave_ref.shape), wave_ref[...], 0.0)
    sums_ref[...] = jnp.where(lines == 0, total(held * held), sums)
    for pair in later:
        finish(pair)


def far_kernel(size, width, left_ref, right_ref, near_part_ref, u_ref, sums_ref, far_ref, out_ref, sum_ref, sums_out_ref):
    _, _, there = place(size, width)
    part = terms(only(there[0], far_ref[...]), left_ref, right_ref, 0, width)
    out_ref[...] = part
    part = near_part_ref[0] + near_part_ref[1] + part
    sum_ref[...] = part
    sums = sums_ref[...]
    square = sums[1:2, 0:1]
    cross = total(u_ref[...].astype(jnp.float32) * part)
    lines = lax.broadcasted_iota(jnp.int32, (8, 128), 0)
    sums_out_ref[...] = jnp.where(lines == 2, jnp.where(square > 0.0, cross / square, 0.0), sums)


def first_kernel(size, width, rows, *refs):
    part_ref, facts_ref, sums_ref, u_ref, left_ref, right_ref = refs[:6]
    row_refs, (out_ref, w_ref, numbers_hbm, numbers_ref, sem) = refs[6 : 6 + rows], refs[6 + rows :]
    _, _, there = place(size, width)
    image = part_ref[...]
    for r, source in enumerate(row_refs):
        piece = terms(only(there[1 + r], source[...]), left_ref, right_ref, r * width, width)
        out_ref[r] = piece
        image = image + piece
    u = u_ref[...].astype(jnp.float32)
    start, square, guess = (sums_ref[n : n + 1, 0:1] for n in range(3))
    rough = jnp.where(live(facts_ref[...], image.shape), image - guess * u, 0.0)
    along, inner = total(u * rough), total(rough * rough)
    shift = jnp.where(square > 0.0, along / square, 0.0)
    rho = guess + shift
    lane = lax.broadcasted_iota(jnp.int32, (1, 128), 1)
    numbers = jnp.zeros((1, 128), jnp.float32)
    for n, value in enumerate((start, square, rho * square, jnp.maximum(inner - shift * along, 0.0), rho)):
        numbers = jnp.where(lane == n, value, numbers)
    for n in range(numbers_ref.shape[0]):
        numbers_ref[n] = numbers
    copy = pltpu.make_async_copy(numbers_ref, numbers_hbm, sem)
    copy.start()
    w_ref[...] = (rough - shift * u).astype(jnp.bfloat16)
    copy.wait()


def image_kernel(size, width, near_ref, far_ref, self_ref, left_hbm, right_hbm, out_ref, left_own, right_own, sems):
    _, _, there = place(size, width)
    own = fetch(left_hbm, right_hbm, left_own, right_own, sems, [(0, 2 + width), (2 + width, width)])
    odd = lax.rem(lax.axis_index("sector"), 2) == 1
    near, far = near_ref[...], only(there[0], far_ref[...])
    finish(own[0])
    image = terms(self_ref[...], left_own, right_own, 0, 2)
    image = image + terms(jnp.where(odd, near, far), left_own, right_own, 2, width)
    finish(own[1])
    out_ref[...] = image + terms(jnp.where(odd, far, near), left_own, right_own, 2 + width, width)


def row_kernel(size, width, rows, part_ref, left_row, right_row, *refs):
    row_refs, (out_ref,) = refs[:rows], refs[rows:]
    _, _, there = place(size, width)
    image = part_ref[...]
    for r, source in enumerate(row_refs):
        image = image + terms(only(there[1 + r], source[...]), left_row, right_row, r * width, width)
    out_ref[...] = image


def second_kernel(size, width, rows, cells, facts_ref, stats_ref, hw_ref, near_part_ref, far_part_ref, row_part_ref,
                  first_hbm, second_hbm, first_ref, second_ref, sems):
    _, partners, _ = place(size, width)
    facts = facts_ref[...]
    stats = stats_ref[:, 0, :]
    sums = jnp.sum(stats, axis=0, keepdims=True)
    start, square, cross, inner = (sums[:, i : i + 1] for i in range(4))
    scale = lax.rsqrt(start / cells + 1e-06) * (1.0 / SCALE)
    rho = cross / square
    gap = stats[:, 4:5] - rho
    residual = inner + jnp.sum(stats[:, 1:2] * gap * gap, axis=0, keepdims=True)
    second_scale = scale * lax.rsqrt(scale * scale * (residual / cells) + 1e-06)
    gaps = [stats_ref[partner, :, 4:5] - rho for partner in partners[: 3 + rows]]
    block = hw_ref.shape[0]
    step = block // HALVES
    col_ok = lax.broadcasted_iota(jnp.int32, (step, block), 1).astype(jnp.float32) < facts[2:3, 0:1]
    row = lax.broadcasted_iota(jnp.int32, (step, block), 0).astype(jnp.float32)
    copies = []
    for n in range(HALVES):
        lines = pl.ds(n * step, step)
        parts = [near_part_ref[0, lines], near_part_ref[1, lines], far_part_ref[lines]]
        parts += [row_part_ref[r, lines] for r in range(rows)]
        cell = (row + n * step < facts[1:2, 0:1]) & col_ok
        image = hw_ref[lines]
        for gap, part in zip(gaps, parts):
            image = image + gap * part
        second_ref[lines] = jnp.where(cell, image, 0.0) * second_scale
        first_ref[lines] = jnp.where(cell, sum(parts[1:], parts[0]), 0.0) * scale
        for e, (source, target) in enumerate(((second_ref, second_hbm), (first_ref, first_hbm))):
            copies.append(pltpu.make_async_copy(source.at[lines], target.at[0, lines], sems.at[n, e]))
            copies[-1].start()
    finish(copies)


def body(wavefunction, sector_dims, left_env, right_env):
    size = lax.axis_size("sector")
    block = wavefunction.shape[1]
    square = (block, block)
    width = (right_env.shape[1] - 2) // 4
    near, row_pairs = swap_pairs(size)
    rows = len(row_pairs)
    cells = float(size * block * block)
    few, every, side, last = ((n,) + square for n in (2 + width, 2 + 2 * width, width, rows * width))
    f32, bf16 = jnp.float32, jnp.bfloat16
    dma = pltpu.SemaphoreType.DMA

    u, far_u, facts = call(
        start_kernel, (pltpu.VMEM(square, bf16),) * 2 + (pltpu.VMEM((8, 128), f32),), [HB, HB], (VM,) * 3,
        [pltpu.VMEM(square, f32), pltpu.SMEM((1, 2), jnp.int32), dma((QUARTERS + 1,))],
    )(hbm(wavefunction), hbm(sector_dims))

    left_env, right_env = hbm(left_env), hbm(right_env)
    u, facts = vmem(u), vmem(facts)
    row_u = [vmem(swap(u, "sector", p)) for p in row_pairs]
    near_u = vmem(swap(u, "sector", near))
    far_u = vmem(far_swap(after(far_u, near_u)))
    near_part, sums, left_far, right_far, left_row, right_row = call(
        functools.partial(near_kernel, size, width, rows),
        (pltpu.VMEM((2,) + square, f32), pltpu.VMEM((8, 128), f32)) + (pltpu.VMEM(side, bf16),) * 2 + (pltpu.VMEM(last, bf16),) * 2,
        [HB] * 3 + [VM] * 3, (VM,) * 6,
        [pltpu.VMEM(few, bf16)] * 2 + [pltpu.VMEM(square, f32), dma((2, 2)), dma((1, 2)), dma((rows, 2)), dma], LONG,
    )(left_env, right_env, hbm(wavefunction), facts, u, near_u)
    near_part, left_row, right_row = vmem(near_part), vmem(left_row), vmem(right_row)
    far_part, part, sums = call(
        functools.partial(far_kernel, size, width), (pltpu.VMEM(square, f32),) * 2 + (pltpu.VMEM((8, 128), f32),),
        [VM] * 6, (VM,) * 3, cost=LONG,
    )(vmem(left_far), vmem(right_far), near_part, u, vmem(sums), far_u)
    far_part = vmem(far_part)
    row_part, w, stats = call(
        functools.partial(first_kernel, size, width, rows),
        (pltpu.VMEM((rows,) + square, f32), pltpu.VMEM(square, bf16), pltpu.HBM((size, 1, 128), f32)),
        [VM] * (6 + rows), (VM, VM, HB), [pltpu.VMEM((size, 1, 128), f32), dma],
    )(vmem(part), facts, vmem(sums), u, left_row, right_row, *row_u)

    w = vmem(w)
    row_w = [vmem(swap(w, "sector", p)) for p in row_pairs]
    near_w = vmem(swap(w, "sector", near))
    far_w = vmem(far_swap(w))
    stats = lax.all_to_all(stats, "sector", 0, 0, tiled=True)
    hw = call(
        functools.partial(image_kernel, size, width), pltpu.VMEM(square, f32), [VM] * 3 + [HB] * 2, VM,
        [pltpu.VMEM(every, bf16)] * 2 + [dma((2, 2))],
    )(near_w, far_w, w, left_env, right_env)
    hw = call(
        functools.partial(row_kernel, size, width, rows), pltpu.VMEM(square, f32), [VM] * (3 + rows), VM,
    )(vmem(hw), left_row, right_row, *row_w)
    return call(
        functools.partial(second_kernel, size, width, rows, cells),
        (jax.ShapeDtypeStruct((1,) + square, f32),) * 2, [VM] * 6, (HB, HB),
        [pltpu.VMEM(square, f32)] * 2 + [dma((HALVES, 2))],
    )(facts, stats, vmem(hw), near_part, far_part, vmem(row_part))


def solution(mesh):
    placed = (
        P(("groups", "sector"), None, None),
        P(("groups", "sector"), None),
        P(("groups", "sector"), None, None, None),
        P(("groups", "sector"), None, None, None),
    )
    return jax.shard_map(
        body,
        mesh=mesh,
        in_specs=placed,
        out_specs=(P(("groups", "sector"), None, None), P(("groups", "sector"), None, None)),
        check_vma=False,
    )
```

```python
import functools

import jax
import jax.numpy as jnp
from jax import lax
from jax.experimental import pallas as pl
from jax.experimental.pallas import tpu as pltpu
from jax.sharding import PartitionSpec as P

QD = 8
SCALE = 1024.0
QUARTERS = 4
HALVES = 2
NT = (((1,), (1,)), ((), ()))
VM = pl.BlockSpec(memory_space=pltpu.VMEM)
HB = pl.BlockSpec(memory_space=pltpu.HBM)
AN = pl.BlockSpec(memory_space=pl.ANY)
COST = pl.CostEstimate(flops=1, bytes_accessed=1, transcendentals=0)
LONG = pl.CostEstimate(flops=4000000000, bytes_accessed=1, transcendentals=0)
PARAMS = pltpu.CompilerParams(vmem_limit_bytes=16 * 1024 * 1024)


def vmem(x):
    return pltpu.with_memory_space_constraint(x, pltpu.VMEM)


def hbm(x):
    return pltpu.with_memory_space_constraint(x, pltpu.HBM)


def call(kernel, out_shape, in_specs, out_specs, scratch=(), cost=COST, aliases={}):
    return pl.pallas_call(
        kernel, out_shape=out_shape, in_specs=in_specs, out_specs=out_specs, scratch_shapes=list(scratch),
        compiler_params=PARAMS, cost_estimate=cost, input_output_aliases=aliases,
    )


def swap(x, axis, pairs):
    to = {a: b for p in pairs for a, b in (p, p[::-1])}
    return lax.ppermute(x, axis, [(s, to.get(s, s)) for s in range(lax.axis_size(axis))])


def swap_pairs(size):
    rows = size // QD
    near = [(s, s + 1) for s in range(0, size, 2)]
    row_even = [(s, s + QD) for r in range(0, rows - 1, 2) for s in range(r * QD, r * QD + QD)]
    row_odd = [(s, s + QD) for r in range(1, rows - 1, 2) for s in range(r * QD, r * QD + QD)]
    return near, [p for p in (row_even, row_odd) if p]


def far_swap(x):
    groups, size = lax.axis_size("groups"), lax.axis_size("sector")
    pairs = []
    for g in range(groups):
        for s in range(size):
            if s % QD == 0 or s % QD == QD - 1:
                to, partner = (g ^ 1 if g ^ 1 < groups else g), s
            else:
                to, partner = g, s + 1 if s % 2 else s - 1
            pairs.append((g * size + s, to * size + partner))
    return lax.ppermute(x, ("groups", "sector"), pairs)


def place(size, width):
    me = lax.axis_index("sector")
    column = lax.rem(me, QD)
    odd = lax.rem(me, 2) == 1
    row_odd = lax.rem(lax.div(me, QD), 2) == 1
    low, high, down, up = 2, 2 + width, 2 + 2 * width, 2 + 3 * width
    offsets = [jnp.where(odd, low, high), jnp.where(odd, high, low),
               jnp.where(row_odd, down, up), jnp.where(row_odd, up, down)]
    partners = [jnp.where(odd, me - 1, me + 1), jnp.where(odd, me + 1, me - 1),
                jnp.where(row_odd, me - QD, me + QD), jnp.where(row_odd, me + QD, me - QD)]
    there = [(column != 0) & (column != QD - 1),
             True if size // QD % 2 == 0 else (partners[2] >= 0) & (partners[2] < size),
             (partners[3] >= 0) & (partners[3] < size)]
    partners = [me] + [jnp.clip(p, 0, size - 1) for p in partners]
    return offsets, partners, there


def live(facts, shape):
    row_ok = lax.broadcasted_iota(jnp.int32, shape, 0).astype(jnp.float32) < facts[1:2, 0:1]
    col_ok = lax.broadcasted_iota(jnp.int32, shape, 1).astype(jnp.float32) < facts[2:3, 0:1]
    return row_ok & col_ok


def total(x):
    return jnp.sum(jnp.sum(x, axis=0, keepdims=True), axis=1, keepdims=True)


def only(there, block):
    return block if there is True else jnp.where(there, block, jnp.zeros_like(block))


def terms(src, left_ref, right_ref, first, count):
    size = src.shape[0]
    right = right_ref[pl.ds(first, count)].reshape(count * size, size)
    partial_t = lax.dot_general(right, src, NT, preferred_element_type=jnp.float32).astype(jnp.bfloat16)
    left = jnp.concatenate([left_ref[first + k] for k in range(count)], axis=1)
    partial_t = jnp.concatenate([partial_t[k * size : (k + 1) * size] for k in range(count)], axis=1)
    return lax.dot_general(left, partial_t, NT, preferred_element_type=jnp.float32)


def fetch(left_hbm, right_hbm, left_ref, right_ref, sems, spans):
    copies = []
    at = 0
    for n, (offset, count) in enumerate(spans):
        pair = [
            pltpu.make_async_copy(source.at[0, pl.ds(offset, count)], target.at[pl.ds(at, count)], sems.at[n, e])
            for e, (source, target) in enumerate(((right_hbm, right_ref), (left_hbm, left_ref)))
        ]
        for copy in pair:
            copy.start()
        copies.append(pair)
        at += count
    return copies


def finish(copies):
    for copy in copies:
        copy.wait()


def start_kernel(wave_hbm, dims_hbm, *refs):
    u_refs, (facts_ref, wave_ref, dims_ref, sems) = refs[:2], refs[2:]
    size = wave_ref.shape[0]
    step = size // QUARTERS
    dims_copy = pltpu.make_async_copy(dims_hbm, dims_ref, sems.at[QUARTERS])
    dims_copy.start()
    copies = [
        pltpu.make_async_copy(wave_hbm.at[0, pl.ds(n * step, step)], wave_ref.at[pl.ds(n * step, step)], sems.at[n])
        for n in range(QUARTERS)
    ]
    for copy in copies:
        copy.start()
    dims_copy.wait()
    row_count, col_count = dims_ref[0, 0], dims_ref[0, 1]
    lines = lax.broadcasted_iota(jnp.int32, (8, 128), 0)
    facts_ref[...] = jnp.where(lines == 1, row_count, jnp.where(lines == 2, col_count, 0)).astype(jnp.float32)
    col_ok = lax.broadcasted_iota(jnp.int32, (step, size), 1) < col_count
    row = lax.broadcasted_iota(jnp.int32, (step, size), 0)
    for n, copy in enumerate(copies):
        copy.wait()
        rows = pl.ds(n * step, step)
        held = jnp.where((row < row_count - n * step) & col_ok, wave_ref[rows], 0.0)
        block = (held * SCALE).astype(jnp.bfloat16)
        for ref in u_refs:
            ref[rows] = block


def pass_kernel(*refs):
    pass


def after(held, first):
    return call(pass_kernel, pltpu.VMEM(held.shape, held.dtype), [AN] * 2, AN, aliases={0: 0})(vmem(held), first)


def near_kernel(size, width, rows, left_hbm, right_hbm, wave_hbm, facts_ref, self_ref, near_ref, out_ref, sums_ref,
                left_far, right_far, left_row, right_row, left_own, right_own, wave_ref, sems, far_sems, row_sems, wave_sem):
    offsets, _, _ = place(size, width)
    wave_copy = pltpu.make_async_copy(wave_hbm.at[0], wave_ref, wave_sem)
    own = fetch(left_hbm, right_hbm, left_own, right_own, sems, [(0, 2), (offsets[0], width)])
    wave_copy.start()
    later = fetch(left_hbm, right_hbm, left_far, right_far, far_sems, [(offsets[1], width)])
    later += fetch(left_hbm, right_hbm, left_row, right_row, row_sems, [(o, width) for o in offsets[2 : 2 + rows]])
    u = self_ref[...].astype(jnp.float32)
    lines = lax.broadcasted_iota(jnp.int32, (8, 128), 0)
    sums = jnp.where(lines == 1, total(u * u), 0.0)
    finish(own[0])
    out_ref[0] = terms(self_ref[...], left_own, right_own, 0, 2)
    finish(own[1])
    out_ref[1] = terms(near_ref[...], left_own, right_own, 2, width)
    wave_copy.wait()
    held = jnp.where(live(facts_ref[...], wave_ref.shape), wave_ref[...], 0.0)
    sums_ref[...] = jnp.where(lines == 0, total(held * held), sums)
    for pair in later:
        finish(pair)


def far_kernel(size, width, left_ref, right_ref, near_part_ref, far_ref, out_ref, sum_ref):
    _, _, there = place(size, width)
    part = terms(only(there[0], far_ref[...]), left_ref, right_ref, 0, width)
    out_ref[...] = part
    sum_ref[...] = near_part_ref[0] + near_part_ref[1] + part


def first_kernel(size, width, rows, *refs):
    part_ref, facts_ref, sums_ref, u_ref, left_ref, right_ref = refs[:6]
    row_refs, (out_ref, w_ref, stats_ref) = refs[6 : 6 + rows], refs[6 + rows :]
    _, _, there = place(size, width)
    image = part_ref[...]
    for r, source in enumerate(row_refs):
        piece = terms(only(there[1 + r], source[...]), left_ref, right_ref, r * width, width)
        out_ref[r] = piece
        image = image + piece
    image = jnp.where(live(facts_ref[...], image.shape), image, 0.0)
    u = u_ref[...].astype(jnp.float32)
    square = sums_ref[1:2, 0:1]
    cross = total(u * image)
    rho = jnp.where(square > 0.0, cross / square, 0.0)
    w = image - rho * u
    w_ref[...] = w.astype(jnp.bfloat16)
    lane = lax.broadcasted_iota(jnp.int32, (1, 128), 1)
    stats = jnp.zeros((1, 128), jnp.float32)
    for n, value in enumerate((sums_ref[0:1, 0:1], square, cross, total(w * w), rho)):
        stats = jnp.where(lane == n, value, stats)
    for n in range(stats_ref.shape[0]):
        stats_ref[n] = stats


def image_kernel(size, width, near_ref, far_ref, self_ref, left_hbm, right_hbm, out_ref, left_own, right_own, sems):
    _, _, there = place(size, width)
    own = fetch(left_hbm, right_hbm, left_own, right_own, sems, [(0, 2 + width), (2 + width, width)])
    odd = lax.rem(lax.axis_index("sector"), 2) == 1
    near, far = near_ref[...], only(there[0], far_ref[...])
    finish(own[0])
    image = terms(self_ref[...], left_own, right_own, 0, 2)
    image = image + terms(jnp.where(odd, near, far), left_own, right_own, 2, width)
    finish(own[1])
    out_ref[...] = image + terms(jnp.where(odd, far, near), left_own, right_own, 2 + width, width)


def row_kernel(size, width, rows, part_ref, left_row, right_row, *refs):
    row_refs, (out_ref,) = refs[:rows], refs[rows:]
    _, _, there = place(size, width)
    image = part_ref[...]
    for r, source in enumerate(row_refs):
        image = image + terms(only(there[1 + r], source[...]), left_row, right_row, r * width, width)
    out_ref[...] = image


def second_kernel(size, width, rows, cells, facts_ref, stats_ref, hw_ref, near_part_ref, far_part_ref, row_part_ref,
                  first_hbm, second_hbm, first_ref, second_ref, sems):
    _, partners, _ = place(size, width)
    facts = facts_ref[...]
    stats = stats_ref[:, 0, :]
    sums = jnp.sum(stats, axis=0, keepdims=True)
    start, square, cross, inner = (sums[:, i : i + 1] for i in range(4))
    scale = lax.rsqrt(start / cells + 1e-06) * (1.0 / SCALE)
    rho = cross / square
    gap = stats[:, 4:5] - rho
    residual = inner + jnp.sum(stats[:, 1:2] * gap * gap, axis=0, keepdims=True)
    second_scale = scale * lax.rsqrt(scale * scale * (residual / cells) + 1e-06)
    gaps = [stats_ref[partner, :, 4:5] - rho for partner in partners[: 3 + rows]]
    block = hw_ref.shape[0]
    step = block // HALVES
    col_ok = lax.broadcasted_iota(jnp.int32, (step, block), 1).astype(jnp.float32) < facts[2:3, 0:1]
    row = lax.broadcasted_iota(jnp.int32, (step, block), 0).astype(jnp.float32)
    copies = []
    for n in range(HALVES):
        lines = pl.ds(n * step, step)
        parts = [near_part_ref[0, lines], near_part_ref[1, lines], far_part_ref[lines]]
        parts += [row_part_ref[r, lines] for r in range(rows)]
        cell = (row + n * step < facts[1:2, 0:1]) & col_ok
        image = hw_ref[lines]
        for gap, part in zip(gaps, parts):
            image = image + gap * part
        second_ref[lines] = jnp.where(cell, image, 0.0) * second_scale
        first_ref[lines] = jnp.where(cell, sum(parts[1:], parts[0]), 0.0) * scale
        for e, (source, target) in enumerate(((second_ref, second_hbm), (first_ref, first_hbm))):
            copies.append(pltpu.make_async_copy(source.at[lines], target.at[0, lines], sems.at[n, e]))
            copies[-1].start()
    finish(copies)


def body(wavefunction, sector_dims, left_env, right_env):
    size = lax.axis_size("sector")
    block = wavefunction.shape[1]
    square = (block, block)
    width = (right_env.shape[1] - 2) // 4
    near, row_pairs = swap_pairs(size)
    rows = len(row_pairs)
    cells = float(size * block * block)
    few, every, side, last = ((n,) + square for n in (2 + width, 2 + 2 * width, width, rows * width))
    f32, bf16 = jnp.float32, jnp.bfloat16
    dma = pltpu.SemaphoreType.DMA

    u, far_u, facts = call(
        start_kernel, (pltpu.VMEM(square, bf16),) * 2 + (pltpu.VMEM((8, 128), f32),), [HB, HB], (VM,) * 3,
        [pltpu.VMEM(square, f32), pltpu.SMEM((1, 2), jnp.int32), dma((QUARTERS + 1,))],
    )(hbm(wavefunction), hbm(sector_dims))

    left_env, right_env = hbm(left_env), hbm(right_env)
    u, facts = vmem(u), vmem(facts)
    row_u = [vmem(swap(u, "sector", p)) for p in row_pairs]
    near_u = vmem(swap(u, "sector", near))
    far_u = vmem(far_swap(far_u))
    near_part, sums, left_far, right_far, left_row, right_row = call(
        functools.partial(near_kernel, size, width, rows),
        (pltpu.VMEM((2,) + square, f32), pltpu.VMEM((8, 128), f32)) + (pltpu.VMEM(side, bf16),) * 2 + (pltpu.VMEM(last, bf16),) * 2,
        [HB] * 3 + [VM] * 3, (VM,) * 6,
        [pltpu.VMEM(few, bf16)] * 2 + [pltpu.VMEM(square, f32), dma((2, 2)), dma((1, 2)), dma((rows, 2)), dma], LONG,
    )(left_env, right_env, hbm(wavefunction), facts, u, near_u)
    near_part, left_row, right_row = vmem(near_part), vmem(left_row), vmem(right_row)
    far_part, part = call(
        functools.partial(far_kernel, size, width), (pltpu.VMEM(square, f32),) * 2, [VM] * 4, (VM,) * 2, cost=LONG,
    )(vmem(left_far), vmem(right_far), near_part, far_u)
    far_part = vmem(far_part)
    row_part, w, stats = call(
        functools.partial(first_kernel, size, width, rows),
        (pltpu.VMEM((rows,) + square, f32), pltpu.VMEM(square, bf16), jax.ShapeDtypeStruct((size, 1, 128), f32)),
        [VM] * (6 + rows), (VM,) * 3,
    )(vmem(part), facts, vmem(sums), u, left_row, right_row, *row_u)

    w = vmem(w)
    row_w = [vmem(swap(w, "sector", p)) for p in row_pairs]
    near_w = vmem(swap(w, "sector", near))
    far_w = vmem(far_swap(w))
    stats = lax.all_to_all(stats, "sector", 0, 0, tiled=True)
    hw = call(
        functools.partial(image_kernel, size, width), pltpu.VMEM(square, f32), [VM] * 3 + [HB] * 2, VM,
        [pltpu.VMEM(every, bf16)] * 2 + [dma((2, 2))],
    )(near_w, far_w, w, left_env, right_env)
    hw = call(
        functools.partial(row_kernel, size, width, rows), pltpu.VMEM(square, f32), [VM] * (3 + rows), VM,
    )(vmem(hw), left_row, right_row, *row_w)
    return call(
        functools.partial(second_kernel, size, width, rows, cells),
        (jax.ShapeDtypeStruct((1,) + square, f32),) * 2, [VM] * 6, (HB, HB),
        [pltpu.VMEM(square, f32)] * 2 + [dma((HALVES, 2))],
    )(facts, stats, vmem(hw), near_part, far_part, vmem(row_part))


def solution(mesh):
    placed = (
        P(("groups", "sector"), None, None),
        P(("groups", "sector"), None),
        P(("groups", "sector"), None, None, None),
        P(("groups", "sector"), None, None, None),
    )
    return jax.shard_map(
        body,
        mesh=mesh,
        in_specs=placed,
        out_specs=(P(("groups", "sector"), None, None), P(("groups", "sector"), None, None)),
        check_vma=False,
    )
```
